32 devices in a mesh: row: 8 (over z, x), col: 4 (over y, core).
Axes of the slice: x: 2, y: 2, z: 4, core: 2. Of those that a mesh axis runs over, the one named last changes fastest.
Arguments:
- hidden_in: bfloat16 [16384, 1024], P('row', 'col'), may hold values from -6 to 6
- out_grad: bfloat16 [16384, 1024], P('row', 'col'), may hold values from -6 to 6
- lengths: int32 [8], P('row'), may hold values from 512 to 2048, as said below
- global_blocks: int32 [8, 2], P('row'), may hold values from 0 to 15, as said below
- rand_blocks: int32 [8, 32, 16, 3], P('row', None, 'col'), may hold values from 0 to 31, as said below
- w_query: float32 [1024, 1024], P('row', 'col'), may hold values from -0.1875 to 0.1875
- b_query: float32 [1024], replicated, may hold values from -3 to 3
- w_key: float32 [1024, 1024], P('row', 'col'), may hold values from -0.1875 to 0.1875
- w_value: float32 [1024, 1024], P('row', 'col'), may hold values from -0.1875 to 0.1875
- b_value: float32 [1024], replicated, may hold values from -3 to 3
- w_out: float32 [1024, 1024], P('col', 'row'), may hold values from -0.75 to 0.75
- b_out: float32 [1024], replicated, may hold values from -3 to 3
- ln1_gain: float32 [1024], replicated, may hold values from 0.25 to 1.75
- ln1_bias: float32 [1024], replicated, may hold values from -3 to 3
- w_up: float32 [1024, 4096], P('row', 'col'), may hold values from -0.1875 to 0.1875
- b_up: float32 [4096], replicated, may hold values from -3 to 3
- w_down: float32 [4096, 1024], P('col', 'row'), may hold values from -0.1875 to 0.1875
- b_down: float32 [1024], replicated, may hold values from -3 to 3
- ln2_gain: float32 [1024], replicated, may hold values from 0.25 to 1.75
- ln2_bias: float32 [1024], replicated, may hold values from -3 to 3
Outputs:
- layer_out: bfloat16 [16384, 1024], P('row', 'col')
- grad_input: bfloat16 [16384, 1024], P('row', 'col')
- grad_w_query: float32 [1024, 1024], P('row', 'col')
- grad_b_query: float32 [1024], replicated
- grad_w_key: float32 [1024, 1024], P('row', 'col')
- grad_w_value: float32 [1024, 1024], P('row', 'col')
- grad_b_value: float32 [1024], replicated
- grad_w_out: float32 [1024, 1024], P('col', 'row')
- grad_b_out: float32 [1024], replicated
- grad_ln1_gain: float32 [1024], replicated
- grad_ln1_bias: float32 [1024], replicated
- grad_w_up: float32 [1024, 4096], P('row', 'col')
- grad_b_up: float32 [4096], replicated
- grad_w_down: float32 [4096, 1024], P('col', 'row')
- grad_b_down: float32 [1024], replicated
- grad_ln2_gain: float32 [1024], replicated
- grad_ln2_bias: float32 [1024], replicated
The draws below stay inside these ranges and needn't reach their ends.
Inputs may be any that keep to these rules, and one draw needn't show every extreme that they name: `lengths`: tokens after the valid ones of a sequence are padding; some sequence is full and some holds 512 valid tokens. `global_blocks`: two different blocks of each sequence, both among its first 16 blocks. `rand_blocks`: for query block i and a head: three different blocks, none of i - 1, i, i + 1 or the sequence's global blocks; they may lie in padding.
All inputs are finite; a program needn't handle non-finite values.
Results may differ from the reference program's by a relative error of at most 0.018.
The reference program's roundings to bfloat16 on the way count: a program that leaves them out, or rounds other values in their place, can miss the bound.
Values may be sent and summed in bfloat16 or wider, within the bound.
A program may use at most 256 MiB of HBM per device.

```python
import math
import jax
import jax.numpy as jnp
from jax import lax

D = 1024
H = 16
DH = 64
FF = 4096
BLK = 64
SEQ = 2048
SLOTS = 8
NB = 32
TOKENS = 16384


def draw_lengths(key, part):
    drawn = jax.random.randint(key, (SLOTS,), SEQ // 4, SEQ + 1)
    shuffled = jax.random.permutation(jax.random.fold_in(key, 1), SLOTS)
    drawn = drawn.at[shuffled[0]].set(SEQ)
    drawn = drawn.at[shuffled[1]].set(SEQ // 4)
    return drawn.astype(jnp.int32)


def pick_globals(key):
    base_key = jax.random.fold_in(key, 7)
    first_ids = jax.random.randint(jax.random.fold_in(base_key, 1), (SLOTS,), 0, NB // 2)
    offset_ids = jax.random.randint(jax.random.fold_in(base_key, 2), (SLOTS,), 1, NB // 2)
    second_ids = (first_ids + offset_ids) % (NB // 2)
    return jnp.stack([first_ids, second_ids], axis=1).astype(jnp.int32)


def draw_global_blocks(key, part):
    return pick_globals(key)


def draw_rand_blocks(key, part):
    global_ids = pick_globals(key)
    scores = jax.random.randint(jax.random.fold_in(key, 11), (SLOTS, NB, H, NB), 0, 2 ** 16)
    blocks = jnp.arange(NB, dtype=jnp.int32)
    scores = scores * NB + blocks
    nearby = jnp.abs(blocks[None, :] - blocks[:, None]) <= 1
    is_global = (blocks[None, :] == global_ids[:, 0:1]) | (blocks[None, :] == global_ids[:, 1:2])
    banned = nearby[None, :, None, :] | is_global[:, None, None, :]
    scores = jnp.where(banned, -1, scores)
    return lax.top_k(scores, 3)[1].astype(jnp.int32)


def steps_of(key, extent, pieces, least, high):
    loudness = 1.0
    for dim, blocks in pieces:
        steps = jax.random.uniform(jax.random.fold_in(jax.random.fold_in(key, 6), dim), (blocks,), jnp.float32, least / len(pieces), high / len(pieces))
        loudness = loudness * jnp.repeat(jnp.exp(steps), extent[dim] // blocks).reshape((-1,) + (1,) * (len(extent) - 1 - dim))
    return loudness


def normal_values(key, dims, width, most, shards=(), held_as=jnp.bfloat16):
    values = width * jax.random.normal(key, dims, jnp.float32)
    if shards:
        values = values * steps_of(key, dims, shards, -0.22, 0.18)
    return jnp.clip(values, -most, most).astype(held_as)


def setup_inputs(seed: int = 0) -> dict:
    keys = jax.random.split(jax.random.key(seed), 21)
    return {
        "hidden_in": normal_values(keys[0], (TOKENS, D), 1.0, 6.0, ((0, 8), (1, 4))),
        "out_grad": normal_values(keys[1], (TOKENS, D), 1.0, 6.0, ((0, 8), (1, 4))),
        "lengths": draw_lengths(jax.random.fold_in(keys[20], 71), 0),
        "global_blocks": draw_global_blocks(jax.random.fold_in(keys[20], 71), 0),
        "rand_blocks": draw_rand_blocks(jax.random.fold_in(keys[20], 71), 0),
        "w_query": normal_values(keys[5], (D, D), D ** -0.5, 0.1875, ((0, 8), (1, 4)), jnp.float32),
        "b_query": normal_values(keys[6], (D,), 0.4, 3.0, (), jnp.float32),
        "w_key": normal_values(keys[7], (D, D), D ** -0.5, 0.1875, ((0, 8), (1, 4)), jnp.float32),
        "w_value": normal_values(keys[8], (D, D), D ** -0.5, 0.1875, ((0, 8), (1, 4)), jnp.float32),
        "b_value": normal_values(keys[9], (D,), 0.5, 3.0, (), jnp.float32),
        "w_out": normal_values(keys[10], (D, D), (D // 16) ** -0.5, 0.75, ((0, 4), (1, 8)), jnp.float32),
        "b_out": normal_values(keys[11], (D,), 0.5, 3.0, (), jnp.float32),
        "ln1_gain": jnp.clip(1.0 + 0.15 * jax.random.normal(keys[12], (D,), jnp.float32), 0.25, 1.75),
        "ln1_bias": normal_values(keys[13], (D,), 0.4, 3.0, (), jnp.float32),
        "w_up": normal_values(keys[14], (D, FF), D ** -0.5, 0.1875, ((0, 8), (1, 4)), jnp.float32),
        "b_up": normal_values(keys[15], (FF,), 0.5, 3.0, (), jnp.float32),
        "w_down": normal_values(keys[16], (FF, D), (FF // 4) ** -0.5, 0.1875, ((0, 4), (1, 8)), jnp.float32),
        "b_down": normal_values(keys[17], (D,), 0.5, 3.0, (), jnp.float32),
        "ln2_gain": jnp.clip(1.0 + 0.15 * jax.random.normal(keys[18], (D,), jnp.float32), 0.25, 1.75),
        "ln2_bias": normal_values(keys[19], (D,), 0.4, 3.0, (), jnp.float32),
    }


@jax.custom_vjp
def low(v):
    return lax.optimization_barrier(v.astype(jnp.bfloat16)).astype(jnp.float32)

@jax.custom_vjp
def low_back(v):
    return v

def low_keep(v):
    return (low(v), None)

def low_pass(kept, grad):
    return (grad,)

def back_keep(v):
    return (v, None)

def back_low(kept, grad):
    return (low(grad),)
low.defvjp(low_keep, low_pass)
low_back.defvjp(back_keep, back_low)
epsilon = 1e-06
precise = lax.Precision.HIGHEST

def matmul(left, right):
    return jnp.dot(left, right, precision=precise, preferred_element_type=jnp.float32)

def gelu_tanh(values_in):
    return jax.nn.gelu(values_in, approximate=True)

def layout(length, global_ids, random_ids, num_blocks, head_count):
    blocks = jnp.arange(num_blocks, dtype=jnp.int32)
    nearby_raw = blocks[:, None] + jnp.arange(-1, 2, dtype=jnp.int32)[None, :]
    near_ok = (nearby_raw >= 0) & (nearby_raw < num_blocks)
    nearby = jnp.clip(nearby_raw, 0, num_blocks - 1)
    global_rows = jnp.broadcast_to(global_ids[None, :], (num_blocks, 2))
    global_ok = jnp.all(global_rows[:, :, None] != nearby_raw[:, None, :], axis=2)
    common = jnp.concatenate([nearby, global_rows], axis=1)
    common_ok = jnp.concatenate([near_ok, global_ok], axis=1)
    key_blocks = jnp.concatenate([jnp.broadcast_to(common[:, None, :], (num_blocks, head_count, 5)), random_ids.astype(jnp.int32)], axis=2)
    block_ok = jnp.concatenate([jnp.broadcast_to(common_ok[:, None, :], (num_blocks, head_count, 5)), jnp.ones((num_blocks, head_count, 3), jnp.bool_)], axis=2)
    positions = key_blocks[:, :, :, None] * BLK + jnp.arange(BLK, dtype=jnp.int32)
    allowed = block_ok[:, :, :, None] & (positions < length)
    return (key_blocks, allowed.reshape(num_blocks, head_count, 8 * BLK))

def take_blocks(rows, key_blocks):
    num_blocks = key_blocks.shape[0]
    head_count = key_blocks.shape[1]
    arranged = rows.reshape(num_blocks, BLK, head_count, DH).transpose(2, 0, 1, 3)
    head_ids = jnp.arange(head_count)[None, :, None]
    return arranged[head_ids, key_blocks].reshape(num_blocks, head_count, 8 * BLK, DH)

def attention(queries, key_rows, value_rows, key_blocks, allowed):
    num_blocks = key_blocks.shape[0]
    head_count = key_blocks.shape[1]
    factor = 1.0 / math.sqrt(DH)
    grouped = queries.reshape(num_blocks, BLK, head_count, DH).transpose(0, 2, 1, 3)
    picked_keys = take_blocks(key_rows, key_blocks)
    picked_values = take_blocks(value_rows, key_blocks)
    scores = low_back(jnp.einsum('nhqd,nhkd->nhqk', grouped, picked_keys, precision=precise) * factor)
    scores = jnp.where(allowed[:, :, None, :], scores, -1e+30)
    highest = lax.optimization_barrier(jnp.max(scores, axis=3, keepdims=True))
    exponent = jnp.exp(scores - highest)
    attn_probs = exponent / lax.optimization_barrier(jnp.sum(exponent, axis=3, keepdims=True))
    context = jnp.einsum('nhqk,nhkd->nhqd', low(attn_probs), picked_values, precision=precise)
    return context.transpose(0, 2, 1, 3).reshape(num_blocks * BLK, head_count * DH)

def layer_norm(summed, gain_vec, offset_vec):
    average = lax.optimization_barrier(jnp.mean(summed, axis=1, keepdims=True))
    squares = lax.optimization_barrier(jnp.mean(summed * summed, axis=1, keepdims=True))
    inv_std = lax.rsqrt(squares - average * average + epsilon)
    return (summed - average) * inv_std * gain_vec + offset_vec

def forward(inputs, params, length, global_ids, random_ids):
    w_query, b_query, w_key, w_value, b_value, w_out, b_out, ln1_gain, ln1_bias, w_up, b_up, w_down, b_down, ln2_gain, ln2_bias = params
    key_blocks, allowed = layout(length, global_ids, random_ids, NB, H)
    queries = low_back(low(matmul(inputs, low(w_query)) + b_query))
    key_rows = low_back(low(matmul(inputs, low(w_key))))
    value_rows = low_back(low(matmul(inputs, low(w_value)) + b_value))
    context = low_back(low(attention(queries, key_rows, value_rows, key_blocks, allowed)))
    attn_out = low_back(matmul(context, low(w_out)) + b_out)
    normed1 = layer_norm(inputs + attn_out, ln1_gain, ln1_bias)
    pre_act = low_back(matmul(low(normed1), low(w_up)) + b_up)
    hidden = low(gelu_tanh(pre_act))
    ffn_out = low_back(matmul(hidden, low(w_down)) + b_down)
    normed2 = layer_norm(normed1 + ffn_out, ln2_gain, ln2_bias)
    valid_rows = (jnp.arange(SEQ) < length)[:, None]
    return jnp.where(valid_rows, normed2, 0.0)

def reference(hidden_in, out_grad, lengths, global_blocks, rand_blocks, w_query, b_query, w_key, w_value, b_value, w_out, b_out, ln1_gain, ln1_bias, w_up, b_up, w_down, b_down, ln2_gain, ln2_bias):
    params = (w_query, b_query, w_key, w_value, b_value, w_out, b_out, ln1_gain, ln1_bias, w_up, b_up, w_down, b_down, ln2_gain, ln2_bias)
    inputs = hidden_in.astype(jnp.float32).reshape(SLOTS, SEQ, D)
    grads_out = out_grad.astype(jnp.float32).reshape(SLOTS, SEQ, D)

    def per_slot(totals, element):
        slot_in, slot_grad, length, global_ids, random_ids = element

        def run(values_in, weights):
            return forward(values_in, weights, length, global_ids, random_ids)
        result, pullback = jax.vjp(run, slot_in, params)
        grad_in, grad_params = pullback(slot_grad)
        totals = jax.tree.map(lambda former, latter: former + latter, totals, grad_params)
        return (totals, (result.astype(jnp.bfloat16), grad_in.astype(jnp.bfloat16)))
    zero_grads = jax.tree.map(jnp.zeros_like, params)
    totals, (results, grad_ins) = lax.scan(per_slot, zero_grads, (inputs, grads_out, lengths, global_blocks, rand_blocks))
    return (results.reshape(TOKENS, D), grad_ins.reshape(TOKENS, D), totals[0], totals[1], totals[2], totals[3], totals[4], totals[5], totals[6], totals[7], totals[8], totals[9], totals[10], totals[11], totals[12], totals[13], totals[14])
```

```python
import functools
import math

import jax
import jax.numpy as jnp
from jax import lax
from jax.experimental import pallas as pl
from jax.experimental.pallas import tpu as pltpu
from jax.sharding import PartitionSpec as P

DH = 64
BLK = 64


epsilon = 1e-06


def gelu_tanh(values_in):
    return jax.nn.gelu(values_in, approximate=True)


def lane_heads(rows, width):
    return lax.broadcasted_iota(jnp.int32, (rows, width), 1) // DH


def by_diagonal(rows, width):
    lane_head = lane_heads(BLK, width)
    zero = jnp.zeros_like(rows)
    return jnp.concatenate(
        [jnp.where(lane_head == head, rows, zero) for head in range(width // DH)], axis=0
    )


def from_diagonal(square, width):
    lane_head = lane_heads(BLK, width)
    result = jnp.zeros((BLK, width), jnp.float32)
    for head in range(width // DH):
        result = jnp.where(lane_head == head, square[head * BLK : (head + 1) * BLK, :], result)
    return result


def slot_starts(step, num_blocks, head_count, globals_ref, random_ref):
    shared = [
        jnp.maximum(step - 1, 0),
        step,
        jnp.minimum(step + 1, num_blocks - 1),
        globals_ref[0],
        globals_ref[1],
    ]
    base = step * (head_count * 3)
    apart = [
        [random_ref[base + head * 3 + slot] for head in range(head_count)] for slot in range(3)
    ]
    at = lambda block: pl.multiple_of(block * BLK, BLK)
    return [at(block) for block in shared], [[at(block) for block in row] for row in apart]


def lane_groups(head_count):
    per_group = min(128 // DH, head_count)
    return [
        (first * DH, per_group * DH, list(range(first, first + per_group)))
        for first in range(0, head_count, per_group)
    ]


def picked_rows(rows_ref, shared, apart, head_count):
    pieces = [rows_ref[pl.ds(start, BLK), :] for start in shared]
    for starts in apart:
        groups = []
        for lane, width, heads in lane_groups(head_count):
            lane_head = lane_heads(BLK, width)
            piece = rows_ref[pl.ds(starts[heads[0]], BLK), lane : lane + width]
            for place, head in enumerate(heads[1:], 1):
                other = rows_ref[pl.ds(starts[head], BLK), lane : lane + width]
                piece = jnp.where(lane_head >= place, other, piece)
            groups.append(piece)
        pieces.append(jnp.concatenate(groups, axis=1) if len(groups) > 1 else groups[0])
    return jnp.concatenate(pieces, axis=0)


def put_rows(sums_ref, values_in, shared, apart, head_count):
    for slot, start in enumerate(shared):
        sums_ref[pl.ds(start, BLK), :] += values_in[slot * BLK : (slot + 1) * BLK, :]
    for slot, starts in enumerate(apart, len(shared)):
        rows = values_in[slot * BLK : (slot + 1) * BLK, :]
        for lane, width, heads in lane_groups(head_count):
            lane_head = lane_heads(BLK, width)
            for place, head in enumerate(heads):
                sums_ref[pl.ds(starts[head], BLK), lane : lane + width] += jnp.where(
                    lane_head == place, rows[:, lane : lane + width], 0.0
                )


def masked_scores(picked_keys, grouped, limits_ref, step, width):
    scores = lax.dot_general(
        picked_keys, grouped, (((1,), (1,)), ((), ())), preferred_element_type=jnp.float32
    )
    row = lax.broadcasted_iota(jnp.int32, (BLK, width), 0)
    return [
        jnp.where(
            row < limits_ref[step, slot : slot + 1, :],
            scores[slot * BLK : (slot + 1) * BLK, :],
            -1e30,
        )
        for slot in range(8)
    ]


def attend_kernel(
    head_count,
    unroll,
    globals_ref,
    random_ref,
    limits_ref,
    queries_ref,
    keys_ref,
    values_ref,
    context_ref,
    highest_ref,
    scale_ref,
):
    width = head_count * DH
    num_blocks = queries_ref.shape[0] // BLK

    def one_block(step):
        shared, apart = slot_starts(step, num_blocks, head_count, globals_ref, random_ref)
        own = pl.ds(pl.multiple_of(step * BLK, BLK), BLK)
        grouped = by_diagonal(queries_ref[own, :] * jnp.bfloat16(1.0 / math.sqrt(DH)), width)
        scores = masked_scores(
            picked_rows(keys_ref, shared, apart, head_count), grouped, limits_ref, step, width
        )
        highest = jnp.max(functools.reduce(jnp.maximum, scores), axis=0, keepdims=True)
        exponent = [jnp.exp(piece - highest) for piece in scores]
        denominator = jnp.sum(sum(exponent[1:], exponent[0]), axis=0, keepdims=True)
        scale = 1.0 / denominator
        attn_probs = jnp.concatenate(
            [(piece * scale).astype(jnp.bfloat16) for piece in exponent], axis=0
        )
        square = lax.dot_general(
            attn_probs,
            picked_rows(values_ref, shared, apart, head_count),
            (((0,), (0,)), ((), ())),
            preferred_element_type=jnp.float32,
        )
        context_ref[own, :] = from_diagonal(square, width).astype(jnp.bfloat16)
        highest_ref[step] = highest
        scale_ref[step] = scale

    @pl.loop(0, num_blocks // unroll)
    def _(turn):
        for place in range(unroll):
            one_block(turn * unroll + place)


def attend_back_kernel(
    head_count,
    unroll,
    globals_ref,
    random_ref,
    limits_ref,
    queries_ref,
    keys_ref,
    values_ref,
    grads_ref,
    highest_ref,
    scale_ref,
    query_grad_ref,
    key_grad_ref,
    value_grad_ref,
    key_sums,
    value_sums,
):
    width = head_count * DH
    num_blocks = queries_ref.shape[0] // BLK
    factor = 1.0 / math.sqrt(DH)
    key_sums[...] = jnp.zeros_like(key_sums)
    value_sums[...] = jnp.zeros_like(value_sums)

    def one_block(step):
        shared, apart = slot_starts(step, num_blocks, head_count, globals_ref, random_ref)
        own = pl.ds(pl.multiple_of(step * BLK, BLK), BLK)
        grouped = by_diagonal(queries_ref[own, :] * jnp.bfloat16(factor), width)
        grouped_grad = by_diagonal(grads_ref[own, :], width)
        picked_keys = picked_rows(keys_ref, shared, apart, head_count)
        picked_values = picked_rows(values_ref, shared, apart, head_count)
        scores = masked_scores(picked_keys, grouped, limits_ref, step, width)
        highest = highest_ref[step]
        scale = scale_ref[step]
        attn_probs = [jnp.exp(piece - highest) * scale for piece in scores]
        prob_grad = lax.dot_general(
            picked_values,
            grouped_grad,
            (((1,), (1,)), ((), ())),
            preferred_element_type=jnp.float32,
        )
        prob_grads = [prob_grad[slot * BLK : (slot + 1) * BLK, :] for slot in range(8)]
        products = [left * right for left, right in zip(attn_probs, prob_grads)]
        total = jnp.sum(sum(products[1:], products[0]), axis=0, keepdims=True)
        score_grad = jnp.concatenate(
            [
                (left * (right - total)).astype(jnp.bfloat16)
                for left, right in zip(attn_probs, prob_grads)
            ],
            axis=0,
        )
        probs_low = jnp.concatenate([piece.astype(jnp.bfloat16) for piece in attn_probs], axis=0)
        square = lax.dot_general(
            score_grad, picked_keys, (((0,), (0,)), ((), ())), preferred_element_type=jnp.float32
        )
        query_grad_ref[own, :] = (from_diagonal(square, width) * factor).astype(jnp.bfloat16)
        key_part = jnp.dot(score_grad, grouped, preferred_element_type=jnp.float32)
        value_part = jnp.dot(probs_low, grouped_grad, preferred_element_type=jnp.float32)
        put_rows(key_sums, key_part, shared, apart, head_count)
        put_rows(value_sums, value_part, shared, apart, head_count)

    @pl.loop(0, num_blocks // unroll)
    def _(turn):
        for place in range(unroll):
            one_block(turn * unroll + place)

    key_grad_ref[...] = key_sums[...].astype(jnp.bfloat16)
    value_grad_ref[...] = value_sums[...].astype(jnp.bfloat16)


def limits_of(length, global_ids, random_ids, num_blocks, head_count):
    blocks = jnp.arange(num_blocks, dtype=jnp.int32)
    nearby_raw = blocks[:, None] + jnp.arange(-1, 2, dtype=jnp.int32)[None, :]
    near_ok = (nearby_raw >= 0) & (nearby_raw < num_blocks)
    global_rows = jnp.broadcast_to(global_ids[None, :], (num_blocks, 2))
    global_ok = jnp.all(global_rows[:, :, None] != nearby_raw[:, None, :], axis=2)
    common = jnp.concatenate([nearby_raw, global_rows], axis=1)
    common_ok = jnp.concatenate([near_ok, global_ok], axis=1)
    common_limit = jnp.where(common_ok, length - common * BLK, 0)
    random_limit = jnp.transpose(length - random_ids * BLK, (0, 2, 1))
    return jnp.concatenate(
        [
            jnp.broadcast_to(common_limit[:, :, None], (num_blocks, 5, head_count * DH)),
            jnp.repeat(random_limit, DH, axis=2),
        ],
        axis=1,
    )


VMEM = pl.BlockSpec(memory_space=pltpu.VMEM)
SMEM = pl.BlockSpec(memory_space=pltpu.SMEM)


def attend(queries, key_rows, value_rows, tables):
    seq_len, width = queries.shape
    head_count = width // DH
    num_blocks = seq_len // BLK
    stat = jax.ShapeDtypeStruct((num_blocks, 1, width), jnp.float32)
    return pl.pallas_call(
        functools.partial(attend_kernel, head_count, 2),
        out_shape=(jax.ShapeDtypeStruct((seq_len, width), jnp.bfloat16), stat, stat),
        in_specs=[SMEM] * 2 + [VMEM] * 4,
        out_specs=[VMEM] * 3,
        compiler_params=pltpu.CompilerParams(vmem_limit_bytes=32 * 1024 * 1024),
        cost_estimate=pl.CostEstimate(
            flops=4 * seq_len * 512 * width * head_count,
            bytes_accessed=8 * seq_len * width,
            transcendentals=seq_len * 512 * head_count,
        ),
    )(*tables, queries, key_rows, value_rows)


def attend_back(queries, key_rows, value_rows, tables, stats, context_grad):
    seq_len, width = queries.shape
    head_count = width // DH
    grad = jax.ShapeDtypeStruct((seq_len, width), jnp.bfloat16)
    return pl.pallas_call(
        functools.partial(attend_back_kernel, head_count, 2),
        out_shape=(grad, grad, grad),
        in_specs=[SMEM] * 2 + [VMEM] * 7,
        out_specs=[VMEM] * 3,
        scratch_shapes=[pltpu.VMEM((seq_len, width), jnp.float32)] * 2,
        compiler_params=pltpu.CompilerParams(vmem_limit_bytes=40 * 1024 * 1024),
        cost_estimate=pl.CostEstimate(
            flops=10 * seq_len * 512 * width * head_count,
            bytes_accessed=14 * seq_len * width,
            transcendentals=seq_len * 512 * head_count,
        ),
    )(*tables, queries, key_rows, value_rows, context_grad, *stats)


def spread(portion):
    return lax.all_gather(portion, "col", axis=0, tiled=True)


def reduce_tokens(partial_value):
    return lax.psum_scatter(
        partial_value.astype(jnp.bfloat16), "col", scatter_dimension=0, tiled=True
    ).astype(jnp.float32)


def to_tokens(portion):
    return lax.all_to_all(portion, "col", split_axis=0, concat_axis=1, tiled=True)


def to_features(portion):
    return lax.all_to_all(portion, "col", split_axis=1, concat_axis=0, tiled=True)


def layer_norm(summed, gain_vec, offset_vec):
    average = jnp.mean(summed, axis=1, keepdims=True)
    squares = jnp.mean(summed * summed, axis=1, keepdims=True)
    inv_std = lax.rsqrt(squares - average * average + epsilon)
    normed = (summed - average) * inv_std
    return (normed * gain_vec + offset_vec, normed, inv_std)


def norm_back(upstream, normed, inv_std, gain_vec):
    scaled = upstream * gain_vec
    left = jnp.mean(scaled, axis=1, keepdims=True)
    right = jnp.mean(scaled * normed, axis=1, keepdims=True)
    result = inv_std * (scaled - left - normed * right)
    return (result, jnp.sum(upstream * normed, axis=0), jnp.sum(upstream, axis=0))


def into_full(portion, start_at, full_len):
    return lax.dynamic_update_slice_in_dim(
        jnp.zeros((full_len,), jnp.float32), portion, start_at, 0
    )


def dot(left, right):
    return jnp.dot(left, right, preferred_element_type=jnp.float32)


def dot_nt(left, right):
    return lax.dot_general(
        left, right, (((1,), (1,)), ((), ())), preferred_element_type=jnp.float32
    )


def dot_tn(left, right):
    return lax.dot_general(
        left, right, (((0,), (0,)), ((), ())), preferred_element_type=jnp.float32
    )


def on_device(
    hidden_in,
    out_grad,
    lengths,
    global_blocks,
    rand_blocks,
    w_query,
    b_query,
    w_key,
    w_value,
    b_value,
    w_out,
    b_out,
    ln1_gain,
    ln1_bias,
    w_up,
    b_up,
    w_down,
    b_down,
    ln2_gain,
    ln2_bias,
):
    low = jnp.bfloat16
    seq_len = hidden_in.shape[0]
    feat_cols = hidden_in.shape[1]
    unit_cols = w_up.shape[1]
    cols = lax.axis_size("col")
    features_all = feat_cols * cols
    units_all = unit_cols * cols
    num_blocks = seq_len // BLK
    head_count = feat_cols // DH
    own_len = seq_len // cols
    column = lax.axis_index("col")
    feat_start = column * feat_cols
    unit_start = column * unit_cols
    own_start = column * own_len
    length = lengths[0]
    tables = (
        global_blocks.reshape(-1),
        rand_blocks.reshape(-1),
        limits_of(length, global_blocks[0], rand_blocks[0], num_blocks, head_count),
    )
    full_qkv = lax.all_gather(
        jnp.concatenate([w_query.astype(low), w_key.astype(low), w_value.astype(low)], axis=1),
        "row",
        axis=0,
        tiled=True,
    )
    features = lax.all_gather(hidden_in, "col", axis=1, tiled=True)
    full_out = lax.all_gather(w_out.astype(low).T, "row", axis=0, tiled=True)
    full_up = lax.all_gather(w_up.astype(low), "row", axis=0, tiled=True)
    full_down = lax.all_gather(w_down.astype(low).T, "row", axis=0, tiled=True)
    own_features = lax.dynamic_slice_in_dim(features, own_start, own_len, 0).astype(jnp.float32)
    own_valid = (own_start + jnp.arange(own_len) < length)[:, None]
    upstream = jnp.where(own_valid, to_tokens(out_grad).astype(jnp.float32), 0.0)

    full_query = full_qkv[:, :feat_cols]
    full_key = full_qkv[:, feat_cols : 2 * feat_cols]
    full_value = full_qkv[:, 2 * feat_cols :]
    queries = (
        dot(features, full_query) + lax.dynamic_slice_in_dim(b_query, feat_start, feat_cols)
    ).astype(low)
    key_rows = dot(features, full_key).astype(low)
    value_rows = (
        dot(features, full_value) + lax.dynamic_slice_in_dim(b_value, feat_start, feat_cols)
    ).astype(low)
    context, *stats = attend(queries, key_rows, value_rows, tables)

    summed1 = own_features + reduce_tokens(dot_nt(context, full_out)) + b_out
    normed1, unit1, inv_std1 = layer_norm(summed1, ln1_gain, ln1_bias)
    normed1_full = spread(normed1.astype(low))
    pre_act = dot(normed1_full, full_up) + lax.dynamic_slice_in_dim(b_up, unit_start, unit_cols)
    activated, gelu_back = jax.vjp(gelu_tanh, pre_act)
    hidden = activated.astype(low)
    summed2 = normed1 + reduce_tokens(dot_nt(hidden, full_down)) + b_down
    normed2, unit2, inv_std2 = layer_norm(summed2, ln2_gain, ln2_bias)
    layer_out = to_features(jnp.where(own_valid, normed2, 0.0).astype(low))

    ffn_grad, gain2_grad, shift2_grad = norm_back(upstream, unit2, inv_std2, ln2_gain)
    ffn_low = ffn_grad.astype(low)
    ffn_full = spread(ffn_low)
    pre_grad = gelu_back(dot(ffn_full, full_down))[0].astype(low)
    normed1_grad = ffn_grad + reduce_tokens(dot_nt(pre_grad, full_up))
    grad_down = dot_tn(ffn_full, hidden)
    grad_up = dot_tn(normed1_full, pre_grad)
    attn_grad, gain1_grad, shift1_grad = norm_back(normed1_grad, unit1, inv_std1, ln1_gain)
    attn_low = attn_grad.astype(low)
    attn_full = spread(attn_low)
    context_grad = dot(attn_full, full_out).astype(low)
    grad_out = dot_tn(attn_full, context)
    query_grad, key_grad, value_grad = attend_back(
        queries, key_rows, value_rows, tables, stats, context_grad
    )
    input_part = (
        dot_nt(query_grad, full_query) + dot_nt(key_grad, full_key) + dot_nt(value_grad, full_value)
    )
    own_part = lax.dynamic_slice_in_dim(input_part, own_start, own_len, 0) + attn_grad
    input_part = lax.dynamic_update_slice_in_dim(input_part, own_part, own_start, 0)
    grad_input = lax.psum_scatter(
        input_part.astype(low), "col", scatter_dimension=1, tiled=True
    )
    grad_qkv = dot_tn(features, jnp.concatenate([query_grad, key_grad, value_grad], axis=1))

    def reduce_rows(partial_value):
        return lax.psum_scatter(
            partial_value.astype(low), "row", scatter_dimension=0, tiled=True
        ).astype(jnp.float32)

    down_share = reduce_rows(grad_down).T
    up_share = reduce_rows(grad_up)
    out_share = reduce_rows(grad_out).T
    qkv_share = reduce_rows(grad_qkv)
    small_grads = lax.psum(
        (
            into_full(jnp.sum(query_grad, axis=0, dtype=jnp.float32), feat_start, features_all),
            into_full(jnp.sum(value_grad, axis=0, dtype=jnp.float32), feat_start, features_all),
            jnp.sum(attn_low, axis=0, dtype=jnp.float32),
            gain1_grad,
            shift1_grad,
            into_full(jnp.sum(pre_grad, axis=0, dtype=jnp.float32), unit_start, units_all),
            jnp.sum(ffn_low, axis=0, dtype=jnp.float32),
            gain2_grad,
            shift2_grad,
        ),
        ("row", "col"),
    )
    return (
        layer_out,
        grad_input,
        qkv_share[:, :feat_cols],
        small_grads[0],
        qkv_share[:, feat_cols : 2 * feat_cols],
        qkv_share[:, 2 * feat_cols :],
        small_grads[1],
        out_share,
        small_grads[2],
        small_grads[3],
        small_grads[4],
        up_share,
        small_grads[5],
        down_share,
        small_grads[6],
        small_grads[7],
        small_grads[8],
    )


def solution(mesh):
    placed = (
        P("row", "col"),
        P("row", "col"),
        P("row"),
        P("row", None),
        P("row", None, "col", None),
        P("row", "col"),
        P(),
        P("row", "col"),
        P("row", "col"),
        P(),
        P("col", "row"),
        P(),
        P(),
        P(),
        P("row", "col"),
        P(),
        P("col", "row"),
        P(),
        P(),
        P(),
    )
    return jax.shard_map(
        on_device,
        mesh=mesh,
        in_specs=placed,
        out_specs=(
            P("row", "col"),
            P("row", "col"),
            P("row", "col"),
            P(),
            P("row", "col"),
            P("row", "col"),
            P(),
            P("col", "row"),
            P(),
            P(),
            P(),
            P("row", "col"),
            P(),
            P("col", "row"),
            P(),
            P(),
            P(),
        ),
        check_vma=False,
    )
```

```python
import functools
import math

import jax
import jax.numpy as jnp
from jax import lax
from jax.experimental import pallas as pl
from jax.experimental.pallas import tpu as pltpu
from jax.sharding import PartitionSpec as P

DH = 64
BLK = 64
MESH = pl.DeviceIdType.MESH


epsilon = 1e-06


def lane_heads(rows, width):
    return lax.broadcasted_iota(jnp.int32, (rows, width), 1) // DH


def by_diagonal(rows, width):
    lane_head = lane_heads(BLK, width)
    zero = jnp.zeros_like(rows)
    return jnp.concatenate(
        [jnp.where(lane_head == head, rows, zero) for head in range(width // DH)], axis=0
    )


def from_diagonal(square, width):
    lane_head = lane_heads(BLK, width)
    result = jnp.zeros((BLK, width), jnp.float32)
    for head in range(width // DH):
        result = jnp.where(lane_head == head, square[head * BLK : (head + 1) * BLK, :], result)
    return result


def slot_starts(step, num_blocks, head_count, globals_ref, random_ref):
    shared = [
        jnp.maximum(step - 1, 0),
        step,
        jnp.minimum(step + 1, num_blocks - 1),
        globals_ref[0],
        globals_ref[1],
    ]
    base = step * (head_count * 3)
    apart = [
        [random_ref[base + head * 3 + slot] for head in range(head_count)] for slot in range(3)
    ]
    at = lambda block: pl.multiple_of(block * BLK, BLK)
    return [at(block) for block in shared], [[at(block) for block in row] for row in apart]


def lane_groups(head_count):
    per_group = min(128 // DH, head_count)
    return [
        (first * DH, per_group * DH, list(range(first, first + per_group)))
        for first in range(0, head_count, per_group)
    ]


def picked_rows(rows_ref, shared, apart, head_count):
    pieces = [rows_ref[pl.ds(start, BLK), :] for start in shared]
    for starts in apart:
        groups = []
        for lane, width, heads in lane_groups(head_count):
            lane_head = lane_heads(BLK, width)
            piece = rows_ref[pl.ds(starts[heads[0]], BLK), lane : lane + width]
            for place, head in enumerate(heads[1:], 1):
                other = rows_ref[pl.ds(starts[head], BLK), lane : lane + width]
                piece = jnp.where(lane_head >= place, other, piece)
            groups.append(piece)
        pieces.append(jnp.concatenate(groups, axis=1) if len(groups) > 1 else groups[0])
    return jnp.concatenate(pieces, axis=0)


def put_rows(sums_ref, values_in, shared, apart, head_count):
    for slot, start in enumerate(shared):
        sums_ref[pl.ds(start, BLK), :] += values_in[slot * BLK : (slot + 1) * BLK, :]
    for slot, starts in enumerate(apart, len(shared)):
        rows = values_in[slot * BLK : (slot + 1) * BLK, :]
        for lane, width, heads in lane_groups(head_count):
            lane_head = lane_heads(BLK, width)
            for place, head in enumerate(heads):
                sums_ref[pl.ds(starts[head], BLK), lane : lane + width] += jnp.where(
                    lane_head == place, rows[:, lane : lane + width], 0.0
                )


def masked_scores(picked_keys, grouped, limits_ref, step, width):
    scores = lax.dot_general(
        picked_keys, grouped, (((1,), (1,)), ((), ())), preferred_element_type=jnp.float32
    )
    row = lax.broadcasted_iota(jnp.int32, (BLK, width), 0)
    return [
        jnp.where(
            row < limits_ref[step, slot : slot + 1, :],
            scores[slot * BLK : (slot + 1) * BLK, :],
            -1e30,
        )
        for slot in range(8)
    ]


def attend_kernel(
    head_count,
    unroll,
    globals_ref,
    random_ref,
    limits_ref,
    queries_ref,
    keys_ref,
    values_ref,
    context_ref,
    highest_ref,
    scale_ref,
):
    width = head_count * DH
    num_blocks = queries_ref.shape[0] // BLK

    def one_block(step):
        shared, apart = slot_starts(step, num_blocks, head_count, globals_ref, random_ref)
        own = pl.ds(pl.multiple_of(step * BLK, BLK), BLK)
        grouped = by_diagonal(queries_ref[own, :] * jnp.bfloat16(1.0 / math.sqrt(DH)), width)
        scores = masked_scores(
            picked_rows(keys_ref, shared, apart, head_count), grouped, limits_ref, step, width
        )
        highest = jnp.max(functools.reduce(jnp.maximum, scores), axis=0, keepdims=True)
        exponent = [jnp.exp(piece - highest) for piece in scores]
        denominator = jnp.sum(sum(exponent[1:], exponent[0]), axis=0, keepdims=True)
        scale = 1.0 / denominator
        attn_probs = jnp.concatenate(
            [(piece * scale).astype(jnp.bfloat16) for piece in exponent], axis=0
        )
        square = lax.dot_general(
            attn_probs,
            picked_rows(values_ref, shared, apart, head_count),
            (((0,), (0,)), ((), ())),
            preferred_element_type=jnp.float32,
        )
        context_ref[own, :] = from_diagonal(square, width).astype(jnp.bfloat16)
        highest_ref[step] = highest
        scale_ref[step] = scale

    @pl.loop(0, num_blocks // unroll)
    def _(turn):
        for place in range(unroll):
            one_block(turn * unroll + place)


def attend_back_kernel(
    head_count,
    unroll,
    globals_ref,
    random_ref,
    limits_ref,
    queries_ref,
    keys_ref,
    values_ref,
    grads_ref,
    highest_ref,
    scale_ref,
    query_grad_ref,
    key_grad_ref,
    value_grad_ref,
    key_sums,
    value_sums,
):
    width = head_count * DH
    num_blocks = queries_ref.shape[0] // BLK
    factor = 1.0 / math.sqrt(DH)
    key_sums[...] = jnp.zeros_like(key_sums)
    value_sums[...] = jnp.zeros_like(value_sums)

    def one_block(step):
        shared, apart = slot_starts(step, num_blocks, head_count, globals_ref, random_ref)
        own = pl.ds(pl.multiple_of(step * BLK, BLK), BLK)
        grouped = by_diagonal(queries_ref[own, :] * jnp.bfloat16(factor), width)
        grouped_grad = by_diagonal(grads_ref[own, :], width)
        picked_keys = picked_rows(keys_ref, shared, apart, head_count)
        picked_values = picked_rows(values_ref, shared, apart, head_count)
        scores = masked_scores(picked_keys, grouped, limits_ref, step, width)
        highest = highest_ref[step]
        scale = scale_ref[step]
        attn_probs = [jnp.exp(piece - highest) * scale for piece in scores]
        prob_grad = lax.dot_general(
            picked_values,
            grouped_grad,
            (((1,), (1,)), ((), ())),
            preferred_element_type=jnp.float32,
        )
        prob_grads = [prob_grad[slot * BLK : (slot + 1) * BLK, :] for slot in range(8)]
        products = [left * right for left, right in zip(attn_probs, prob_grads)]
        total = jnp.sum(sum(products[1:], products[0]), axis=0, keepdims=True)
        score_grad = jnp.concatenate(
            [
                (left * (right - total)).astype(jnp.bfloat16)
                for left, right in zip(attn_probs, prob_grads)
            ],
            axis=0,
        )
        probs_low = jnp.concatenate([piece.astype(jnp.bfloat16) for piece in attn_probs], axis=0)
        square = lax.dot_general(
            score_grad, picked_keys, (((0,), (0,)), ((), ())), preferred_element_type=jnp.float32
        )
        query_grad_ref[own, :] = (from_diagonal(square, width) * factor).astype(jnp.bfloat16)
        key_part = jnp.dot(score_grad, grouped, preferred_element_type=jnp.float32)
        value_part = jnp.dot(probs_low, grouped_grad, preferred_element_type=jnp.float32)
        put_rows(key_sums, key_part, shared, apart, head_count)
        put_rows(value_sums, value_part, shared, apart, head_count)

    @pl.loop(0, num_blocks // unroll)
    def _(turn):
        for place in range(unroll):
            one_block(turn * unroll + place)

    key_grad_ref[...] = key_sums[...].astype(jnp.bfloat16)
    value_grad_ref[...] = value_sums[...].astype(jnp.bfloat16)


def limits_of(length, global_ids, random_ids, num_blocks, head_count):
    blocks = jnp.arange(num_blocks, dtype=jnp.int32)
    nearby_raw = blocks[:, None] + jnp.arange(-1, 2, dtype=jnp.int32)[None, :]
    near_ok = (nearby_raw >= 0) & (nearby_raw < num_blocks)
    global_rows = jnp.broadcast_to(global_ids[None, :], (num_blocks, 2))
    global_ok = jnp.all(global_rows[:, :, None] != nearby_raw[:, None, :], axis=2)
    common = jnp.concatenate([nearby_raw, global_rows], axis=1)
    common_ok = jnp.concatenate([near_ok, global_ok], axis=1)
    common_limit = jnp.where(common_ok, length - common * BLK, 0)
    random_limit = jnp.transpose(length - random_ids * BLK, (0, 2, 1))
    return jnp.concatenate(
        [
            jnp.broadcast_to(common_limit[:, :, None], (num_blocks, 5, head_count * DH)),
            jnp.repeat(random_limit, DH, axis=2),
        ],
        axis=1,
    )


VMEM = pl.BlockSpec(memory_space=pltpu.VMEM)
SMEM = pl.BlockSpec(memory_space=pltpu.SMEM)


def attend(queries, key_rows, value_rows, tables):
    seq_len, width = queries.shape
    head_count = width // DH
    num_blocks = seq_len // BLK
    stat = jax.ShapeDtypeStruct((num_blocks, 1, width), jnp.float32)
    return pl.pallas_call(
        functools.partial(attend_kernel, head_count, 2),
        out_shape=(jax.ShapeDtypeStruct((seq_len, width), jnp.bfloat16), stat, stat),
        in_specs=[SMEM] * 2 + [VMEM] * 4,
        out_specs=[VMEM] * 3,
        compiler_params=pltpu.CompilerParams(vmem_limit_bytes=32 * 1024 * 1024),
        cost_estimate=pl.CostEstimate(
            flops=4 * seq_len * 512 * width * head_count,
            bytes_accessed=8 * seq_len * width,
            transcendentals=seq_len * 512 * head_count,
        ),
    )(*tables, queries, key_rows, value_rows)


def attend_back(queries, key_rows, value_rows, tables, stats, context_grad):
    seq_len, width = queries.shape
    head_count = width // DH
    grad = jax.ShapeDtypeStruct((seq_len, width), jnp.bfloat16)
    return pl.pallas_call(
        functools.partial(attend_back_kernel, head_count, 2),
        out_shape=(grad, grad, grad),
        in_specs=[SMEM] * 2 + [VMEM] * 7,
        out_specs=[VMEM] * 3,
        scratch_shapes=[pltpu.VMEM((seq_len, width), jnp.float32)] * 2,
        compiler_params=pltpu.CompilerParams(vmem_limit_bytes=40 * 1024 * 1024),
        cost_estimate=pl.CostEstimate(
            flops=10 * seq_len * 512 * width * head_count,
            bytes_accessed=14 * seq_len * width,
            transcendentals=seq_len * 512 * head_count,
        ),
    )(*tables, queries, key_rows, value_rows, context_grad, *stats)


def dot(left, right):
    return jnp.dot(left, right, preferred_element_type=jnp.float32)


def dot_nt(left, right):
    return lax.dot_general(
        left, right, (((1,), (1,)), ((), ())), preferred_element_type=jnp.float32
    )


def dot_tn(left, right):
    return lax.dot_general(
        left, right, (((0,), (0,)), ((), ())), preferred_element_type=jnp.float32
    )


def gelu_parts(values_in):
    factor = math.sqrt(2.0 / math.pi)
    square = values_in * values_in
    bent = jnp.tanh(factor * (values_in + 0.044715 * (values_in * square)))
    half = 0.5 * (1.0 + bent)
    slope = half + (0.5 * values_in) * (1.0 - bent * bent) * (
        factor + (3.0 * 0.044715 * factor) * square
    )
    return (values_in * half, slope)


def norm_parts(summed):
    average = jnp.mean(summed, axis=1, keepdims=True)
    squares = jnp.mean(summed * summed, axis=1, keepdims=True)
    inv_std = lax.rsqrt(squares - average * average + epsilon)
    return ((summed - average) * inv_std, inv_std)


def norm_back(upstream, normed, inv_std, gain_vec):
    scaled = upstream * gain_vec
    left = jnp.mean(scaled, axis=1, keepdims=True)
    right = jnp.mean(scaled * normed, axis=1, keepdims=True)
    return inv_std * (scaled - left - normed * right)


CHUNKS = 4


def middle_kernel(
    levels,
    context_ref,
    inputs_ref,
    upstream_ref,
    out_ref,
    up_ref,
    down_ref,
    vectors_ref,
    b_up_ref,
    layer_out_ref,
    context_grad_ref,
    attn_full,
    small_ref,
    up_small_ref,
    grad_up_ref,
    grad_down_ref,
    grad_out_ref,
    context_sib,
    out_sib,
    up_sib,
    down_sib,
    normed_full,
    ffn_full,
    hidden,
    slope,
    pre_grad,
    unit1,
    inv1,
    ffn_keep,
    part_own,
    send_buf,
    recv_buf,
    context_send,
    stage,
    stage_small,
    send_sem,
    recv_sem,
    core_send,
    core_recv,
    stage_sem,
):
    low = jnp.bfloat16
    row, column = lax.axis_index("row"), lax.axis_index("col")
    core = lax.rem(column, 2)
    level = lax.div(column, 2)
    sibling = (row, column + 1 - 2 * core)
    own_len = inputs_ref.shape[0]
    step = own_len // CHUNKS
    b_out, gain1, shift1, b_down, gain2, shift2 = (
        vectors_ref.at[place : place + 1, :] for place in range(6)
    )

    def peer_level(offset):
        return lax.rem(level + offset, levels)

    barrier = pltpu.get_barrier_semaphore()
    pl.semaphore_signal(barrier, inc=1, device_id=sibling, device_id_type=MESH)
    for offset in range(1, levels):
        pl.semaphore_signal(
            barrier,
            inc=1,
            device_id=(row, peer_level(offset) * 2 + core),
            device_id_type=MESH,
        )
    pl.semaphore_wait(barrier, levels)

    def to_sibling(source, target, place):
        return pltpu.make_async_remote_copy(
            src_ref=source,
            dst_ref=target,
            send_sem=core_send.at[place],
            recv_sem=core_recv.at[place],
            device_id=sibling,
            device_id_type=MESH,
        )

    def rows_of(place, chunk):
        return pl.ds(pl.multiple_of(place * own_len + chunk * step, step), step)

    def own_rows(chunk):
        return pl.ds(pl.multiple_of(chunk * step, step), step)

    def exchange(kind, chunk, offset, source, target):
        return pltpu.make_async_remote_copy(
            src_ref=source,
            dst_ref=target,
            send_sem=send_sem.at[kind, chunk, offset - 1],
            recv_sem=recv_sem.at[kind, chunk, levels - offset - 1],
            device_id=(row, peer_level(offset) * 2 + core),
            device_id_type=MESH,
        )

    def sum_copy(kind, chunk, offset):
        return exchange(
            kind,
            chunk,
            offset,
            send_buf.at[kind // 2, offset - 1, own_rows(chunk)],
            recv_buf.at[kind // 2, levels - offset - 1, own_rows(chunk)],
        )

    def spread_copy(kind, chunk, offset):
        whole = {1: normed_full, 3: ffn_full, 5: attn_full}[kind]
        rows = rows_of(level, chunk)
        return exchange(kind, chunk, offset, whole.at[rows], whole.at[rows])

    def received(kind, chunk):
        return sum(
            recv_buf[kind // 2, place, own_rows(chunk), :].astype(jnp.float32)
            for place in range(levels - 1)
        )

    offsets = range(1, levels)
    context_copies = [
        to_sibling(
            context_ref.at[
                pl.ds(pl.multiple_of((place * 2 + 1 - core) * own_len, own_len), own_len)
            ],
            context_sib.at[pl.ds(place * own_len, own_len)],
            place,
        )
        for place in range(levels)
    ]
    out_copy = to_sibling(out_ref, out_sib, levels)
    up_copy = to_sibling(up_ref, up_sib, levels + 1)
    down_copy = to_sibling(down_ref, down_sib, levels + 2)
    for copy in context_copies + [out_copy, up_copy, down_copy]:
        copy.start()
    small_ref[...] = jnp.zeros_like(small_ref)
    up_small_ref[...] = jnp.zeros_like(up_small_ref)
    for copy in context_copies:
        copy.wait()
    out_copy.wait()

    def context_rows(place, chunk):
        start = (place * 2 + core) * own_len + chunk * step
        return pl.ds(pl.multiple_of(start, step), step)

    def attn_part(place, chunk):
        return dot_nt(context_ref[context_rows(place, chunk), :], out_ref[...]) + dot_nt(
            context_sib[rows_of(place, chunk), :], out_sib[...]
        )

    @pl.loop(0, CHUNKS)
    def _(chunk):
        for offset in offsets:
            send_buf[0, offset - 1, own_rows(chunk), :] = attn_part(
                peer_level(offset), chunk
            ).astype(low)
            sum_copy(0, chunk, offset).start()

    @pl.loop(0, CHUNKS)
    def _(chunk):
        rows = own_rows(chunk)
        summed = (
            inputs_ref[rows, :].astype(jnp.float32) + attn_part(level, chunk) + b_out[...]
        )
        for offset in offsets:
            sum_copy(0, chunk, offset).wait_recv()
        normed, inv_std = norm_parts(summed + received(0, chunk))
        unit1[rows, :] = normed
        inv1[rows, :] = inv_std
        normed_full[rows_of(level, chunk), :] = (normed * gain1[...] + shift1[...]).astype(low)
        for offset in offsets:
            spread_copy(1, chunk, offset).start()

    up_copy.wait()
    down_copy.wait()
    sides = ((up_ref, down_ref), (up_sib, down_sib))

    def feed_forward(place, chunk):
        rows = rows_of(place, chunk)
        normed = normed_full[rows, :]
        total = None
        for side, (up_side, down_side) in enumerate(sides):
            active, bend = gelu_parts(dot(normed, up_side[...]) + b_up_ref[side : side + 1, :])
            active = active.astype(low)
            hidden[side, rows, :] = active
            slope[side, rows, :] = bend
            part = dot_nt(active, down_side[...])
            total = part if total is None else total + part
        return total

    @pl.loop(0, CHUNKS)
    def _(chunk):
        part_own[own_rows(chunk), :] = feed_forward(level, chunk)
        for offset in offsets:
            spread_copy(1, chunk, levels - offset).wait_recv()
            send_buf[1, offset - 1, own_rows(chunk), :] = feed_forward(
                peer_level(offset), chunk
            ).astype(low)
            sum_copy(2, chunk, offset).start()

    @pl.loop(0, CHUNKS)
    def _(chunk):
        rows = own_rows(chunk)
        normed1 = unit1[rows, :] * gain1[...] + shift1[...]
        summed = normed1 + part_own[rows, :] + b_down[...]
        for offset in offsets:
            sum_copy(2, chunk, offset).wait_recv()
        normed, inv_std = norm_parts(summed + received(2, chunk))
        layer_out_ref[rows, :] = (normed * gain2[...] + shift2[...]).astype(low)
        upstream = upstream_ref[rows, :].astype(jnp.float32)
        grad = norm_back(upstream, normed, inv_std, gain2[...])
        ffn_keep[rows, :] = grad
        grad_low = grad.astype(low)
        ffn_full[rows_of(level, chunk), :] = grad_low
        for offset in offsets:
            spread_copy(3, chunk, offset).start()
        small_ref[0:1, :] += jnp.sum(upstream * normed, axis=0, keepdims=True)
        small_ref[1:2, :] += jnp.sum(upstream, axis=0, keepdims=True)
        small_ref[2:3, :] += jnp.sum(grad_low.astype(jnp.float32), axis=0, keepdims=True)

    def feed_back(place, chunk):
        rows = rows_of(place, chunk)
        upstream = ffn_full[rows, :]
        total = None
        for side, (up_side, down_side) in enumerate(sides):
            grad = (dot(upstream, down_side[...]) * slope[side, rows, :]).astype(low)
            pre_grad[side, rows, :] = grad
            up_small_ref[side : side + 1, :] += jnp.sum(
                grad.astype(jnp.float32), axis=0, keepdims=True
            )
            part = dot_nt(grad, up_side[...])
            total = part if total is None else total + part
        return total

    @pl.loop(0, CHUNKS)
    def _(chunk):
        part_own[own_rows(chunk), :] = feed_back(level, chunk)
        for offset in offsets:
            spread_copy(3, chunk, levels - offset).wait_recv()
            send_buf[2, offset - 1, own_rows(chunk), :] = feed_back(
                peer_level(offset), chunk
            ).astype(low)
            sum_copy(4, chunk, offset).start()

    def weight_grad(left_ref, right_of, target_ref, buffer):
        tile = buffer.shape[1]
        tiles = left_ref.shape[1] // tile

        def put(side, turn):
            return pltpu.make_async_copy(
                buffer.at[lax.rem(turn, 2)],
                target_ref.at[side, pl.ds(pl.multiple_of(turn * tile, tile), tile)],
                stage_sem.at[lax.rem(turn, 2)],
            )

        for side in range(2):

            @pl.loop(0, tiles)
            def _(turn):
                @pl.when(turn >= 2)
                def _():
                    put(side, turn - 2).wait()

                left = left_ref[:, pl.ds(pl.multiple_of(turn * tile, tile), tile)]
                buffer[lax.rem(turn, 2)] = dot_tn(left, right_of(side)).astype(low)
                put(side, turn).start()

            for turn in range(max(tiles - 2, 0), tiles):
                put(side, turn).wait()

    weight_grad(ffn_full, lambda side: hidden[side], grad_down_ref, stage)

    @pl.loop(0, CHUNKS)
    def _(chunk):
        rows = own_rows(chunk)
        upstream = ffn_keep[rows, :] + part_own[rows, :]
        for offset in offsets:
            sum_copy(4, chunk, offset).wait_recv()
        upstream = upstream + received(4, chunk)
        normed = unit1[rows, :]
        grad_low = norm_back(upstream, normed, inv1[rows, :], gain1[...]).astype(low)
        attn_full[rows_of(level, chunk), :] = grad_low
        for offset in offsets:
            spread_copy(5, chunk, offset).start()
        small_ref[3:4, :] += jnp.sum(upstream * normed, axis=0, keepdims=True)
        small_ref[4:5, :] += jnp.sum(upstream, axis=0, keepdims=True)
        small_ref[5:6, :] += jnp.sum(grad_low.astype(jnp.float32), axis=0, keepdims=True)

    weight_grad(normed_full, lambda side: pre_grad[side], grad_up_ref, stage)

    def context_back(place, chunk):
        rows = rows_of(place, chunk)
        upstream = attn_full[rows, :]
        context_grad_ref[context_rows(place, chunk), :] = dot(upstream, out_ref[...]).astype(low)
        context_send[rows, :] = dot(upstream, out_sib[...]).astype(low)

    @pl.loop(0, CHUNKS)
    def _(chunk):
        context_back(level, chunk)
        for offset in offsets:
            spread_copy(5, chunk, levels - offset).wait_recv()
            context_back(peer_level(offset), chunk)

    back_copies = [
        to_sibling(
            context_send.at[pl.ds(place * own_len, own_len)],
            context_grad_ref.at[
                pl.ds(pl.multiple_of((place * 2 + core) * own_len, own_len), own_len)
            ],
            levels + 3 + place,
        )
        for place in range(levels)
    ]
    for copy in back_copies:
        copy.start()

    own_context = jnp.concatenate(
        [
            context_ref[
                pl.ds(pl.multiple_of((place * 2 + core) * own_len, own_len), own_len), :
            ]
            for place in range(levels)
        ],
        axis=0,
    )
    weight_grad(
        attn_full,
        lambda side: context_sib[...] if side else own_context,
        grad_out_ref,
        stage_small,
    )
    for copy in back_copies:
        copy.wait()
    for kind in range(6):

        @pl.loop(0, CHUNKS)
        def _(chunk):
            for offset in offsets:
                if kind % 2:
                    spread_copy(kind, chunk, offset).wait_send()
                else:
                    sum_copy(kind, chunk, offset).wait_send()


def middle(levels, context, inputs, upstream, out_own, up_own, down_own, vectors, b_up_pair):
    low, full = jnp.bfloat16, jnp.float32
    own_len, features = inputs.shape
    seq_len, width = context.shape
    units = up_own.shape[1]
    tokens = levels * own_len
    others = levels - 1
    tile = 256
    shape = jax.ShapeDtypeStruct
    hbm = pl.BlockSpec(memory_space=pl.ANY)
    return pl.pallas_call(
        functools.partial(middle_kernel, levels),
        out_shape=(
            shape((own_len, features), low),
            shape((seq_len, width), low),
            shape((tokens, features), low),
            shape((8, features), full),
            shape((2, units), full),
            shape((2, features, units), low),
            shape((2, features, units), low),
            shape((2, features, width), low),
        ),
        in_specs=[VMEM] * 8,
        out_specs=[VMEM] * 5 + [hbm] * 3,
        scratch_shapes=[
            pltpu.VMEM((tokens, width), low),
            pltpu.VMEM((features, width), low),
            pltpu.VMEM((features, units), low),
            pltpu.VMEM((features, units), low),
            pltpu.VMEM((tokens, features), low),
            pltpu.VMEM((tokens, features), low),
            pltpu.VMEM((2, tokens, units), low),
            pltpu.VMEM((2, tokens, units), full),
            pltpu.VMEM((2, tokens, units), low),
            pltpu.VMEM((own_len, features), full),
            pltpu.VMEM((own_len, 1), full),
            pltpu.VMEM((own_len, features), full),
            pltpu.VMEM((own_len, features), full),
            pltpu.VMEM((3, others, own_len, features), low),
            pltpu.VMEM((3, others, own_len, features), low),
            pltpu.VMEM((tokens, width), low),
            pltpu.VMEM((2, tile, units), low),
            pltpu.VMEM((2, tile, width), low),
            pltpu.SemaphoreType.DMA((6, CHUNKS, others)),
            pltpu.SemaphoreType.DMA((6, CHUNKS, others)),
            pltpu.SemaphoreType.DMA((2 * levels + 3,)),
            pltpu.SemaphoreType.DMA((2 * levels + 3,)),
            pltpu.SemaphoreType.DMA((2,)),
        ],
        compiler_params=pltpu.CompilerParams(
            collective_id=1, has_side_effects=True, vmem_limit_bytes=60 * 1024 * 1024
        ),
        cost_estimate=pl.CostEstimate(
            flops=2 * tokens * features * (12 * units + 6 * width),
            bytes_accessed=40 * 1024 * 1024,
            transcendentals=2 * tokens * units,
        ),
    )(context, inputs, upstream, out_own, up_own, down_own, vectors, b_up_pair)


def to_tokens(portion):
    return lax.all_to_all(portion, "col", split_axis=0, concat_axis=1, tiled=True)


def to_features(portion):
    return lax.all_to_all(portion, "col", split_axis=1, concat_axis=0, tiled=True)


def into_full(portion, start_at, full_len):
    return lax.dynamic_update_slice_in_dim(
        jnp.zeros((full_len,), jnp.float32), portion, start_at, 0
    )


def on_device(
    hidden_in,
    out_grad,
    lengths,
    global_blocks,
    rand_blocks,
    w_query,
    b_query,
    w_key,
    w_value,
    b_value,
    w_out,
    b_out,
    ln1_gain,
    ln1_bias,
    w_up,
    b_up,
    w_down,
    b_down,
    ln2_gain,
    ln2_bias,
):
    low = jnp.bfloat16
    seq_len = hidden_in.shape[0]
    feat_cols = hidden_in.shape[1]
    unit_cols = w_up.shape[1]
    cols = lax.axis_size("col")
    features_all = feat_cols * cols
    units_all = unit_cols * cols
    num_blocks = seq_len // BLK
    head_count = feat_cols // DH
    own_len = seq_len // cols
    column = lax.axis_index("col")
    feat_start = column * feat_cols
    unit_start = column * unit_cols
    own_start = column * own_len
    length = lengths[0]
    tables = (
        global_blocks.reshape(-1),
        rand_blocks.reshape(-1),
        limits_of(length, global_blocks[0], rand_blocks[0], num_blocks, head_count),
    )
    full_qkv = lax.all_gather(
        jnp.concatenate([w_query.astype(low), w_key.astype(low), w_value.astype(low)], axis=1),
        "row",
        axis=0,
        tiled=True,
    )
    features = lax.all_gather(hidden_in, "col", axis=1, tiled=True)
    full_out = lax.all_gather(w_out.astype(low).T, "row", axis=0, tiled=True)
    full_up = lax.all_gather(w_up.astype(low), "row", axis=0, tiled=True)
    full_down = lax.all_gather(w_down.astype(low).T, "row", axis=0, tiled=True)
    own_features = lax.dynamic_slice_in_dim(features, own_start, own_len, 0)
    valid = (jnp.arange(seq_len) < length)[:, None]
    upstream = to_tokens(jnp.where(valid, out_grad, 0))

    full_query = full_qkv[:, :feat_cols]
    full_key = full_qkv[:, feat_cols : 2 * feat_cols]
    full_value = full_qkv[:, 2 * feat_cols :]
    queries = (
        dot(features, full_query) + lax.dynamic_slice_in_dim(b_query, feat_start, feat_cols)
    ).astype(low)
    key_rows = dot(features, full_key).astype(low)
    value_rows = (
        dot(features, full_value) + lax.dynamic_slice_in_dim(b_value, feat_start, feat_cols)
    ).astype(low)
    context, *stats = attend(queries, key_rows, value_rows, tables)

    sibling = column + 1 - 2 * lax.rem(column, 2)
    layer_own, context_grad, attn_full, small, up_small, grad_up, grad_down, grad_out = middle(
        cols // 2,
        context,
        own_features,
        upstream,
        full_out,
        full_up,
        full_down,
        jnp.stack([b_out, ln1_gain, ln1_bias, b_down, ln2_gain, ln2_bias, b_out, b_out]),
        jnp.stack(
            [
                lax.dynamic_slice_in_dim(b_up, unit_start, unit_cols),
                lax.dynamic_slice_in_dim(b_up, sibling * unit_cols, unit_cols),
            ]
        ),
    )
    layer_out = jnp.where(valid, to_features(layer_own), 0)
    query_grad, key_grad, value_grad = attend_back(
        queries, key_rows, value_rows, tables, stats, context_grad
    )
    input_part = (
        dot_nt(query_grad, full_query) + dot_nt(key_grad, full_key) + dot_nt(value_grad, full_value)
    )
    own_part = lax.dynamic_slice_in_dim(input_part, own_start, own_len, 0) + (
        lax.dynamic_slice_in_dim(attn_full, lax.div(column, 2) * own_len, own_len, 0)
    )
    input_part = lax.dynamic_update_slice_in_dim(input_part, own_part, own_start, 0)
    grad_input = lax.psum_scatter(
        input_part.astype(low), "col", scatter_dimension=1, tiled=True
    )
    grad_qkv = dot_tn(features, jnp.concatenate([query_grad, key_grad, value_grad], axis=1))

    def reduce_rows(partial_value):
        return lax.psum_scatter(
            partial_value.astype(low), "row", scatter_dimension=0, tiled=True
        ).astype(jnp.float32)

    swap = [(place, place + 1 - 2 * (place % 2)) for place in range(cols)]

    def both_cores(pair):
        return pair[0].astype(jnp.float32) + lax.ppermute(pair[1], "col", swap)

    down_share = reduce_rows(both_cores(grad_down)).T
    up_share = reduce_rows(both_cores(grad_up))
    out_share = reduce_rows(both_cores(grad_out)).T
    qkv_share = reduce_rows(grad_qkv)
    small_grads = lax.psum(
        (
            into_full(jnp.sum(query_grad, axis=0, dtype=jnp.float32), feat_start, features_all),
            into_full(jnp.sum(value_grad, axis=0, dtype=jnp.float32), feat_start, features_all),
            small,
            into_full(up_small[0], unit_start, units_all)
            + into_full(up_small[1], sibling * unit_cols, units_all),
        ),
        ("row", "col"),
    )
    return (
        layer_out,
        grad_input,
        qkv_share[:, :feat_cols],
        small_grads[0],
        qkv_share[:, feat_cols : 2 * feat_cols],
        qkv_share[:, 2 * feat_cols :],
        small_grads[1],
        out_share,
        small_grads[2][5],
        small_grads[2][3],
        small_grads[2][4],
        up_share,
        small_grads[3],
        down_share,
        small_grads[2][2],
        small_grads[2][0],
        small_grads[2][1],
    )


def solution(mesh):
    placed = (
        P("row", "col"),
        P("row", "col"),
        P("row"),
        P("row", None),
        P("row", None, "col", None),
        P("row", "col"),
        P(),
        P("row", "col"),
        P("row", "col"),
        P(),
        P("col", "row"),
        P(),
        P(),
        P(),
        P("row", "col"),
        P(),
        P("col", "row"),
        P(),
        P(),
        P(),
    )
    return jax.shard_map(
        on_device,
        mesh=mesh,
        in_specs=placed,
        out_specs=(
            P("row", "col"),
            P("row", "col"),
            P("row", "col"),
            P(),
            P("row", "col"),
            P("row", "col"),
            P(),
            P("col", "row"),
            P(),
            P(),
            P(),
            P("row", "col"),
            P(),
            P("col", "row"),
            P(),
            P(),
            P(),
        ),
        check_vma=False,
    )
```

```python
import functools
import math

import jax
import jax.numpy as jnp
from jax import lax
from jax.experimental import pallas as pl
from jax.experimental.pallas import tpu as pltpu
from jax.sharding import PartitionSpec as P

DH = 64
BLK = 64
MESH = pl.DeviceIdType.MESH


epsilon = 1e-06


def lane_heads(rows, width):
    return lax.broadcasted_iota(jnp.int32, (rows, width), 1) // DH


def by_diagonal(rows, width):
    lane_head = lane_heads(BLK, width)
    zero = jnp.zeros_like(rows)
    return jnp.concatenate(
        [jnp.where(lane_head == head, rows, zero) for head in range(width // DH)], axis=0
    )


def from_diagonal(square, width):
    lane_head = lane_heads(BLK, width)
    result = jnp.zeros((BLK, width), jnp.float32)
    for head in range(width // DH):
        result = jnp.where(lane_head == head, square[head * BLK : (head + 1) * BLK, :], result)
    return result


def slot_starts(step, num_blocks, head_count, globals_ref, random_ref):
    shared = [
        jnp.maximum(step - 1, 0),
        step,
        jnp.minimum(step + 1, num_blocks - 1),
        globals_ref[0],
        globals_ref[1],
    ]
    base = step * (head_count * 3)
    apart = [
        [random_ref[base + head * 3 + slot] for head in range(head_count)] for slot in range(3)
    ]
    at = lambda block: pl.multiple_of(block * BLK, BLK)
    return [at(block) for block in shared], [[at(block) for block in row] for row in apart]


def lane_groups(head_count):
    per_group = min(128 // DH, head_count)
    return [
        (first * DH, per_group * DH, list(range(first, first + per_group)))
        for first in range(0, head_count, per_group)
    ]


def picked_rows(rows_ref, shared, apart, head_count):
    pieces = [rows_ref[pl.ds(start, BLK), :] for start in shared]
    for starts in apart:
        groups = []
        for lane, width, heads in lane_groups(head_count):
            lane_head = lane_heads(BLK, width)
            piece = rows_ref[pl.ds(starts[heads[0]], BLK), lane : lane + width]
            for place, head in enumerate(heads[1:], 1):
                other = rows_ref[pl.ds(starts[head], BLK), lane : lane + width]
                piece = jnp.where(lane_head >= place, other, piece)
            groups.append(piece)
        pieces.append(jnp.concatenate(groups, axis=1) if len(groups) > 1 else groups[0])
    return jnp.concatenate(pieces, axis=0)


def put_rows(sums_ref, values_in, shared, apart, head_count):
    for slot, start in enumerate(shared):
        sums_ref[pl.ds(start, BLK), :] += values_in[slot * BLK : (slot + 1) * BLK, :]
    for slot, starts in enumerate(apart, len(shared)):
        rows = values_in[slot * BLK : (slot + 1) * BLK, :]
        for lane, width, heads in lane_groups(head_count):
            lane_head = lane_heads(BLK, width)
            for place, head in enumerate(heads):
                sums_ref[pl.ds(starts[head], BLK), lane : lane + width] += jnp.where(
                    lane_head == place, rows[:, lane : lane + width], 0.0
                )


def masked_scores(picked_keys, grouped, limits_ref, step, width):
    scores = lax.dot_general(
        picked_keys, grouped, (((1,), (1,)), ((), ())), preferred_element_type=jnp.float32
    )
    row = lax.broadcasted_iota(jnp.int32, (BLK, width), 0)
    return [
        jnp.where(
            row < limits_ref[step, slot : slot + 1, :],
            scores[slot * BLK : (slot + 1) * BLK, :],
            -1e30,
        )
        for slot in range(8)
    ]


def attend_kernel(
    head_count,
    unroll,
    globals_ref,
    random_ref,
    limits_ref,
    queries_ref,
    keys_ref,
    values_ref,
    context_ref,
    highest_ref,
    scale_ref,
):
    width = head_count * DH
    num_blocks = queries_ref.shape[0] // BLK

    def one_block(step):
        shared, apart = slot_starts(step, num_blocks, head_count, globals_ref, random_ref)
        own = pl.ds(pl.multiple_of(step * BLK, BLK), BLK)
        grouped = by_diagonal(queries_ref[own, :] * jnp.bfloat16(1.0 / math.sqrt(DH)), width)
        scores = masked_scores(
            picked_rows(keys_ref, shared, apart, head_count), grouped, limits_ref, step, width
        )
        highest = jnp.max(functools.reduce(jnp.maximum, scores), axis=0, keepdims=True)
        exponent = [jnp.exp(piece - highest) for piece in scores]
        denominator = jnp.sum(sum(exponent[1:], exponent[0]), axis=0, keepdims=True)
        scale = 1.0 / denominator
        attn_probs = jnp.concatenate(
            [(piece * scale).astype(jnp.bfloat16) for piece in exponent], axis=0
        )
        square = lax.dot_general(
            attn_probs,
            picked_rows(values_ref, shared, apart, head_count),
            (((0,), (0,)), ((), ())),
            preferred_element_type=jnp.float32,
        )
        context_ref[own, :] = from_diagonal(square, width).astype(jnp.bfloat16)
        highest_ref[step] = highest
        scale_ref[step] = scale

    @pl.loop(0, num_blocks // unroll)
    def _(turn):
        for place in range(unroll):
            one_block(turn * unroll + place)


def attend_back_kernel(
    head_count,
    unroll,
    globals_ref,
    random_ref,
    limits_ref,
    queries_ref,
    keys_ref,
    values_ref,
    grads_ref,
    highest_ref,
    scale_ref,
    grads_out_ref,
    bias_ref,
    key_sums,
    value_sums,
    query_total,
):
    width = head_count * DH
    num_blocks = queries_ref.shape[0] // BLK
    factor = 1.0 / math.sqrt(DH)
    key_sums[...] = jnp.zeros_like(key_sums)
    value_sums[...] = jnp.zeros_like(value_sums)
    query_total[...] = jnp.zeros_like(query_total)

    def one_block(step):
        shared, apart = slot_starts(step, num_blocks, head_count, globals_ref, random_ref)
        own = pl.ds(pl.multiple_of(step * BLK, BLK), BLK)
        grouped = by_diagonal(queries_ref[own, :] * jnp.bfloat16(factor), width)
        grouped_grad = by_diagonal(grads_ref[own, :], width)
        picked_keys = picked_rows(keys_ref, shared, apart, head_count)
        picked_values = picked_rows(values_ref, shared, apart, head_count)
        scores = masked_scores(picked_keys, grouped, limits_ref, step, width)
        highest = highest_ref[step]
        scale = scale_ref[step]
        attn_probs = [jnp.exp(piece - highest) * scale for piece in scores]
        prob_grad = lax.dot_general(
            picked_values,
            grouped_grad,
            (((1,), (1,)), ((), ())),
            preferred_element_type=jnp.float32,
        )
        prob_grads = [prob_grad[slot * BLK : (slot + 1) * BLK, :] for slot in range(8)]
        products = [left * right for left, right in zip(attn_probs, prob_grads)]
        total = jnp.sum(sum(products[1:], products[0]), axis=0, keepdims=True)
        score_grad = jnp.concatenate(
            [
                (left * (right - total)).astype(jnp.bfloat16)
                for left, right in zip(attn_probs, prob_grads)
            ],
            axis=0,
        )
        probs_low = jnp.concatenate([piece.astype(jnp.bfloat16) for piece in attn_probs], axis=0)
        square = lax.dot_general(
            score_grad, picked_keys, (((0,), (0,)), ((), ())), preferred_element_type=jnp.float32
        )
        query_grad = (from_diagonal(square, width) * factor).astype(jnp.bfloat16)
        grads_out_ref[own, :width] = query_grad
        query_total[...] += jnp.sum(
            query_grad.astype(jnp.float32).reshape(BLK // 8, 8, width), axis=0
        )
        key_part = jnp.dot(score_grad, grouped, preferred_element_type=jnp.float32)
        value_part = jnp.dot(probs_low, grouped_grad, preferred_element_type=jnp.float32)
        put_rows(key_sums, key_part, shared, apart, head_count)
        put_rows(value_sums, value_part, shared, apart, head_count)

    @pl.loop(0, num_blocks // unroll)
    def _(turn):
        for place in range(unroll):
            one_block(turn * unroll + place)

    value_grad = value_sums[...].astype(jnp.bfloat16)
    grads_out_ref[:, width : 2 * width] = key_sums[...].astype(jnp.bfloat16)
    grads_out_ref[:, 2 * width :] = value_grad
    bias_ref[0:1, :] = jnp.sum(query_total[...], axis=0, keepdims=True)
    bias_ref[1:2, :] = jnp.sum(value_grad.astype(jnp.float32), axis=0, keepdims=True)


def limits_of(length, global_ids, random_ids, num_blocks, head_count):
    blocks = jnp.arange(num_blocks, dtype=jnp.int32)
    nearby_raw = blocks[:, None] + jnp.arange(-1, 2, dtype=jnp.int32)[None, :]
    near_ok = (nearby_raw >= 0) & (nearby_raw < num_blocks)
    global_rows = jnp.broadcast_to(global_ids[None, :], (num_blocks, 2))
    global_ok = jnp.all(global_rows[:, :, None] != nearby_raw[:, None, :], axis=2)
    common = jnp.concatenate([nearby_raw, global_rows], axis=1)
    common_ok = jnp.concatenate([near_ok, global_ok], axis=1)
    common_limit = jnp.where(common_ok, length - common * BLK, 0)
    random_limit = jnp.transpose(length - random_ids * BLK, (0, 2, 1))
    return jnp.concatenate(
        [
            jnp.broadcast_to(common_limit[:, :, None], (num_blocks, 5, head_count * DH)),
            jnp.repeat(random_limit, DH, axis=2),
        ],
        axis=1,
    )


VMEM = pl.BlockSpec(memory_space=pltpu.VMEM)
SMEM = pl.BlockSpec(memory_space=pltpu.SMEM)


def attend(queries, key_rows, value_rows, tables):
    seq_len, width = queries.shape
    head_count = width // DH
    num_blocks = seq_len // BLK
    stat = jax.ShapeDtypeStruct((num_blocks, 1, width), jnp.float32)
    return pl.pallas_call(
        functools.partial(attend_kernel, head_count, 2),
        out_shape=(jax.ShapeDtypeStruct((seq_len, width), jnp.bfloat16), stat, stat),
        in_specs=[SMEM] * 2 + [VMEM] * 4,
        out_specs=[VMEM] * 3,
        compiler_params=pltpu.CompilerParams(vmem_limit_bytes=32 * 1024 * 1024),
        cost_estimate=pl.CostEstimate(
            flops=4 * seq_len * 512 * width * head_count,
            bytes_accessed=8 * seq_len * width,
            transcendentals=seq_len * 512 * head_count,
        ),
    )(*tables, queries, key_rows, value_rows)


def attend_back(queries, key_rows, value_rows, tables, stats, context_grad):
    seq_len, width = queries.shape
    head_count = width // DH
    return pl.pallas_call(
        functools.partial(attend_back_kernel, head_count, 2),
        out_shape=(
            jax.ShapeDtypeStruct((seq_len, 3 * width), jnp.bfloat16),
            jax.ShapeDtypeStruct((2, width), jnp.float32),
        ),
        in_specs=[SMEM] * 2 + [VMEM] * 7,
        out_specs=[VMEM] * 2,
        scratch_shapes=[pltpu.VMEM((seq_len, width), jnp.float32)] * 2
        + [pltpu.VMEM((8, width), jnp.float32)],
        compiler_params=pltpu.CompilerParams(vmem_limit_bytes=40 * 1024 * 1024),
        cost_estimate=pl.CostEstimate(
            flops=10 * seq_len * 512 * width * head_count,
            bytes_accessed=14 * seq_len * width,
            transcendentals=seq_len * 512 * head_count,
        ),
    )(*tables, queries, key_rows, value_rows, context_grad, *stats)


def dot(left, right):
    return jnp.dot(left, right, preferred_element_type=jnp.float32)


def dot_nt(left, right):
    return lax.dot_general(
        left, right, (((1,), (1,)), ((), ())), preferred_element_type=jnp.float32
    )


def dot_tn(left, right):
    return lax.dot_general(
        left, right, (((0,), (0,)), ((), ())), preferred_element_type=jnp.float32
    )


def gelu_parts(values_in):
    factor = math.sqrt(2.0 / math.pi)
    square = values_in * values_in
    bent = jnp.tanh(factor * (values_in + 0.044715 * (values_in * square)))
    half = 0.5 * (1.0 + bent)
    slope = half + (0.5 * values_in) * (1.0 - bent * bent) * (
        factor + (3.0 * 0.044715 * factor) * square
    )
    return (values_in * half, slope)


def norm_parts(summed):
    average = jnp.mean(summed, axis=1, keepdims=True)
    squares = jnp.mean(summed * summed, axis=1, keepdims=True)
    inv_std = lax.rsqrt(squares - average * average + epsilon)
    return ((summed - average) * inv_std, inv_std)


def norm_back(upstream, normed, inv_std, gain_vec):
    scaled = upstream * gain_vec
    left = jnp.mean(scaled, axis=1, keepdims=True)
    right = jnp.mean(scaled * normed, axis=1, keepdims=True)
    return inv_std * (scaled - left - normed * right)


CHUNKS = 4


def middle_kernel(
    levels,
    context_ref,
    inputs_ref,
    upstream_ref,
    valid_ref,
    out_ref,
    up_ref,
    down_ref,
    vectors_ref,
    b_up_ref,
    layer_out_ref,
    context_grad_ref,
    attn_full,
    small_ref,
    up_small_ref,
    grad_up_ref,
    grad_down_ref,
    grad_out_ref,
    context_sib,
    out_sib,
    up_sib,
    down_sib,
    normed_full,
    ffn_full,
    hidden,
    slope,
    pre_grad,
    unit1,
    inv1,
    ffn_keep,
    part_own,
    send_buf,
    recv_buf,
    context_send,
    stage,
    stage_small,
    send_sem,
    recv_sem,
    core_send,
    core_recv,
    stage_sem,
):
    low = jnp.bfloat16
    row, column = lax.axis_index("row"), lax.axis_index("col")
    core = lax.rem(column, 2)
    level = lax.div(column, 2)
    sibling = (row, column + 1 - 2 * core)
    own_len = inputs_ref.shape[0]
    step = own_len // CHUNKS
    b_out, gain1, shift1, b_down, gain2, shift2 = (
        vectors_ref.at[place : place + 1, :] for place in range(6)
    )

    def peer_level(offset):
        return lax.rem(level + offset, levels)

    barrier = pltpu.get_barrier_semaphore()
    pl.semaphore_signal(barrier, inc=1, device_id=sibling, device_id_type=MESH)
    for offset in range(1, levels):
        pl.semaphore_signal(
            barrier,
            inc=1,
            device_id=(row, peer_level(offset) * 2 + core),
            device_id_type=MESH,
        )
    pl.semaphore_wait(barrier, levels)

    def to_sibling(source, target, place):
        return pltpu.make_async_remote_copy(
            src_ref=source,
            dst_ref=target,
            send_sem=core_send.at[place],
            recv_sem=core_recv.at[place],
            device_id=sibling,
            device_id_type=MESH,
        )

    def rows_of(place, chunk):
        return pl.ds(pl.multiple_of(place * own_len + chunk * step, step), step)

    def own_rows(chunk):
        return pl.ds(pl.multiple_of(chunk * step, step), step)

    def exchange(kind, chunk, offset, source, target):
        return pltpu.make_async_remote_copy(
            src_ref=source,
            dst_ref=target,
            send_sem=send_sem.at[kind, chunk, offset - 1],
            recv_sem=recv_sem.at[kind, chunk, levels - offset - 1],
            device_id=(row, peer_level(offset) * 2 + core),
            device_id_type=MESH,
        )

    def sum_copy(kind, chunk, offset):
        return exchange(
            kind,
            chunk,
            offset,
            send_buf.at[kind // 2, offset - 1, own_rows(chunk)],
            recv_buf.at[kind // 2, levels - offset - 1, own_rows(chunk)],
        )

    def spread_copy(kind, chunk, offset):
        whole = {1: normed_full, 3: ffn_full, 5: attn_full}[kind]
        rows = rows_of(level, chunk)
        return exchange(kind, chunk, offset, whole.at[rows], whole.at[rows])

    def received(kind, chunk):
        return sum(
            recv_buf[kind // 2, place, own_rows(chunk), :].astype(jnp.float32)
            for place in range(levels - 1)
        )

    offsets = range(1, levels)
    context_copies = [
        to_sibling(
            context_ref.at[
                pl.ds(pl.multiple_of((place * 2 + 1 - core) * own_len, own_len), own_len)
            ],
            context_sib.at[pl.ds(place * own_len, own_len)],
            place,
        )
        for place in range(levels)
    ]
    out_copy = to_sibling(out_ref, out_sib, levels)
    up_copy = to_sibling(up_ref, up_sib, levels + 1)
    down_copy = to_sibling(down_ref, down_sib, levels + 2)
    for copy in context_copies + [out_copy, up_copy, down_copy]:
        copy.start()
    small_ref[...] = jnp.zeros_like(small_ref)
    up_small_ref[...] = jnp.zeros_like(up_small_ref)
    for copy in context_copies:
        copy.wait()
    out_copy.wait()

    def context_rows(place, chunk):
        start = (place * 2 + core) * own_len + chunk * step
        return pl.ds(pl.multiple_of(start, step), step)

    def attn_part(place, chunk):
        return dot_nt(context_ref[context_rows(place, chunk), :], out_ref[...]) + dot_nt(
            context_sib[rows_of(place, chunk), :], out_sib[...]
        )

    @pl.loop(0, CHUNKS)
    def _(chunk):
        for offset in offsets:
            send_buf[0, offset - 1, own_rows(chunk), :] = attn_part(
                peer_level(offset), chunk
            ).astype(low)
            sum_copy(0, chunk, offset).start()

    @pl.loop(0, CHUNKS)
    def _(chunk):
        rows = own_rows(chunk)
        summed = (
            inputs_ref[rows, :].astype(jnp.float32) + attn_part(level, chunk) + b_out[...]
        )
        for offset in offsets:
            sum_copy(0, chunk, offset).wait_recv()
        normed, inv_std = norm_parts(summed + received(0, chunk))
        unit1[rows, :] = normed
        inv1[rows, :] = inv_std
        normed_full[rows_of(level, chunk), :] = (normed * gain1[...] + shift1[...]).astype(low)
        for offset in offsets:
            spread_copy(1, chunk, offset).start()

    up_copy.wait()
    down_copy.wait()
    sides = ((up_ref, down_ref), (up_sib, down_sib))

    def feed_forward(place, chunk):
        rows = rows_of(place, chunk)
        normed = normed_full[rows, :]
        total = None
        for side, (up_side, down_side) in enumerate(sides):
            active, bend = gelu_parts(dot(normed, up_side[...]) + b_up_ref[side : side + 1, :])
            active = active.astype(low)
            hidden[side, rows, :] = active
            slope[side, rows, :] = bend
            part = dot_nt(active, down_side[...])
            total = part if total is None else total + part
        return total

    @pl.loop(0, CHUNKS)
    def _(chunk):
        part_own[own_rows(chunk), :] = feed_forward(level, chunk)
        for offset in offsets:
            spread_copy(1, chunk, levels - offset).wait_recv()
            send_buf[1, offset - 1, own_rows(chunk), :] = feed_forward(
                peer_level(offset), chunk
            ).astype(low)
            sum_copy(2, chunk, offset).start()

    @pl.loop(0, CHUNKS)
    def _(chunk):
        rows = own_rows(chunk)
        normed1 = unit1[rows, :] * gain1[...] + shift1[...]
        summed = normed1 + part_own[rows, :] + b_down[...]
        for offset in offsets:
            sum_copy(2, chunk, offset).wait_recv()
        normed, inv_std = norm_parts(summed + received(2, chunk))
        layer_out_ref[rows, :] = jnp.where(
            valid_ref[rows, :] > 0, normed * gain2[...] + shift2[...], 0.0
        ).astype(low)
        upstream = upstream_ref[rows, :].astype(jnp.float32)
        grad = norm_back(upstream, normed, inv_std, gain2[...])
        ffn_keep[rows, :] = grad
        grad_low = grad.astype(low)
        ffn_full[rows_of(level, chunk), :] = grad_low
        for offset in offsets:
            spread_copy(3, chunk, offset).start()
        small_ref[0:1, :] += jnp.sum(upstream * normed, axis=0, keepdims=True)
        small_ref[1:2, :] += jnp.sum(upstream, axis=0, keepdims=True)
        small_ref[2:3, :] += jnp.sum(grad_low.astype(jnp.float32), axis=0, keepdims=True)

    def feed_back(place, chunk):
        rows = rows_of(place, chunk)
        upstream = ffn_full[rows, :]
        total = None
        for side, (up_side, down_side) in enumerate(sides):
            grad = (dot(upstream, down_side[...]) * slope[side, rows, :]).astype(low)
            pre_grad[side, rows, :] = grad
            up_small_ref[side : side + 1, :] += jnp.sum(
                grad.astype(jnp.float32), axis=0, keepdims=True
            )
            part = dot_nt(grad, up_side[...])
            total = part if total is None else total + part
        return total

    @pl.loop(0, CHUNKS)
    def _(chunk):
        part_own[own_rows(chunk), :] = feed_back(level, chunk)
        for offset in offsets:
            spread_copy(3, chunk, levels - offset).wait_recv()
            send_buf[2, offset - 1, own_rows(chunk), :] = feed_back(
                peer_level(offset), chunk
            ).astype(low)
            sum_copy(4, chunk, offset).start()

    def weight_grad(left_ref, right_of, target_ref, buffer):
        tile = buffer.shape[1]
        tiles = left_ref.shape[1] // tile

        def put(side, turn):
            return pltpu.make_async_copy(
                buffer.at[lax.rem(turn, 2)],
                target_ref.at[side, pl.ds(pl.multiple_of(turn * tile, tile), tile)],
                stage_sem.at[lax.rem(turn, 2)],
            )

        for side in range(2):

            @pl.loop(0, tiles)
            def _(turn):
                @pl.when(turn >= 2)
                def _():
                    put(side, turn - 2).wait()

                left = left_ref[:, pl.ds(pl.multiple_of(turn * tile, tile), tile)]
                buffer[lax.rem(turn, 2)] = dot_tn(left, right_of(side)).astype(low)
                put(side, turn).start()

            for turn in range(max(tiles - 2, 0), tiles):
                put(side, turn).wait()

    weight_grad(ffn_full, lambda side: hidden[side], grad_down_ref, stage)

    @pl.loop(0, CHUNKS)
    def _(chunk):
        rows = own_rows(chunk)
        upstream = ffn_keep[rows, :] + part_own[rows, :]
        for offset in offsets:
            sum_copy(4, chunk, offset).wait_recv()
        upstream = upstream + received(4, chunk)
        normed = unit1[rows, :]
        grad_low = norm_back(upstream, normed, inv1[rows, :], gain1[...]).astype(low)
        attn_full[rows_of(level, chunk), :] = grad_low
        for offset in offsets:
            spread_copy(5, chunk, offset).start()
        small_ref[3:4, :] += jnp.sum(upstream * normed, axis=0, keepdims=True)
        small_ref[4:5, :] += jnp.sum(upstream, axis=0, keepdims=True)
        small_ref[5:6, :] += jnp.sum(grad_low.astype(jnp.float32), axis=0, keepdims=True)

    weight_grad(normed_full, lambda side: pre_grad[side], grad_up_ref, stage)

    def context_back(place, chunk):
        rows = rows_of(place, chunk)
        upstream = attn_full[rows, :]
        context_grad_ref[context_rows(place, chunk), :] = dot(upstream, out_ref[...]).astype(low)
        context_send[rows, :] = dot(upstream, out_sib[...]).astype(low)

    @pl.loop(0, CHUNKS)
    def _(chunk):
        context_back(level, chunk)
        for offset in offsets:
            spread_copy(5, chunk, levels - offset).wait_recv()
            context_back(peer_level(offset), chunk)

    back_copies = [
        to_sibling(
            context_send.at[pl.ds(place * own_len, own_len)],
            context_grad_ref.at[
                pl.ds(pl.multiple_of((place * 2 + core) * own_len, own_len), own_len)
            ],
            levels + 3 + place,
        )
        for place in range(levels)
    ]
    for copy in back_copies:
        copy.start()

    own_context = jnp.concatenate(
        [
            context_ref[
                pl.ds(pl.multiple_of((place * 2 + core) * own_len, own_len), own_len), :
            ]
            for place in range(levels)
        ],
        axis=0,
    )
    weight_grad(
        attn_full,
        lambda side: context_sib[...] if side else own_context,
        grad_out_ref,
        stage_small,
    )
    for copy in back_copies:
        copy.wait()
    for kind in range(6):

        @pl.loop(0, CHUNKS)
        def _(chunk):
            for offset in offsets:
                if kind % 2:
                    spread_copy(kind, chunk, offset).wait_send()
                else:
                    sum_copy(kind, chunk, offset).wait_send()


def middle(
    levels, context, inputs, upstream, valid, out_own, up_own, down_own, vectors, b_up_pair
):
    low, full = jnp.bfloat16, jnp.float32
    own_len, features = inputs.shape
    seq_len, width = context.shape
    units = up_own.shape[1]
    tokens = levels * own_len
    others = levels - 1
    tile = 256
    shape = jax.ShapeDtypeStruct
    hbm = pl.BlockSpec(memory_space=pl.ANY)
    return pl.pallas_call(
        functools.partial(middle_kernel, levels),
        out_shape=(
            shape((own_len, features), low),
            shape((seq_len, width), low),
            shape((tokens, features), low),
            shape((8, features), full),
            shape((2, units), full),
            shape((2, features, units), low),
            shape((2, features, units), low),
            shape((2, features, width), low),
        ),
        in_specs=[VMEM] * 9,
        out_specs=[VMEM] * 5 + [hbm] * 3,
        scratch_shapes=[
            pltpu.VMEM((tokens, width), low),
            pltpu.VMEM((features, width), low),
            pltpu.VMEM((features, units), low),
            pltpu.VMEM((features, units), low),
            pltpu.VMEM((tokens, features), low),
            pltpu.VMEM((tokens, features), low),
            pltpu.VMEM((2, tokens, units), low),
            pltpu.VMEM((2, tokens, units), full),
            pltpu.VMEM((2, tokens, units), low),
            pltpu.VMEM((own_len, features), full),
            pltpu.VMEM((own_len, 1), full),
            pltpu.VMEM((own_len, features), full),
            pltpu.VMEM((own_len, features), full),
            pltpu.VMEM((3, others, own_len, features), low),
            pltpu.VMEM((3, others, own_len, features), low),
            pltpu.VMEM((tokens, width), low),
            pltpu.VMEM((2, tile, units), low),
            pltpu.VMEM((2, tile, width), low),
            pltpu.SemaphoreType.DMA((6, CHUNKS, others)),
            pltpu.SemaphoreType.DMA((6, CHUNKS, others)),
            pltpu.SemaphoreType.DMA((2 * levels + 3,)),
            pltpu.SemaphoreType.DMA((2 * levels + 3,)),
            pltpu.SemaphoreType.DMA((2,)),
        ],
        compiler_params=pltpu.CompilerParams(
            collective_id=1, has_side_effects=True, vmem_limit_bytes=60 * 1024 * 1024
        ),
        cost_estimate=pl.CostEstimate(
            flops=2 * tokens * features * (12 * units + 6 * width),
            bytes_accessed=40 * 1024 * 1024,
            transcendentals=2 * tokens * units,
        ),
    )(context, inputs, upstream, valid, out_own, up_own, down_own, vectors, b_up_pair)


KINDS = 4


def end_kernel(
    levels,
    across,
    along,
    query_key_value_ref,
    weights_ref,
    features_ref,
    attn_ref,
    layer_ref,
    small_ref,
    down_ref,
    up_ref,
    out_ref,
    grad_input_ref,
    layer_out_ref,
    small_out_ref,
    share_down_ref,
    share_up_ref,
    share_out_ref,
    share_qkv_ref,
    down_sib,
    up_sib,
    out_sib,
    qkv_sums,
    down_got,
    up_got,
    out_got,
    qkv_got,
    down_pass,
    up_pass,
    out_pass,
    qkv_pass,
    down_in,
    up_in,
    out_in,
    qkv_in,
    core_out,
    core_in,
    level_out,
    level_in,
    attn_in,
    small_sums,
    small_in,
    core_send,
    core_recv,
    part_send,
    part_recv,
    level_send,
    level_recv,
    layer_send,
    layer_recv,
    across_send,
    across_recv,
    along_send,
    along_recv,
    small_send,
    small_recv,
    keep_sem,
):
    low, full = jnp.bfloat16, jnp.float32
    row, column = lax.axis_index("row"), lax.axis_index("col")
    core, level = lax.rem(column, 2), lax.div(column, 2)
    fast, slow = lax.rem(row, across), lax.div(row, across)
    cols = 2 * levels
    seq_len = features_ref.shape[0]
    own_len = seq_len // cols
    width = grad_input_ref.shape[1]
    shard = share_qkv_ref.shape[0]
    other = 1 - core
    sibling = (row, level * 2 + other)
    offsets = range(1, levels)

    def peer_level(offset):
        return lax.rem(level + offset, levels)

    def fast_peer(offset):
        return slow * across + lax.rem(fast + offset, across)

    def slow_peer(offset):
        return lax.rem(slow + offset, along) * across + fast

    barrier = pltpu.get_barrier_semaphore()
    greeted = [sibling]
    for offset in offsets:
        greeted += [(row, peer_level(offset) * 2 + core), (row, peer_level(offset) * 2 + other)]
    greeted += [(fast_peer(offset), column) for offset in range(1, across)]
    greeted += [(slow_peer(offset), column) for offset in range(1, along)]
    for device in greeted:
        pl.semaphore_signal(barrier, inc=1, device_id=device, device_id_type=MESH)
    pl.semaphore_wait(barrier, len(greeted))

    def remote(source, target, send, recv, device):
        return pltpu.make_async_remote_copy(
            src_ref=source,
            dst_ref=target,
            send_sem=send,
            recv_sem=recv,
            device_id=device,
            device_id_type=MESH,
        )

    def block(start, size):
        return pl.ds(pl.multiple_of(start * size, size), size)

    core_copies = [
        remote(source.at[1], target, core_send.at[place], core_recv.at[place], sibling)
        for place, (source, target) in enumerate(
            [(down_ref, down_sib), (up_ref, up_sib), (out_ref, out_sib)]
        )
    ]
    attn_copy = remote(
        attn_ref.at[:, block(level * 2 + other, width)],
        attn_in,
        core_send.at[3],
        core_recv.at[3],
        sibling,
    )

    partners = [sibling]
    bit = 1
    while bit < levels:
        partners.append((row, (level + bit - 2 * bit * lax.rem(lax.div(level, bit), 2)) * 2 + core))
        bit *= 2
    bit = 1
    while bit < across * along:
        partners.append((row + bit - 2 * bit * lax.rem(lax.div(row, bit), 2), column))
        bit *= 2

    def small_copy(turn):
        return remote(
            small_sums.at[turn],
            small_in.at[turn],
            small_send.at[turn],
            small_recv.at[turn],
            partners[turn],
        )

    small_turn = [0]

    def small_step():
        turn = small_turn[0]
        if turn > len(partners):
            return
        if turn > 0:
            small_copy(turn - 1).wait()
            small_sums[turn] = small_sums[turn - 1] + small_in[turn - 1]
        if turn < len(partners):
            small_copy(turn).start()
        small_turn[0] += 1

    def layer_copy(target, place_out, place_in):
        return remote(
            layer_ref.at[:, block(target, width)],
            layer_out_ref.at[block(column, own_len)],
            layer_send.at[place_out],
            layer_recv.at[place_in],
            (row, target),
        )

    layer_copies = [layer_copy(level * 2 + other, 0, 0)]
    for offset in offsets:
        back = levels - offset
        layer_copies.append(
            layer_copy(peer_level(offset) * 2 + core, 2 * offset - 1, 2 * back - 1)
        )
        layer_copies.append(layer_copy(peer_level(offset) * 2 + other, 2 * offset, 2 * back))
    layer_keep = pltpu.make_async_copy(
        layer_ref.at[:, block(column, width)], layer_out_ref.at[block(column, own_len)], keep_sem
    )

    small_sums[0] = small_ref[...]
    core_copies[0].start()
    small_step()
    for copy in core_copies[1:] + [attn_copy]:
        copy.start()
    layer_keep.start()
    for copy in layer_copies:
        copy.start()

    def input_part(turn, target):
        return dot_nt(
            query_key_value_ref[block(turn, own_len), :], weights_ref[block(target, width), :]
        )

    def part_copy(turn, place):
        rows = block(turn, own_len)
        return remote(
            core_out.at[place, rows],
            core_in.at[place, rows],
            part_send.at[turn, place],
            part_recv.at[turn, place],
            sibling,
        )

    @pl.loop(0, cols)
    def _(turn):
        for place in range(levels):
            core_out[place, block(turn, own_len), :] = input_part(turn, place * 2 + other).astype(
                low
            )
            part_copy(turn, place).start()

    sums = (down_sib, up_sib, out_sib, qkv_sums)
    firsts = (down_ref, up_ref, out_ref)
    got = (down_got, up_got, out_got, qkv_got)
    passed = (down_pass, up_pass, out_pass, qkv_pass)
    landed = (down_in, up_in, out_in, qkv_in)
    shares = (share_down_ref, share_up_ref, share_out_ref, share_qkv_ref)

    def across_copy(kind, turn, offset):
        return remote(
            sums[kind].at[block(turn * across + lax.rem(fast + offset, across), shard)],
            got[kind].at[across - offset - 1, block(turn, shard)],
            across_send.at[kind, turn, offset - 1],
            across_recv.at[kind, turn, across - offset - 1],
            (fast_peer(offset), column),
        )

    def along_copy(kind, offset):
        return remote(
            passed[kind].at[offset - 1],
            landed[kind].at[along - offset - 1],
            along_send.at[kind, offset - 1],
            along_recv.at[kind, along - offset - 1],
            (slow_peer(offset), column),
        )

    def give_across(kind, turn):
        for offset in range(1, across):
            across_copy(kind, turn, offset).start()

    for kind in range(3):
        core_copies[kind].wait()

        @pl.loop(0, along)
        def _(turn):
            rows = block(turn, across * shard)
            sums[kind][rows, :] = (
                firsts[kind][0, rows, :].astype(full) + sums[kind][rows, :].astype(full)
            ).astype(low)
            give_across(kind, turn)

        small_step()

    @pl.loop(0, along)
    def _(turn):
        rows = block(turn, across * shard)
        qkv_sums[rows, :] = dot_tn(features_ref[:, rows], query_key_value_ref[...]).astype(low)
        give_across(3, turn)

    small_step()

    def level_copy(turn, offset):
        rows = block(turn, own_len)
        return remote(
            level_out.at[offset - 1, rows],
            level_in.at[levels - offset - 1, rows],
            level_send.at[turn, offset - 1],
            level_recv.at[turn, levels - offset - 1],
            (row, peer_level(offset) * 2 + core),
        )

    @pl.loop(0, cols)
    def _(turn):
        rows = block(turn, own_len)
        for offset in offsets:
            place = peer_level(offset)
            part = input_part(turn, place * 2 + core)
            part_copy(turn, place).wait_recv()
            level_out[offset - 1, rows, :] = (part + core_in[place, rows, :].astype(full)).astype(
                low
            )
            level_copy(turn, offset).start()

    small_step()

    def own_shard(kind, turn):
        for offset in range(1, across):
            across_copy(kind, turn, offset).wait_recv()
        total = sums[kind][block(turn * across + fast, shard), :].astype(full)
        for place in range(across - 1):
            total += got[kind][place, block(turn, shard), :].astype(full)
        return total

    for kind in range(KINDS):
        for offset in range(1, along):
            turn = lax.rem(slow + offset, along)
            passed[kind][offset - 1] = own_shard(kind, turn).astype(low)
            along_copy(kind, offset).start()
        shares[kind][...] = own_shard(kind, slow)

    while small_turn[0] <= len(partners):
        small_step()
    small_out_ref[...] = small_sums[len(partners)]

    attn_copy.wait()

    def finish_input(turn, attn_part):
        rows = block(turn, own_len)
        total = input_part(turn, column) + attn_part.astype(full)
        part_copy(turn, level).wait_recv()
        total += core_in[level, rows, :].astype(full)
        for offset in offsets:
            level_copy(turn, offset).wait_recv()
        for place in range(levels - 1):
            total += level_in[place, rows, :].astype(full)
        grad_input_ref[rows, :] = total.astype(low)

    @pl.loop(0, levels)
    def _(place):
        rows = block(place, own_len)
        finish_input(place * 2 + core, attn_ref[rows, block(column, width)])
        finish_input(place * 2 + other, attn_in[rows, :])

    for kind in range(KINDS):
        total = shares[kind][...]
        for offset in range(1, along):
            along_copy(kind, offset).wait_recv()
        for place in range(along - 1):
            total += landed[kind][place].astype(full)
        shares[kind][...] = total

    layer_keep.wait()
    for copy in layer_copies:
        copy.wait()
    for kind in range(KINDS):
        for offset in range(1, along):
            along_copy(kind, offset).wait_send()

        @pl.loop(0, along)
        def _(turn):
            for offset in range(1, across):
                across_copy(kind, turn, offset).wait_send()

    @pl.loop(0, cols)
    def _(turn):
        for place in range(levels):
            part_copy(turn, place).wait_send()
        for offset in offsets:
            level_copy(turn, offset).wait_send()


def finish(
    levels, rows, query_key_value, weights, features, attn_full, layer_own, small, down, up, out
):
    low, full = jnp.bfloat16, jnp.float32
    shape = jax.ShapeDtypeStruct
    across = 2 if rows <= 8 else rows // 4
    along = rows // across
    seq_len, features_all = features.shape
    width = query_key_value.shape[1] // 3
    own_len = layer_own.shape[0]
    shard = features_all // rows
    widths = [down.shape[2], up.shape[2], out.shape[2], 3 * width]
    others = levels - 1
    cols = 2 * levels
    turns = 1 + (levels - 1).bit_length() + (rows - 1).bit_length()
    dma = pltpu.SemaphoreType.DMA
    return pl.pallas_call(
        functools.partial(end_kernel, levels, across, along),
        out_shape=(
            shape((seq_len, width), low),
            shape((seq_len, width), low),
            shape(small.shape, full),
            *(shape((shard, each), full) for each in widths),
        ),
        in_specs=[VMEM] * 9,
        out_specs=[VMEM] * 7,
        scratch_shapes=[
            *(pltpu.VMEM((features_all, each), low) for each in widths),
            *(pltpu.VMEM((across - 1, along * shard, each), low) for each in widths),
            *(pltpu.VMEM((along - 1, shard, each), low) for each in widths),
            *(pltpu.VMEM((along - 1, shard, each), low) for each in widths),
            pltpu.VMEM((levels, seq_len, width), low),
            pltpu.VMEM((levels, seq_len, width), low),
            pltpu.VMEM((others, seq_len, width), low),
            pltpu.VMEM((others, seq_len, width), low),
            pltpu.VMEM((levels * own_len, width), low),
            pltpu.VMEM((turns + 1, *small.shape), full),
            pltpu.VMEM((turns, *small.shape), full),
            dma((4,)),
            dma((4,)),
            dma((cols, levels)),
            dma((cols, levels)),
            dma((cols, others)),
            dma((cols, others)),
            dma((cols,)),
            dma((cols,)),
            dma((KINDS, along, across - 1)),
            dma((KINDS, along, across - 1)),
            dma((KINDS, along - 1)),
            dma((KINDS, along - 1)),
            dma((turns,)),
            dma((turns,)),
            dma,
        ],
        compiler_params=pltpu.CompilerParams(
            collective_id=2, has_side_effects=True, vmem_limit_bytes=60 * 1024 * 1024
        ),
        cost_estimate=pl.CostEstimate(
            flops=4 * seq_len * features_all * 3 * width,
            bytes_accessed=40 * 1024 * 1024,
            transcendentals=0,
        ),
    )(query_key_value, weights, features, attn_full, layer_own, small, down, up, out)


def to_tokens(portion):
    return lax.all_to_all(portion, "col", split_axis=0, concat_axis=1, tiled=True)


def into_full(portion, start_at, full_len):
    return lax.dynamic_update_slice_in_dim(
        jnp.zeros((full_len,), jnp.float32), portion, start_at, 0
    )


def on_device(
    hidden_in,
    out_grad,
    lengths,
    global_blocks,
    rand_blocks,
    w_query,
    b_query,
    w_key,
    w_value,
    b_value,
    w_out,
    b_out,
    ln1_gain,
    ln1_bias,
    w_up,
    b_up,
    w_down,
    b_down,
    ln2_gain,
    ln2_bias,
):
    low = jnp.bfloat16
    seq_len = hidden_in.shape[0]
    feat_cols = hidden_in.shape[1]
    unit_cols = w_up.shape[1]
    cols = lax.axis_size("col")
    features_all = feat_cols * cols
    units_all = unit_cols * cols
    num_blocks = seq_len // BLK
    head_count = feat_cols // DH
    own_len = seq_len // cols
    column = lax.axis_index("col")
    feat_start = column * feat_cols
    unit_start = column * unit_cols
    own_start = column * own_len
    length = lengths[0]
    tables = (
        global_blocks.reshape(-1),
        rand_blocks.reshape(-1),
        limits_of(length, global_blocks[0], rand_blocks[0], num_blocks, head_count),
    )
    full_qkv = lax.all_gather(
        jnp.concatenate([w_query.astype(low), w_key.astype(low), w_value.astype(low)], axis=1),
        "row",
        axis=0,
        tiled=True,
    )
    features = lax.all_gather(hidden_in, "col", axis=1, tiled=True)
    full_out = lax.all_gather(w_out.astype(low).T, "row", axis=0, tiled=True)
    full_up = lax.all_gather(w_up.astype(low), "row", axis=0, tiled=True)
    full_down = lax.all_gather(w_down.astype(low).T, "row", axis=0, tiled=True)
    own_features = lax.dynamic_slice_in_dim(features, own_start, own_len, 0)
    valid = (jnp.arange(seq_len) < length)[:, None]
    upstream = to_tokens(jnp.where(valid, out_grad, 0))
    own_valid = (own_start + jnp.arange(own_len) < length).astype(jnp.float32)[:, None]

    full_query = full_qkv[:, :feat_cols]
    full_key = full_qkv[:, feat_cols : 2 * feat_cols]
    full_value = full_qkv[:, 2 * feat_cols :]
    queries = (
        dot(features, full_query) + lax.dynamic_slice_in_dim(b_query, feat_start, feat_cols)
    ).astype(low)
    key_rows = dot(features, full_key).astype(low)
    value_rows = (
        dot(features, full_value) + lax.dynamic_slice_in_dim(b_value, feat_start, feat_cols)
    ).astype(low)
    context, *stats = attend(queries, key_rows, value_rows, tables)

    sibling = column + 1 - 2 * lax.rem(column, 2)
    layer_own, context_grad, attn_full, small, up_small, grad_up, grad_down, grad_out = middle(
        cols // 2,
        context,
        own_features,
        upstream,
        own_valid,
        full_out,
        full_up,
        full_down,
        jnp.stack([b_out, ln1_gain, ln1_bias, b_down, ln2_gain, ln2_bias, b_out, b_out]),
        jnp.stack(
            [
                lax.dynamic_slice_in_dim(b_up, unit_start, unit_cols),
                lax.dynamic_slice_in_dim(b_up, sibling * unit_cols, unit_cols),
            ]
        ),
    )
    query_key_value, bias_sums = attend_back(
        queries, key_rows, value_rows, tables, stats, context_grad
    )
    up_sums = into_full(up_small[0], unit_start, units_all) + into_full(
        up_small[1], sibling * unit_cols, units_all
    )
    bias_full = lax.dynamic_update_slice(
        jnp.zeros((4, features_all), jnp.float32), bias_sums, (0, feat_start)
    )
    grad_input, layer_out, small, down_share, up_share, out_share, qkv_share = finish(
        cols // 2,
        lax.axis_size("row"),
        query_key_value,
        full_qkv,
        features,
        attn_full,
        layer_own,
        jnp.concatenate([small, up_sums.reshape(-1, features_all), bias_full], axis=0),
        grad_down,
        grad_up,
        grad_out,
    )
    return (
        layer_out,
        grad_input,
        qkv_share[:, :feat_cols],
        small[-4],
        qkv_share[:, feat_cols : 2 * feat_cols],
        qkv_share[:, 2 * feat_cols :],
        small[-3],
        out_share.T,
        small[5],
        small[3],
        small[4],
        up_share,
        small[8:-4].reshape(-1),
        down_share.T,
        small[2],
        small[0],
        small[1],
    )


def solution(mesh):
    placed = (
        P("row", "col"),
        P("row", "col"),
        P("row"),
        P("row", None),
        P("row", None, "col", None),
        P("row", "col"),
        P(),
        P("row", "col"),
        P("row", "col"),
        P(),
        P("col", "row"),
        P(),
        P(),
        P(),
        P("row", "col"),
        P(),
        P("col", "row"),
        P(),
        P(),
        P(),
    )
    return jax.shard_map(
        on_device,
        mesh=mesh,
        in_specs=placed,
        out_specs=(
            P("row", "col"),
            P("row", "col"),
            P("row", "col"),
            P(),
            P("row", "col"),
            P("row", "col"),
            P(),
            P("col", "row"),
            P(),
            P(),
            P(),
            P("row", "col"),
            P(),
            P("col", "row"),
            P(),
            P(),
            P(),
        ),
        check_vma=False,
    )
```

```python
import functools
import math

import jax
import jax.numpy as jnp
from jax import lax
from jax.experimental import pallas as pl
from jax.experimental.pallas import tpu as pltpu
from jax.sharding import PartitionSpec as P

DH = 64
BLK = 64
MESH = pl.DeviceIdType.MESH
KINDS = 4


epsilon = 1e-06


def lane_heads(rows, width):
    return lax.broadcasted_iota(jnp.int32, (rows, width), 1) // DH


def by_diagonal(rows, width):
    lane_head = lane_heads(BLK, width)
    zero = jnp.zeros_like(rows)
    return jnp.concatenate(
        [jnp.where(lane_head == head, rows, zero) for head in range(width // DH)], axis=0
    )


def from_diagonal(square, width):
    lane_head = lane_heads(BLK, width)
    result = jnp.zeros((BLK, width), jnp.float32)
    for head in range(width // DH):
        result = jnp.where(lane_head == head, square[head * BLK : (head + 1) * BLK, :], result)
    return result


def slot_starts(step, num_blocks, head_count, globals_ref, random_ref):
    shared = [
        jnp.maximum(step - 1, 0),
        step,
        jnp.minimum(step + 1, num_blocks - 1),
        globals_ref[0],
        globals_ref[1],
    ]
    base = step * (head_count * 3)
    apart = [
        [random_ref[base + head * 3 + slot] for head in range(head_count)] for slot in range(3)
    ]
    return shared, apart


def lane_groups(head_count):
    per_group = min(128 // DH, head_count)
    return [
        (first * DH, per_group * DH, list(range(first, first + per_group)))
        for first in range(0, head_count, per_group)
    ]


def picked_rows(rows_ref, shared, apart, head_count):
    pieces = [rows_ref[block] for block in shared]
    for blocks in apart:
        groups = []
        for lane, width, heads in lane_groups(head_count):
            lane_head = lane_heads(BLK, width)
            piece = rows_ref[blocks[heads[0]], :, lane : lane + width]
            for place, head in enumerate(heads[1:], 1):
                other = rows_ref[blocks[head], :, lane : lane + width]
                piece = jnp.where(lane_head >= place, other, piece)
            groups.append(piece)
        pieces.append(jnp.concatenate(groups, axis=1) if len(groups) > 1 else groups[0])
    return jnp.concatenate(pieces, axis=0)


def put_rows(sums_ref, values_in, shared, apart, head_count):
    for slot, block in enumerate(shared):
        sums_ref[block] += values_in[slot * BLK : (slot + 1) * BLK, :]
    for slot, blocks in enumerate(apart, len(shared)):
        rows = values_in[slot * BLK : (slot + 1) * BLK, :]
        for lane, width, heads in lane_groups(head_count):
            lane_head = lane_heads(BLK, width)
            for place, head in enumerate(heads):
                sums_ref[blocks[head], :, lane : lane + width] += jnp.where(
                    lane_head == place, rows[:, lane : lane + width], 0.0
                )


def masked_scores(picked_keys, grouped, limits_ref, step, width):
    scores = lax.dot_general(
        picked_keys, grouped, (((1,), (1,)), ((), ())), preferred_element_type=jnp.float32
    )
    row = lax.broadcasted_iota(jnp.int32, (BLK, width), 0)
    return [
        jnp.where(
            row < limits_ref[step, slot : slot + 1, :],
            scores[slot * BLK : (slot + 1) * BLK, :],
            -1e30,
        )
        for slot in range(8)
    ]


def attend_blocks(
    first, count, unroll, globals_ref, random_ref, limits_ref, refs, context_ref, stat_refs
):
    queries_ref, keys_ref, values_ref = refs
    highest_ref, scale_ref = stat_refs
    seq_len, width = queries_ref.shape
    head_count = width // DH
    num_blocks = seq_len // BLK

    def one_block(step):
        shared, apart = slot_starts(step, num_blocks, head_count, globals_ref, random_ref)
        own = pl.ds(pl.multiple_of(step * BLK, BLK), BLK)
        grouped = by_diagonal(queries_ref[own, :] * jnp.bfloat16(1.0 / math.sqrt(DH)), width)
        scores = masked_scores(
            picked_rows(keys_ref, shared, apart, head_count), grouped, limits_ref, step, width
        )
        highest = jnp.max(functools.reduce(jnp.maximum, scores), axis=0, keepdims=True)
        exponent = [jnp.exp(piece - highest) for piece in scores]
        denominator = jnp.sum(sum(exponent[1:], exponent[0]), axis=0, keepdims=True)
        scale = 1.0 / denominator
        attn_probs = jnp.concatenate(
            [(piece * scale).astype(jnp.bfloat16) for piece in exponent], axis=0
        )
        square = lax.dot_general(
            attn_probs,
            picked_rows(values_ref, shared, apart, head_count),
            (((0,), (0,)), ((), ())),
            preferred_element_type=jnp.float32,
        )
        context_ref[own, :] = from_diagonal(square, width).astype(jnp.bfloat16)
        highest_ref[step] = highest
        scale_ref[step] = scale

    @pl.loop(0, count // unroll)
    def _(turn):
        for place in range(unroll):
            one_block(first + turn * unroll + place)


def attend_back_kernel(
    head_count,
    unroll,
    globals_ref,
    random_ref,
    limits_ref,
    queries_ref,
    keys_ref,
    values_ref,
    grads_ref,
    highest_ref,
    scale_ref,
    grads_out_ref,
    bias_ref,
    key_sums,
    value_sums,
    query_total,
):
    width = head_count * DH
    num_blocks = queries_ref.shape[0] // BLK
    factor = 1.0 / math.sqrt(DH)
    key_sums[...] = jnp.zeros_like(key_sums)
    value_sums[...] = jnp.zeros_like(value_sums)
    query_total[...] = jnp.zeros_like(query_total)

    def one_block(step):
        shared, apart = slot_starts(step, num_blocks, head_count, globals_ref, random_ref)
        own = pl.ds(pl.multiple_of(step * BLK, BLK), BLK)
        grouped = by_diagonal(queries_ref[own, :] * jnp.bfloat16(factor), width)
        grouped_grad = by_diagonal(grads_ref[own, :], width)
        picked_keys = picked_rows(keys_ref, shared, apart, head_count)
        picked_values = picked_rows(values_ref, shared, apart, head_count)
        scores = masked_scores(picked_keys, grouped, limits_ref, step, width)
        highest = highest_ref[step]
        scale = scale_ref[step]
        attn_probs = [jnp.exp(piece - highest) * scale for piece in scores]
        prob_grad = lax.dot_general(
            picked_values,
            grouped_grad,
            (((1,), (1,)), ((), ())),
            preferred_element_type=jnp.float32,
        )
        prob_grads = [prob_grad[slot * BLK : (slot + 1) * BLK, :] for slot in range(8)]
        products = [left * right for left, right in zip(attn_probs, prob_grads)]
        total = jnp.sum(sum(products[1:], products[0]), axis=0, keepdims=True)
        score_grad = jnp.concatenate(
            [
                (left * (right - total)).astype(jnp.bfloat16)
                for left, right in zip(attn_probs, prob_grads)
            ],
            axis=0,
        )
        probs_low = jnp.concatenate([piece.astype(jnp.bfloat16) for piece in attn_probs], axis=0)
        square = lax.dot_general(
            score_grad, picked_keys, (((0,), (0,)), ((), ())), preferred_element_type=jnp.float32
        )
        query_grad = (from_diagonal(square, width) * factor).astype(jnp.bfloat16)
        grads_out_ref[own, :width] = query_grad
        query_total[...] += jnp.sum(
            query_grad.astype(jnp.float32).reshape(BLK // 8, 8, width), axis=0
        )
        key_part = jnp.dot(score_grad, grouped, preferred_element_type=jnp.float32)
        value_part = jnp.dot(probs_low, grouped_grad, preferred_element_type=jnp.float32)
        put_rows(key_sums, key_part, shared, apart, head_count)
        put_rows(value_sums, value_part, shared, apart, head_count)

    @pl.loop(0, num_blocks // unroll)
    def _(turn):
        for place in range(unroll):
            one_block(turn * unroll + place)

    value_grad = value_sums[...].reshape(queries_ref.shape).astype(jnp.bfloat16)
    seq_len = queries_ref.shape[0]
    grads_out_ref[:, width : 2 * width] = key_sums[...].reshape(seq_len, width).astype(jnp.bfloat16)
    grads_out_ref[:, 2 * width :] = value_grad
    bias_ref[0:1, :] = jnp.sum(query_total[...], axis=0, keepdims=True)
    bias_ref[1:2, :] = jnp.sum(value_grad.astype(jnp.float32), axis=0, keepdims=True)


def limits_of(length, global_ids, random_ids, num_blocks, head_count):
    blocks = jnp.arange(num_blocks, dtype=jnp.int32)
    nearby_raw = blocks[:, None] + jnp.arange(-1, 2, dtype=jnp.int32)[None, :]
    near_ok = (nearby_raw >= 0) & (nearby_raw < num_blocks)
    global_rows = jnp.broadcast_to(global_ids[None, :], (num_blocks, 2))
    global_ok = jnp.all(global_rows[:, :, None] != nearby_raw[:, None, :], axis=2)
    common = jnp.concatenate([nearby_raw, global_rows], axis=1)
    common_ok = jnp.concatenate([near_ok, global_ok], axis=1)
    common_limit = jnp.where(common_ok, length - common * BLK, 0)
    random_limit = jnp.transpose(length - random_ids * BLK, (0, 2, 1))
    return jnp.concatenate(
        [
            jnp.broadcast_to(common_limit[:, :, None], (num_blocks, 5, head_count * DH)),
            jnp.repeat(random_limit, DH, axis=2),
        ],
        axis=1,
    )


VMEM = pl.BlockSpec(memory_space=pltpu.VMEM)
SMEM = pl.BlockSpec(memory_space=pltpu.SMEM)


def attend_back(queries, key_rows, value_rows, tables, stats, context_grad):
    seq_len, width = queries.shape
    head_count = width // DH
    return pl.pallas_call(
        functools.partial(attend_back_kernel, head_count, 2),
        out_shape=(
            jax.ShapeDtypeStruct((seq_len, 3 * width), jnp.bfloat16),
            jax.ShapeDtypeStruct((2, width), jnp.float32),
        ),
        in_specs=[SMEM] * 2 + [VMEM] * 7,
        out_specs=[VMEM] * 2,
        scratch_shapes=[pltpu.VMEM((seq_len // BLK, BLK, width), jnp.float32)] * 2
        + [pltpu.VMEM((8, width), jnp.float32)],
        compiler_params=pltpu.CompilerParams(vmem_limit_bytes=40 * 1024 * 1024),
        cost_estimate=pl.CostEstimate(
            flops=10 * seq_len * 512 * width * head_count,
            bytes_accessed=14 * seq_len * width,
            transcendentals=seq_len * 512 * head_count,
        ),
    )(*tables, queries, key_rows, value_rows, context_grad, *stats)


def dot(left, right):
    return jnp.dot(left, right, preferred_element_type=jnp.float32)


def dot_nt(left, right):
    return lax.dot_general(
        left, right, (((1,), (1,)), ((), ())), preferred_element_type=jnp.float32
    )


def dot_tn(left, right):
    return lax.dot_general(
        left, right, (((0,), (0,)), ((), ())), preferred_element_type=jnp.float32
    )


def gelu_parts(values_in):
    factor = math.sqrt(2.0 / math.pi)
    square = values_in * values_in
    bent = jnp.tanh(factor * (values_in + 0.044715 * (values_in * square)))
    half = 0.5 * (1.0 + bent)
    slope = half + (0.5 * values_in) * (1.0 - bent * bent) * (
        factor + (3.0 * 0.044715 * factor) * square
    )
    return (values_in * half, slope)


def norm_parts(summed):
    average = jnp.mean(summed, axis=1, keepdims=True)
    squares = jnp.mean(summed * summed, axis=1, keepdims=True)
    inv_std = lax.rsqrt(squares - average * average + epsilon)
    return ((summed - average) * inv_std, inv_std)


def norm_back(upstream, normed, inv_std, gain_vec):
    scaled = upstream * gain_vec
    left = jnp.mean(scaled, axis=1, keepdims=True)
    right = jnp.mean(scaled * normed, axis=1, keepdims=True)
    return inv_std * (scaled - left - normed * right)


CHUNKS = 4


def middle_kernel(
    levels,
    context_ref,
    inputs_ref,
    upstream_ref,
    valid_ref,
    out_ref,
    up_ref,
    down_ref,
    vectors_ref,
    b_up_ref,
    layer_out_ref,
    context_grad_ref,
    attn_full,
    small_ref,
    up_small_ref,
    grad_up_ref,
    grad_down_ref,
    grad_out_ref,
    context_sib,
    out_sib,
    up_sib,
    down_sib,
    normed_full,
    ffn_full,
    hidden,
    slope,
    pre_grad,
    unit1,
    inv1,
    ffn_keep,
    part_own,
    send_buf,
    recv_buf,
    context_send,
    stage,
    stage_small,
    send_sem,
    recv_sem,
    core_send,
    core_recv,
    stage_sem,
):
    low = jnp.bfloat16
    row, column = lax.axis_index("row"), lax.axis_index("col")
    core = lax.rem(column, 2)
    level = lax.div(column, 2)
    sibling = (row, column + 1 - 2 * core)
    own_len = inputs_ref.shape[0]
    step = own_len // CHUNKS
    b_out, gain1, shift1, b_down, gain2, shift2 = (
        vectors_ref.at[place : place + 1, :] for place in range(6)
    )

    def peer_level(offset):
        return lax.rem(level + offset, levels)

    barrier = pltpu.get_barrier_semaphore()
    pl.semaphore_signal(barrier, inc=1, device_id=sibling, device_id_type=MESH)
    for offset in range(1, levels):
        pl.semaphore_signal(
            barrier,
            inc=1,
            device_id=(row, peer_level(offset) * 2 + core),
            device_id_type=MESH,
        )
    pl.semaphore_wait(barrier, levels)

    def to_sibling(source, target, place):
        return pltpu.make_async_remote_copy(
            src_ref=source,
            dst_ref=target,
            send_sem=core_send.at[place],
            recv_sem=core_recv.at[place],
            device_id=sibling,
            device_id_type=MESH,
        )

    def rows_of(place, chunk):
        return pl.ds(pl.multiple_of(place * own_len + chunk * step, step), step)

    def own_rows(chunk):
        return pl.ds(pl.multiple_of(chunk * step, step), step)

    def exchange(kind, chunk, offset, source, target):
        return pltpu.make_async_remote_copy(
            src_ref=source,
            dst_ref=target,
            send_sem=send_sem.at[kind, chunk, offset - 1],
            recv_sem=recv_sem.at[kind, chunk, levels - offset - 1],
            device_id=(row, peer_level(offset) * 2 + core),
            device_id_type=MESH,
        )

    def sum_copy(kind, chunk, offset):
        return exchange(
            kind,
            chunk,
            offset,
            send_buf.at[kind // 2, offset - 1, own_rows(chunk)],
            recv_buf.at[kind // 2, levels - offset - 1, own_rows(chunk)],
        )

    def spread_copy(kind, chunk, offset):
        whole = {1: normed_full, 3: ffn_full, 5: attn_full}[kind]
        rows = rows_of(level, chunk)
        return exchange(kind, chunk, offset, whole.at[rows], whole.at[rows])

    def received(kind, chunk):
        return sum(
            recv_buf[kind // 2, place, own_rows(chunk), :].astype(jnp.float32)
            for place in range(levels - 1)
        )

    offsets = range(1, levels)
    context_copies = [
        to_sibling(
            context_ref.at[
                pl.ds(pl.multiple_of((place * 2 + 1 - core) * own_len, own_len), own_len)
            ],
            context_sib.at[pl.ds(place * own_len, own_len)],
            place,
        )
        for place in range(levels)
    ]
    out_copy = to_sibling(out_ref, out_sib, levels)
    up_copy = to_sibling(up_ref, up_sib, levels + 1)
    down_copy = to_sibling(down_ref, down_sib, levels + 2)
    for copy in context_copies + [out_copy, up_copy, down_copy]:
        copy.start()
    small_ref[...] = jnp.zeros_like(small_ref)
    up_small_ref[...] = jnp.zeros_like(up_small_ref)
    for copy in context_copies:
        copy.wait()
    out_copy.wait()

    def context_rows(place, chunk):
        start = (place * 2 + core) * own_len + chunk * step
        return pl.ds(pl.multiple_of(start, step), step)

    def attn_part(place, chunk):
        return dot_nt(context_ref[context_rows(place, chunk), :], out_ref[...]) + dot_nt(
            context_sib[rows_of(place, chunk), :], out_sib[...]
        )

    @pl.loop(0, CHUNKS)
    def _(chunk):
        for offset in offsets:
            send_buf[0, offset - 1, own_rows(chunk), :] = attn_part(
                peer_level(offset), chunk
            ).astype(low)
            sum_copy(0, chunk, offset).start()

    @pl.loop(0, CHUNKS)
    def _(chunk):
        rows = own_rows(chunk)
        summed = (
            inputs_ref[rows, :].astype(jnp.float32) + attn_part(level, chunk) + b_out[...]
        )
        for offset in offsets:
            sum_copy(0, chunk, offset).wait_recv()
        normed, inv_std = norm_parts(summed + received(0, chunk))
        unit1[rows, :] = normed
        inv1[rows, :] = inv_std
        normed_full[rows_of(level, chunk), :] = (normed * gain1[...] + shift1[...]).astype(low)
        for offset in offsets:
            spread_copy(1, chunk, offset).start()

    up_copy.wait()
    down_copy.wait()
    sides = ((up_ref, down_ref), (up_sib, down_sib))

    def feed_forward(place, chunk):
        rows = rows_of(place, chunk)
        normed = normed_full[rows, :]
        total = None
        for side, (up_side, down_side) in enumerate(sides):
            active, bend = gelu_parts(dot(normed, up_side[...]) + b_up_ref[side : side + 1, :])
            active = active.astype(low)
            hidden[side, rows, :] = active
            slope[side, rows, :] = bend
            part = dot_nt(active, down_side[...])
            total = part if total is None else total + part
        return total

    @pl.loop(0, CHUNKS)
    def _(chunk):
        part_own[own_rows(chunk), :] = feed_forward(level, chunk)
        for offset in offsets:
            spread_copy(1, chunk, levels - offset).wait_recv()
            send_buf[1, offset - 1, own_rows(chunk), :] = feed_forward(
                peer_level(offset), chunk
            ).astype(low)
            sum_copy(2, chunk, offset).start()

    @pl.loop(0, CHUNKS)
    def _(chunk):
        rows = own_rows(chunk)
        normed1 = unit1[rows, :] * gain1[...] + shift1[...]
        summed = normed1 + part_own[rows, :] + b_down[...]
        for offset in offsets:
            sum_copy(2, chunk, offset).wait_recv()
        normed, inv_std = norm_parts(summed + received(2, chunk))
        layer_out_ref[rows, :] = jnp.where(
            valid_ref[rows, :] > 0, normed * gain2[...] + shift2[...], 0.0
        ).astype(low)
        upstream = upstream_ref[rows, :].astype(jnp.float32)
        grad = norm_back(upstream, normed, inv_std, gain2[...])
        ffn_keep[rows, :] = grad
        grad_low = grad.astype(low)
        ffn_full[rows_of(level, chunk), :] = grad_low
        for offset in offsets:
            spread_copy(3, chunk, offset).start()
        small_ref[0:1, :] += jnp.sum(upstream * normed, axis=0, keepdims=True)
        small_ref[1:2, :] += jnp.sum(upstream, axis=0, keepdims=True)
        small_ref[2:3, :] += jnp.sum(grad_low.astype(jnp.float32), axis=0, keepdims=True)

    def feed_back(place, chunk):
        rows = rows_of(place, chunk)
        upstream = ffn_full[rows, :]
        total = None
        for side, (up_side, down_side) in enumerate(sides):
            grad = (dot(upstream, down_side[...]) * slope[side, rows, :]).astype(low)
            pre_grad[side, rows, :] = grad
            up_small_ref[side : side + 1, :] += jnp.sum(
                grad.astype(jnp.float32), axis=0, keepdims=True
            )
            part = dot_nt(grad, up_side[...])
            total = part if total is None else total + part
        return total

    @pl.loop(0, CHUNKS)
    def _(chunk):
        part_own[own_rows(chunk), :] = feed_back(level, chunk)
        for offset in offsets:
            spread_copy(3, chunk, levels - offset).wait_recv()
            send_buf[2, offset - 1, own_rows(chunk), :] = feed_back(
                peer_level(offset), chunk
            ).astype(low)
            sum_copy(4, chunk, offset).start()

    def weight_grad(left_ref, right_of, target_ref, buffer):
        tile = buffer.shape[1]
        tiles = left_ref.shape[1] // tile

        def put(side, turn):
            return pltpu.make_async_copy(
                buffer.at[lax.rem(turn, 2)],
                target_ref.at[side, pl.ds(pl.multiple_of(turn * tile, tile), tile)],
                stage_sem.at[lax.rem(turn, 2)],
            )

        for side in range(2):

            @pl.loop(0, tiles)
            def _(turn):
                @pl.when(turn >= 2)
                def _():
                    put(side, turn - 2).wait()

                left = left_ref[:, pl.ds(pl.multiple_of(turn * tile, tile), tile)]
                buffer[lax.rem(turn, 2)] = dot_tn(left, right_of(side)).astype(low)
                put(side, turn).start()

            for turn in range(max(tiles - 2, 0), tiles):
                put(side, turn).wait()

    weight_grad(ffn_full, lambda side: hidden[side], grad_down_ref, stage)

    @pl.loop(0, CHUNKS)
    def _(chunk):
        rows = own_rows(chunk)
        upstream = ffn_keep[rows, :] + part_own[rows, :]
        for offset in offsets:
            sum_copy(4, chunk, offset).wait_recv()
        upstream = upstream + received(4, chunk)
        normed = unit1[rows, :]
        grad_low = norm_back(upstream, normed, inv1[rows, :], gain1[...]).astype(low)
        attn_full[rows_of(level, chunk), :] = grad_low
        for offset in offsets:
            spread_copy(5, chunk, offset).start()
        small_ref[3:4, :] += jnp.sum(upstream * normed, axis=0, keepdims=True)
        small_ref[4:5, :] += jnp.sum(upstream, axis=0, keepdims=True)
        small_ref[5:6, :] += jnp.sum(grad_low.astype(jnp.float32), axis=0, keepdims=True)

    weight_grad(normed_full, lambda side: pre_grad[side], grad_up_ref, stage)

    def context_back(place, chunk):
        rows = rows_of(place, chunk)
        upstream = attn_full[rows, :]
        context_grad_ref[context_rows(place, chunk), :] = dot(upstream, out_ref[...]).astype(low)
        context_send[rows, :] = dot(upstream, out_sib[...]).astype(low)

    @pl.loop(0, CHUNKS)
    def _(chunk):
        context_back(level, chunk)
        for offset in offsets:
            spread_copy(5, chunk, levels - offset).wait_recv()
            context_back(peer_level(offset), chunk)

    back_copies = [
        to_sibling(
            context_send.at[pl.ds(place * own_len, own_len)],
            context_grad_ref.at[
                pl.ds(pl.multiple_of((place * 2 + core) * own_len, own_len), own_len)
            ],
            levels + 3 + place,
        )
        for place in range(levels)
    ]
    for copy in back_copies:
        copy.start()

    own_context = jnp.concatenate(
        [
            context_ref[
                pl.ds(pl.multiple_of((place * 2 + core) * own_len, own_len), own_len), :
            ]
            for place in range(levels)
        ],
        axis=0,
    )
    weight_grad(
        attn_full,
        lambda side: context_sib[...] if side else own_context,
        grad_out_ref,
        stage_small,
    )
    for copy in back_copies:
        copy.wait()
    for kind in range(6):

        @pl.loop(0, CHUNKS)
        def _(chunk):
            for offset in offsets:
                if kind % 2:
                    spread_copy(kind, chunk, offset).wait_send()
                else:
                    sum_copy(kind, chunk, offset).wait_send()


def middle(
    levels, context, inputs, upstream, valid, out_own, up_own, down_own, vectors, b_up_pair
):
    low, full = jnp.bfloat16, jnp.float32
    own_len, features = inputs.shape
    seq_len, width = context.shape
    units = up_own.shape[1]
    tokens = levels * own_len
    others = levels - 1
    tile = 256
    shape = jax.ShapeDtypeStruct
    hbm = pl.BlockSpec(memory_space=pl.ANY)
    return pl.pallas_call(
        functools.partial(middle_kernel, levels),
        out_shape=(
            shape((own_len, features), low),
            shape((seq_len, width), low),
            shape((tokens, features), low),
            shape((8, features), full),
            shape((2, units), full),
            shape((2, features, units), low),
            shape((2, features, units), low),
            shape((2, features, width), low),
        ),
        in_specs=[VMEM] * 9,
        out_specs=[VMEM] * 5 + [hbm] * 3,
        scratch_shapes=[
            pltpu.VMEM((tokens, width), low),
            pltpu.VMEM((features, width), low),
            pltpu.VMEM((features, units), low),
            pltpu.VMEM((features, units), low),
            pltpu.VMEM((tokens, features), low),
            pltpu.VMEM((tokens, features), low),
            pltpu.VMEM((2, tokens, units), low),
            pltpu.VMEM((2, tokens, units), full),
            pltpu.VMEM((2, tokens, units), low),
            pltpu.VMEM((own_len, features), full),
            pltpu.VMEM((own_len, 1), full),
            pltpu.VMEM((own_len, features), full),
            pltpu.VMEM((own_len, features), full),
            pltpu.VMEM((3, others, own_len, features), low),
            pltpu.VMEM((3, others, own_len, features), low),
            pltpu.VMEM((tokens, width), low),
            pltpu.VMEM((2, tile, units), low),
            pltpu.VMEM((2, tile, width), low),
            pltpu.SemaphoreType.DMA((6, CHUNKS, others)),
            pltpu.SemaphoreType.DMA((6, CHUNKS, others)),
            pltpu.SemaphoreType.DMA((2 * levels + 3,)),
            pltpu.SemaphoreType.DMA((2 * levels + 3,)),
            pltpu.SemaphoreType.DMA((2,)),
        ],
        compiler_params=pltpu.CompilerParams(
            collective_id=1, has_side_effects=True, vmem_limit_bytes=60 * 1024 * 1024
        ),
        cost_estimate=pl.CostEstimate(
            flops=2 * tokens * features * (12 * units + 6 * width),
            bytes_accessed=40 * 1024 * 1024,
            transcendentals=2 * tokens * units,
        ),
    )(context, inputs, upstream, valid, out_own, up_own, down_own, vectors, b_up_pair)


def front_kernel(
    levels,
    across,
    along,
    globals_ref,
    random_ref,
    limits_ref,
    hidden_ref,
    grads_ref,
    b_query_ref,
    b_value_ref,
    part_qkv_ref,
    part_out_ref,
    part_up_ref,
    part_down_ref,
    features_ref,
    own_ref,
    upstream_ref,
    queries_ref,
    keys_ref,
    values_ref,
    context_ref,
    highest_ref,
    scale_ref,
    full_qkv_ref,
    full_out_ref,
    full_up_ref,
    full_down_ref,
    level_send,
    level_recv,
    core_send,
    core_recv,
    swap_send,
    swap_recv,
    along_send,
    along_recv,
    across_send,
    across_recv,
):
    low, full = jnp.bfloat16, jnp.float32
    row, column = lax.axis_index("row"), lax.axis_index("col")
    core, level = lax.rem(column, 2), lax.div(column, 2)
    fast, slow = lax.rem(row, across), lax.div(row, across)
    cols = 2 * levels
    seq_len, width = hidden_ref.shape
    own_len = seq_len // cols
    shard = part_qkv_ref.shape[0]
    other = 1 - core
    sibling = (row, level * 2 + other)
    offsets = range(1, levels)

    def peer_level(offset):
        return lax.rem(level + offset, levels)

    def fast_peer(offset):
        return slow * across + lax.rem(fast + offset, across)

    def slow_peer(offset):
        return lax.rem(slow + offset, along) * across + fast

    barrier = pltpu.get_barrier_semaphore()
    greeted = [sibling]
    for offset in offsets:
        greeted += [(row, peer_level(offset) * 2 + core), (row, peer_level(offset) * 2 + other)]
    greeted += [(fast_peer(offset), column) for offset in range(1, across)]
    greeted += [(slow_peer(offset), column) for offset in range(1, along)]
    for device in greeted:
        pl.semaphore_signal(barrier, inc=1, device_id=device, device_id_type=MESH)
    pl.semaphore_wait(barrier, len(greeted))

    def remote(source, target, send, recv, device):
        return pltpu.make_async_remote_copy(
            src_ref=source,
            dst_ref=target,
            send_sem=send,
            recv_sem=recv,
            device_id=device,
            device_id_type=MESH,
        )

    def block(start, size):
        return pl.ds(pl.multiple_of(start * size, size), size)

    def level_copy(turn, offset):
        rows = block(turn, own_len)
        return remote(
            hidden_ref.at[rows],
            features_ref.at[rows, block(column, width)],
            level_send.at[turn, offset - 1],
            level_recv.at[turn, levels - offset - 1],
            (row, peer_level(offset) * 2 + core),
        )

    def core_copy(turn, offset):
        view = features_ref.at[block(turn, own_len), block(peer_level(offset) * 2 + core, width)]
        return remote(
            view, view, core_send.at[turn, offset], core_recv.at[turn, offset], sibling
        )

    @pl.loop(0, cols)
    def _(turn):
        for offset in offsets:
            level_copy(turn, offset).start()
        rows = block(turn, own_len)
        features_ref[rows, block(column, width)] = hidden_ref[rows, :]
        core_copy(turn, 0).start()

    parts = (part_qkv_ref, part_out_ref, part_up_ref, part_down_ref)
    fulls = (full_qkv_ref, full_out_ref, full_up_ref, full_down_ref)

    def shard_rows(place):
        return block(place * across + fast, shard)

    def along_copy(kind, offset):
        view = fulls[kind].at[shard_rows(slow)]
        return remote(
            view,
            view,
            along_send.at[kind, offset - 1],
            along_recv.at[kind, along - offset - 1],
            (slow_peer(offset), column),
        )

    def across_copy(kind, place, offset):
        view = fulls[kind].at[shard_rows(place)]
        return remote(
            view,
            view,
            across_send.at[kind, place, offset - 1],
            across_recv.at[kind, place, across - offset - 1],
            (fast_peer(offset), column),
        )

    for kind in range(KINDS):
        fulls[kind][shard_rows(slow), :] = parts[kind][...]
        for offset in range(1, along):
            along_copy(kind, offset).start()
        for offset in range(1, across):
            across_copy(kind, slow, offset).start()

    def swap_copy(target, place_out, place_in):
        return remote(
            grads_ref.at[block(target, own_len)],
            upstream_ref.at[:, block(column, width)],
            swap_send.at[place_out],
            swap_recv.at[place_in],
            (row, target),
        )

    swaps = [swap_copy(level * 2 + other, 0, 0)]
    for offset in offsets:
        back = levels - offset
        swaps.append(swap_copy(peer_level(offset) * 2 + core, 2 * offset - 1, 2 * back - 1))
        swaps.append(swap_copy(peer_level(offset) * 2 + other, 2 * offset, 2 * back))
    for copy in swaps:
        copy.start()
    upstream_ref[:, block(column, width)] = grads_ref[block(column, own_len), :]

    def pass_on(kind):
        for offset in range(1, along):
            along_copy(kind, along - offset).wait_recv()
            for step in range(1, across):
                across_copy(kind, lax.rem(slow + offset, along), step).start()

    def await_shards(kind):
        @pl.loop(0, along)
        def _(place):
            for offset in range(1, across):
                across_copy(kind, place, offset).wait_recv()

    pass_on(0)
    await_shards(0)

    @pl.loop(0, cols)
    def _(turn):
        rows = block(turn, own_len)
        for offset in offsets:
            level_copy(turn, levels - offset).wait_recv()
            core_copy(turn, offset).start()
        for offset in range(levels):
            core_copy(turn, offset).wait_recv()
        values_in = features_ref[rows, :]
        queries_ref[rows, :] = (
            dot(values_in, full_qkv_ref[:, :width]) + b_query_ref[...]
        ).astype(low)
        blocks = pl.ds(turn * (own_len // BLK), own_len // BLK)
        by_block = (own_len // BLK, BLK, width)
        keys_ref[blocks] = (
            dot(values_in, full_qkv_ref[:, width : 2 * width]).astype(low).reshape(by_block)
        )
        values_ref[blocks] = (
            (dot(values_in, full_qkv_ref[:, 2 * width :]) + b_value_ref[...])
            .astype(low)
            .reshape(by_block)
        )

    own_ref[...] = features_ref[block(column, own_len), :]
    pass_on(1)
    count = seq_len // BLK // 4
    for part in range(4):
        attend_blocks(
            part * count,
            count,
            2,
            globals_ref,
            random_ref,
            limits_ref,
            (queries_ref, keys_ref, values_ref),
            context_ref,
            (highest_ref, scale_ref),
        )
        if part == 1:
            pass_on(2)
    pass_on(3)
    for kind in range(1, KINDS):
        await_shards(kind)
    for copy in swaps:
        copy.wait()
    for kind in range(KINDS):
        for offset in range(1, along):
            along_copy(kind, offset).wait_send()

        @pl.loop(0, along)
        def _(place):
            for offset in range(1, across):
                across_copy(kind, place, offset).wait_send()

    @pl.loop(0, cols)
    def _(turn):
        for offset in offsets:
            level_copy(turn, offset).wait_send()
        for offset in range(levels):
            core_copy(turn, offset).wait_send()


def across_of(rows):
    return 2 if rows <= 8 else rows // 4


def front(levels, rows, tables, hidden_in, grads, biases, parts):
    low, full = jnp.bfloat16, jnp.float32
    shape = jax.ShapeDtypeStruct
    across = across_of(rows)
    along = rows // across
    seq_len, width = hidden_in.shape
    cols = 2 * levels
    own_len = seq_len // cols
    features_all = width * cols
    others = levels - 1
    stat = shape((seq_len // BLK, 1, width), full)
    dma = pltpu.SemaphoreType.DMA
    return pl.pallas_call(
        functools.partial(front_kernel, levels, across, along),
        out_shape=(
            shape((seq_len, features_all), low),
            shape((own_len, features_all), low),
            shape((own_len, features_all), low),
            shape((seq_len, width), low),
            shape((seq_len // BLK, BLK, width), low),
            shape((seq_len // BLK, BLK, width), low),
            shape((seq_len, width), low),
            stat,
            stat,
            *(shape((part.shape[0] * rows, part.shape[1]), low) for part in parts),
        ),
        in_specs=[SMEM] * 2 + [VMEM] * 9,
        out_specs=[VMEM] * 13,
        scratch_shapes=[
            dma((cols, others)),
            dma((cols, others)),
            dma((cols, levels)),
            dma((cols, levels)),
            dma((cols,)),
            dma((cols,)),
            dma((KINDS, along - 1)),
            dma((KINDS, along - 1)),
            dma((KINDS, along, across - 1)),
            dma((KINDS, along, across - 1)),
        ],
        compiler_params=pltpu.CompilerParams(
            collective_id=3, has_side_effects=True, vmem_limit_bytes=48 * 1024 * 1024
        ),
        cost_estimate=pl.CostEstimate(
            flops=2 * seq_len * features_all * 3 * width,
            bytes_accessed=20 * 1024 * 1024,
            transcendentals=seq_len * 512 * (width // DH),
        ),
    )(*tables, hidden_in, grads, *biases, *parts)


def end_kernel(
    levels,
    across,
    along,
    query_key_value_ref,
    weights_ref,
    features_ref,
    attn_ref,
    layer_ref,
    small_ref,
    down_ref,
    up_ref,
    out_ref,
    grad_input_ref,
    layer_out_ref,
    small_out_ref,
    share_down_ref,
    share_up_ref,
    share_out_ref,
    share_qkv_ref,
    down_sib,
    up_sib,
    out_sib,
    qkv_sums,
    down_got,
    up_got,
    out_got,
    qkv_got,
    down_pass,
    up_pass,
    out_pass,
    qkv_pass,
    down_in,
    up_in,
    out_in,
    qkv_in,
    core_out,
    core_in,
    level_out,
    level_in,
    attn_in,
    small_sums,
    small_in,
    core_send,
    core_recv,
    part_send,
    part_recv,
    level_send,
    level_recv,
    layer_send,
    layer_recv,
    across_send,
    across_recv,
    along_send,
    along_recv,
    small_send,
    small_recv,
    keep_sem,
):
    low, full = jnp.bfloat16, jnp.float32
    row, column = lax.axis_index("row"), lax.axis_index("col")
    core, level = lax.rem(column, 2), lax.div(column, 2)
    fast, slow = lax.rem(row, across), lax.div(row, across)
    cols = 2 * levels
    seq_len = features_ref.shape[0]
    own_len = seq_len // cols
    width = grad_input_ref.shape[1]
    shard = share_qkv_ref.shape[0]
    other = 1 - core
    sibling = (row, level * 2 + other)
    offsets = range(1, levels)

    def peer_level(offset):
        return lax.rem(level + offset, levels)

    def fast_peer(offset):
        return slow * across + lax.rem(fast + offset, across)

    def slow_peer(offset):
        return lax.rem(slow + offset, along) * across + fast

    barrier = pltpu.get_barrier_semaphore()
    greeted = [sibling]
    for offset in offsets:
        greeted += [(row, peer_level(offset) * 2 + core), (row, peer_level(offset) * 2 + other)]
    greeted += [(fast_peer(offset), column) for offset in range(1, across)]
    greeted += [(slow_peer(offset), column) for offset in range(1, along)]
    for device in greeted:
        pl.semaphore_signal(barrier, inc=1, device_id=device, device_id_type=MESH)
    pl.semaphore_wait(barrier, len(greeted))

    def remote(source, target, send, recv, device):
        return pltpu.make_async_remote_copy(
            src_ref=source,
            dst_ref=target,
            send_sem=send,
            recv_sem=recv,
            device_id=device,
            device_id_type=MESH,
        )

    def block(start, size):
        return pl.ds(pl.multiple_of(start * size, size), size)

    core_copies = [
        remote(source.at[1], target, core_send.at[place], core_recv.at[place], sibling)
        for place, (source, target) in enumerate(
            [(down_ref, down_sib), (up_ref, up_sib), (out_ref, out_sib)]
        )
    ]
    attn_copy = remote(
        attn_ref.at[:, block(level * 2 + other, width)],
        attn_in,
        core_send.at[3],
        core_recv.at[3],
        sibling,
    )

    partners = [sibling]
    bit = 1
    while bit < levels:
        partners.append((row, (level + bit - 2 * bit * lax.rem(lax.div(level, bit), 2)) * 2 + core))
        bit *= 2
    bit = 1
    while bit < across * along:
        partners.append((row + bit - 2 * bit * lax.rem(lax.div(row, bit), 2), column))
        bit *= 2

    def small_copy(turn):
        return remote(
            small_sums.at[turn],
            small_in.at[turn],
            small_send.at[turn],
            small_recv.at[turn],
            partners[turn],
        )

    small_turn = [0]

    def small_step():
        turn = small_turn[0]
        if turn > len(partners):
            return
        if turn > 0:
            small_copy(turn - 1).wait()
            small_sums[turn] = small_sums[turn - 1] + small_in[turn - 1]
        if turn < len(partners):
            small_copy(turn).start()
        small_turn[0] += 1

    def layer_copy(target, place_out, place_in):
        return remote(
            layer_ref.at[:, block(target, width)],
            layer_out_ref.at[block(column, own_len)],
            layer_send.at[place_out],
            layer_recv.at[place_in],
            (row, target),
        )

    layer_copies = [layer_copy(level * 2 + other, 0, 0)]
    for offset in offsets:
        back = levels - offset
        layer_copies.append(
            layer_copy(peer_level(offset) * 2 + core, 2 * offset - 1, 2 * back - 1)
        )
        layer_copies.append(layer_copy(peer_level(offset) * 2 + other, 2 * offset, 2 * back))
    layer_keep = pltpu.make_async_copy(
        layer_ref.at[:, block(column, width)], layer_out_ref.at[block(column, own_len)], keep_sem
    )

    small_sums[0] = small_ref[...]
    core_copies[0].start()
    small_step()
    for copy in core_copies[1:] + [attn_copy]:
        copy.start()
    layer_keep.start()
    for copy in layer_copies:
        copy.start()

    def input_part(turn, target):
        return dot_nt(
            query_key_value_ref[block(turn, own_len), :], weights_ref[block(target, width), :]
        )

    def part_copy(turn, place):
        rows = block(turn, own_len)
        return remote(
            core_out.at[place, rows],
            core_in.at[place, rows],
            part_send.at[turn, place],
            part_recv.at[turn, place],
            sibling,
        )

    @pl.loop(0, cols)
    def _(turn):
        for place in range(levels):
            core_out[place, block(turn, own_len), :] = input_part(turn, place * 2 + other).astype(
                low
            )
            part_copy(turn, place).start()

    sums = (down_sib, up_sib, out_sib, qkv_sums)
    firsts = (down_ref, up_ref, out_ref)
    got = (down_got, up_got, out_got, qkv_got)
    passed = (down_pass, up_pass, out_pass, qkv_pass)
    landed = (down_in, up_in, out_in, qkv_in)
    shares = (share_down_ref, share_up_ref, share_out_ref, share_qkv_ref)

    def across_copy(kind, turn, offset):
        return remote(
            sums[kind].at[block(turn * across + lax.rem(fast + offset, across), shard)],
            got[kind].at[across - offset - 1, block(turn, shard)],
            across_send.at[kind, turn, offset - 1],
            across_recv.at[kind, turn, across - offset - 1],
            (fast_peer(offset), column),
        )

    def along_copy(kind, offset):
        return remote(
            passed[kind].at[offset - 1],
            landed[kind].at[along - offset - 1],
            along_send.at[kind, offset - 1],
            along_recv.at[kind, along - offset - 1],
            (slow_peer(offset), column),
        )

    def give_across(kind, turn):
        for offset in range(1, across):
            across_copy(kind, turn, offset).start()

    for kind in range(3):
        core_copies[kind].wait()

        @pl.loop(0, along)
        def _(turn):
            rows = block(turn, across * shard)
            sums[kind][rows, :] = (
                firsts[kind][0, rows, :].astype(full) + sums[kind][rows, :].astype(full)
            ).astype(low)
            give_across(kind, turn)

        small_step()

    @pl.loop(0, along)
    def _(turn):
        rows = block(turn, across * shard)
        qkv_sums[rows, :] = dot_tn(features_ref[:, rows], query_key_value_ref[...]).astype(low)
        give_across(3, turn)

    small_step()

    def level_copy(turn, offset):
        rows = block(turn, own_len)
        return remote(
            level_out.at[offset - 1, rows],
            level_in.at[levels - offset - 1, rows],
            level_send.at[turn, offset - 1],
            level_recv.at[turn, levels - offset - 1],
            (row, peer_level(offset) * 2 + core),
        )

    @pl.loop(0, cols)
    def _(turn):
        rows = block(turn, own_len)
        for offset in offsets:
            place = peer_level(offset)
            part = input_part(turn, place * 2 + core)
            part_copy(turn, place).wait_recv()
            level_out[offset - 1, rows, :] = (part + core_in[place, rows, :].astype(full)).astype(
                low
            )
            level_copy(turn, offset).start()

    small_step()

    def own_shard(kind, turn):
        for offset in range(1, across):
            across_copy(kind, turn, offset).wait_recv()
        total = sums[kind][block(turn * across + fast, shard), :].astype(full)
        for place in range(across - 1):
            total += got[kind][place, block(turn, shard), :].astype(full)
        return total

    for kind in range(KINDS):
        for offset in range(1, along):
            turn = lax.rem(slow + offset, along)
            passed[kind][offset - 1] = own_shard(kind, turn).astype(low)
            along_copy(kind, offset).start()
        shares[kind][...] = own_shard(kind, slow)

    while small_turn[0] <= len(partners):
        small_step()
    small_out_ref[...] = small_sums[len(partners)]

    attn_copy.wait()

    def finish_input(turn, attn_part):
        rows = block(turn, own_len)
        total = input_part(turn, column) + attn_part.astype(full)
        part_copy(turn, level).wait_recv()
        total += core_in[level, rows, :].astype(full)
        for offset in offsets:
            level_copy(turn, offset).wait_recv()
        for place in range(levels - 1):
            total += level_in[place, rows, :].astype(full)
        grad_input_ref[rows, :] = total.astype(low)

    @pl.loop(0, levels)
    def _(place):
        rows = block(place, own_len)
        finish_input(place * 2 + core, attn_ref[rows, block(column, width)])
        finish_input(place * 2 + other, attn_in[rows, :])

    for kind in range(KINDS):
        total = shares[kind][...]
        for offset in range(1, along):
            along_copy(kind, offset).wait_recv()
        for place in range(along - 1):
            total += landed[kind][place].astype(full)
        shares[kind][...] = total

    layer_keep.wait()
    for copy in layer_copies:
        copy.wait()
    for kind in range(KINDS):
        for offset in range(1, along):
            along_copy(kind, offset).wait_send()

        @pl.loop(0, along)
        def _(turn):
            for offset in range(1, across):
                across_copy(kind, turn, offset).wait_send()

    @pl.loop(0, cols)
    def _(turn):
        for place in range(levels):
            part_copy(turn, place).wait_send()
        for offset in offsets:
            level_copy(turn, offset).wait_send()


def finish(
    levels, rows, query_key_value, weights, features, attn_full, layer_own, small, down, up, out
):
    low, full = jnp.bfloat16, jnp.float32
    shape = jax.ShapeDtypeStruct
    across = across_of(rows)
    along = rows // across
    seq_len, features_all = features.shape
    width = query_key_value.shape[1] // 3
    own_len = layer_own.shape[0]
    shard = features_all // rows
    widths = [down.shape[2], up.shape[2], out.shape[2], 3 * width]
    others = levels - 1
    cols = 2 * levels
    turns = 1 + (levels - 1).bit_length() + (rows - 1).bit_length()
    dma = pltpu.SemaphoreType.DMA
    return pl.pallas_call(
        functools.partial(end_kernel, levels, across, along),
        out_shape=(
            shape((seq_len, width), low),
            shape((seq_len, width), low),
            shape(small.shape, full),
            *(shape((shard, each), full) for each in widths),
        ),
        in_specs=[VMEM] * 9,
        out_specs=[VMEM] * 7,
        scratch_shapes=[
            *(pltpu.VMEM((features_all, each), low) for each in widths),
            *(pltpu.VMEM((across - 1, along * shard, each), low) for each in widths),
            *(pltpu.VMEM((along - 1, shard, each), low) for each in widths),
            *(pltpu.VMEM((along - 1, shard, each), low) for each in widths),
            pltpu.VMEM((levels, seq_len, width), low),
            pltpu.VMEM((levels, seq_len, width), low),
            pltpu.VMEM((others, seq_len, width), low),
            pltpu.VMEM((others, seq_len, width), low),
            pltpu.VMEM((levels * own_len, width), low),
            pltpu.VMEM((turns + 1, *small.shape), full),
            pltpu.VMEM((turns, *small.shape), full),
            dma((4,)),
            dma((4,)),
            dma((cols, levels)),
            dma((cols, levels)),
            dma((cols, others)),
            dma((cols, others)),
            dma((cols,)),
            dma((cols,)),
            dma((KINDS, along, across - 1)),
            dma((KINDS, along, across - 1)),
            dma((KINDS, along - 1)),
            dma((KINDS, along - 1)),
            dma((turns,)),
            dma((turns,)),
            dma,
        ],
        compiler_params=pltpu.CompilerParams(
            collective_id=2, has_side_effects=True, vmem_limit_bytes=60 * 1024 * 1024
        ),
        cost_estimate=pl.CostEstimate(
            flops=4 * seq_len * features_all * 3 * width,
            bytes_accessed=40 * 1024 * 1024,
            transcendentals=0,
        ),
    )(query_key_value, weights, features, attn_full, layer_own, small, down, up, out)


def into_full(portion, start_at, full_len):
    return lax.dynamic_update_slice_in_dim(
        jnp.zeros((full_len,), jnp.float32), portion, start_at, 0
    )


def on_device(
    hidden_in,
    out_grad,
    lengths,
    global_blocks,
    rand_blocks,
    w_query,
    b_query,
    w_key,
    w_value,
    b_value,
    w_out,
    b_out,
    ln1_gain,
    ln1_bias,
    w_up,
    b_up,
    w_down,
    b_down,
    ln2_gain,
    ln2_bias,
):
    low = jnp.bfloat16
    seq_len = hidden_in.shape[0]
    feat_cols = hidden_in.shape[1]
    unit_cols = w_up.shape[1]
    cols = lax.axis_size("col")
    features_all = feat_cols * cols
    units_all = unit_cols * cols
    num_blocks = seq_len // BLK
    head_count = feat_cols // DH
    own_len = seq_len // cols
    column = lax.axis_index("col")
    feat_start = column * feat_cols
    unit_start = column * unit_cols
    own_start = column * own_len
    length = lengths[0]
    tables = (
        global_blocks.reshape(-1),
        rand_blocks.reshape(-1),
        limits_of(length, global_blocks[0], rand_blocks[0], num_blocks, head_count),
    )
    valid = (jnp.arange(seq_len) < length)[:, None]
    own_valid = (own_start + jnp.arange(own_len) < length).astype(jnp.float32)[:, None]
    (
        features,
        own_features,
        upstream,
        queries,
        key_rows,
        value_rows,
        context,
        *stats,
        full_qkv,
        full_out,
        full_up,
        full_down,
    ) = front(
        cols // 2,
        lax.axis_size("row"),
        tables,
        hidden_in,
        jnp.where(valid, out_grad, 0),
        (
            lax.dynamic_slice_in_dim(b_query, feat_start, feat_cols)[None, :],
            lax.dynamic_slice_in_dim(b_value, feat_start, feat_cols)[None, :],
        ),
        (
            jnp.concatenate([w_query, w_key, w_value], axis=1).astype(low),
            w_out.T.astype(low),
            w_up.astype(low),
            w_down.T.astype(low),
        ),
    )

    sibling = column + 1 - 2 * lax.rem(column, 2)
    layer_own, context_grad, attn_full, small, up_small, grad_up, grad_down, grad_out = middle(
        cols // 2,
        context,
        own_features,
        upstream,
        own_valid,
        full_out,
        full_up,
        full_down,
        jnp.stack([b_out, ln1_gain, ln1_bias, b_down, ln2_gain, ln2_bias, b_out, b_out]),
        jnp.stack(
            [
                lax.dynamic_slice_in_dim(b_up, unit_start, unit_cols),
                lax.dynamic_slice_in_dim(b_up, sibling * unit_cols, unit_cols),
            ]
        ),
    )
    query_key_value, bias_sums = attend_back(
        queries, key_rows, value_rows, tables, stats, context_grad
    )
    up_sums = into_full(up_small[0], unit_start, units_all) + into_full(
        up_small[1], sibling * unit_cols, units_all
    )
    bias_full = lax.dynamic_update_slice(
        jnp.zeros((4, features_all), jnp.float32), bias_sums, (0, feat_start)
    )
    grad_input, layer_out, small, down_share, up_share, out_share, qkv_share = finish(
        cols // 2,
        lax.axis_size("row"),
        query_key_value,
        full_qkv,
        features,
        attn_full,
        layer_own,
        jnp.concatenate([small, up_sums.reshape(-1, features_all), bias_full], axis=0),
        grad_down,
        grad_up,
        grad_out,
    )
    return (
        layer_out,
        grad_input,
        qkv_share[:, :feat_cols],
        small[-4],
        qkv_share[:, feat_cols : 2 * feat_cols],
        qkv_share[:, 2 * feat_cols :],
        small[-3],
        out_share.T,
        small[5],
        small[3],
        small[4],
        up_share,
        small[8:-4].reshape(-1),
        down_share.T,
        small[2],
        small[0],
        small[1],
    )


def solution(mesh):
    placed = (
        P("row", "col"),
        P("row", "col"),
        P("row"),
        P("row", None),
        P("row", None, "col", None),
        P("row", "col"),
        P(),
        P("row", "col"),
        P("row", "col"),
        P(),
        P("col", "row"),
        P(),
        P(),
        P(),
        P("row", "col"),
        P(),
        P("col", "row"),
        P(),
        P(),
        P(),
    )
    return jax.shard_map(
        on_device,
        mesh=mesh,
        in_specs=placed,
        out_specs=(
            P("row", "col"),
            P("row", "col"),
            P("row", "col"),
            P(),
            P("row", "col"),
            P("row", "col"),
            P(),
            P("col", "row"),
            P(),
            P(),
            P(),
            P("row", "col"),
            P(),
            P("col", "row"),
            P(),
            P(),
            P(),
        ),
        check_vma=False,
    )
```

```python
import functools
import math

import jax
import jax.numpy as jnp
from jax import lax
from jax.experimental import pallas as pl
from jax.experimental.pallas import tpu as pltpu
from jax.sharding import PartitionSpec as P

DH = 64
BLK = 64
MESH = pl.DeviceIdType.MESH


epsilon = 1e-06


def lane_heads(rows, width):
    return lax.broadcasted_iota(jnp.int32, (rows, width), 1) // DH


def by_diagonal(rows, width):
    lane_head = lane_heads(BLK, width)
    zero = jnp.zeros_like(rows)
    return jnp.concatenate(
        [jnp.where(lane_head == head, rows, zero) for head in range(width // DH)], axis=0
    )


def from_diagonal(square, width):
    lane_head = lane_heads(BLK, width)
    result = jnp.zeros((BLK, width), jnp.float32)
    for head in range(width // DH):
        result = jnp.where(lane_head == head, square[head * BLK : (head + 1) * BLK, :], result)
    return result


def slot_starts(step, num_blocks, head_count, globals_ref, random_ref):
    shared = [
        jnp.maximum(step - 1, 0),
        step,
        jnp.minimum(step + 1, num_blocks - 1),
        globals_ref[0],
        globals_ref[1],
    ]
    base = step * (head_count * 3)
    apart = [
        [random_ref[base + head * 3 + slot] for head in range(head_count)] for slot in range(3)
    ]
    return shared, apart


def lane_groups(head_count):
    per_group = min(128 // DH, head_count)
    return [
        (first * DH, per_group * DH, list(range(first, first + per_group)))
        for first in range(0, head_count, per_group)
    ]


def picked_rows(rows_ref, shared, apart, head_count):
    pieces = [rows_ref[block] for block in shared]
    for blocks in apart:
        groups = []
        for lane, width, heads in lane_groups(head_count):
            lane_head = lane_heads(BLK, width)
            piece = rows_ref[blocks[heads[0]], :, lane : lane + width]
            for place, head in enumerate(heads[1:], 1):
                other = rows_ref[blocks[head], :, lane : lane + width]
                piece = jnp.where(lane_head >= place, other, piece)
            groups.append(piece)
        pieces.append(jnp.concatenate(groups, axis=1) if len(groups) > 1 else groups[0])
    return jnp.concatenate(pieces, axis=0)


def put_rows(sums_ref, values_in, shared, apart, head_count):
    for slot, block in enumerate(shared):
        sums_ref[block] += values_in[slot * BLK : (slot + 1) * BLK, :]
    for slot, blocks in enumerate(apart, len(shared)):
        rows = values_in[slot * BLK : (slot + 1) * BLK, :]
        for lane, width, heads in lane_groups(head_count):
            lane_head = lane_heads(BLK, width)
            for place, head in enumerate(heads):
                sums_ref[blocks[head], :, lane : lane + width] += jnp.where(
                    lane_head == place, rows[:, lane : lane + width], 0.0
                )


def masked_scores(picked_keys, grouped, limits_ref, step, width):
    scores = lax.dot_general(
        picked_keys, grouped, (((1,), (1,)), ((), ())), preferred_element_type=jnp.float32
    )
    row = lax.broadcasted_iota(jnp.int32, (BLK, width), 0)
    return [
        jnp.where(
            row < limits_ref[step, slot : slot + 1, :],
            scores[slot * BLK : (slot + 1) * BLK, :],
            -1e30,
        )
        for slot in range(8)
    ]


def attend_blocks(
    first, count, unroll, globals_ref, random_ref, limits_ref, refs, context_ref, stat_refs
):
    queries_ref, keys_ref, values_ref = refs
    highest_ref, scale_ref = stat_refs
    seq_len, width = queries_ref.shape
    head_count = width // DH
    num_blocks = seq_len // BLK

    def one_block(step):
        shared, apart = slot_starts(step, num_blocks, head_count, globals_ref, random_ref)
        own = pl.ds(pl.multiple_of(step * BLK, BLK), BLK)
        grouped = by_diagonal(queries_ref[own, :] * jnp.bfloat16(1.0 / math.sqrt(DH)), width)
        scores = masked_scores(
            picked_rows(keys_ref, shared, apart, head_count), grouped, limits_ref, step, width
        )
        highest = jnp.max(functools.reduce(jnp.maximum, scores), axis=0, keepdims=True)
        exponent = [jnp.exp(piece - highest) for piece in scores]
        denominator = jnp.sum(sum(exponent[1:], exponent[0]), axis=0, keepdims=True)
        scale = 1.0 / denominator
        attn_probs = jnp.concatenate(
            [(piece * scale).astype(jnp.bfloat16) for piece in exponent], axis=0
        )
        square = lax.dot_general(
            attn_probs,
            picked_rows(values_ref, shared, apart, head_count),
            (((0,), (0,)), ((), ())),
            preferred_element_type=jnp.float32,
        )
        context_ref[own, :] = from_diagonal(square, width).astype(jnp.bfloat16)
        highest_ref[step] = highest
        scale_ref[step] = scale

    @pl.loop(0, count // unroll)
    def _(turn):
        for place in range(unroll):
            one_block(first + turn * unroll + place)


def attend_back_kernel(
    head_count,
    unroll,
    globals_ref,
    random_ref,
    limits_ref,
    queries_ref,
    keys_ref,
    values_ref,
    grads_ref,
    highest_ref,
    scale_ref,
    grads_out_ref,
    bias_ref,
    key_sums,
    value_sums,
    query_total,
):
    width = head_count * DH
    num_blocks = queries_ref.shape[0] // BLK
    factor = 1.0 / math.sqrt(DH)
    key_sums[...] = jnp.zeros_like(key_sums)
    value_sums[...] = jnp.zeros_like(value_sums)
    query_total[...] = jnp.zeros_like(query_total)

    def one_block(step):
        shared, apart = slot_starts(step, num_blocks, head_count, globals_ref, random_ref)
        own = pl.ds(pl.multiple_of(step * BLK, BLK), BLK)
        grouped = by_diagonal(queries_ref[own, :] * jnp.bfloat16(factor), width)
        grouped_grad = by_diagonal(grads_ref[own, :], width)
        picked_keys = picked_rows(keys_ref, shared, apart, head_count)
        picked_values = picked_rows(values_ref, shared, apart, head_count)
        scores = masked_scores(picked_keys, grouped, limits_ref, step, width)
        highest = highest_ref[step]
        scale = scale_ref[step]
        attn_probs = [jnp.exp(piece - highest) * scale for piece in scores]
        prob_grad = lax.dot_general(
            picked_values,
            grouped_grad,
            (((1,), (1,)), ((), ())),
            preferred_element_type=jnp.float32,
        )
        prob_grads = [prob_grad[slot * BLK : (slot + 1) * BLK, :] for slot in range(8)]
        products = [left * right for left, right in zip(attn_probs, prob_grads)]
        total = jnp.sum(sum(products[1:], products[0]), axis=0, keepdims=True)
        score_grad = jnp.concatenate(
            [
                (left * (right - total)).astype(jnp.bfloat16)
                for left, right in zip(attn_probs, prob_grads)
            ],
            axis=0,
        )
        probs_low = jnp.concatenate([piece.astype(jnp.bfloat16) for piece in attn_probs], axis=0)
        square = lax.dot_general(
            score_grad, picked_keys, (((0,), (0,)), ((), ())), preferred_element_type=jnp.float32
        )
        query_grad = (from_diagonal(square, width) * factor).astype(jnp.bfloat16)
        grads_out_ref[own, :width] = query_grad
        query_total[...] += jnp.sum(
            query_grad.astype(jnp.float32).reshape(BLK // 8, 8, width), axis=0
        )
        key_part = jnp.dot(score_grad, grouped, preferred_element_type=jnp.float32)
        value_part = jnp.dot(probs_low, grouped_grad, preferred_element_type=jnp.float32)
        put_rows(key_sums, key_part, shared, apart, head_count)
        put_rows(value_sums, value_part, shared, apart, head_count)

    @pl.loop(0, num_blocks // unroll)
    def _(turn):
        for place in range(unroll):
            one_block(turn * unroll + place)

    value_grad = value_sums[...].reshape(queries_ref.shape).astype(jnp.bfloat16)
    seq_len = queries_ref.shape[0]
    grads_out_ref[:, width : 2 * width] = key_sums[...].reshape(seq_len, width).astype(jnp.bfloat16)
    grads_out_ref[:, 2 * width :] = value_grad
    bias_ref[0:1, :] = jnp.sum(query_total[...], axis=0, keepdims=True)
    bias_ref[1:2, :] = jnp.sum(value_grad.astype(jnp.float32), axis=0, keepdims=True)


def limits_of(length, global_ids, random_ids, num_blocks, head_count):
    blocks = jnp.arange(num_blocks, dtype=jnp.int32)
    nearby_raw = blocks[:, None] + jnp.arange(-1, 2, dtype=jnp.int32)[None, :]
    near_ok = (nearby_raw >= 0) & (nearby_raw < num_blocks)
    global_rows = jnp.broadcast_to(global_ids[None, :], (num_blocks, 2))
    global_ok = jnp.all(global_rows[:, :, None] != nearby_raw[:, None, :], axis=2)
    common = jnp.concatenate([nearby_raw, global_rows], axis=1)
    common_ok = jnp.concatenate([near_ok, global_ok], axis=1)
    common_limit = jnp.where(common_ok, length - common * BLK, 0)
    random_limit = jnp.transpose(length - random_ids * BLK, (0, 2, 1))
    return jnp.concatenate(
        [
            jnp.broadcast_to(common_limit[:, :, None], (num_blocks, 5, head_count * DH)),
            jnp.repeat(random_limit, DH, axis=2),
        ],
        axis=1,
    )


VMEM = pl.BlockSpec(memory_space=pltpu.VMEM)
SMEM = pl.BlockSpec(memory_space=pltpu.SMEM)


def attend_back(queries, key_rows, value_rows, tables, stats, context_grad):
    seq_len, width = queries.shape
    head_count = width // DH
    return pl.pallas_call(
        functools.partial(attend_back_kernel, head_count, 2),
        out_shape=(
            jax.ShapeDtypeStruct((seq_len, 3 * width), jnp.bfloat16),
            jax.ShapeDtypeStruct((2, width), jnp.float32),
        ),
        in_specs=[SMEM] * 2 + [VMEM] * 7,
        out_specs=[VMEM] * 2,
        scratch_shapes=[pltpu.VMEM((seq_len // BLK, BLK, width), jnp.float32)] * 2
        + [pltpu.VMEM((8, width), jnp.float32)],
        compiler_params=pltpu.CompilerParams(vmem_limit_bytes=40 * 1024 * 1024),
        cost_estimate=pl.CostEstimate(
            flops=10 * seq_len * 512 * width * head_count,
            bytes_accessed=14 * seq_len * width,
            transcendentals=seq_len * 512 * head_count,
        ),
    )(*tables, queries, key_rows, value_rows, context_grad, *stats)


FRONT_KINDS = 3
SEGMENTS = 8


def front_kernel(
    levels,
    across,
    along,
    globals_ref,
    random_ref,
    limits_ref,
    hidden_ref,
    grads_ref,
    b_query_ref,
    b_value_ref,
    part_qkv_ref,
    part_out_ref,
    part_up_ref,
    features_ref,
    own_ref,
    upstream_ref,
    queries_ref,
    keys_ref,
    values_ref,
    context_ref,
    highest_ref,
    scale_ref,
    full_qkv_ref,
    full_out_ref,
    full_up_ref,
    level_send,
    level_recv,
    core_send,
    core_recv,
    swap_send,
    swap_recv,
    along_send,
    along_recv,
    across_send,
    across_recv,
):
    low, full = jnp.bfloat16, jnp.float32
    row, column = lax.axis_index("row"), lax.axis_index("col")
    core, level = lax.rem(column, 2), lax.div(column, 2)
    fast, slow = lax.rem(row, across), lax.div(row, across)
    cols = 2 * levels
    seq_len, width = hidden_ref.shape
    own_len = seq_len // cols
    shard = part_qkv_ref.shape[0]
    other = 1 - core
    sibling = (row, level * 2 + other)
    offsets = range(1, levels)

    def peer_level(offset):
        return lax.rem(level + offset, levels)

    def fast_peer(offset):
        return slow * across + lax.rem(fast + offset, across)

    def slow_peer(offset):
        return lax.rem(slow + offset, along) * across + fast

    barrier = pltpu.get_barrier_semaphore()
    greeted = [sibling]
    for offset in offsets:
        greeted += [(row, peer_level(offset) * 2 + core), (row, peer_level(offset) * 2 + other)]
    greeted += [(fast_peer(offset), column) for offset in range(1, across)]
    greeted += [(slow_peer(offset), column) for offset in range(1, along)]
    for device in greeted:
        pl.semaphore_signal(barrier, inc=1, device_id=device, device_id_type=MESH)
    pl.semaphore_wait(barrier, len(greeted))

    def remote(source, target, send, recv, device):
        return pltpu.make_async_remote_copy(
            src_ref=source,
            dst_ref=target,
            send_sem=send,
            recv_sem=recv,
            device_id=device,
            device_id_type=MESH,
        )

    def block(start, size):
        return pl.ds(pl.multiple_of(start * size, size), size)

    def level_copy(turn, offset):
        rows = block(turn, own_len)
        return remote(
            hidden_ref.at[rows],
            features_ref.at[rows, block(column, width)],
            level_send.at[turn, offset - 1],
            level_recv.at[turn, levels - offset - 1],
            (row, peer_level(offset) * 2 + core),
        )

    def core_copy(turn, offset):
        view = features_ref.at[block(turn, own_len), block(peer_level(offset) * 2 + core, width)]
        return remote(
            view, view, core_send.at[turn, offset], core_recv.at[turn, offset], sibling
        )

    @pl.loop(0, cols)
    def _(turn):
        for offset in offsets:
            level_copy(turn, offset).start()
        rows = block(turn, own_len)
        features_ref[rows, block(column, width)] = hidden_ref[rows, :]
        core_copy(turn, 0).start()

    parts = (part_qkv_ref, part_out_ref, part_up_ref)
    fulls = (full_qkv_ref, full_out_ref, full_up_ref)

    def shard_rows(place):
        return block(place * across + fast, shard)

    def along_copy(kind, offset):
        view = fulls[kind].at[shard_rows(slow)]
        return remote(
            view,
            view,
            along_send.at[kind, offset - 1],
            along_recv.at[kind, along - offset - 1],
            (slow_peer(offset), column),
        )

    def across_copy(kind, place, offset):
        view = fulls[kind].at[shard_rows(place)]
        return remote(
            view,
            view,
            across_send.at[kind, place, offset - 1],
            across_recv.at[kind, place, across - offset - 1],
            (fast_peer(offset), column),
        )

    for kind in range(FRONT_KINDS):
        fulls[kind][shard_rows(slow), :] = parts[kind][...]
        for offset in range(1, along):
            along_copy(kind, offset).start()
        for offset in range(1, across):
            across_copy(kind, slow, offset).start()

    def swap_copy(target, place_out, place_in):
        return remote(
            grads_ref.at[block(target, own_len)],
            upstream_ref.at[:, block(column, width)],
            swap_send.at[place_out],
            swap_recv.at[place_in],
            (row, target),
        )

    swaps = [swap_copy(level * 2 + other, 0, 0)]
    for offset in offsets:
        back = levels - offset
        swaps.append(swap_copy(peer_level(offset) * 2 + core, 2 * offset - 1, 2 * back - 1))
        swaps.append(swap_copy(peer_level(offset) * 2 + other, 2 * offset, 2 * back))
    for copy in swaps:
        copy.start()
    upstream_ref[:, block(column, width)] = grads_ref[block(column, own_len), :]

    waiting = [(kind, offset) for kind in range(FRONT_KINDS) for offset in range(1, along)]

    def pass_on(count):
        for kind, offset in waiting[:count]:
            along_copy(kind, along - offset).wait_recv()
            for step in range(1, across):
                across_copy(kind, lax.rem(slow + offset, along), step).start()
        del waiting[:count]

    def await_shards(kind):
        @pl.loop(0, along)
        def _(place):
            for offset in range(1, across):
                across_copy(kind, place, offset).wait_recv()

    pass_on(along - 1)
    await_shards(0)

    def project(turn):
        rows = block(turn, own_len)
        for offset in offsets:
            level_copy(turn, levels - offset).wait_recv()
            core_copy(turn, offset).start()
        for offset in range(levels):
            core_copy(turn, offset).wait_recv()
        values_in = features_ref[rows, :]
        queries_ref[rows, :] = (
            dot(values_in, full_qkv_ref[:, :width]) + b_query_ref[...]
        ).astype(low)
        blocks = pl.ds(turn * (own_len // BLK), own_len // BLK)
        by_block = (own_len // BLK, BLK, width)
        keys_ref[blocks] = (
            dot(values_in, full_qkv_ref[:, width : 2 * width]).astype(low).reshape(by_block)
        )
        values_ref[blocks] = (
            (dot(values_in, full_qkv_ref[:, 2 * width :]) + b_value_ref[...])
            .astype(low)
            .reshape(by_block)
        )

    for turn in range(cols):
        project(turn)
        pass_on(1)
    own_ref[...] = features_ref[block(column, own_len), :]
    count = seq_len // BLK // SEGMENTS
    for part in range(SEGMENTS):
        attend_blocks(
            part * count,
            count,
            2,
            globals_ref,
            random_ref,
            limits_ref,
            (queries_ref, keys_ref, values_ref),
            context_ref,
            (highest_ref, scale_ref),
        )
        pass_on(part % 2)
    pass_on(len(waiting))
    for kind in range(1, FRONT_KINDS):
        await_shards(kind)
    for copy in swaps:
        copy.wait()
    for kind in range(FRONT_KINDS):
        for offset in range(1, along):
            along_copy(kind, offset).wait_send()

        @pl.loop(0, along)
        def _(place):
            for offset in range(1, across):
                across_copy(kind, place, offset).wait_send()

    @pl.loop(0, cols)
    def _(turn):
        for offset in offsets:
            level_copy(turn, offset).wait_send()
        for offset in range(levels):
            core_copy(turn, offset).wait_send()


def across_of(rows):
    return 2 if rows <= 8 else rows // 4


def front(levels, rows, tables, hidden_in, grads, biases, parts):
    low, full = jnp.bfloat16, jnp.float32
    shape = jax.ShapeDtypeStruct
    across = across_of(rows)
    along = rows // across
    seq_len, width = hidden_in.shape
    cols = 2 * levels
    own_len = seq_len // cols
    features_all = width * cols
    others = levels - 1
    stat = shape((seq_len // BLK, 1, width), full)
    dma = pltpu.SemaphoreType.DMA
    return pl.pallas_call(
        functools.partial(front_kernel, levels, across, along),
        out_shape=(
            shape((seq_len, features_all), low),
            shape((own_len, features_all), low),
            shape((own_len, features_all), low),
            shape((seq_len, width), low),
            shape((seq_len // BLK, BLK, width), low),
            shape((seq_len // BLK, BLK, width), low),
            shape((seq_len, width), low),
            stat,
            stat,
            *(shape((part.shape[0] * rows, part.shape[1]), low) for part in parts),
        ),
        in_specs=[SMEM] * 2 + [VMEM] * 8,
        out_specs=[VMEM] * 12,
        scratch_shapes=[
            dma((cols, others)),
            dma((cols, others)),
            dma((cols, levels)),
            dma((cols, levels)),
            dma((cols,)),
            dma((cols,)),
            dma((FRONT_KINDS, along - 1)),
            dma((FRONT_KINDS, along - 1)),
            dma((FRONT_KINDS, along, across - 1)),
            dma((FRONT_KINDS, along, across - 1)),
        ],
        compiler_params=pltpu.CompilerParams(
            collective_id=3, has_side_effects=True, vmem_limit_bytes=48 * 1024 * 1024
        ),
        cost_estimate=pl.CostEstimate(
            flops=2 * seq_len * features_all * 3 * width,
            bytes_accessed=20 * 1024 * 1024,
            transcendentals=seq_len * 512 * (width // DH),
        ),
    )(*tables, hidden_in, grads, *biases, *parts)


def dot(left, right):
    return jnp.dot(left, right, preferred_element_type=jnp.float32)


def dot_nt(left, right):
    return lax.dot_general(
        left, right, (((1,), (1,)), ((), ())), preferred_element_type=jnp.float32
    )


def dot_tn(left, right):
    return lax.dot_general(
        left, right, (((0,), (0,)), ((), ())), preferred_element_type=jnp.float32
    )


def gelu_parts(values_in):
    factor = math.sqrt(2.0 / math.pi)
    square = values_in * values_in
    bent = jnp.tanh(factor * (values_in + 0.044715 * (values_in * square)))
    half = 0.5 * (1.0 + bent)
    slope = half + (0.5 * values_in) * (1.0 - bent * bent) * (
        factor + (3.0 * 0.044715 * factor) * square
    )
    return (values_in * half, slope)


def norm_parts(summed):
    average = jnp.mean(summed, axis=1, keepdims=True)
    squares = jnp.mean(summed * summed, axis=1, keepdims=True)
    inv_std = lax.rsqrt(squares - average * average + epsilon)
    return ((summed - average) * inv_std, inv_std)


def norm_back(upstream, normed, inv_std, gain_vec):
    scaled = upstream * gain_vec
    left = jnp.mean(scaled, axis=1, keepdims=True)
    right = jnp.mean(scaled * normed, axis=1, keepdims=True)
    return inv_std * (scaled - left - normed * right)


CHUNKS = 4


def middle_kernel(
    levels,
    across,
    along,
    context_ref,
    inputs_ref,
    upstream_ref,
    valid_ref,
    out_ref,
    up_ref,
    part_down_ref,
    vectors_ref,
    b_up_ref,
    layer_out_ref,
    context_grad_ref,
    attn_full,
    small_ref,
    up_small_ref,
    share_down_ref,
    up_part_ref,
    grad_out_ref,
    context_sib,
    out_sib,
    up_sib,
    down_full,
    down_sib,
    normed_full,
    ffn_full,
    hidden,
    slope,
    pre_grad,
    unit1,
    inv1,
    ffn_keep,
    part_own,
    send_buf,
    recv_buf,
    context_send,
    stage,
    down_sums,
    up_sums,
    down_got,
    up_got,
    down_pass,
    down_in,
    send_sem,
    recv_sem,
    core_send,
    core_recv,
    shard_send,
    shard_recv,
    along_send,
    along_recv,
    across_send,
    across_recv,
    stage_sem,
):
    low = jnp.bfloat16
    row, column = lax.axis_index("row"), lax.axis_index("col")
    core = lax.rem(column, 2)
    level = lax.div(column, 2)
    sibling = (row, column + 1 - 2 * core)
    fast, slow = lax.rem(row, across), lax.div(row, across)
    shard = part_down_ref.shape[0]
    own_len = inputs_ref.shape[0]
    step = own_len // CHUNKS
    b_out, gain1, shift1, b_down, gain2, shift2 = (
        vectors_ref.at[place : place + 1, :] for place in range(6)
    )

    def peer_level(offset):
        return lax.rem(level + offset, levels)

    def fast_peer(offset):
        return slow * across + lax.rem(fast + offset, across)

    def slow_peer(offset):
        return lax.rem(slow + offset, along) * across + fast

    barrier = pltpu.get_barrier_semaphore()
    greeted = [sibling]
    greeted += [(row, peer_level(offset) * 2 + core) for offset in range(1, levels)]
    greeted += [(fast_peer(offset), column) for offset in range(1, across)]
    greeted += [(slow_peer(offset), column) for offset in range(1, along)]
    for device in greeted:
        pl.semaphore_signal(barrier, inc=1, device_id=device, device_id_type=MESH)
    pl.semaphore_wait(barrier, len(greeted))

    def remote(source, target, send, recv, device):
        return pltpu.make_async_remote_copy(
            src_ref=source,
            dst_ref=target,
            send_sem=send,
            recv_sem=recv,
            device_id=device,
            device_id_type=MESH,
        )

    def block(start, size):
        return pl.ds(pl.multiple_of(start * size, size), size)

    def to_sibling(source, target, place):
        return remote(source, target, core_send.at[place], core_recv.at[place], sibling)

    def shard_view(ref, place, position):
        return ref.at[block(place * across + position, shard)]

    def along_down(offset):
        view = shard_view(down_full, slow, fast)
        return remote(
            view,
            view,
            along_send.at[0, offset - 1],
            along_recv.at[0, along - offset - 1],
            (slow_peer(offset), column),
        )

    def across_down(place, offset):
        view = shard_view(down_full, place, fast)
        return remote(
            view,
            view,
            across_send.at[0, place, offset - 1],
            across_recv.at[0, place, across - offset - 1],
            (fast_peer(offset), column),
        )

    def core_down(place, offset):
        position = lax.rem(fast + offset, across)
        return remote(
            shard_view(down_full, place, position),
            shard_view(down_sib, place, position),
            shard_send.at[place, offset],
            shard_recv.at[place, offset],
            sibling,
        )

    def pass_down(place):
        for offset in range(1, across):
            across_down(place, offset).start()
        core_down(place, 0).start()

    def rows_of(place, chunk):
        return pl.ds(pl.multiple_of(place * own_len + chunk * step, step), step)

    def own_rows(chunk):
        return pl.ds(pl.multiple_of(chunk * step, step), step)

    def exchange(kind, chunk, offset, source, target):
        return pltpu.make_async_remote_copy(
            src_ref=source,
            dst_ref=target,
            send_sem=send_sem.at[kind, chunk, offset - 1],
            recv_sem=recv_sem.at[kind, chunk, levels - offset - 1],
            device_id=(row, peer_level(offset) * 2 + core),
            device_id_type=MESH,
        )

    def sum_copy(kind, chunk, offset):
        return exchange(
            kind,
            chunk,
            offset,
            send_buf.at[kind // 2, offset - 1, own_rows(chunk)],
            recv_buf.at[kind // 2, levels - offset - 1, own_rows(chunk)],
        )

    def spread_copy(kind, chunk, offset):
        whole = {1: normed_full, 3: ffn_full, 5: attn_full}[kind]
        rows = rows_of(level, chunk)
        return exchange(kind, chunk, offset, whole.at[rows], whole.at[rows])

    def received(kind, chunk):
        return sum(
            recv_buf[kind // 2, place, own_rows(chunk), :].astype(jnp.float32)
            for place in range(levels - 1)
        )

    offsets = range(1, levels)
    context_copies = [
        to_sibling(
            context_ref.at[
                pl.ds(pl.multiple_of((place * 2 + 1 - core) * own_len, own_len), own_len)
            ],
            context_sib.at[pl.ds(place * own_len, own_len)],
            place,
        )
        for place in range(levels)
    ]
    out_copy = to_sibling(out_ref, out_sib, levels)
    up_copy = to_sibling(up_ref, up_sib, levels + 1)
    for copy in context_copies + [out_copy]:
        copy.start()
    down_full[block(slow * across + fast, shard), :] = part_down_ref[...]
    for offset in range(1, along):
        along_down(offset).start()
    pass_down(slow)
    up_copy.start()
    small_ref[...] = jnp.zeros_like(small_ref)
    up_small_ref[...] = jnp.zeros_like(up_small_ref)
    for copy in context_copies:
        copy.wait()
    out_copy.wait()

    def context_rows(place, chunk):
        start = (place * 2 + core) * own_len + chunk * step
        return pl.ds(pl.multiple_of(start, step), step)

    def attn_part(place, chunk):
        return dot_nt(context_ref[context_rows(place, chunk), :], out_ref[...]) + dot_nt(
            context_sib[rows_of(place, chunk), :], out_sib[...]
        )

    @pl.loop(0, CHUNKS)
    def _(chunk):
        for offset in offsets:
            send_buf[0, offset - 1, own_rows(chunk), :] = attn_part(
                peer_level(offset), chunk
            ).astype(low)
            sum_copy(0, chunk, offset).start()

    for chunk in range(CHUNKS):
        rows = own_rows(chunk)
        summed = (
            inputs_ref[rows, :].astype(jnp.float32) + attn_part(level, chunk) + b_out[...]
        )
        for offset in offsets:
            sum_copy(0, chunk, offset).wait_recv()
        normed, inv_std = norm_parts(summed + received(0, chunk))
        unit1[rows, :] = normed
        inv1[rows, :] = inv_std
        normed_full[rows_of(level, chunk), :] = (normed * gain1[...] + shift1[...]).astype(low)
        for offset in offsets:
            spread_copy(1, chunk, offset).start()
        for offset in range(1, along):
            if min(offset, CHUNKS - 1) == chunk:
                along_down(along - offset).wait_recv()
                pass_down(lax.rem(slow + offset, along))

    for turn in range(along):
        place = lax.rem(slow + turn, along)
        for offset in range(1, across):
            across_down(place, across - offset).wait_recv()
            core_down(place, offset).start()
    up_copy.wait()

    @pl.loop(0, along)
    def _(place):
        for offset in range(across):
            core_down(place, offset).wait_recv()

    sides = ((up_ref, down_full), (up_sib, down_sib))

    def feed_forward(place, chunk):
        rows = rows_of(place, chunk)
        normed = normed_full[rows, :]
        total = None
        for side, (up_side, down_side) in enumerate(sides):
            active, bend = gelu_parts(dot(normed, up_side[...]) + b_up_ref[side : side + 1, :])
            active = active.astype(low)
            hidden[side, rows, :] = active
            slope[side, rows, :] = bend.astype(low)
            part = dot_nt(active, down_side[...])
            total = part if total is None else total + part
        return total

    @pl.loop(0, CHUNKS)
    def _(chunk):
        part_own[own_rows(chunk), :] = feed_forward(level, chunk)
        for offset in offsets:
            spread_copy(1, chunk, levels - offset).wait_recv()
            send_buf[1, offset - 1, own_rows(chunk), :] = feed_forward(
                peer_level(offset), chunk
            ).astype(low)
            sum_copy(2, chunk, offset).start()

    @pl.loop(0, CHUNKS)
    def _(chunk):
        rows = own_rows(chunk)
        normed1 = unit1[rows, :] * gain1[...] + shift1[...]
        summed = normed1 + part_own[rows, :] + b_down[...]
        for offset in offsets:
            sum_copy(2, chunk, offset).wait_recv()
        normed, inv_std = norm_parts(summed + received(2, chunk))
        layer_out_ref[rows, :] = jnp.where(
            valid_ref[rows, :] > 0, normed * gain2[...] + shift2[...], 0.0
        ).astype(low)
        upstream = upstream_ref[rows, :].astype(jnp.float32)
        grad = norm_back(upstream, normed, inv_std, gain2[...])
        ffn_keep[rows, :] = grad
        grad_low = grad.astype(low)
        ffn_full[rows_of(level, chunk), :] = grad_low
        for offset in offsets:
            spread_copy(3, chunk, offset).start()
        small_ref[0:1, :] += jnp.sum(upstream * normed, axis=0, keepdims=True)
        small_ref[1:2, :] += jnp.sum(upstream, axis=0, keepdims=True)
        small_ref[2:3, :] += jnp.sum(grad_low.astype(jnp.float32), axis=0, keepdims=True)

    def feed_back(place, chunk):
        rows = rows_of(place, chunk)
        upstream = ffn_full[rows, :]
        total = None
        for side, (up_side, down_side) in enumerate(sides):
            grad = (
                dot(upstream, down_side[...]) * slope[side, rows, :].astype(jnp.float32)
            ).astype(low)
            pre_grad[side, rows, :] = grad
            up_small_ref[side : side + 1, :] += jnp.sum(
                grad.astype(jnp.float32), axis=0, keepdims=True
            )
            part = dot_nt(grad, up_side[...])
            total = part if total is None else total + part
        return total

    @pl.loop(0, CHUNKS)
    def _(chunk):
        part_own[own_rows(chunk), :] = feed_back(level, chunk)
        for offset in offsets:
            spread_copy(3, chunk, levels - offset).wait_recv()
            send_buf[2, offset - 1, own_rows(chunk), :] = feed_back(
                peer_level(offset), chunk
            ).astype(low)
            sum_copy(4, chunk, offset).start()

    tile = across * shard
    lefts, rights = (ffn_full, normed_full), (hidden, pre_grad)
    sums, got = (down_sums, up_sums), (down_got, up_got)

    def grad_tile(kind, side, turn):
        return dot_tn(lefts[kind][:, block(turn, tile)], rights[kind][side])

    def core_grad(kind):
        return to_sibling(
            slope.at[kind, : sums[kind].shape[0]], sums[kind], 2 * levels + 2 + kind
        )

    def across_grad(kind, turn, offset):
        return remote(
            sums[kind].at[block(turn * across + lax.rem(fast + offset, across), shard)],
            got[kind].at[across - offset - 1, block(turn, shard)],
            across_send.at[1 + kind, turn, offset - 1],
            across_recv.at[1 + kind, turn, across - offset - 1],
            (fast_peer(offset), column),
        )

    def along_grad(offset):
        return remote(
            down_pass.at[offset - 1],
            down_in.at[along - offset - 1],
            along_send.at[1, offset - 1],
            along_recv.at[1, along - offset - 1],
            (slow_peer(offset), column),
        )

    def own_shard(kind, turn):
        for offset in range(1, across):
            across_grad(kind, turn, offset).wait_recv()
        total = sums[kind][block(turn * across + fast, shard), :].astype(jnp.float32)
        for place in range(across - 1):
            total += got[kind][place, block(turn, shard), :].astype(jnp.float32)
        return total

    for kind in range(2):

        @pl.loop(0, along)
        def _(turn):
            slope[kind, block(turn, tile), :] = grad_tile(kind, 1, turn).astype(low)

        core_grad(kind).start()
    for kind in range(2):
        core_grad(kind).wait_recv()

        @pl.loop(0, along)
        def _(turn):
            rows = block(turn, tile)
            sums[kind][rows, :] = (
                grad_tile(kind, 0, turn) + sums[kind][rows, :].astype(jnp.float32)
            ).astype(low)
            for offset in range(1, across):
                across_grad(kind, turn, offset).start()

    @pl.loop(0, CHUNKS)
    def _(chunk):
        rows = own_rows(chunk)
        upstream = ffn_keep[rows, :] + part_own[rows, :]
        for offset in offsets:
            sum_copy(4, chunk, offset).wait_recv()
        upstream = upstream + received(4, chunk)
        normed = unit1[rows, :]
        grad_low = norm_back(upstream, normed, inv1[rows, :], gain1[...]).astype(low)
        attn_full[rows_of(level, chunk), :] = grad_low
        for offset in offsets:
            spread_copy(5, chunk, offset).start()
        small_ref[3:4, :] += jnp.sum(upstream * normed, axis=0, keepdims=True)
        small_ref[4:5, :] += jnp.sum(upstream, axis=0, keepdims=True)
        small_ref[5:6, :] += jnp.sum(grad_low.astype(jnp.float32), axis=0, keepdims=True)

    for offset in range(1, along):
        down_pass[offset - 1] = own_shard(0, lax.rem(slow + offset, along)).astype(low)
        along_grad(offset).start()
    share_down_ref[...] = own_shard(0, slow)

    def context_back(place, chunk):
        rows = rows_of(place, chunk)
        upstream = attn_full[rows, :]
        context_grad_ref[context_rows(place, chunk), :] = dot(upstream, out_ref[...]).astype(low)
        context_send[rows, :] = dot(upstream, out_sib[...]).astype(low)

    @pl.loop(0, CHUNKS)
    def _(chunk):
        context_back(level, chunk)
        for offset in offsets:
            spread_copy(5, chunk, levels - offset).wait_recv()
            context_back(peer_level(offset), chunk)

    back_copies = [
        to_sibling(
            context_send.at[pl.ds(place * own_len, own_len)],
            context_grad_ref.at[
                pl.ds(pl.multiple_of((place * 2 + core) * own_len, own_len), own_len)
            ],
            levels + 2 + place,
        )
        for place in range(levels)
    ]
    for copy in back_copies:
        copy.start()

    own_context = jnp.concatenate(
        [
            context_ref[
                pl.ds(pl.multiple_of((place * 2 + core) * own_len, own_len), own_len), :
            ]
            for place in range(levels)
        ],
        axis=0,
    )

    def out_put(side):
        return pltpu.make_async_copy(stage.at[side], grad_out_ref.at[side], stage_sem.at[side])

    for side, right in enumerate((own_context, context_sib[...])):
        stage[side] = dot_tn(attn_full[...], right).astype(low)
        out_put(side).start()
    for turn in range(along):
        up_part_ref[turn] = own_shard(1, turn).astype(low)
    total = share_down_ref[...]
    for offset in range(1, along):
        along_grad(offset).wait_recv()
    for place in range(along - 1):
        total += down_in[place].astype(jnp.float32)
    share_down_ref[...] = total
    for side in range(2):
        out_put(side).wait()
    for kind in range(2):
        core_grad(kind).wait_send()
    for offset in range(1, along):
        along_down(offset).wait_send()
        along_grad(offset).wait_send()

    @pl.loop(0, along)
    def _(place):
        for offset in range(1, across):
            across_down(place, offset).wait_send()
            across_grad(0, place, offset).wait_send()
            across_grad(1, place, offset).wait_send()
        for offset in range(across):
            core_down(place, offset).wait_send()

    for copy in back_copies:
        copy.wait()
    for kind in range(6):

        @pl.loop(0, CHUNKS)
        def _(chunk):
            for offset in offsets:
                if kind % 2:
                    spread_copy(kind, chunk, offset).wait_send()
                else:
                    sum_copy(kind, chunk, offset).wait_send()


def middle(
    levels, rows, context, inputs, upstream, valid, out_own, up_own, part_down, vectors, b_up_pair
):
    low, full = jnp.bfloat16, jnp.float32
    across = across_of(rows)
    along = rows // across
    own_len, features = inputs.shape
    seq_len, width = context.shape
    shard, units = part_down.shape
    tokens = levels * own_len
    others = levels - 1
    shape = jax.ShapeDtypeStruct
    hbm = pl.BlockSpec(memory_space=pl.ANY)
    dma = pltpu.SemaphoreType.DMA
    vmem = pltpu.VMEM
    return pl.pallas_call(
        functools.partial(middle_kernel, levels, across, along),
        out_shape=(
            shape((own_len, features), low),
            shape((seq_len, width), low),
            shape((tokens, features), low),
            shape((8, features), full),
            shape((2, units), full),
            shape((shard, units), full),
            shape((along, shard, units), low),
            shape((2, features, width), low),
        ),
        in_specs=[VMEM] * 9,
        out_specs=[VMEM] * 7 + [hbm],
        scratch_shapes=[
            vmem((tokens, width), low),
            vmem((features, width), low),
            vmem((features, units), low),
            vmem((features, units), low),
            vmem((features, units), low),
            vmem((tokens, features), low),
            vmem((tokens, features), low),
            vmem((2, tokens, units), low),
            vmem((2, max(tokens, features), units), low),
            vmem((2, tokens, units), low),
            vmem((own_len, features), full),
            vmem((own_len, 1), full),
            vmem((own_len, features), full),
            vmem((own_len, features), full),
            vmem((3, others, own_len, features), low),
            vmem((3, others, own_len, features), low),
            vmem((tokens, width), low),
            vmem((2, features, width), low),
            vmem((features, units), low),
            vmem((features, units), low),
            vmem((across - 1, along * shard, units), low),
            vmem((across - 1, along * shard, units), low),
            vmem((along - 1, shard, units), low),
            vmem((along - 1, shard, units), low),
            dma((6, CHUNKS, others)),
            dma((6, CHUNKS, others)),
            dma((2 * levels + 4,)),
            dma((2 * levels + 4,)),
            dma((along, across)),
            dma((along, across)),
            dma((2, along - 1)),
            dma((2, along - 1)),
            dma((3, along, across - 1)),
            dma((3, along, across - 1)),
            dma((2,)),
        ],
        compiler_params=pltpu.CompilerParams(
            collective_id=1, has_side_effects=True, vmem_limit_bytes=62 * 1024 * 1024
        ),
        cost_estimate=pl.CostEstimate(
            flops=2 * tokens * features * (12 * units + 6 * width),
            bytes_accessed=20 * 1024 * 1024,
            transcendentals=2 * tokens * units,
        ),
    )(context, inputs, upstream, valid, out_own, up_own, part_down, vectors, b_up_pair)


def end_kernel(
    levels,
    across,
    along,
    query_key_value_ref,
    weights_ref,
    features_ref,
    attn_ref,
    layer_ref,
    small_ref,
    out_ref,
    up_ref,
    grad_input_ref,
    layer_out_ref,
    small_out_ref,
    share_out_ref,
    share_qkv_ref,
    share_up_ref,
    out_sib,
    qkv_sums,
    out_got,
    qkv_got,
    out_pass,
    qkv_pass,
    out_in,
    qkv_in,
    up_in,
    core_out,
    core_in,
    level_out,
    level_in,
    attn_in,
    small_sums,
    small_in,
    core_send,
    core_recv,
    part_send,
    part_recv,
    level_send,
    level_recv,
    layer_send,
    layer_recv,
    across_send,
    across_recv,
    along_send,
    along_recv,
    small_send,
    small_recv,
    keep_sem,
):
    low, full = jnp.bfloat16, jnp.float32
    row, column = lax.axis_index("row"), lax.axis_index("col")
    core, level = lax.rem(column, 2), lax.div(column, 2)
    fast, slow = lax.rem(row, across), lax.div(row, across)
    cols = 2 * levels
    seq_len = features_ref.shape[0]
    own_len = seq_len // cols
    width = grad_input_ref.shape[1]
    shard = share_qkv_ref.shape[0]
    other = 1 - core
    sibling = (row, level * 2 + other)
    offsets = range(1, levels)

    def peer_level(offset):
        return lax.rem(level + offset, levels)

    def fast_peer(offset):
        return slow * across + lax.rem(fast + offset, across)

    def slow_peer(offset):
        return lax.rem(slow + offset, along) * across + fast

    barrier = pltpu.get_barrier_semaphore()
    greeted = [sibling]
    for offset in offsets:
        greeted += [(row, peer_level(offset) * 2 + core), (row, peer_level(offset) * 2 + other)]
    greeted += [(fast_peer(offset), column) for offset in range(1, across)]
    greeted += [(slow_peer(offset), column) for offset in range(1, along)]
    for device in greeted:
        pl.semaphore_signal(barrier, inc=1, device_id=device, device_id_type=MESH)
    pl.semaphore_wait(barrier, len(greeted))

    def remote(source, target, send, recv, device):
        return pltpu.make_async_remote_copy(
            src_ref=source,
            dst_ref=target,
            send_sem=send,
            recv_sem=recv,
            device_id=device,
            device_id_type=MESH,
        )

    def block(start, size):
        return pl.ds(pl.multiple_of(start * size, size), size)

    out_copy = remote(out_ref.at[1], out_sib, core_send.at[0], core_recv.at[0], sibling)
    attn_copy = remote(
        attn_ref.at[:, block(level * 2 + other, width)],
        attn_in,
        core_send.at[1],
        core_recv.at[1],
        sibling,
    )

    partners = [sibling]
    bit = 1
    while bit < levels:
        partners.append((row, (level + bit - 2 * bit * lax.rem(lax.div(level, bit), 2)) * 2 + core))
        bit *= 2
    bit = 1
    while bit < across * along:
        partners.append((row + bit - 2 * bit * lax.rem(lax.div(row, bit), 2), column))
        bit *= 2

    def small_copy(turn):
        return remote(
            small_sums.at[turn],
            small_in.at[turn],
            small_send.at[turn],
            small_recv.at[turn],
            partners[turn],
        )

    small_turn = [0]

    def small_step():
        turn = small_turn[0]
        if turn > len(partners):
            return
        if turn > 0:
            small_copy(turn - 1).wait()
            small_sums[turn] = small_sums[turn - 1] + small_in[turn - 1]
        if turn < len(partners):
            small_copy(turn).start()
        small_turn[0] += 1

    def layer_copy(target, place_out, place_in):
        return remote(
            layer_ref.at[:, block(target, width)],
            layer_out_ref.at[block(column, own_len)],
            layer_send.at[place_out],
            layer_recv.at[place_in],
            (row, target),
        )

    layer_copies = [layer_copy(level * 2 + other, 0, 0)]
    for offset in offsets:
        back = levels - offset
        layer_copies.append(
            layer_copy(peer_level(offset) * 2 + core, 2 * offset - 1, 2 * back - 1)
        )
        layer_copies.append(layer_copy(peer_level(offset) * 2 + other, 2 * offset, 2 * back))
    layer_keep = pltpu.make_async_copy(
        layer_ref.at[:, block(column, width)], layer_out_ref.at[block(column, own_len)], keep_sem
    )

    small_sums[0] = small_ref[...]
    small_step()
    out_copy.start()
    attn_copy.start()
    layer_keep.start()
    for copy in layer_copies:
        copy.start()

    def input_part(turn, target):
        return dot_nt(
            query_key_value_ref[block(turn, own_len), :], weights_ref[block(target, width), :]
        )

    def part_copy(turn, place):
        rows = block(turn, own_len)
        return remote(
            core_out.at[place, rows],
            core_in.at[place, rows],
            part_send.at[turn, place],
            part_recv.at[turn, place],
            sibling,
        )

    def give_core():
        @pl.loop(0, cols)
        def _(turn):
            for place in range(levels):
                core_out[place, block(turn, own_len), :] = input_part(
                    turn, place * 2 + other
                ).astype(low)
                part_copy(turn, place).start()

    sums = (out_sib, qkv_sums)
    got = (out_got, qkv_got)
    passed = (out_pass, qkv_pass)
    landed = (out_in, qkv_in, up_in)
    shares = (share_out_ref, share_qkv_ref, share_up_ref)

    def across_copy(kind, turn, offset):
        return remote(
            sums[kind].at[block(turn * across + lax.rem(fast + offset, across), shard)],
            got[kind].at[across - offset - 1, block(turn, shard)],
            across_send.at[kind, turn, offset - 1],
            across_recv.at[kind, turn, across - offset - 1],
            (fast_peer(offset), column),
        )

    def along_copy(kind, offset):
        if kind == 2:
            source = up_ref.at[lax.rem(slow + offset, along)]
        else:
            source = passed[kind].at[offset - 1]
        return remote(
            source,
            landed[kind].at[along - offset - 1],
            along_send.at[kind, offset - 1],
            along_recv.at[kind, along - offset - 1],
            (slow_peer(offset), column),
        )

    def give_across(kind, turn):
        for offset in range(1, across):
            across_copy(kind, turn, offset).start()

    def sum_cores():
        out_copy.wait()

        @pl.loop(0, along)
        def _(turn):
            rows = block(turn, across * shard)
            out_sib[rows, :] = (
                out_ref[0, rows, :].astype(full) + out_sib[rows, :].astype(full)
            ).astype(low)
            give_across(0, turn)

    def weight_grad():
        @pl.loop(0, along)
        def _(turn):
            rows = block(turn, across * shard)
            qkv_sums[rows, :] = dot_tn(features_ref[:, rows], query_key_value_ref[...]).astype(low)
            give_across(1, turn)

    def level_copy(turn, offset):
        rows = block(turn, own_len)
        return remote(
            level_out.at[offset - 1, rows],
            level_in.at[levels - offset - 1, rows],
            level_send.at[turn, offset - 1],
            level_recv.at[turn, levels - offset - 1],
            (row, peer_level(offset) * 2 + core),
        )

    def give_levels():
        @pl.loop(0, cols)
        def _(turn):
            rows = block(turn, own_len)
            for offset in offsets:
                place = peer_level(offset)
                part = input_part(turn, place * 2 + core)
                part_copy(turn, place).wait_recv()
                level_out[offset - 1, rows, :] = (
                    part + core_in[place, rows, :].astype(full)
                ).astype(low)
                level_copy(turn, offset).start()

    def own_shard(kind, turn):
        for offset in range(1, across):
            across_copy(kind, turn, offset).wait_recv()
        total = sums[kind][block(turn * across + fast, shard), :].astype(full)
        for place in range(across - 1):
            total += got[kind][place, block(turn, shard), :].astype(full)
        return total

    def give_along(kind):
        for offset in range(1, along):
            turn = lax.rem(slow + offset, along)
            passed[kind][offset - 1] = own_shard(kind, turn).astype(low)
            along_copy(kind, offset).start()
        shares[kind][...] = own_shard(kind, slow)

    def finish_input(turn, attn_part):
        rows = block(turn, own_len)
        total = input_part(turn, column) + attn_part.astype(full)
        part_copy(turn, level).wait_recv()
        total += core_in[level, rows, :].astype(full)
        for offset in offsets:
            level_copy(turn, offset).wait_recv()
        for place in range(levels - 1):
            total += level_in[place, rows, :].astype(full)
        grad_input_ref[rows, :] = total.astype(low)

    def finish_inputs():
        attn_copy.wait()

        @pl.loop(0, levels)
        def _(place):
            rows = block(place, own_len)
            finish_input(place * 2 + core, attn_ref[rows, block(column, width)])
            finish_input(place * 2 + other, attn_in[rows, :])

    for offset in range(1, along):
        along_copy(2, offset).start()
    share_up_ref[...] = up_ref[slow].astype(full)
    weight_grad()
    small_step()
    give_core()
    sum_cores()
    small_step()
    give_levels()
    small_step()
    give_along(1)
    small_step()
    give_along(0)
    small_step()
    finish_inputs()
    while small_turn[0] <= len(partners):
        small_step()
    small_out_ref[...] = small_sums[len(partners)]

    for kind in range(3):
        total = shares[kind][...]
        for offset in range(1, along):
            along_copy(kind, offset).wait_recv()
        for place in range(along - 1):
            total += landed[kind][place].astype(full)
        shares[kind][...] = total

    layer_keep.wait()
    for copy in layer_copies:
        copy.wait()
    for kind in range(3):
        for offset in range(1, along):
            along_copy(kind, offset).wait_send()
    for kind in range(2):

        @pl.loop(0, along)
        def _(turn):
            for offset in range(1, across):
                across_copy(kind, turn, offset).wait_send()

    @pl.loop(0, cols)
    def _(turn):
        for place in range(levels):
            part_copy(turn, place).wait_send()
        for offset in offsets:
            level_copy(turn, offset).wait_send()


def finish(
    levels, rows, query_key_value, weights, features, attn_full, layer_own, small, out, up
):
    low, full = jnp.bfloat16, jnp.float32
    shape = jax.ShapeDtypeStruct
    across = across_of(rows)
    along = rows // across
    seq_len, features_all = features.shape
    width = query_key_value.shape[1] // 3
    own_len = layer_own.shape[0]
    shard = features_all // rows
    widths = [out.shape[2], 3 * width]
    units = up.shape[2]
    others = levels - 1
    cols = 2 * levels
    turns = 1 + (levels - 1).bit_length() + (rows - 1).bit_length()
    dma = pltpu.SemaphoreType.DMA
    return pl.pallas_call(
        functools.partial(end_kernel, levels, across, along),
        out_shape=(
            shape((seq_len, width), low),
            shape((seq_len, width), low),
            shape(small.shape, full),
            *(shape((shard, each), full) for each in widths + [units]),
        ),
        in_specs=[VMEM] * 8,
        out_specs=[VMEM] * 6,
        scratch_shapes=[
            *(pltpu.VMEM((features_all, each), low) for each in widths),
            *(pltpu.VMEM((across - 1, along * shard, each), low) for each in widths),
            *(pltpu.VMEM((along - 1, shard, each), low) for each in widths),
            *(pltpu.VMEM((along - 1, shard, each), low) for each in widths + [units]),
            pltpu.VMEM((levels, seq_len, width), low),
            pltpu.VMEM((levels, seq_len, width), low),
            pltpu.VMEM((others, seq_len, width), low),
            pltpu.VMEM((others, seq_len, width), low),
            pltpu.VMEM((levels * own_len, width), low),
            pltpu.VMEM((turns + 1, *small.shape), full),
            pltpu.VMEM((turns, *small.shape), full),
            dma((2,)),
            dma((2,)),
            dma((cols, levels)),
            dma((cols, levels)),
            dma((cols, others)),
            dma((cols, others)),
            dma((cols,)),
            dma((cols,)),
            dma((2, along, across - 1)),
            dma((2, along, across - 1)),
            dma((3, along - 1)),
            dma((3, along - 1)),
            dma((turns,)),
            dma((turns,)),
            dma,
        ],
        compiler_params=pltpu.CompilerParams(
            collective_id=2, has_side_effects=True, vmem_limit_bytes=60 * 1024 * 1024
        ),
        cost_estimate=pl.CostEstimate(
            flops=4 * seq_len * features_all * 3 * width,
            bytes_accessed=40 * 1024 * 1024,
            transcendentals=0,
        ),
    )(query_key_value, weights, features, attn_full, layer_own, small, out, up)


def into_full(portion, start_at, full_len):
    return lax.dynamic_update_slice_in_dim(
        jnp.zeros((full_len,), jnp.float32), portion, start_at, 0
    )


def on_device(
    hidden_in,
    out_grad,
    lengths,
    global_blocks,
    rand_blocks,
    w_query,
    b_query,
    w_key,
    w_value,
    b_value,
    w_out,
    b_out,
    ln1_gain,
    ln1_bias,
    w_up,
    b_up,
    w_down,
    b_down,
    ln2_gain,
    ln2_bias,
):
    low = jnp.bfloat16
    seq_len = hidden_in.shape[0]
    feat_cols = hidden_in.shape[1]
    unit_cols = w_up.shape[1]
    cols = lax.axis_size("col")
    features_all = feat_cols * cols
    units_all = unit_cols * cols
    num_blocks = seq_len // BLK
    head_count = feat_cols // DH
    own_len = seq_len // cols
    column = lax.axis_index("col")
    feat_start = column * feat_cols
    unit_start = column * unit_cols
    own_start = column * own_len
    length = lengths[0]
    tables = (
        global_blocks.reshape(-1),
        rand_blocks.reshape(-1),
        limits_of(length, global_blocks[0], rand_blocks[0], num_blocks, head_count),
    )
    valid = (jnp.arange(seq_len) < length)[:, None]
    own_valid = (own_start + jnp.arange(own_len) < length).astype(jnp.float32)[:, None]
    (
        features,
        own_features,
        upstream,
        queries,
        key_rows,
        value_rows,
        context,
        *stats,
        full_qkv,
        full_out,
        full_up,
    ) = front(
        cols // 2,
        lax.axis_size("row"),
        tables,
        hidden_in,
        jnp.where(valid, out_grad, 0),
        (
            lax.dynamic_slice_in_dim(b_query, feat_start, feat_cols)[None, :],
            lax.dynamic_slice_in_dim(b_value, feat_start, feat_cols)[None, :],
        ),
        (
            jnp.concatenate([w_query, w_key, w_value], axis=1).astype(low),
            w_out.T.astype(low),
            w_up.astype(low),
        ),
    )

    sibling = column + 1 - 2 * lax.rem(column, 2)
    layer_own, context_grad, attn_full, small, up_small, down_share, up_part, grad_out = middle(
        cols // 2,
        lax.axis_size("row"),
        context,
        own_features,
        upstream,
        own_valid,
        full_out,
        full_up,
        w_down.T.astype(low),
        jnp.stack([b_out, ln1_gain, ln1_bias, b_down, ln2_gain, ln2_bias, b_out, b_out]),
        jnp.stack(
            [
                lax.dynamic_slice_in_dim(b_up, unit_start, unit_cols),
                lax.dynamic_slice_in_dim(b_up, sibling * unit_cols, unit_cols),
            ]
        ),
    )
    query_key_value, bias_sums = attend_back(
        queries, key_rows, value_rows, tables, stats, context_grad
    )
    up_sums = into_full(up_small[0], unit_start, units_all) + into_full(
        up_small[1], sibling * unit_cols, units_all
    )
    bias_full = lax.dynamic_update_slice(
        jnp.zeros((4, features_all), jnp.float32), bias_sums, (0, feat_start)
    )
    grad_input, layer_out, small, out_share, qkv_share, up_share = finish(
        cols // 2,
        lax.axis_size("row"),
        query_key_value,
        full_qkv,
        features,
        attn_full,
        layer_own,
        jnp.concatenate([small, up_sums.reshape(-1, features_all), bias_full], axis=0),
        grad_out,
        up_part,
    )
    return (
        layer_out,
        grad_input,
        qkv_share[:, :feat_cols],
        small[-4],
        qkv_share[:, feat_cols : 2 * feat_cols],
        qkv_share[:, 2 * feat_cols :],
        small[-3],
        out_share.T,
        small[5],
        small[3],
        small[4],
        up_share,
        small[8:-4].reshape(-1),
        down_share.T,
        small[2],
        small[0],
        small[1],
    )


def solution(mesh):
    placed = (
        P("row", "col"),
        P("row", "col"),
        P("row"),
        P("row", None),
        P("row", None, "col", None),
        P("row", "col"),
        P(),
        P("row", "col"),
        P("row", "col"),
        P(),
        P("col", "row"),
        P(),
        P(),
        P(),
        P("row", "col"),
        P(),
        P("col", "row"),
        P(),
        P(),
        P(),
    )
    return jax.shard_map(
        on_device,
        mesh=mesh,
        in_specs=placed,
        out_specs=(
            P("row", "col"),
            P("row", "col"),
            P("row", "col"),
            P(),
            P("row", "col"),
            P("row", "col"),
            P(),
            P("col", "row"),
            P(),
            P(),
            P(),
            P("row", "col"),
            P(),
            P("col", "row"),
            P(),
            P(),
            P(),
        ),
        check_vma=False,
    )
```

```python
import functools
import math

import jax
import jax.numpy as jnp
from jax import lax
from jax.experimental import pallas as pl
from jax.experimental.pallas import tpu as pltpu
from jax.sharding import PartitionSpec as P

DH = 64
BLK = 64
MESH = pl.DeviceIdType.MESH


epsilon = 1e-06


def lane_heads(rows, width):
    return lax.broadcasted_iota(jnp.int32, (rows, width), 1) // DH


def by_diagonal(rows, width):
    lane_head = lane_heads(BLK, width)
    zero = jnp.zeros_like(rows)
    return jnp.concatenate(
        [jnp.where(lane_head == head, rows, zero) for head in range(width // DH)], axis=0
    )


def from_diagonal(square, width):
    lane_head = lane_heads(BLK, width)
    result = jnp.zeros((BLK, width), jnp.float32)
    for head in range(width // DH):
        result = jnp.where(lane_head == head, square[head * BLK : (head + 1) * BLK, :], result)
    return result


def slot_starts(step, num_blocks, head_count, globals_ref, random_ref):
    shared = [
        jnp.maximum(step - 1, 0),
        step,
        jnp.minimum(step + 1, num_blocks - 1),
        globals_ref[0],
        globals_ref[1],
    ]
    base = step * (head_count * 3)
    apart = [
        [random_ref[base + head * 3 + slot] for head in range(head_count)] for slot in range(3)
    ]
    return shared, apart


def lane_groups(head_count):
    per_group = min(128 // DH, head_count)
    return [
        (first * DH, per_group * DH, list(range(first, first + per_group)))
        for first in range(0, head_count, per_group)
    ]


def picked_rows(rows_ref, shared, apart, head_count):
    pieces = [rows_ref[block] for block in shared]
    for blocks in apart:
        groups = []
        for lane, width, heads in lane_groups(head_count):
            lane_head = lane_heads(BLK, width)
            piece = rows_ref[blocks[heads[0]], :, lane : lane + width]
            for place, head in enumerate(heads[1:], 1):
                other = rows_ref[blocks[head], :, lane : lane + width]
                piece = jnp.where(lane_head >= place, other, piece)
            groups.append(piece)
        pieces.append(jnp.concatenate(groups, axis=1) if len(groups) > 1 else groups[0])
    return jnp.concatenate(pieces, axis=0)


def put_rows(sums_ref, values_in, shared, apart, head_count):
    for slot, block in enumerate(shared):
        sums_ref[block] += values_in[slot * BLK : (slot + 1) * BLK, :]
    for slot, blocks in enumerate(apart, len(shared)):
        rows = values_in[slot * BLK : (slot + 1) * BLK, :]
        for lane, width, heads in lane_groups(head_count):
            lane_head = lane_heads(BLK, width)
            for place, head in enumerate(heads):
                sums_ref[blocks[head], :, lane : lane + width] += jnp.where(
                    lane_head == place, rows[:, lane : lane + width], 0.0
                )


def masked_scores(picked_keys, grouped, limits_ref, step, width):
    scores = lax.dot_general(
        picked_keys, grouped, (((1,), (1,)), ((), ())), preferred_element_type=jnp.float32
    )
    row = lax.broadcasted_iota(jnp.int32, (BLK, width), 0)
    return [
        jnp.where(
            row < limits_ref[step, slot : slot + 1, :],
            scores[slot * BLK : (slot + 1) * BLK, :],
            -1e30,
        )
        for slot in range(8)
    ]


def attend_blocks(
    first, count, unroll, globals_ref, random_ref, limits_ref, refs, context_ref, stat_refs
):
    queries_ref, keys_ref, values_ref = refs
    highest_ref, scale_ref = stat_refs
    seq_len, width = queries_ref.shape
    head_count = width // DH
    num_blocks = seq_len // BLK

    def one_block(step):
        shared, apart = slot_starts(step, num_blocks, head_count, globals_ref, random_ref)
        own = pl.ds(pl.multiple_of(step * BLK, BLK), BLK)
        grouped = by_diagonal(queries_ref[own, :] * jnp.bfloat16(1.0 / math.sqrt(DH)), width)
        scores = masked_scores(
            picked_rows(keys_ref, shared, apart, head_count), grouped, limits_ref, step, width
        )
        highest = jnp.max(functools.reduce(jnp.maximum, scores), axis=0, keepdims=True)
        exponent = [jnp.exp(piece - highest) for piece in scores]
        denominator = jnp.sum(sum(exponent[1:], exponent[0]), axis=0, keepdims=True)
        scale = 1.0 / denominator
        attn_probs = jnp.concatenate(
            [(piece * scale).astype(jnp.bfloat16) for piece in exponent], axis=0
        )
        square = lax.dot_general(
            attn_probs,
            picked_rows(values_ref, shared, apart, head_count),
            (((0,), (0,)), ((), ())),
            preferred_element_type=jnp.float32,
        )
        context_ref[own, :] = from_diagonal(square, width).astype(jnp.bfloat16)
        highest_ref[step] = highest
        scale_ref[step] = scale

    @pl.loop(0, count // unroll)
    def _(turn):
        for place in range(unroll):
            one_block(first + turn * unroll + place)


def attend_back_kernel(
    head_count,
    unroll,
    globals_ref,
    random_ref,
    limits_ref,
    queries_ref,
    keys_ref,
    values_ref,
    grads_ref,
    highest_ref,
    scale_ref,
    grads_out_ref,
    bias_ref,
    key_sums,
    value_sums,
    query_total,
):
    width = head_count * DH
    num_blocks = queries_ref.shape[0] // BLK
    factor = 1.0 / math.sqrt(DH)
    key_sums[...] = jnp.zeros_like(key_sums)
    value_sums[...] = jnp.zeros_like(value_sums)
    query_total[...] = jnp.zeros_like(query_total)

    def one_block(step):
        shared, apart = slot_starts(step, num_blocks, head_count, globals_ref, random_ref)
        own = pl.ds(pl.multiple_of(step * BLK, BLK), BLK)
        grouped = by_diagonal(queries_ref[own, :] * jnp.bfloat16(factor), width)
        grouped_grad = by_diagonal(grads_ref[own, :], width)
        picked_keys = picked_rows(keys_ref, shared, apart, head_count)
        picked_values = picked_rows(values_ref, shared, apart, head_count)
        scores = masked_scores(picked_keys, grouped, limits_ref, step, width)
        highest = highest_ref[step]
        scale = scale_ref[step]
        attn_probs = [jnp.exp(piece - highest) * scale for piece in scores]
        prob_grad = lax.dot_general(
            picked_values,
            grouped_grad,
            (((1,), (1,)), ((), ())),
            preferred_element_type=jnp.float32,
        )
        prob_grads = [prob_grad[slot * BLK : (slot + 1) * BLK, :] for slot in range(8)]
        products = [left * right for left, right in zip(attn_probs, prob_grads)]
        total = jnp.sum(sum(products[1:], products[0]), axis=0, keepdims=True)
        score_grad = jnp.concatenate(
            [
                (left * (right - total)).astype(jnp.bfloat16)
                for left, right in zip(attn_probs, prob_grads)
            ],
            axis=0,
        )
        probs_low = jnp.concatenate([piece.astype(jnp.bfloat16) for piece in attn_probs], axis=0)
        square = lax.dot_general(
            score_grad, picked_keys, (((0,), (0,)), ((), ())), preferred_element_type=jnp.float32
        )
        query_grad = (from_diagonal(square, width) * factor).astype(jnp.bfloat16)
        grads_out_ref[own, :width] = query_grad
        query_total[...] += jnp.sum(
            query_grad.astype(jnp.float32).reshape(BLK // 8, 8, width), axis=0
        )
        key_part = jnp.dot(score_grad, grouped, preferred_element_type=jnp.float32)
        value_part = jnp.dot(probs_low, grouped_grad, preferred_element_type=jnp.float32)
        put_rows(key_sums, key_part, shared, apart, head_count)
        put_rows(value_sums, value_part, shared, apart, head_count)

    @pl.loop(0, num_blocks // unroll)
    def _(turn):
        for place in range(unroll):
            one_block(turn * unroll + place)

    value_grad = value_sums[...].reshape(queries_ref.shape).astype(jnp.bfloat16)
    seq_len = queries_ref.shape[0]
    grads_out_ref[:, width : 2 * width] = key_sums[...].reshape(seq_len, width).astype(jnp.bfloat16)
    grads_out_ref[:, 2 * width :] = value_grad
    bias_ref[0:1, :] = jnp.sum(query_total[...], axis=0, keepdims=True)
    bias_ref[1:2, :] = jnp.sum(value_grad.astype(jnp.float32), axis=0, keepdims=True)


def limits_of(length, global_ids, random_ids, num_blocks, head_count):
    blocks = jnp.arange(num_blocks, dtype=jnp.int32)
    nearby_raw = blocks[:, None] + jnp.arange(-1, 2, dtype=jnp.int32)[None, :]
    near_ok = (nearby_raw >= 0) & (nearby_raw < num_blocks)
    global_rows = jnp.broadcast_to(global_ids[None, :], (num_blocks, 2))
    global_ok = jnp.all(global_rows[:, :, None] != nearby_raw[:, None, :], axis=2)
    common = jnp.concatenate([nearby_raw, global_rows], axis=1)
    common_ok = jnp.concatenate([near_ok, global_ok], axis=1)
    common_limit = jnp.where(common_ok, length - common * BLK, 0)
    random_limit = jnp.transpose(length - random_ids * BLK, (0, 2, 1))
    return jnp.concatenate(
        [
            jnp.broadcast_to(common_limit[:, :, None], (num_blocks, 5, head_count * DH)),
            jnp.repeat(random_limit, DH, axis=2),
        ],
        axis=1,
    )


VMEM = pl.BlockSpec(memory_space=pltpu.VMEM)
SMEM = pl.BlockSpec(memory_space=pltpu.SMEM)


def attend_back(queries, key_rows, value_rows, tables, stats, context_grad):
    seq_len, width = queries.shape
    head_count = width // DH
    return pl.pallas_call(
        functools.partial(attend_back_kernel, head_count, 8),
        out_shape=(
            jax.ShapeDtypeStruct((seq_len, 3 * width), jnp.bfloat16),
            jax.ShapeDtypeStruct((2, width), jnp.float32),
        ),
        in_specs=[SMEM] * 2 + [VMEM] * 7,
        out_specs=[VMEM] * 2,
        scratch_shapes=[pltpu.VMEM((seq_len // BLK, BLK, width), jnp.float32)] * 2
        + [pltpu.VMEM((8, width), jnp.float32)],
        compiler_params=pltpu.CompilerParams(vmem_limit_bytes=40 * 1024 * 1024),
        cost_estimate=pl.CostEstimate(
            flops=10 * seq_len * 512 * width * head_count,
            bytes_accessed=14 * seq_len * width,
            transcendentals=seq_len * 512 * head_count,
        ),
    )(*tables, queries, key_rows, value_rows, context_grad, *stats)


KINDS = 4
CHUNKS = 4


def front_kernel(
    levels,
    across,
    along,
    globals_ref,
    random_ref,
    limits_ref,
    hidden_ref,
    grads_ref,
    b_query_ref,
    b_value_ref,
    part_qkv_ref,
    part_out_ref,
    part_up_ref,
    part_down_ref,
    vectors_ref,
    features_ref,
    own_ref,
    upstream_ref,
    queries_ref,
    keys_ref,
    values_ref,
    context_ref,
    highest_ref,
    scale_ref,
    full_qkv_ref,
    full_out_ref,
    full_up_ref,
    full_down_ref,
    out_sib,
    up_sib,
    down_sib,
    context_sib,
    normed_full,
    unit1,
    inv1,
    sum_out,
    sum_in,
    level_send,
    level_recv,
    core_send,
    core_recv,
    swap_send,
    swap_recv,
    along_send,
    along_recv,
    across_send,
    across_recv,
    shard_send,
    shard_recv,
    context_send,
    context_recv,
    sum_send,
    sum_recv,
    normed_send,
    normed_recv,
):
    low, full = jnp.bfloat16, jnp.float32
    row, column = lax.axis_index("row"), lax.axis_index("col")
    core, level = lax.rem(column, 2), lax.div(column, 2)
    fast, slow = lax.rem(row, across), lax.div(row, across)
    cols = 2 * levels
    seq_len, width = hidden_ref.shape
    own_len = seq_len // cols
    shard = part_qkv_ref.shape[0]
    other = 1 - core
    sibling = (row, level * 2 + other)
    offsets = range(1, levels)

    def peer_level(offset):
        return lax.rem(level + offset, levels)

    def fast_peer(offset):
        return slow * across + lax.rem(fast + offset, across)

    def slow_peer(offset):
        return lax.rem(slow + offset, along) * across + fast

    barrier = pltpu.get_barrier_semaphore()
    greeted = [sibling]
    for offset in offsets:
        greeted += [(row, peer_level(offset) * 2 + core), (row, peer_level(offset) * 2 + other)]
    greeted += [(fast_peer(offset), column) for offset in range(1, across)]
    greeted += [(slow_peer(offset), column) for offset in range(1, along)]
    for device in greeted:
        pl.semaphore_signal(barrier, inc=1, device_id=device, device_id_type=MESH)
    pl.semaphore_wait(barrier, len(greeted))

    def remote(source, target, send, recv, device):
        return pltpu.make_async_remote_copy(
            src_ref=source,
            dst_ref=target,
            send_sem=send,
            recv_sem=recv,
            device_id=device,
            device_id_type=MESH,
        )

    def block(start, size):
        return pl.ds(pl.multiple_of(start * size, size), size)

    def level_copy(turn, offset):
        rows = block(turn, own_len)
        return remote(
            hidden_ref.at[rows],
            features_ref.at[rows, block(column, width)],
            level_send.at[turn, offset - 1],
            level_recv.at[turn, levels - offset - 1],
            (row, peer_level(offset) * 2 + core),
        )

    def core_copy(turn, offset):
        view = features_ref.at[block(turn, own_len), block(peer_level(offset) * 2 + core, width)]
        return remote(
            view, view, core_send.at[turn, offset], core_recv.at[turn, offset], sibling
        )

    @pl.loop(0, cols)
    def _(turn):
        for offset in offsets:
            level_copy(turn, offset).start()
        rows = block(turn, own_len)
        features_ref[rows, block(column, width)] = hidden_ref[rows, :]
        core_copy(turn, 0).start()

    parts = (part_qkv_ref, part_out_ref, part_up_ref, part_down_ref)
    fulls = (full_qkv_ref, full_out_ref, full_up_ref, full_down_ref)
    sibs = (None, out_sib, up_sib, down_sib)

    def shard_rows(place):
        return block(place * across + fast, shard)

    def along_copy(kind, offset):
        view = fulls[kind].at[shard_rows(slow)]
        return remote(
            view,
            view,
            along_send.at[kind, offset - 1],
            along_recv.at[kind, along - offset - 1],
            (slow_peer(offset), column),
        )

    def across_copy(kind, place, offset):
        view = fulls[kind].at[shard_rows(place)]
        return remote(
            view,
            view,
            across_send.at[kind, place, offset - 1],
            across_recv.at[kind, place, across - offset - 1],
            (fast_peer(offset), column),
        )

    def core_shard(kind, place, offset):
        rows = block(place * across + lax.rem(fast + offset, across), shard)
        return remote(
            fulls[kind].at[rows],
            sibs[kind].at[rows],
            shard_send.at[kind - 1, place, offset],
            shard_recv.at[kind - 1, place, offset],
            sibling,
        )

    for kind in range(KINDS):
        fulls[kind][shard_rows(slow), :] = parts[kind][...]
        for offset in range(1, along):
            along_copy(kind, offset).start()
        for offset in range(1, across):
            across_copy(kind, slow, offset).start()
        if kind > 0:
            core_shard(kind, slow, 0).start()

    def swap_copy(target, place_out, place_in):
        return remote(
            grads_ref.at[block(target, own_len)],
            upstream_ref.at[:, block(column, width)],
            swap_send.at[place_out],
            swap_recv.at[place_in],
            (row, target),
        )

    swaps = [swap_copy(level * 2 + other, 0, 0)]
    for offset in offsets:
        back = levels - offset
        swaps.append(swap_copy(peer_level(offset) * 2 + core, 2 * offset - 1, 2 * back - 1))
        swaps.append(swap_copy(peer_level(offset) * 2 + other, 2 * offset, 2 * back))
    for copy in swaps:
        copy.start()
    upstream_ref[:, block(column, width)] = grads_ref[block(column, own_len), :]

    waiting = [(kind, offset) for kind in range(KINDS) for offset in range(1, along)]

    def pass_on(count):
        for kind, offset in waiting[:count]:
            along_copy(kind, along - offset).wait_recv()
            for step in range(1, across):
                across_copy(kind, lax.rem(slow + offset, along), step).start()
            if kind > 0:
                core_shard(kind, lax.rem(slow + offset, along), 0).start()
        del waiting[:count]

    def await_shards(kind):
        @pl.loop(0, along)
        def _(place):
            for offset in range(1, across):
                across_copy(kind, place, across - offset).wait_recv()
                if kind > 0:
                    core_shard(kind, place, offset).start()

    def await_sibling(kind):
        @pl.loop(0, along)
        def _(place):
            for offset in range(across):
                core_shard(kind, place, offset).wait_recv()

    pass_on(along - 1)
    await_shards(0)

    def project(turn):
        rows = block(turn, own_len)
        for offset in offsets:
            level_copy(turn, levels - offset).wait_recv()
            core_copy(turn, offset).start()
        for offset in range(levels):
            core_copy(turn, offset).wait_recv()
        values_in = features_ref[rows, :]
        queries_ref[rows, :] = (
            dot(values_in, full_qkv_ref[:, :width]) + b_query_ref[...]
        ).astype(low)
        blocks = pl.ds(turn * (own_len // BLK), own_len // BLK)
        by_block = (own_len // BLK, BLK, width)
        keys_ref[blocks] = (
            dot(values_in, full_qkv_ref[:, width : 2 * width]).astype(low).reshape(by_block)
        )
        values_ref[blocks] = (
            (dot(values_in, full_qkv_ref[:, 2 * width :]) + b_value_ref[...])
            .astype(low)
            .reshape(by_block)
        )

    for turn in range(cols):
        project(turn)
        pass_on(1)
    own_ref[...] = features_ref[block(column, own_len), :]
    step = own_len // CHUNKS
    halves = 2
    count = own_len // BLK // halves
    b_out, gain1, shift1 = (vectors_ref.at[place : place + 1, :] for place in range(3))

    def attend_half(quarter, half):
        attend_blocks(
            (quarter * halves + half) * count,
            count,
            min(count, 4),
            globals_ref,
            random_ref,
            limits_ref,
            (queries_ref, keys_ref, values_ref),
            context_ref,
            (highest_ref, scale_ref),
        )

    def context_copy(place, half):
        rows = own_len // halves
        return remote(
            context_ref.at[block((place * 2 + other) * halves + half, rows)],
            context_sib.at[block(place * halves + half, rows)],
            context_send.at[place, half],
            context_recv.at[place, half],
            sibling,
        )

    def chunk_rows(place, chunk):
        return block(place * CHUNKS + chunk, step)

    def attn_part(place, chunk):
        return dot_nt(
            context_ref[chunk_rows(place * 2 + core, chunk), :], full_out_ref[...]
        ) + dot_nt(context_sib[chunk_rows(place, chunk), :], out_sib[...])

    def sum_copy(chunk, offset):
        rows = block(chunk, step)
        return remote(
            sum_out.at[offset - 1, rows],
            sum_in.at[levels - offset - 1, rows],
            sum_send.at[chunk, offset - 1],
            sum_recv.at[chunk, levels - offset - 1],
            (row, peer_level(offset) * 2 + core),
        )

    def normed_copy(chunk, offset):
        view = normed_full.at[chunk_rows(level, chunk)]
        return remote(
            view,
            view,
            normed_send.at[chunk, offset - 1],
            normed_recv.at[chunk, levels - offset - 1],
            (row, peer_level(offset) * 2 + core),
        )

    for offset in list(offsets) + [0]:
        place = peer_level(offset)
        for half in range(halves):
            attend_half(place * 2 + other, half)
            context_copy(place, half).start()
            pass_on(half if len(waiting) > along - 1 else 0)
        if offset == 1:
            await_shards(1)
        for half in range(halves):
            attend_half(place * 2 + core, half)
            if offset == 1 and half == 0:
                await_sibling(1)
            context_copy(place, half).wait_recv()
            per_half = CHUNKS // halves
            for chunk in range(half * per_half, (half + 1) * per_half):
                if offset:
                    sum_out[offset - 1, block(chunk, step), :] = attn_part(place, chunk).astype(
                        low
                    )
                    sum_copy(chunk, offset).start()
        pass_on(1 if len(waiting) > along - 1 else 0)
    pass_on(max(len(waiting) - (along - 1), 0))
    await_shards(2)
    for chunk in range(CHUNKS):
        rows = block(chunk, step)
        summed = own_ref[rows, :].astype(full) + attn_part(level, chunk) + b_out[...]
        for offset in offsets:
            sum_copy(chunk, offset).wait_recv()
        for place in range(levels - 1):
            summed += sum_in[place, rows, :].astype(full)
        normed, inv_std = norm_parts(summed)
        unit1[rows, :] = normed
        inv1[rows, :] = inv_std
        normed_full[chunk_rows(level, chunk), :] = (normed * gain1[...] + shift1[...]).astype(low)
        for offset in offsets:
            normed_copy(chunk, offset).start()
        pass_on(1 if chunk else 0)
    pass_on(len(waiting))
    await_shards(3)
    for chunk in range(CHUNKS):
        for offset in offsets:
            normed_copy(chunk, offset).wait()
            sum_copy(chunk, offset).wait_send()
    for kind in range(2, KINDS):
        await_sibling(kind)
    for place in range(levels):
        for half in range(halves):
            context_copy(place, half).wait_send()
    for copy in swaps:
        copy.wait()
    for kind in range(KINDS):
        for offset in range(1, along):
            along_copy(kind, offset).wait_send()

        @pl.loop(0, along)
        def _(place):
            for offset in range(1, across):
                across_copy(kind, place, offset).wait_send()
            if kind > 0:
                for offset in range(across):
                    core_shard(kind, place, offset).wait_send()

    @pl.loop(0, cols)
    def _(turn):
        for offset in offsets:
            level_copy(turn, offset).wait_send()
        for offset in range(levels):
            core_copy(turn, offset).wait_send()


def across_of(rows):
    return 2 if rows <= 8 else rows // 4


def front(levels, rows, tables, hidden_in, grads, biases, parts, vectors):
    low, full = jnp.bfloat16, jnp.float32
    shape = jax.ShapeDtypeStruct
    across = across_of(rows)
    along = rows // across
    seq_len, width = hidden_in.shape
    cols = 2 * levels
    own_len = seq_len // cols
    features_all = width * cols
    others = levels - 1
    stat = shape((seq_len // BLK, 1, width), full)
    dma = pltpu.SemaphoreType.DMA
    return pl.pallas_call(
        functools.partial(front_kernel, levels, across, along),
        out_shape=(
            shape((seq_len, features_all), low),
            shape((own_len, features_all), low),
            shape((own_len, features_all), low),
            shape((seq_len, width), low),
            shape((seq_len // BLK, BLK, width), low),
            shape((seq_len // BLK, BLK, width), low),
            shape((seq_len, width), low),
            stat,
            stat,
            *(shape((part.shape[0] * rows, part.shape[1]), low) for part in parts),
            *(shape((part.shape[0] * rows, part.shape[1]), low) for part in parts[1:]),
            shape((levels * own_len, width), low),
            shape((levels * own_len, features_all), low),
            shape((own_len, features_all), full),
            shape((own_len, 1), full),
        ),
        in_specs=[SMEM] * 2 + [VMEM] * 10,
        out_specs=[VMEM] * 20,
        scratch_shapes=[
            pltpu.VMEM((others, own_len, features_all), low),
            pltpu.VMEM((others, own_len, features_all), low),
            dma((cols, others)),
            dma((cols, others)),
            dma((cols, levels)),
            dma((cols, levels)),
            dma((cols,)),
            dma((cols,)),
            dma((KINDS, along - 1)),
            dma((KINDS, along - 1)),
            dma((KINDS, along, across - 1)),
            dma((KINDS, along, across - 1)),
            dma((KINDS - 1, along, across)),
            dma((KINDS - 1, along, across)),
            dma((levels, 2)),
            dma((levels, 2)),
            *(dma((CHUNKS, others)) for _ in range(4)),
        ],
        compiler_params=pltpu.CompilerParams(
            collective_id=3, has_side_effects=True, vmem_limit_bytes=56 * 1024 * 1024
        ),
        cost_estimate=pl.CostEstimate(
            flops=2 * seq_len * features_all * 3 * width,
            bytes_accessed=20 * 1024 * 1024,
            transcendentals=seq_len * 512 * (width // DH),
        ),
    )(*tables, hidden_in, grads, *biases, *parts, vectors)


def dot(left, right):
    return jnp.dot(left, right, preferred_element_type=jnp.float32)


def dot_nt(left, right):
    return lax.dot_general(
        left, right, (((1,), (1,)), ((), ())), preferred_element_type=jnp.float32
    )


def dot_tn(left, right):
    return lax.dot_general(
        left, right, (((0,), (0,)), ((), ())), preferred_element_type=jnp.float32
    )


def gelu_parts(values_in):
    factor = math.sqrt(2.0 / math.pi)
    square = values_in * values_in
    bent = jnp.tanh(factor * (values_in + 0.044715 * (values_in * square)))
    half = 0.5 * (1.0 + bent)
    slope = half + (0.5 * values_in) * (1.0 - bent * bent) * (
        factor + (3.0 * 0.044715 * factor) * square
    )
    return (values_in * half, slope)


def norm_parts(summed):
    average = jnp.mean(summed, axis=1, keepdims=True)
    squares = jnp.mean(summed * summed, axis=1, keepdims=True)
    inv_std = lax.rsqrt(squares - average * average + epsilon)
    return ((summed - average) * inv_std, inv_std)


def norm_back(upstream, normed, inv_std, gain_vec):
    scaled = upstream * gain_vec
    left = jnp.mean(scaled, axis=1, keepdims=True)
    right = jnp.mean(scaled * normed, axis=1, keepdims=True)
    return inv_std * (scaled - left - normed * right)


def middle_kernel(
    levels,
    across,
    along,
    context_ref,
    context_sib,
    upstream_ref,
    valid_ref,
    out_ref,
    out_sib,
    up_ref,
    up_sib,
    down_full,
    down_sib,
    normed_full,
    unit1,
    inv1,
    vectors_ref,
    b_up_ref,
    layer_out_ref,
    context_grad_ref,
    attn_full,
    small_ref,
    up_small_ref,
    share_down_ref,
    up_part_ref,
    grad_out_ref,
    ffn_full,
    hidden,
    slope,
    pre_grad,
    ffn_keep,
    part_own,
    send_buf,
    recv_buf,
    context_send,
    stage,
    down_sums,
    up_sums,
    down_got,
    up_got,
    down_pass,
    down_in,
    send_sem,
    recv_sem,
    core_send,
    core_recv,
    along_send,
    along_recv,
    across_send,
    across_recv,
    stage_sem,
):
    low = jnp.bfloat16
    row, column = lax.axis_index("row"), lax.axis_index("col")
    core = lax.rem(column, 2)
    level = lax.div(column, 2)
    sibling = (row, column + 1 - 2 * core)
    fast, slow = lax.rem(row, across), lax.div(row, across)
    shard = share_down_ref.shape[0]
    own_len = upstream_ref.shape[0]
    step = own_len // CHUNKS
    b_out, gain1, shift1, b_down, gain2, shift2 = (
        vectors_ref.at[place : place + 1, :] for place in range(6)
    )

    def peer_level(offset):
        return lax.rem(level + offset, levels)

    def fast_peer(offset):
        return slow * across + lax.rem(fast + offset, across)

    def slow_peer(offset):
        return lax.rem(slow + offset, along) * across + fast

    barrier = pltpu.get_barrier_semaphore()
    greeted = [sibling]
    greeted += [(row, peer_level(offset) * 2 + core) for offset in range(1, levels)]
    greeted += [(fast_peer(offset), column) for offset in range(1, across)]
    greeted += [(slow_peer(offset), column) for offset in range(1, along)]
    for device in greeted:
        pl.semaphore_signal(barrier, inc=1, device_id=device, device_id_type=MESH)
    pl.semaphore_wait(barrier, len(greeted))

    def remote(source, target, send, recv, device):
        return pltpu.make_async_remote_copy(
            src_ref=source,
            dst_ref=target,
            send_sem=send,
            recv_sem=recv,
            device_id=device,
            device_id_type=MESH,
        )

    def block(start, size):
        return pl.ds(pl.multiple_of(start * size, size), size)

    def to_sibling(source, target, place):
        return remote(source, target, core_send.at[place], core_recv.at[place], sibling)

    def rows_of(place, chunk):
        return pl.ds(pl.multiple_of(place * own_len + chunk * step, step), step)

    def own_rows(chunk):
        return pl.ds(pl.multiple_of(chunk * step, step), step)

    def exchange(kind, chunk, offset, source, target):
        return pltpu.make_async_remote_copy(
            src_ref=source,
            dst_ref=target,
            send_sem=send_sem.at[kind - 2, chunk, offset - 1],
            recv_sem=recv_sem.at[kind - 2, chunk, levels - offset - 1],
            device_id=(row, peer_level(offset) * 2 + core),
            device_id_type=MESH,
        )

    def sum_copy(kind, chunk, offset):
        return exchange(
            kind,
            chunk,
            offset,
            send_buf.at[kind // 2 - 1, offset - 1, own_rows(chunk)],
            recv_buf.at[kind // 2 - 1, levels - offset - 1, own_rows(chunk)],
        )

    def spread_copy(kind, chunk, offset):
        whole = {3: ffn_full, 5: attn_full}[kind]
        rows = rows_of(level, chunk)
        return exchange(kind, chunk, offset, whole.at[rows], whole.at[rows])

    def received(kind, chunk):
        return sum(
            recv_buf[kind // 2 - 1, place, own_rows(chunk), :].astype(jnp.float32)
            for place in range(levels - 1)
        )

    offsets = range(1, levels)
    small_ref[...] = jnp.zeros_like(small_ref)
    up_small_ref[...] = jnp.zeros_like(up_small_ref)
    def context_rows(place, chunk):
        start = (place * 2 + core) * own_len + chunk * step
        return pl.ds(pl.multiple_of(start, step), step)

    sides = ((up_ref, down_full), (up_sib, down_sib))

    def feed_forward(place, chunk):
        rows = rows_of(place, chunk)
        normed = normed_full[rows, :]
        total = None
        for side, (up_side, down_side) in enumerate(sides):
            active, bend = gelu_parts(dot(normed, up_side[...]) + b_up_ref[side : side + 1, :])
            active = active.astype(low)
            hidden[side, rows, :] = active
            slope[side, rows, :] = bend.astype(low)
            part = dot_nt(active, down_side[...])
            total = part if total is None else total + part
        return total

    @pl.loop(0, CHUNKS)
    def _(chunk):
        for offset in offsets:
            send_buf[0, offset - 1, own_rows(chunk), :] = feed_forward(
                peer_level(offset), chunk
            ).astype(low)
            sum_copy(2, chunk, offset).start()

    @pl.loop(0, CHUNKS)
    def _(chunk):
        rows = own_rows(chunk)
        part_own[rows, :] = feed_forward(level, chunk)
        normed1 = unit1[rows, :] * gain1[...] + shift1[...]
        summed = normed1 + part_own[rows, :] + b_down[...]
        for offset in offsets:
            sum_copy(2, chunk, offset).wait_recv()
        normed, inv_std = norm_parts(summed + received(2, chunk))
        layer_out_ref[rows, :] = jnp.where(
            valid_ref[rows, :] > 0, normed * gain2[...] + shift2[...], 0.0
        ).astype(low)
        upstream = upstream_ref[rows, :].astype(jnp.float32)
        grad = norm_back(upstream, normed, inv_std, gain2[...])
        ffn_keep[rows, :] = grad
        grad_low = grad.astype(low)
        ffn_full[rows_of(level, chunk), :] = grad_low
        for offset in offsets:
            spread_copy(3, chunk, offset).start()
        small_ref[0:1, :] += jnp.sum(upstream * normed, axis=0, keepdims=True)
        small_ref[1:2, :] += jnp.sum(upstream, axis=0, keepdims=True)
        small_ref[2:3, :] += jnp.sum(grad_low.astype(jnp.float32), axis=0, keepdims=True)

    def feed_back(place, chunk):
        rows = rows_of(place, chunk)
        upstream = ffn_full[rows, :]
        total = None
        for side, (up_side, down_side) in enumerate(sides):
            grad = (
                dot(upstream, down_side[...]) * slope[side, rows, :].astype(jnp.float32)
            ).astype(low)
            pre_grad[side, rows, :] = grad
            up_small_ref[side : side + 1, :] += jnp.sum(
                grad.astype(jnp.float32), axis=0, keepdims=True
            )
            part = dot_nt(grad, up_side[...])
            total = part if total is None else total + part
        return total

    @pl.loop(0, CHUNKS)
    def _(chunk):
        part_own[own_rows(chunk), :] = feed_back(level, chunk)
        for offset in offsets:
            spread_copy(3, chunk, levels - offset).wait_recv()
            send_buf[1, offset - 1, own_rows(chunk), :] = feed_back(
                peer_level(offset), chunk
            ).astype(low)
            sum_copy(4, chunk, offset).start()

    tile = across * shard
    lefts, rights = (ffn_full, normed_full), (hidden, pre_grad)
    sums, got = (down_sums, up_sums), (down_got, up_got)

    def grad_tile(kind, side, turn):
        return dot_tn(lefts[kind][:, block(turn, tile)], rights[kind][side])

    def core_grad(kind):
        return to_sibling(
            slope.at[kind, : sums[kind].shape[0]], sums[kind], levels + kind
        )

    def across_grad(kind, turn, offset):
        return remote(
            sums[kind].at[block(turn * across + lax.rem(fast + offset, across), shard)],
            got[kind].at[across - offset - 1, block(turn, shard)],
            across_send.at[kind, turn, offset - 1],
            across_recv.at[kind, turn, across - offset - 1],
            (fast_peer(offset), column),
        )

    def along_grad(offset):
        return remote(
            down_pass.at[offset - 1],
            down_in.at[along - offset - 1],
            along_send.at[offset - 1],
            along_recv.at[along - offset - 1],
            (slow_peer(offset), column),
        )

    def own_shard(kind, turn):
        for offset in range(1, across):
            across_grad(kind, turn, offset).wait_recv()
        total = sums[kind][block(turn * across + fast, shard), :].astype(jnp.float32)
        for place in range(across - 1):
            total += got[kind][place, block(turn, shard), :].astype(jnp.float32)
        return total

    for kind in range(2):

        @pl.loop(0, along)
        def _(turn):
            slope[kind, block(turn, tile), :] = grad_tile(kind, 1, turn).astype(low)

        core_grad(kind).start()
    for kind in range(2):
        core_grad(kind).wait_recv()

        @pl.loop(0, along)
        def _(turn):
            rows = block(turn, tile)
            sums[kind][rows, :] = (
                grad_tile(kind, 0, turn) + sums[kind][rows, :].astype(jnp.float32)
            ).astype(low)
            for offset in range(1, across):
                across_grad(kind, turn, offset).start()

    @pl.loop(0, CHUNKS)
    def _(chunk):
        rows = own_rows(chunk)
        upstream = ffn_keep[rows, :] + part_own[rows, :]
        for offset in offsets:
            sum_copy(4, chunk, offset).wait_recv()
        upstream = upstream + received(4, chunk)
        normed = unit1[rows, :]
        grad_low = norm_back(upstream, normed, inv1[rows, :], gain1[...]).astype(low)
        attn_full[rows_of(level, chunk), :] = grad_low
        for offset in offsets:
            spread_copy(5, chunk, offset).start()
        small_ref[3:4, :] += jnp.sum(upstream * normed, axis=0, keepdims=True)
        small_ref[4:5, :] += jnp.sum(upstream, axis=0, keepdims=True)
        small_ref[5:6, :] += jnp.sum(grad_low.astype(jnp.float32), axis=0, keepdims=True)

    for offset in range(1, along):
        down_pass[offset - 1] = own_shard(0, lax.rem(slow + offset, along)).astype(low)
        along_grad(offset).start()
    share_down_ref[...] = own_shard(0, slow)

    def context_back(place, chunk):
        rows = rows_of(place, chunk)
        upstream = attn_full[rows, :]
        context_grad_ref[context_rows(place, chunk), :] = dot(upstream, out_ref[...]).astype(low)
        context_send[rows, :] = dot(upstream, out_sib[...]).astype(low)

    @pl.loop(0, CHUNKS)
    def _(chunk):
        context_back(level, chunk)
        for offset in offsets:
            spread_copy(5, chunk, levels - offset).wait_recv()
            context_back(peer_level(offset), chunk)

    back_copies = [
        to_sibling(
            context_send.at[pl.ds(place * own_len, own_len)],
            context_grad_ref.at[
                pl.ds(pl.multiple_of((place * 2 + core) * own_len, own_len), own_len)
            ],
            place,
        )
        for place in range(levels)
    ]
    for copy in back_copies:
        copy.start()

    own_context = jnp.concatenate(
        [
            context_ref[
                pl.ds(pl.multiple_of((place * 2 + core) * own_len, own_len), own_len), :
            ]
            for place in range(levels)
        ],
        axis=0,
    )

    def out_put(side):
        return pltpu.make_async_copy(stage.at[side], grad_out_ref.at[side], stage_sem.at[side])

    for side, right in enumerate((own_context, context_sib[...])):
        stage[side] = dot_tn(attn_full[...], right).astype(low)
        out_put(side).start()
    for turn in range(along):
        up_part_ref[turn] = own_shard(1, turn).astype(low)
    total = share_down_ref[...]
    for offset in range(1, along):
        along_grad(offset).wait_recv()
    for place in range(along - 1):
        total += down_in[place].astype(jnp.float32)
    share_down_ref[...] = total
    for side in range(2):
        out_put(side).wait()
    for kind in range(2):
        core_grad(kind).wait_send()
    for offset in range(1, along):
        along_grad(offset).wait_send()

    @pl.loop(0, along)
    def _(place):
        for offset in range(1, across):
            across_grad(0, place, offset).wait_send()
            across_grad(1, place, offset).wait_send()

    for copy in back_copies:
        copy.wait()
    for kind in range(2, 6):

        @pl.loop(0, CHUNKS)
        def _(chunk):
            for offset in offsets:
                if kind % 2:
                    spread_copy(kind, chunk, offset).wait_send()
                else:
                    sum_copy(kind, chunk, offset).wait_send()


def middle(
    levels,
    rows,
    context,
    context_sib,
    upstream,
    valid,
    weights,
    normed_full,
    unit1,
    inv1,
    vectors,
    b_up_pair,
):
    low, full = jnp.bfloat16, jnp.float32
    across = across_of(rows)
    along = rows // across
    own_len, features = upstream.shape
    seq_len, width = context.shape
    units = weights[2].shape[1]
    shard = features // rows
    tokens = levels * own_len
    others = levels - 1
    shape = jax.ShapeDtypeStruct
    hbm = pl.BlockSpec(memory_space=pl.ANY)
    dma = pltpu.SemaphoreType.DMA
    vmem = pltpu.VMEM
    return pl.pallas_call(
        functools.partial(middle_kernel, levels, across, along),
        out_shape=(
            shape((own_len, features), low),
            shape((seq_len, width), low),
            shape((tokens, features), low),
            shape((8, features), full),
            shape((2, units), full),
            shape((shard, units), full),
            shape((along, shard, units), low),
            shape((2, features, width), low),
        ),
        in_specs=[VMEM] * 15,
        out_specs=[VMEM] * 7 + [hbm],
        scratch_shapes=[
            vmem((tokens, features), low),
            vmem((2, tokens, units), low),
            vmem((2, max(tokens, features), units), low),
            vmem((2, tokens, units), low),
            vmem((own_len, features), full),
            vmem((own_len, features), full),
            vmem((2, others, own_len, features), low),
            vmem((2, others, own_len, features), low),
            vmem((tokens, width), low),
            vmem((2, features, width), low),
            vmem((features, units), low),
            vmem((features, units), low),
            vmem((across - 1, along * shard, units), low),
            vmem((across - 1, along * shard, units), low),
            vmem((along - 1, shard, units), low),
            vmem((along - 1, shard, units), low),
            dma((4, CHUNKS, others)),
            dma((4, CHUNKS, others)),
            dma((levels + 2,)),
            dma((levels + 2,)),
            dma((along - 1,)),
            dma((along - 1,)),
            dma((2, along, across - 1)),
            dma((2, along, across - 1)),
            dma((2,)),
        ],
        compiler_params=pltpu.CompilerParams(
            collective_id=1, has_side_effects=True, vmem_limit_bytes=62 * 1024 * 1024
        ),
        cost_estimate=pl.CostEstimate(
            flops=2 * tokens * features * (12 * units + 6 * width),
            bytes_accessed=20 * 1024 * 1024,
            transcendentals=2 * tokens * units,
        ),
    )(
        context,
        context_sib,
        upstream,
        valid,
        *weights,
        normed_full,
        unit1,
        inv1,
        vectors,
        b_up_pair,
    )


def end_kernel(
    levels,
    across,
    along,
    query_key_value_ref,
    weights_ref,
    features_ref,
    attn_ref,
    layer_ref,
    small_ref,
    out_ref,
    up_ref,
    grad_input_ref,
    layer_out_ref,
    small_out_ref,
    share_out_ref,
    share_qkv_ref,
    share_up_ref,
    out_sib,
    qkv_sums,
    out_got,
    qkv_got,
    out_pass,
    qkv_pass,
    out_in,
    qkv_in,
    up_in,
    core_out,
    core_in,
    level_out,
    level_in,
    attn_in,
    small_sums,
    small_in,
    core_send,
    core_recv,
    part_send,
    part_recv,
    level_send,
    level_recv,
    layer_send,
    layer_recv,
    across_send,
    across_recv,
    along_send,
    along_recv,
    small_send,
    small_recv,
    keep_sem,
):
    low, full = jnp.bfloat16, jnp.float32
    row, column = lax.axis_index("row"), lax.axis_index("col")
    core, level = lax.rem(column, 2), lax.div(column, 2)
    fast, slow = lax.rem(row, across), lax.div(row, across)
    cols = 2 * levels
    seq_len = features_ref.shape[0]
    own_len = seq_len // cols
    width = grad_input_ref.shape[1]
    shard = share_qkv_ref.shape[0]
    other = 1 - core
    sibling = (row, level * 2 + other)
    offsets = range(1, levels)

    def peer_level(offset):
        return lax.rem(level + offset, levels)

    def fast_peer(offset):
        return slow * across + lax.rem(fast + offset, across)

    def slow_peer(offset):
        return lax.rem(slow + offset, along) * across + fast

    barrier = pltpu.get_barrier_semaphore()
    greeted = [sibling]
    for offset in offsets:
        greeted += [(row, peer_level(offset) * 2 + core), (row, peer_level(offset) * 2 + other)]
    greeted += [(fast_peer(offset), column) for offset in range(1, across)]
    greeted += [(slow_peer(offset), column) for offset in range(1, along)]
    for device in greeted:
        pl.semaphore_signal(barrier, inc=1, device_id=device, device_id_type=MESH)
    pl.semaphore_wait(barrier, len(greeted))

    def remote(source, target, send, recv, device):
        return pltpu.make_async_remote_copy(
            src_ref=source,
            dst_ref=target,
            send_sem=send,
            recv_sem=recv,
            device_id=device,
            device_id_type=MESH,
        )

    def block(start, size):
        return pl.ds(pl.multiple_of(start * size, size), size)

    out_copy = remote(out_ref.at[1], out_sib, core_send.at[0], core_recv.at[0], sibling)
    attn_copy = remote(
        attn_ref.at[:, block(level * 2 + other, width)],
        attn_in,
        core_send.at[1],
        core_recv.at[1],
        sibling,
    )

    partners = [sibling]
    bit = 1
    while bit < levels:
        partners.append((row, (level + bit - 2 * bit * lax.rem(lax.div(level, bit), 2)) * 2 + core))
        bit *= 2
    bit = 1
    while bit < across * along:
        partners.append((row + bit - 2 * bit * lax.rem(lax.div(row, bit), 2), column))
        bit *= 2

    def small_copy(turn):
        return remote(
            small_sums.at[turn],
            small_in.at[turn],
            small_send.at[turn],
            small_recv.at[turn],
            partners[turn],
        )

    small_turn = [0]

    def small_step():
        turn = small_turn[0]
        if turn > len(partners):
            return
        if turn > 0:
            small_copy(turn - 1).wait()
            small_sums[turn] = small_sums[turn - 1] + small_in[turn - 1]
        if turn < len(partners):
            small_copy(turn).start()
        small_turn[0] += 1

    def layer_copy(target, place_out, place_in):
        return remote(
            layer_ref.at[:, block(target, width)],
            layer_out_ref.at[block(column, own_len)],
            layer_send.at[place_out],
            layer_recv.at[place_in],
            (row, target),
        )

    layer_copies = [layer_copy(level * 2 + other, 0, 0)]
    for offset in offsets:
        back = levels - offset
        layer_copies.append(
            layer_copy(peer_level(offset) * 2 + core, 2 * offset - 1, 2 * back - 1)
        )
        layer_copies.append(layer_copy(peer_level(offset) * 2 + other, 2 * offset, 2 * back))
    layer_keep = pltpu.make_async_copy(
        layer_ref.at[:, block(column, width)], layer_out_ref.at[block(column, own_len)], keep_sem
    )

    small_sums[0] = small_ref[...]
    small_step()
    out_copy.start()
    attn_copy.start()
    layer_keep.start()
    for copy in layer_copies:
        copy.start()

    def input_part(turn, target):
        return dot_nt(
            query_key_value_ref[block(turn, own_len), :], weights_ref[block(target, width), :]
        )

    def part_copy(turn, place):
        rows = block(turn, own_len)
        return remote(
            core_out.at[place, rows],
            core_in.at[place, rows],
            part_send.at[turn, place],
            part_recv.at[turn, place],
            sibling,
        )

    def give_core():
        @pl.loop(0, cols)
        def _(turn):
            for place in range(levels):
                core_out[place, block(turn, own_len), :] = input_part(
                    turn, place * 2 + other
                ).astype(low)
                part_copy(turn, place).start()

    sums = (out_sib, qkv_sums)
    got = (out_got, qkv_got)
    passed = (out_pass, qkv_pass)
    landed = (out_in, qkv_in, up_in)
    shares = (share_out_ref, share_qkv_ref, share_up_ref)

    def across_copy(kind, turn, offset):
        return remote(
            sums[kind].at[block(turn * across + lax.rem(fast + offset, across), shard)],
            got[kind].at[across - offset - 1, block(turn, shard)],
            across_send.at[kind, turn, offset - 1],
            across_recv.at[kind, turn, across - offset - 1],
            (fast_peer(offset), column),
        )

    def along_copy(kind, offset):
        if kind == 2:
            source = up_ref.at[lax.rem(slow + offset, along)]
        else:
            source = passed[kind].at[offset - 1]
        return remote(
            source,
            landed[kind].at[along - offset - 1],
            along_send.at[kind, offset - 1],
            along_recv.at[kind, along - offset - 1],
            (slow_peer(offset), column),
        )

    def give_across(kind, turn):
        for offset in range(1, across):
            across_copy(kind, turn, offset).start()

    def sum_cores():
        out_copy.wait()

        @pl.loop(0, along)
        def _(turn):
            rows = block(turn, across * shard)
            out_sib[rows, :] = (
                out_ref[0, rows, :].astype(full) + out_sib[rows, :].astype(full)
            ).astype(low)
            give_across(0, turn)

    def weight_grad():
        @pl.loop(0, along)
        def _(turn):
            rows = block(turn, across * shard)
            qkv_sums[rows, :] = dot_tn(features_ref[:, rows], query_key_value_ref[...]).astype(low)
            give_across(1, turn)

    def level_copy(turn, offset):
        rows = block(turn, own_len)
        return remote(
            level_out.at[offset - 1, rows],
            level_in.at[levels - offset - 1, rows],
            level_send.at[turn, offset - 1],
            level_recv.at[turn, levels - offset - 1],
            (row, peer_level(offset) * 2 + core),
        )

    def give_levels():
        @pl.loop(0, cols)
        def _(turn):
            rows = block(turn, own_len)
            for offset in offsets:
                place = peer_level(offset)
                part = input_part(turn, place * 2 + core)
                part_copy(turn, place).wait_recv()
                level_out[offset - 1, rows, :] = (
                    part + core_in[place, rows, :].astype(full)
                ).astype(low)
                level_copy(turn, offset).start()

    def own_shard(kind, turn):
        for offset in range(1, across):
            across_copy(kind, turn, offset).wait_recv()
        total = sums[kind][block(turn * across + fast, shard), :].astype(full)
        for place in range(across - 1):
            total += got[kind][place, block(turn, shard), :].astype(full)
        return total

    def give_along(kind):
        for offset in range(1, along):
            turn = lax.rem(slow + offset, along)
            passed[kind][offset - 1] = own_shard(kind, turn).astype(low)
            along_copy(kind, offset).start()
        shares[kind][...] = own_shard(kind, slow)

    def finish_input(turn, attn_part):
        rows = block(turn, own_len)
        total = input_part(turn, column) + attn_part.astype(full)
        part_copy(turn, level).wait_recv()
        total += core_in[level, rows, :].astype(full)
        for offset in offsets:
            level_copy(turn, offset).wait_recv()
        for place in range(levels - 1):
            total += level_in[place, rows, :].astype(full)
        grad_input_ref[rows, :] = total.astype(low)

    def finish_inputs():
        attn_copy.wait()

        @pl.loop(0, levels)
        def _(place):
            rows = block(place, own_len)
            finish_input(place * 2 + core, attn_ref[rows, block(column, width)])
            finish_input(place * 2 + other, attn_in[rows, :])

    for offset in range(1, along):
        along_copy(2, offset).start()
    share_up_ref[...] = up_ref[slow].astype(full)
    weight_grad()
    small_step()
    give_core()
    sum_cores()
    small_step()
    give_levels()
    small_step()
    give_along(1)
    small_step()
    give_along(0)
    small_step()
    finish_inputs()
    while small_turn[0] <= len(partners):
        small_step()
    small_out_ref[...] = small_sums[len(partners)]

    for kind in range(3):
        total = shares[kind][...]
        for offset in range(1, along):
            along_copy(kind, offset).wait_recv()
        for place in range(along - 1):
            total += landed[kind][place].astype(full)
        shares[kind][...] = total

    layer_keep.wait()
    for copy in layer_copies:
        copy.wait()
    for kind in range(3):
        for offset in range(1, along):
            along_copy(kind, offset).wait_send()
    for kind in range(2):

        @pl.loop(0, along)
        def _(turn):
            for offset in range(1, across):
                across_copy(kind, turn, offset).wait_send()

    @pl.loop(0, cols)
    def _(turn):
        for place in range(levels):
            part_copy(turn, place).wait_send()
        for offset in offsets:
            level_copy(turn, offset).wait_send()


def finish(
    levels, rows, query_key_value, weights, features, attn_full, layer_own, small, out, up
):
    low, full = jnp.bfloat16, jnp.float32
    shape = jax.ShapeDtypeStruct
    across = across_of(rows)
    along = rows // across
    seq_len, features_all = features.shape
    width = query_key_value.shape[1] // 3
    own_len = layer_own.shape[0]
    shard = features_all // rows
    widths = [out.shape[2], 3 * width]
    units = up.shape[2]
    others = levels - 1
    cols = 2 * levels
    turns = 1 + (levels - 1).bit_length() + (rows - 1).bit_length()
    dma = pltpu.SemaphoreType.DMA
    return pl.pallas_call(
        functools.partial(end_kernel, levels, across, along),
        out_shape=(
            shape((seq_len, width), low),
            shape((seq_len, width), low),
            shape(small.shape, full),
            *(shape((shard, each), full) for each in widths + [units]),
        ),
        in_specs=[VMEM] * 8,
        out_specs=[VMEM] * 6,
        scratch_shapes=[
            *(pltpu.VMEM((features_all, each), low) for each in widths),
            *(pltpu.VMEM((across - 1, along * shard, each), low) for each in widths),
            *(pltpu.VMEM((along - 1, shard, each), low) for each in widths),
            *(pltpu.VMEM((along - 1, shard, each), low) for each in widths + [units]),
            pltpu.VMEM((levels, seq_len, width), low),
            pltpu.VMEM((levels, seq_len, width), low),
            pltpu.VMEM((others, seq_len, width), low),
            pltpu.VMEM((others, seq_len, width), low),
            pltpu.VMEM((levels * own_len, width), low),
            pltpu.VMEM((turns + 1, *small.shape), full),
            pltpu.VMEM((turns, *small.shape), full),
            dma((2,)),
            dma((2,)),
            dma((cols, levels)),
            dma((cols, levels)),
            dma((cols, others)),
            dma((cols, others)),
            dma((cols,)),
            dma((cols,)),
            dma((2, along, across - 1)),
            dma((2, along, across - 1)),
            dma((3, along - 1)),
            dma((3, along - 1)),
            dma((turns,)),
            dma((turns,)),
            dma,
        ],
        compiler_params=pltpu.CompilerParams(
            collective_id=2, has_side_effects=True, vmem_limit_bytes=60 * 1024 * 1024
        ),
        cost_estimate=pl.CostEstimate(
            flops=4 * seq_len * features_all * 3 * width,
            bytes_accessed=40 * 1024 * 1024,
            transcendentals=0,
        ),
    )(query_key_value, weights, features, attn_full, layer_own, small, out, up)


def into_full(portion, start_at, full_len):
    return lax.dynamic_update_slice_in_dim(
        jnp.zeros((full_len,), jnp.float32), portion, start_at, 0
    )


def on_device(
    hidden_in,
    out_grad,
    lengths,
    global_blocks,
    rand_blocks,
    w_query,
    b_query,
    w_key,
    w_value,
    b_value,
    w_out,
    b_out,
    ln1_gain,
    ln1_bias,
    w_up,
    b_up,
    w_down,
    b_down,
    ln2_gain,
    ln2_bias,
):
    low = jnp.bfloat16
    seq_len = hidden_in.shape[0]
    feat_cols = hidden_in.shape[1]
    unit_cols = w_up.shape[1]
    cols = lax.axis_size("col")
    features_all = feat_cols * cols
    units_all = unit_cols * cols
    num_blocks = seq_len // BLK
    head_count = feat_cols // DH
    own_len = seq_len // cols
    column = lax.axis_index("col")
    feat_start = column * feat_cols
    unit_start = column * unit_cols
    own_start = column * own_len
    length = lengths[0]
    tables = (
        global_blocks.reshape(-1),
        rand_blocks.reshape(-1),
        limits_of(length, global_blocks[0], rand_blocks[0], num_blocks, head_count),
    )
    vectors = jnp.stack([b_out, ln1_gain, ln1_bias, b_down, ln2_gain, ln2_bias, b_out, b_out])
    valid = (jnp.arange(seq_len) < length)[:, None]
    own_valid = (own_start + jnp.arange(own_len) < length).astype(jnp.float32)[:, None]
    (
        features,
        own_features,
        upstream,
        queries,
        key_rows,
        value_rows,
        context,
        highest,
        scale,
        full_qkv,
        full_out,
        full_up,
        full_down,
        out_sib,
        up_sib,
        down_sib,
        context_sib,
        normed_full,
        unit1,
        inv1,
    ) = front(
        cols // 2,
        lax.axis_size("row"),
        tables,
        hidden_in,
        jnp.where(valid, out_grad, 0),
        (
            lax.dynamic_slice_in_dim(b_query, feat_start, feat_cols)[None, :],
            lax.dynamic_slice_in_dim(b_value, feat_start, feat_cols)[None, :],
        ),
        (
            jnp.concatenate([w_query, w_key, w_value], axis=1).astype(low),
            w_out.T.astype(low),
            w_up.astype(low),
            w_down.T.astype(low),
        ),
        vectors,
    )

    sibling = column + 1 - 2 * lax.rem(column, 2)
    layer_own, context_grad, attn_full, small, up_small, down_share, up_part, grad_out = middle(
        cols // 2,
        lax.axis_size("row"),
        context,
        context_sib,
        upstream,
        own_valid,
        (full_out, out_sib, full_up, up_sib, full_down, down_sib),
        normed_full,
        unit1,
        inv1,
        vectors,
        jnp.stack(
            [
                lax.dynamic_slice_in_dim(b_up, unit_start, unit_cols),
                lax.dynamic_slice_in_dim(b_up, sibling * unit_cols, unit_cols),
            ]
        ),
    )
    query_key_value, bias_sums = attend_back(
        queries, key_rows, value_rows, tables, (highest, scale), context_grad
    )
    up_sums = into_full(up_small[0], unit_start, units_all) + into_full(
        up_small[1], sibling * unit_cols, units_all
    )
    bias_full = lax.dynamic_update_slice(
        jnp.zeros((4, features_all), jnp.float32), bias_sums, (0, feat_start)
    )
    grad_input, layer_out, small, out_share, qkv_share, up_share = finish(
        cols // 2,
        lax.axis_size("row"),
        query_key_value,
        full_qkv,
        features,
        attn_full,
        layer_own,
        jnp.concatenate([small, up_sums.reshape(-1, features_all), bias_full], axis=0),
        grad_out,
        up_part,
    )
    return (
        layer_out,
        grad_input,
        qkv_share[:, :feat_cols],
        small[-4],
        qkv_share[:, feat_cols : 2 * feat_cols],
        qkv_share[:, 2 * feat_cols :],
        small[-3],
        out_share.T,
        small[5],
        small[3],
        small[4],
        up_share,
        small[8:-4].reshape(-1),
        down_share.T,
        small[2],
        small[0],
        small[1],
    )


def solution(mesh):
    placed = (
        P("row", "col"),
        P("row", "col"),
        P("row"),
        P("row", None),
        P("row", None, "col", None),
        P("row", "col"),
        P(),
        P("row", "col"),
        P("row", "col"),
        P(),
        P("col", "row"),
        P(),
        P(),
        P(),
        P("row", "col"),
        P(),
        P("col", "row"),
        P(),
        P(),
        P(),
    )
    return jax.shard_map(
        on_device,
        mesh=mesh,
        in_specs=placed,
        out_specs=(
            P("row", "col"),
            P("row", "col"),
            P("row", "col"),
            P(),
            P("row", "col"),
            P("row", "col"),
            P(),
            P("col", "row"),
            P(),
            P(),
            P(),
            P("row", "col"),
            P(),
            P("col", "row"),
            P(),
            P(),
            P(),
        ),
        check_vma=False,
    )
```

```python
import functools
import math

import jax
import jax.numpy as jnp
from jax import lax
from jax.experimental import pallas as pl
from jax.experimental.pallas import tpu as pltpu
from jax.sharding import PartitionSpec as P

DH = 64
BLK = 64
MESH = pl.DeviceIdType.MESH


epsilon = 1e-06


def lane_heads(rows, width):
    return lax.broadcasted_iota(jnp.int32, (rows, width), 1) // DH


def by_diagonal(rows, width):
    lane_head = lane_heads(BLK, width)
    zero = jnp.zeros_like(rows)
    return jnp.concatenate(
        [jnp.where(lane_head == head, rows, zero) for head in range(width // DH)], axis=0
    )


def from_diagonal(square, width):
    lane_head = lane_heads(BLK, width)
    result = jnp.zeros((BLK, width), jnp.float32)
    for head in range(width // DH):
        result = jnp.where(lane_head == head, square[head * BLK : (head + 1) * BLK, :], result)
    return result


def slot_starts(step, num_blocks, head_count, globals_ref, random_ref):
    shared = [
        jnp.maximum(step - 1, 0),
        step,
        jnp.minimum(step + 1, num_blocks - 1),
        globals_ref[0],
        globals_ref[1],
    ]
    base = step * (head_count * 3)
    apart = [
        [random_ref[base + head * 3 + slot] for head in range(head_count)] for slot in range(3)
    ]
    return shared, apart


def lane_groups(head_count):
    per_group = min(128 // DH, head_count)
    return [
        (first * DH, per_group * DH, list(range(first, first + per_group)))
        for first in range(0, head_count, per_group)
    ]


def picked_rows(rows_ref, shared, apart, head_count):
    pieces = [rows_ref[block] for block in shared]
    for blocks in apart:
        groups = []
        for lane, width, heads in lane_groups(head_count):
            lane_head = lane_heads(BLK, width)
            piece = rows_ref[blocks[heads[0]], :, lane : lane + width]
            for place, head in enumerate(heads[1:], 1):
                other = rows_ref[blocks[head], :, lane : lane + width]
                piece = jnp.where(lane_head >= place, other, piece)
            groups.append(piece)
        pieces.append(jnp.concatenate(groups, axis=1) if len(groups) > 1 else groups[0])
    return jnp.concatenate(pieces, axis=0)


def put_rows(sums_ref, values_in, shared, apart, head_count):
    for slot, block in enumerate(shared):
        sums_ref[block] += values_in[slot * BLK : (slot + 1) * BLK, :]
    for slot, blocks in enumerate(apart, len(shared)):
        rows = values_in[slot * BLK : (slot + 1) * BLK, :]
        for lane, width, heads in lane_groups(head_count):
            lane_head = lane_heads(BLK, width)
            for place, head in enumerate(heads):
                sums_ref[blocks[head], :, lane : lane + width] += jnp.where(
                    lane_head == place, rows[:, lane : lane + width], 0.0
                )


def masked_scores(picked_keys, grouped, step, num_blocks, length, shared, apart):
    width = grouped.shape[1]
    scores = lax.dot_general(
        picked_keys, grouped, (((1,), (1,)), ((), ())), preferred_element_type=jnp.float32
    )
    listed = [step >= 1, True, step + 1 < num_blocks]
    listed += [(block < step - 1) | (block > step + 1) for block in shared[3:]]
    limits = [
        jnp.where(there, length - block * BLK, 0) for there, block in zip(listed, shared)
    ]
    lane_head = lane_heads(1, width)
    for blocks in apart:
        limit = length - jnp.full((1, width), blocks[0], jnp.int32) * BLK
        for head, block in enumerate(blocks[1:], 1):
            limit = jnp.where(lane_head >= head, length - block * BLK, limit)
        limits.append(limit)
    row = lax.broadcasted_iota(jnp.int32, (BLK, width), 0)
    return [
        jnp.where(row < limit, scores[slot * BLK : (slot + 1) * BLK, :], -1e30)
        for slot, limit in enumerate(limits)
    ]


def attend_blocks(
    first, count, unroll, length_ref, globals_ref, random_ref, refs, context_ref, stat_refs
):
    queries_ref, keys_ref, values_ref = refs
    highest_ref, scale_ref = stat_refs
    seq_len, width = queries_ref.shape
    head_count = width // DH
    num_blocks = seq_len // BLK

    def one_block(step):
        shared, apart = slot_starts(step, num_blocks, head_count, globals_ref, random_ref)
        own = pl.ds(pl.multiple_of(step * BLK, BLK), BLK)
        grouped = by_diagonal(queries_ref[own, :] * jnp.bfloat16(1.0 / math.sqrt(DH)), width)
        scores = masked_scores(
            picked_rows(keys_ref, shared, apart, head_count),
            grouped,
            step,
            num_blocks,
            length_ref[0],
            shared,
            apart,
        )
        highest = jnp.max(functools.reduce(jnp.maximum, scores), axis=0, keepdims=True)
        exponent = [jnp.exp(piece - highest) for piece in scores]
        denominator = jnp.sum(sum(exponent[1:], exponent[0]), axis=0, keepdims=True)
        scale = 1.0 / denominator
        attn_probs = jnp.concatenate(
            [(piece * scale).astype(jnp.bfloat16) for piece in exponent], axis=0
        )
        square = lax.dot_general(
            attn_probs,
            picked_rows(values_ref, shared, apart, head_count),
            (((0,), (0,)), ((), ())),
            preferred_element_type=jnp.float32,
        )
        context_ref[own, :] = from_diagonal(square, width).astype(jnp.bfloat16)
        highest_ref[step] = highest
        scale_ref[step] = scale

    @pl.loop(0, count // unroll)
    def _(turn):
        for place in range(unroll):
            one_block(first + turn * unroll + place)


def attend_back_kernel(
    head_count,
    unroll,
    length_ref,
    globals_ref,
    random_ref,
    queries_ref,
    keys_ref,
    values_ref,
    grads_ref,
    highest_ref,
    scale_ref,
    grads_out_ref,
    bias_ref,
    key_sums,
    value_sums,
    query_total,
):
    width = head_count * DH
    num_blocks = queries_ref.shape[0] // BLK
    factor = 1.0 / math.sqrt(DH)
    key_sums[...] = jnp.zeros_like(key_sums)
    value_sums[...] = jnp.zeros_like(value_sums)
    query_total[...] = jnp.zeros_like(query_total)

    def one_block(step):
        shared, apart = slot_starts(step, num_blocks, head_count, globals_ref, random_ref)
        own = pl.ds(pl.multiple_of(step * BLK, BLK), BLK)
        grouped = by_diagonal(queries_ref[own, :] * jnp.bfloat16(factor), width)
        grouped_grad = by_diagonal(grads_ref[own, :], width)
        picked_keys = picked_rows(keys_ref, shared, apart, head_count)
        picked_values = picked_rows(values_ref, shared, apart, head_count)
        scores = masked_scores(
            picked_keys, grouped, step, num_blocks, length_ref[0], shared, apart
        )
        highest = highest_ref[step]
        scale = scale_ref[step]
        attn_probs = [jnp.exp(piece - highest) * scale for piece in scores]
        prob_grad = lax.dot_general(
            picked_values,
            grouped_grad,
            (((1,), (1,)), ((), ())),
            preferred_element_type=jnp.float32,
        )
        prob_grads = [prob_grad[slot * BLK : (slot + 1) * BLK, :] for slot in range(8)]
        products = [left * right for left, right in zip(attn_probs, prob_grads)]
        total = jnp.sum(sum(products[1:], products[0]), axis=0, keepdims=True)
        score_grad = jnp.concatenate(
            [
                (left * (right - total)).astype(jnp.bfloat16)
                for left, right in zip(attn_probs, prob_grads)
            ],
            axis=0,
        )
        probs_low = jnp.concatenate([piece.astype(jnp.bfloat16) for piece in attn_probs], axis=0)
        square = lax.dot_general(
            score_grad, picked_keys, (((0,), (0,)), ((), ())), preferred_element_type=jnp.float32
        )
        query_grad = (from_diagonal(square, width) * factor).astype(jnp.bfloat16)
        grads_out_ref[own, :width] = query_grad
        query_total[...] += jnp.sum(
            query_grad.astype(jnp.float32).reshape(BLK // 8, 8, width), axis=0
        )
        key_part = jnp.dot(score_grad, grouped, preferred_element_type=jnp.float32)
        value_part = jnp.dot(probs_low, grouped_grad, preferred_element_type=jnp.float32)
        put_rows(key_sums, key_part, shared, apart, head_count)
        put_rows(value_sums, value_part, shared, apart, head_count)

    @pl.loop(0, num_blocks // unroll)
    def _(turn):
        for place in range(unroll):
            one_block(turn * unroll + place)

    value_grad = value_sums[...].reshape(queries_ref.shape).astype(jnp.bfloat16)
    seq_len = queries_ref.shape[0]
    grads_out_ref[:, width : 2 * width] = key_sums[...].reshape(seq_len, width).astype(jnp.bfloat16)
    grads_out_ref[:, 2 * width :] = value_grad
    bias_ref[0:1, :] = jnp.sum(query_total[...], axis=0, keepdims=True)
    bias_ref[1:2, :] = jnp.sum(value_grad.astype(jnp.float32), axis=0, keepdims=True)


VMEM = pl.BlockSpec(memory_space=pltpu.VMEM)
SMEM = pl.BlockSpec(memory_space=pltpu.SMEM)


def attend_back(queries, key_rows, value_rows, tables, stats, context_grad):
    seq_len, width = queries.shape
    head_count = width // DH
    return pl.pallas_call(
        functools.partial(attend_back_kernel, head_count, 8),
        out_shape=(
            jax.ShapeDtypeStruct((seq_len, 3 * width), jnp.bfloat16),
            jax.ShapeDtypeStruct((2, width), jnp.float32),
        ),
        in_specs=[SMEM] * 3 + [VMEM] * 6,
        out_specs=[VMEM] * 2,
        scratch_shapes=[pltpu.VMEM((seq_len // BLK, BLK, width), jnp.float32)] * 2
        + [pltpu.VMEM((8, width), jnp.float32)],
        compiler_params=pltpu.CompilerParams(vmem_limit_bytes=40 * 1024 * 1024),
        cost_estimate=pl.CostEstimate(
            flops=10 * seq_len * 512 * width * head_count,
            bytes_accessed=14 * seq_len * width,
            transcendentals=seq_len * 512 * head_count,
        ),
    )(*tables, queries, key_rows, value_rows, context_grad, *stats)


KINDS = 4
CHUNKS = 4


def front_kernel(
    levels,
    across,
    along,
    length_ref,
    globals_ref,
    random_ref,
    hidden_ref,
    grads_ref,
    b_query_ref,
    b_value_ref,
    w_query_ref,
    w_key_ref,
    w_value_ref,
    w_out_ref,
    w_up_ref,
    w_down_ref,
    b_out,
    gain1,
    shift1,
    features_ref,
    own_ref,
    upstream_ref,
    queries_ref,
    keys_ref,
    values_ref,
    context_ref,
    highest_ref,
    scale_ref,
    full_qkv_ref,
    full_out_ref,
    full_up_ref,
    full_down_ref,
    out_sib,
    up_sib,
    down_sib,
    context_sib,
    normed_full,
    unit1,
    inv1,
    sum_out,
    sum_in,
    level_send,
    level_recv,
    core_send,
    core_recv,
    swap_send,
    swap_recv,
    along_send,
    along_recv,
    across_send,
    across_recv,
    shard_send,
    shard_recv,
    context_send,
    context_recv,
    sum_send,
    sum_recv,
    normed_send,
    normed_recv,
):
    low, full = jnp.bfloat16, jnp.float32
    row, column = lax.axis_index("row"), lax.axis_index("col")
    core, level = lax.rem(column, 2), lax.div(column, 2)
    fast, slow = lax.rem(row, across), lax.div(row, across)
    cols = 2 * levels
    seq_len, width = hidden_ref.shape
    own_len = seq_len // cols
    shard = w_query_ref.shape[0]
    other = 1 - core
    sibling = (row, level * 2 + other)
    offsets = range(1, levels)

    def peer_level(offset):
        return lax.rem(level + offset, levels)

    def fast_peer(offset):
        return slow * across + lax.rem(fast + offset, across)

    def line_peer(shift):
        return ((slow + shift) * across + fast, column)

    barrier = pltpu.get_barrier_semaphore()
    greeted = [sibling]
    for offset in offsets:
        greeted += [(row, peer_level(offset) * 2 + core), (row, peer_level(offset) * 2 + other)]
    greeted += [(fast_peer(offset), column) for offset in range(1, across)]
    greeted += [
        (lax.rem(slow + offset, along) * across + fast, column) for offset in range(1, along)
    ]
    for device in greeted:
        pl.semaphore_signal(barrier, inc=1, device_id=device, device_id_type=MESH)
    pl.semaphore_wait(barrier, len(greeted))

    def remote(source, target, send, recv, device):
        return pltpu.make_async_remote_copy(
            src_ref=source,
            dst_ref=target,
            send_sem=send,
            recv_sem=recv,
            device_id=device,
            device_id_type=MESH,
        )

    def block(start, size):
        return pl.ds(pl.multiple_of(start * size, size), size)

    def level_copy(turn, offset):
        rows = block(turn, own_len)
        return remote(
            hidden_ref.at[rows],
            features_ref.at[rows, block(column, width)],
            level_send.at[turn, offset - 1],
            level_recv.at[turn, levels - offset - 1],
            (row, peer_level(offset) * 2 + core),
        )

    def core_copy(turn, offset):
        view = features_ref.at[block(turn, own_len), block(peer_level(offset) * 2 + core, width)]
        return remote(
            view, view, core_send.at[turn, offset], core_recv.at[turn, offset], sibling
        )

    @pl.loop(0, cols)
    def _(turn):
        for offset in offsets:
            level_copy(turn, offset).start()
        rows = block(turn, own_len)
        features_ref[rows, block(column, width)] = hidden_ref[rows, :]
        core_copy(turn, 0).start()

    fulls = (full_qkv_ref, full_out_ref, full_up_ref, full_down_ref)
    sibs = (None, out_sib, up_sib, down_sib)

    def shard_rows(place):
        return block(place * across + fast, shard)

    def line_copy(kind, way, hop):
        view = fulls[kind].at[shard_rows(slow - (1 - 2 * way) * hop)]
        return remote(
            view,
            view,
            along_send.at[kind, way, hop],
            along_recv.at[kind, way, hop],
            line_peer(1 - 2 * way),
        )

    def line_can_send(way, hop):
        if way == 0:
            return (slow >= hop) & (slow < along - 1)
        return (slow < along - hop) & (slow > 0)

    def line_send(kind, hop):
        for way in range(2):

            @pl.when(line_can_send(way, hop))
            def _():
                line_copy(kind, way, hop).start()

    def line_got(way, hop):
        place = slow - (1 - 2 * way) * (hop + 1)
        return place, ((place >= 0) if way == 0 else (place < along))

    def line_wait(kind, way, hop):
        place, _ = line_got(way, hop)
        view = fulls[kind].at[shard_rows(place)]
        remote(
            view,
            view,
            along_send.at[kind, way, hop],
            along_recv.at[kind, way, hop],
            line_peer(-(1 - 2 * way)),
        ).wait_recv()

    def across_copy(kind, place, offset):
        view = fulls[kind].at[shard_rows(place)]
        return remote(
            view,
            view,
            across_send.at[kind, place, offset - 1],
            across_recv.at[kind, place, across - offset - 1],
            (fast_peer(offset), column),
        )

    def core_shard(kind, place, offset):
        rows = block(place * across + lax.rem(fast + offset, across), shard)
        return remote(
            fulls[kind].at[rows],
            sibs[kind].at[rows],
            shard_send.at[kind - 1, place, offset],
            shard_recv.at[kind - 1, place, offset],
            sibling,
        )

    for place, ref in enumerate((w_query_ref, w_key_ref, w_value_ref)):
        full_qkv_ref[shard_rows(slow), place * width : (place + 1) * width] = ref[...].astype(low)
    line_send(0, 0)
    full_out_ref[shard_rows(slow), :] = w_out_ref[...].T.astype(low)
    full_up_ref[shard_rows(slow), :] = w_up_ref[...].astype(low)
    full_down_ref[shard_rows(slow), :] = w_down_ref[...].T.astype(low)

    def swap_copy(target, place_out, place_in):
        return remote(
            grads_ref.at[block(target, own_len)],
            upstream_ref.at[:, block(column, width)],
            swap_send.at[place_out],
            swap_recv.at[place_in],
            (row, target),
        )

    swaps = [swap_copy(level * 2 + other, 0, 0)]
    for offset in offsets:
        back = levels - offset
        swaps.append(swap_copy(peer_level(offset) * 2 + core, 2 * offset - 1, 2 * back - 1))
        swaps.append(swap_copy(peer_level(offset) * 2 + other, 2 * offset, 2 * back))
    for copy in swaps:
        copy.start()
    upstream_ref[:, block(column, width)] = grads_ref[block(column, own_len), :]

    def pass_shard(kind, place):
        for step in range(1, across):
            across_copy(kind, place, step).start()
        if kind > 0:
            core_shard(kind, place, 0).start()

    hops = range(along - 1)
    waiting = [(1, hop) for hop in hops] + [(3, -1), (2, 0), (3, 0)]
    waiting += [(kind, hop) for hop in hops if hop > 0 for kind in (2, 3)]

    def pass_on(count=1):
        pass_these(waiting[:count])
        del waiting[:count]

    def pass_these(shards):
        for kind, hop in shards:
            if hop < 0:
                pass_shard(kind, slow)
                continue
            for way in range(2):
                place, there = line_got(way, hop)

                @pl.when(there)
                def _():
                    line_wait(kind, way, hop)
                    if hop < along - 2:

                        @pl.when(line_can_send(way, hop + 1))
                        def _():
                            line_copy(kind, way, hop + 1).start()

                    pass_shard(kind, place)
    def await_shards(kind):
        @pl.loop(0, along)
        def _(place):
            for offset in range(1, across):
                across_copy(kind, place, across - offset).wait_recv()
                if kind > 0:
                    core_shard(kind, place, offset).start()

    def await_sibling(kind):
        @pl.loop(0, along)
        def _(place):
            for offset in range(across):
                core_shard(kind, place, offset).wait_recv()

    pass_these([(0, hop) for hop in range(-1, along - 2)])
    for kind in range(1, KINDS):
        line_send(kind, 0)
    pass_these([(0, along - 2), (1, -1), (2, -1)])
    await_shards(0)

    def project(turn):
        rows = block(turn, own_len)
        for offset in offsets:
            level_copy(turn, levels - offset).wait_recv()
            core_copy(turn, offset).start()
        for offset in range(levels):
            core_copy(turn, offset).wait_recv()
        values_in = features_ref[rows, :]
        queries_ref[rows, :] = (
            dot(values_in, full_qkv_ref[:, :width]) + b_query_ref[:, block(column, width)]
        ).astype(low)
        blocks = pl.ds(turn * (own_len // BLK), own_len // BLK)
        by_block = (own_len // BLK, BLK, width)
        keys_ref[blocks] = (
            dot(values_in, full_qkv_ref[:, width : 2 * width]).astype(low).reshape(by_block)
        )
        values_ref[blocks] = (
            (dot(values_in, full_qkv_ref[:, 2 * width :]) + b_value_ref[:, block(column, width)])
            .astype(low)
            .reshape(by_block)
        )

    for turn in range(cols):
        project(turn)
        pass_on(1 if (3, -1) in waiting else 0)
    while (2, 0) in waiting:
        pass_on()
    own_ref[...] = features_ref[block(column, own_len), :]
    step = own_len // CHUNKS
    halves = 2
    count = own_len // BLK // halves

    def attend_half(quarter, half):
        attend_blocks(
            (quarter * halves + half) * count,
            count,
            min(count, 4),
            length_ref,
            globals_ref,
            random_ref,
            (queries_ref, keys_ref, values_ref),
            context_ref,
            (highest_ref, scale_ref),
        )

    def context_copy(place, half):
        rows = own_len // halves
        return remote(
            context_ref.at[block((place * 2 + other) * halves + half, rows)],
            context_sib.at[block(place * halves + half, rows)],
            context_send.at[place, half],
            context_recv.at[place, half],
            sibling,
        )

    def chunk_rows(place, chunk):
        return block(place * CHUNKS + chunk, step)

    def attn_part(place, chunk):
        return dot_nt(
            context_ref[chunk_rows(place * 2 + core, chunk), :], full_out_ref[...]
        ) + dot_nt(context_sib[chunk_rows(place, chunk), :], out_sib[...])

    def sum_copy(chunk, offset):
        rows = block(chunk, step)
        return remote(
            sum_out.at[offset - 1, rows],
            sum_in.at[levels - offset - 1, rows],
            sum_send.at[chunk, offset - 1],
            sum_recv.at[chunk, levels - offset - 1],
            (row, peer_level(offset) * 2 + core),
        )

    def normed_copy(chunk, offset):
        view = normed_full.at[chunk_rows(level, chunk)]
        return remote(
            view,
            view,
            normed_send.at[chunk, offset - 1],
            normed_recv.at[chunk, levels - offset - 1],
            (row, peer_level(offset) * 2 + core),
        )

    for offset in list(offsets) + [0]:
        place = peer_level(offset)
        for half in range(halves):
            attend_half(place * 2 + other, half)
            context_copy(place, half).start()
            pass_on(1 - half if offset else half)
        if offset == 1:
            await_shards(1)
        for half in range(halves):
            attend_half(place * 2 + core, half)
            if offset == 1 and half == 0:
                await_sibling(1)
            context_copy(place, half).wait_recv()
            per_half = CHUNKS // halves
            for chunk in range(half * per_half, (half + 1) * per_half):
                if offset:
                    sum_out[offset - 1, block(chunk, step), :] = attn_part(place, chunk).astype(
                        low
                    )
                    sum_copy(chunk, offset).start()
            pass_on(1 if offset else half)
    pass_on(len(waiting))
    for chunk in range(CHUNKS):
        rows = block(chunk, step)
        summed = own_ref[rows, :].astype(full) + attn_part(level, chunk) + b_out[...]
        for offset in offsets:
            sum_copy(chunk, offset).wait_recv()
        for place in range(levels - 1):
            summed += sum_in[place, rows, :].astype(full)
        normed, inv_std = norm_parts(summed)
        unit1[rows, :] = normed
        inv1[rows, :] = inv_std
        normed_full[chunk_rows(level, chunk), :] = (normed * gain1[...] + shift1[...]).astype(low)
        for offset in offsets:
            normed_copy(chunk, offset).start()
    await_shards(2)
    await_shards(3)
    for chunk in range(CHUNKS):
        for offset in offsets:
            normed_copy(chunk, offset).wait()
            sum_copy(chunk, offset).wait_send()
    for kind in range(2, KINDS):
        await_sibling(kind)
    for place in range(levels):
        for half in range(halves):
            context_copy(place, half).wait_send()
    for copy in swaps:
        copy.wait()
    for kind in range(KINDS):
        for hop in range(along - 1):
            for way in range(2):

                @pl.when(line_can_send(way, hop))
                def _():
                    line_copy(kind, way, hop).wait_send()

        @pl.loop(0, along)
        def _(place):
            for offset in range(1, across):
                across_copy(kind, place, offset).wait_send()
            if kind > 0:
                for offset in range(across):
                    core_shard(kind, place, offset).wait_send()

    @pl.loop(0, cols)
    def _(turn):
        for offset in offsets:
            level_copy(turn, offset).wait_send()
        for offset in range(levels):
            core_copy(turn, offset).wait_send()


def across_of(rows):
    return 2 if rows <= 8 else rows // 4


def front(levels, rows, tables, hidden_in, grads, biases, weights, vectors):
    low, full = jnp.bfloat16, jnp.float32
    shape = jax.ShapeDtypeStruct
    across = across_of(rows)
    along = rows // across
    seq_len, width = hidden_in.shape
    cols = 2 * levels
    own_len = seq_len // cols
    features_all = width * cols
    units = weights[4].shape[1]
    widths = (3 * width, width, units, units)
    others = levels - 1
    stat = shape((seq_len // BLK, 1, width), full)
    dma = pltpu.SemaphoreType.DMA
    return pl.pallas_call(
        functools.partial(front_kernel, levels, across, along),
        out_shape=(
            shape((seq_len, features_all), low),
            shape((own_len, features_all), low),
            shape((own_len, features_all), low),
            shape((seq_len, width), low),
            shape((seq_len // BLK, BLK, width), low),
            shape((seq_len // BLK, BLK, width), low),
            shape((seq_len, width), low),
            stat,
            stat,
            *(shape((features_all, each), low) for each in widths),
            *(shape((features_all, each), low) for each in widths[1:]),
            shape((levels * own_len, width), low),
            shape((levels * own_len, features_all), low),
            shape((own_len, features_all), full),
            shape((own_len, 1), full),
        ),
        in_specs=[SMEM] * 3 + [VMEM] * 13,
        out_specs=[VMEM] * 20,
        scratch_shapes=[
            pltpu.VMEM((others, own_len, features_all), low),
            pltpu.VMEM((others, own_len, features_all), low),
            dma((cols, others)),
            dma((cols, others)),
            dma((cols, levels)),
            dma((cols, levels)),
            dma((cols,)),
            dma((cols,)),
            dma((KINDS, 2, along - 1)),
            dma((KINDS, 2, along - 1)),
            dma((KINDS, along, across - 1)),
            dma((KINDS, along, across - 1)),
            dma((KINDS - 1, along, across)),
            dma((KINDS - 1, along, across)),
            dma((levels, 2)),
            dma((levels, 2)),
            *(dma((CHUNKS, others)) for _ in range(4)),
        ],
        compiler_params=pltpu.CompilerParams(
            collective_id=3, has_side_effects=True, vmem_limit_bytes=56 * 1024 * 1024
        ),
        cost_estimate=pl.CostEstimate(
            flops=2 * seq_len * features_all * 3 * width,
            bytes_accessed=20 * 1024 * 1024,
            transcendentals=seq_len * 512 * (width // DH),
        ),
    )(*tables, hidden_in, grads, *biases, *weights, *vectors)


def dot(left, right):
    return jnp.dot(left, right, preferred_element_type=jnp.float32)


def dot_nt(left, right):
    return lax.dot_general(
        left, right, (((1,), (1,)), ((), ())), preferred_element_type=jnp.float32
    )


def dot_tn(left, right):
    return lax.dot_general(
        left, right, (((0,), (0,)), ((), ())), preferred_element_type=jnp.float32
    )


def gelu_parts(values_in):
    factor = math.sqrt(2.0 / math.pi)
    square = values_in * values_in
    bent = jnp.tanh(factor * (values_in + 0.044715 * (values_in * square)))
    half = 0.5 * (1.0 + bent)
    slope = half + (0.5 * values_in) * (1.0 - bent * bent) * (
        factor + (3.0 * 0.044715 * factor) * square
    )
    return (values_in * half, slope)


def norm_parts(summed):
    average = jnp.mean(summed, axis=1, keepdims=True)
    squares = jnp.mean(summed * summed, axis=1, keepdims=True)
    inv_std = lax.rsqrt(squares - average * average + epsilon)
    return ((summed - average) * inv_std, inv_std)


def norm_back(upstream, normed, inv_std, gain_vec):
    scaled = upstream * gain_vec
    left = jnp.mean(scaled, axis=1, keepdims=True)
    right = jnp.mean(scaled * normed, axis=1, keepdims=True)
    return inv_std * (scaled - left - normed * right)


def middle_kernel(
    levels,
    across,
    along,
    length_ref,
    context_ref,
    context_sib,
    upstream_ref,
    out_ref,
    out_sib,
    up_ref,
    up_sib,
    down_full,
    down_sib,
    normed_full,
    unit1,
    inv1,
    gain1,
    shift1,
    b_down,
    gain2,
    shift2,
    b_up_ref,
    layer_out_ref,
    context_grad_ref,
    attn_full,
    small_ref,
    up_small_ref,
    share_down_ref,
    up_part_ref,
    up_own_ref,
    grad_out_ref,
    ffn_full,
    hidden,
    slope,
    pre_grad,
    ffn_keep,
    part_own,
    send_buf,
    recv_buf,
    context_send,
    stage,
    down_sums,
    up_sums,
    down_got,
    up_got,
    down_pass,
    down_in,
    send_sem,
    recv_sem,
    core_send,
    core_recv,
    along_send,
    along_recv,
    across_send,
    across_recv,
    stage_sem,
):
    low = jnp.bfloat16
    row, column = lax.axis_index("row"), lax.axis_index("col")
    core = lax.rem(column, 2)
    level = lax.div(column, 2)
    sibling = (row, column + 1 - 2 * core)
    fast, slow = lax.rem(row, across), lax.div(row, across)
    shard = share_down_ref.shape[0]
    own_len = upstream_ref.shape[0]
    units = up_ref.shape[1]
    step = own_len // CHUNKS

    def peer_level(offset):
        return lax.rem(level + offset, levels)

    def fast_peer(offset):
        return slow * across + lax.rem(fast + offset, across)

    barrier = pltpu.get_barrier_semaphore()
    greeted = [sibling]
    greeted += [(row, peer_level(offset) * 2 + core) for offset in range(1, levels)]
    greeted += [(fast_peer(offset), column) for offset in range(1, across)]
    greeted += [
        (lax.rem(slow + offset, along) * across + fast, column) for offset in range(1, along)
    ]
    for device in greeted:
        pl.semaphore_signal(barrier, inc=1, device_id=device, device_id_type=MESH)
    pl.semaphore_wait(barrier, len(greeted))

    def remote(source, target, send, recv, device):
        return pltpu.make_async_remote_copy(
            src_ref=source,
            dst_ref=target,
            send_sem=send,
            recv_sem=recv,
            device_id=device,
            device_id_type=MESH,
        )

    def block(start, size):
        return pl.ds(pl.multiple_of(start * size, size), size)

    def to_sibling(source, target, place):
        return remote(source, target, core_send.at[place], core_recv.at[place], sibling)

    def rows_of(place, chunk):
        return pl.ds(pl.multiple_of(place * own_len + chunk * step, step), step)

    def own_rows(chunk):
        return pl.ds(pl.multiple_of(chunk * step, step), step)

    def exchange(kind, chunk, offset, source, target):
        return pltpu.make_async_remote_copy(
            src_ref=source,
            dst_ref=target,
            send_sem=send_sem.at[kind - 2, chunk, offset - 1],
            recv_sem=recv_sem.at[kind - 2, chunk, levels - offset - 1],
            device_id=(row, peer_level(offset) * 2 + core),
            device_id_type=MESH,
        )

    def sum_copy(kind, chunk, offset):
        return exchange(
            kind,
            chunk,
            offset,
            send_buf.at[kind // 2 - 1, offset - 1, own_rows(chunk)],
            recv_buf.at[kind // 2 - 1, levels - offset - 1, own_rows(chunk)],
        )

    def spread_copy(kind, chunk, offset):
        whole = {3: ffn_full, 5: attn_full}[kind]
        rows = rows_of(level, chunk)
        return exchange(kind, chunk, offset, whole.at[rows], whole.at[rows])

    def received(kind, chunk):
        return sum(
            recv_buf[kind // 2 - 1, place, own_rows(chunk), :].astype(jnp.float32)
            for place in range(levels - 1)
        )

    offsets = range(1, levels)
    small_ref[...] = jnp.zeros_like(small_ref)
    up_small_ref[...] = jnp.zeros_like(up_small_ref)
    def context_rows(place, chunk):
        start = (place * 2 + core) * own_len + chunk * step
        return pl.ds(pl.multiple_of(start, step), step)

    sides = ((up_ref, down_full), (up_sib, down_sib))

    def feed_forward(place, chunk):
        rows = rows_of(place, chunk)
        normed = normed_full[rows, :]
        total = None
        for side, (up_side, down_side) in enumerate(sides):
            bias = b_up_ref[:, block(column + side * (1 - 2 * core), units)]
            active, bend = gelu_parts(dot(normed, up_side[...]) + bias)
            active = active.astype(low)
            hidden[side, rows, :] = active
            slope[side, rows, :] = bend.astype(low)
            part = dot_nt(active, down_side[...])
            total = part if total is None else total + part
        return total

    @pl.loop(0, CHUNKS)
    def _(chunk):
        for offset in offsets:
            send_buf[0, offset - 1, own_rows(chunk), :] = feed_forward(
                peer_level(offset), chunk
            ).astype(low)
            sum_copy(2, chunk, offset).start()

    @pl.loop(0, CHUNKS)
    def _(chunk):
        rows = own_rows(chunk)
        part_own[rows, :] = feed_forward(level, chunk)
        normed1 = unit1[rows, :] * gain1[...] + shift1[...]
        summed = normed1 + part_own[rows, :] + b_down[...]
        for offset in offsets:
            sum_copy(2, chunk, offset).wait_recv()
        normed, inv_std = norm_parts(summed + received(2, chunk))
        position = lax.broadcasted_iota(jnp.int32, (step, 1), 0) + (
            column * own_len + chunk * step
        )
        valid = position < length_ref[0]
        layer_out_ref[rows, :] = jnp.where(
            valid, normed * gain2[...] + shift2[...], 0.0
        ).astype(low)
        upstream = jnp.where(valid, upstream_ref[rows, :].astype(jnp.float32), 0.0)
        grad = norm_back(upstream, normed, inv_std, gain2[...])
        ffn_keep[rows, :] = grad
        grad_low = grad.astype(low)
        ffn_full[rows_of(level, chunk), :] = grad_low
        for offset in offsets:
            spread_copy(3, chunk, offset).start()
        small_ref[0:1, :] += jnp.sum(upstream * normed, axis=0, keepdims=True)
        small_ref[1:2, :] += jnp.sum(upstream, axis=0, keepdims=True)
        small_ref[2:3, :] += jnp.sum(grad_low.astype(jnp.float32), axis=0, keepdims=True)

    def feed_back(place, chunk):
        rows = rows_of(place, chunk)
        upstream = ffn_full[rows, :]
        total = None
        for side, (up_side, down_side) in enumerate(sides):
            grad = (
                dot(upstream, down_side[...]) * slope[side, rows, :].astype(jnp.float32)
            ).astype(low)
            pre_grad[side, rows, :] = grad
            up_small_ref[side : side + 1, :] += jnp.sum(
                grad.astype(jnp.float32), axis=0, keepdims=True
            )
            part = dot_nt(grad, up_side[...])
            total = part if total is None else total + part
        return total

    @pl.loop(0, CHUNKS)
    def _(chunk):
        part_own[own_rows(chunk), :] = feed_back(level, chunk)
        for offset in offsets:
            spread_copy(3, chunk, levels - offset).wait_recv()
            send_buf[1, offset - 1, own_rows(chunk), :] = feed_back(
                peer_level(offset), chunk
            ).astype(low)
            sum_copy(4, chunk, offset).start()

    tile = across * shard
    lefts, rights = (ffn_full, normed_full), (hidden, pre_grad)
    sums, got = (down_sums, up_sums), (down_got, up_got)

    def grad_tile(kind, side, turn):
        return dot_tn(lefts[kind][:, block(turn, tile)], rights[kind][side])

    def core_grad(kind):
        return to_sibling(
            slope.at[kind, : sums[kind].shape[0]], sums[kind], levels + kind
        )

    def across_grad(kind, turn, offset):
        return remote(
            sums[kind].at[block(turn * across + lax.rem(fast + offset, across), shard)],
            got[kind].at[across - offset - 1, block(turn, shard)],
            across_send.at[kind, turn, offset - 1],
            across_recv.at[kind, turn, across - offset - 1],
            (fast_peer(offset), column),
        )

    def own_shard(kind, turn):
        for offset in range(1, across):
            across_grad(kind, turn, offset).wait_recv()
        total = sums[kind][block(turn * across + fast, shard), :].astype(jnp.float32)
        for place in range(across - 1):
            total += got[kind][place, block(turn, shard), :].astype(jnp.float32)
        return total

    def line_peer(shift):
        return ((slow + shift) * across + fast, column)

    def line_copy(kind, way, target):
        return remote(
            line_out[kind].at[way, target],
            line_in[kind].at[way, target],
            along_send.at[kind, way, target],
            along_recv.at[kind, way, target],
            line_peer(1 - 2 * way),
        )

    def line_step(kind, hop):
        for way in range(2):
            position = hop if way == 0 else along - 1 - hop
            targets = range(along - 1, hop, -1) if way == 0 else range(0, along - 1 - hop)

            @pl.when(slow == position)
            def _():
                for target in targets:
                    total = own_shard(kind, target)
                    if hop > 0:
                        line_copy(kind, way, target).wait_recv()
                        total += line_in[kind][way, target].astype(jnp.float32)
                    line_out[kind][way, target] = total.astype(jnp.bfloat16)
                    line_copy(kind, way, target).start()

    def line_finish(kind):
        for way in range(2):

            @pl.when((slow > 0) if way == 0 else (slow < along - 1))
            def _():
                line_copy(kind, way, slow).wait_recv()
                shares[kind][...] += line_in[kind][way, slow].astype(jnp.float32)

    def line_sent(kind):
        for way in range(2):
            for target in range(along):

                @pl.when((slow < target) if way == 0 else (slow > target))
                def _():
                    line_copy(kind, way, target).wait_send()

    def sum_grad(kind):
        core_grad(kind).wait_recv()

        @pl.loop(0, along)
        def _(turn):
            rows = block(turn, tile)
            sums[kind][rows, :] = (
                grad_tile(kind, 0, turn) + sums[kind][rows, :].astype(jnp.float32)
            ).astype(low)
            for offset in range(1, across):
                across_grad(kind, turn, offset).start()

    line_out, line_in, shares = (down_pass,), (down_in,), (share_down_ref,)
    for kind in range(2):

        @pl.loop(0, along)
        def _(turn):
            slope[kind, block(turn, tile), :] = grad_tile(kind, 1, turn).astype(low)

        core_grad(kind).start()
        if kind:
            sum_grad(kind - 1)
    sum_grad(1)

    @pl.loop(0, CHUNKS)
    def _(chunk):
        rows = own_rows(chunk)
        upstream = ffn_keep[rows, :] + part_own[rows, :]
        for offset in offsets:
            sum_copy(4, chunk, offset).wait_recv()
        upstream = upstream + received(4, chunk)
        normed = unit1[rows, :]
        grad_low = norm_back(upstream, normed, inv1[rows, :], gain1[...]).astype(low)
        attn_full[rows_of(level, chunk), :] = grad_low
        for offset in offsets:
            spread_copy(5, chunk, offset).start()
        small_ref[3:4, :] += jnp.sum(upstream * normed, axis=0, keepdims=True)
        small_ref[4:5, :] += jnp.sum(upstream, axis=0, keepdims=True)
        small_ref[5:6, :] += jnp.sum(grad_low.astype(jnp.float32), axis=0, keepdims=True)

    share_down_ref[...] = own_shard(0, slow)
    line_step(0, 0)

    def context_back(place, chunk):
        rows = rows_of(place, chunk)
        upstream = attn_full[rows, :]
        context_grad_ref[context_rows(place, chunk), :] = dot(upstream, out_ref[...]).astype(low)
        context_send[rows, :] = dot(upstream, out_sib[...]).astype(low)

    for chunk in range(CHUNKS):
        context_back(level, chunk)
        for offset in offsets:
            spread_copy(5, chunk, levels - offset).wait_recv()
            context_back(peer_level(offset), chunk)
        if 0 < chunk < along - 1:
            line_step(0, chunk)
    for hop in range(CHUNKS, along - 1):
        line_step(0, hop)

    back_copies = [
        to_sibling(
            context_send.at[pl.ds(place * own_len, own_len)],
            context_grad_ref.at[
                pl.ds(pl.multiple_of((place * 2 + core) * own_len, own_len), own_len)
            ],
            place,
        )
        for place in range(levels)
    ]
    for copy in back_copies:
        copy.start()

    own_context = jnp.concatenate(
        [
            context_ref[
                pl.ds(pl.multiple_of((place * 2 + core) * own_len, own_len), own_len), :
            ]
            for place in range(levels)
        ],
        axis=0,
    )

    def out_put(side):
        return pltpu.make_async_copy(stage.at[side], grad_out_ref.at[side], stage_sem.at[side])

    for side, right in enumerate((own_context, context_sib[...])):
        stage[side] = dot_tn(attn_full[...], right).astype(low)
        out_put(side).start()
    for shift in range(1, along):
        up_part_ref[shift - 1] = own_shard(1, lax.rem(slow + shift, along)).astype(low)
    up_own_ref[...] = own_shard(1, slow)
    line_finish(0)
    for side in range(2):
        out_put(side).wait()
    for kind in range(2):
        core_grad(kind).wait_send()
    line_sent(0)

    @pl.loop(0, along)
    def _(place):
        for offset in range(1, across):
            across_grad(0, place, offset).wait_send()
            across_grad(1, place, offset).wait_send()

    for copy in back_copies:
        copy.wait()
    for kind in range(2, 6):

        @pl.loop(0, CHUNKS)
        def _(chunk):
            for offset in offsets:
                if kind % 2:
                    spread_copy(kind, chunk, offset).wait_send()
                else:
                    sum_copy(kind, chunk, offset).wait_send()


def middle(
    levels,
    rows,
    length,
    context,
    context_sib,
    upstream,
    weights,
    normed_full,
    unit1,
    inv1,
    vectors,
    b_up,
):
    low, full = jnp.bfloat16, jnp.float32
    across = across_of(rows)
    along = rows // across
    own_len, features = upstream.shape
    seq_len, width = context.shape
    units = weights[2].shape[1]
    shard = features // rows
    tokens = levels * own_len
    others = levels - 1
    shape = jax.ShapeDtypeStruct
    hbm = pl.BlockSpec(memory_space=pl.ANY)
    dma = pltpu.SemaphoreType.DMA
    vmem = pltpu.VMEM
    return pl.pallas_call(
        functools.partial(middle_kernel, levels, across, along),
        out_shape=(
            shape((own_len, features), low),
            shape((seq_len, width), low),
            shape((tokens, features), low),
            shape((8, features), full),
            shape((2, units), full),
            shape((shard, units), full),
            shape((along - 1, shard, units), low),
            shape((shard, units), full),
            shape((2, features, width), low),
        ),
        in_specs=[SMEM] + [VMEM] * 18,
        out_specs=[VMEM] * 8 + [hbm],
        scratch_shapes=[
            vmem((tokens, features), low),
            vmem((2, tokens, units), low),
            vmem((2, max(tokens, features), units), low),
            vmem((2, tokens, units), low),
            vmem((own_len, features), full),
            vmem((own_len, features), full),
            vmem((2, others, own_len, features), low),
            vmem((2, others, own_len, features), low),
            vmem((tokens, width), low),
            vmem((2, features, width), low),
            vmem((features, units), low),
            vmem((features, units), low),
            vmem((across - 1, along * shard, units), low),
            vmem((across - 1, along * shard, units), low),
            vmem((2, along, shard, units), low),
            vmem((2, along, shard, units), low),
            dma((4, CHUNKS, others)),
            dma((4, CHUNKS, others)),
            dma((levels + 2,)),
            dma((levels + 2,)),
            dma((1, 2, along)),
            dma((1, 2, along)),
            dma((2, along, across - 1)),
            dma((2, along, across - 1)),
            dma((2,)),
        ],
        compiler_params=pltpu.CompilerParams(
            collective_id=1, has_side_effects=True, vmem_limit_bytes=62 * 1024 * 1024
        ),
        cost_estimate=pl.CostEstimate(
            flops=2 * tokens * features * (12 * units + 6 * width),
            bytes_accessed=20 * 1024 * 1024,
            transcendentals=2 * tokens * units,
        ),
    )(
        length,
        context,
        context_sib,
        upstream,
        *weights,
        normed_full,
        unit1,
        inv1,
        *vectors,
        b_up,
    )


def end_kernel(
    levels,
    across,
    along,
    query_key_value_ref,
    weights_ref,
    features_ref,
    attn_ref,
    layer_ref,
    small_ref,
    up_small_ref,
    bias_ref,
    out_ref,
    grad_input_ref,
    layer_out_ref,
    small_out_ref,
    share_ref,
    out_sib,
    sums,
    got,
    line_out,
    line_in,
    core_out,
    core_in,
    level_out,
    level_in,
    attn_in,
    small_sums,
    small_in,
    core_send,
    core_recv,
    part_send,
    part_recv,
    level_send,
    level_recv,
    layer_send,
    layer_recv,
    across_send,
    across_recv,
    along_send,
    along_recv,
    small_send,
    small_recv,
    keep_sem,
):
    low, full = jnp.bfloat16, jnp.float32
    row, column = lax.axis_index("row"), lax.axis_index("col")
    core, level = lax.rem(column, 2), lax.div(column, 2)
    fast, slow = lax.rem(row, across), lax.div(row, across)
    cols = 2 * levels
    seq_len = features_ref.shape[0]
    own_len = seq_len // cols
    width = grad_input_ref.shape[1]
    shard = share_ref.shape[0]
    other = 1 - core
    sibling = (row, level * 2 + other)
    offsets = range(1, levels)

    def peer_level(offset):
        return lax.rem(level + offset, levels)

    def fast_peer(offset):
        return slow * across + lax.rem(fast + offset, across)

    def slow_peer(offset):
        return lax.rem(slow + offset, along) * across + fast

    barrier = pltpu.get_barrier_semaphore()
    greeted = [sibling]
    for offset in offsets:
        greeted += [(row, peer_level(offset) * 2 + core), (row, peer_level(offset) * 2 + other)]
    greeted += [(fast_peer(offset), column) for offset in range(1, across)]
    greeted += [(slow_peer(offset), column) for offset in range(1, along)]
    for device in greeted:
        pl.semaphore_signal(barrier, inc=1, device_id=device, device_id_type=MESH)
    pl.semaphore_wait(barrier, len(greeted))

    def remote(source, target, send, recv, device):
        return pltpu.make_async_remote_copy(
            src_ref=source,
            dst_ref=target,
            send_sem=send,
            recv_sem=recv,
            device_id=device,
            device_id_type=MESH,
        )

    def block(start, size):
        return pl.ds(pl.multiple_of(start * size, size), size)

    out_copy = remote(out_ref.at[1], out_sib, core_send.at[0], core_recv.at[0], sibling)
    attn_copy = remote(
        attn_ref.at[:, block(level * 2 + other, width)],
        attn_in,
        core_send.at[1],
        core_recv.at[1],
        sibling,
    )

    partners = [sibling]
    bit = 1
    while bit < levels:
        partners.append((row, (level + bit - 2 * bit * lax.rem(lax.div(level, bit), 2)) * 2 + core))
        bit *= 2
    bit = 1
    while bit < across * along:
        partners.append((row + bit - 2 * bit * lax.rem(lax.div(row, bit), 2), column))
        bit *= 2

    def small_copy(turn):
        return remote(
            small_sums.at[turn],
            small_in.at[turn],
            small_send.at[turn],
            small_recv.at[turn],
            partners[turn],
        )

    small_turn = [0]

    def small_step():
        turn = small_turn[0]
        if turn > len(partners):
            return
        if turn > 0:
            small_copy(turn - 1).wait()
            small_sums[turn] = small_sums[turn - 1] + small_in[turn - 1]
        if turn < len(partners):
            small_copy(turn).start()
        small_turn[0] += 1

    def layer_copy(target, place_out, place_in):
        return remote(
            layer_ref.at[:, block(target, width)],
            layer_out_ref.at[block(column, own_len)],
            layer_send.at[place_out],
            layer_recv.at[place_in],
            (row, target),
        )

    layer_copies = [layer_copy(level * 2 + other, 0, 0)]
    for offset in offsets:
        back = levels - offset
        layer_copies.append(
            layer_copy(peer_level(offset) * 2 + core, 2 * offset - 1, 2 * back - 1)
        )
        layer_copies.append(layer_copy(peer_level(offset) * 2 + other, 2 * offset, 2 * back))
    layer_keep = pltpu.make_async_copy(
        layer_ref.at[:, block(column, width)], layer_out_ref.at[block(column, own_len)], keep_sem
    )

    features_all = weights_ref.shape[0]
    units = up_small_ref.shape[1]
    first_up = small_ref.shape[0]
    small_sums[0] = jnp.zeros_like(small_in[0])
    small_sums[0, :first_up, :] = small_ref[...]
    for side in range(2):
        start = (column + side * (1 - 2 * core)) * units
        small_sums[
            0,
            pl.ds(first_up + lax.div(start, features_all), 1),
            pl.ds(pl.multiple_of(lax.rem(start, features_all), units), units),
        ] = up_small_ref[side : side + 1, :]
    first_bias = small_in.shape[1] - 4
    small_sums[0, first_bias : first_bias + 2, block(column, width)] = bias_ref[...]
    small_step()
    out_copy.start()
    attn_copy.start()
    layer_keep.start()
    for copy in layer_copies:
        copy.start()

    def input_part(turn, target):
        return dot_nt(
            query_key_value_ref[block(turn, own_len), :], weights_ref[block(target, width), :]
        )

    def part_copy(turn, place):
        rows = block(turn, own_len)
        return remote(
            core_out.at[place, rows],
            core_in.at[place, rows],
            part_send.at[turn, place],
            part_recv.at[turn, place],
            sibling,
        )

    def give_core():
        @pl.loop(0, cols)
        def _(turn):
            for place in range(levels):
                core_out[place, block(turn, own_len), :] = input_part(
                    turn, place * 2 + other
                ).astype(low)
                part_copy(turn, place).start()

    def across_copy(turn, offset):
        return remote(
            sums.at[block(turn * across + lax.rem(fast + offset, across), shard)],
            got.at[across - offset - 1, block(turn, shard)],
            across_send.at[turn, offset - 1],
            across_recv.at[turn, across - offset - 1],
            (fast_peer(offset), column),
        )

    def weight_grad(turn):
        rows = block(turn, across * shard)
        sums[rows, : 3 * width] = dot_tn(features_ref[:, rows], query_key_value_ref[...]).astype(
            low
        )
        sums[rows, 3 * width :] = (
            out_ref[0, rows, :].astype(full) + out_sib[rows, :].astype(full)
        ).astype(low)
        for offset in range(1, across):
            across_copy(turn, offset).start()

    def level_copy(turn, offset):
        rows = block(turn, own_len)
        return remote(
            level_out.at[offset - 1, rows],
            level_in.at[levels - offset - 1, rows],
            level_send.at[turn, offset - 1],
            level_recv.at[turn, levels - offset - 1],
            (row, peer_level(offset) * 2 + core),
        )

    def give_levels():
        @pl.loop(0, cols)
        def _(turn):
            rows = block(turn, own_len)
            for offset in offsets:
                place = peer_level(offset)
                part = input_part(turn, place * 2 + core)
                part_copy(turn, place).wait_recv()
                level_out[offset - 1, rows, :] = (
                    part + core_in[place, rows, :].astype(full)
                ).astype(low)
                level_copy(turn, offset).start()

    def own_shard(turn):
        for offset in range(1, across):
            across_copy(turn, offset).wait_recv()
        total = sums[block(turn * across + fast, shard), :].astype(full)
        for place in range(across - 1):
            total += got[place, block(turn, shard), :].astype(full)
        return total

    def line_copy(way, target):
        return remote(
            line_out.at[way, target],
            line_in.at[way, target],
            along_send.at[way, target],
            along_recv.at[way, target],
            ((slow + 1 - 2 * way) * across + fast, column),
        )

    def line_step(hop, near):
        if hop >= along - 1 - near:
            return
        for way in range(2):
            target = along - 1 - near if way == 0 else near
            position = hop if way == 0 else along - 1 - hop

            @pl.when(slow == position)
            def _():
                total = own_shard(target)
                if hop > 0:
                    line_copy(way, target).wait_recv()
                    total += line_in[way, target].astype(full)
                line_out[way, target] = total.astype(low)
                line_copy(way, target).start()

    def finish_input(turn, attn_part):
        rows = block(turn, own_len)
        total = input_part(turn, column) + attn_part.astype(full)
        part_copy(turn, level).wait_recv()
        total += core_in[level, rows, :].astype(full)
        for offset in offsets:
            level_copy(turn, offset).wait_recv()
        for place in range(levels - 1):
            total += level_in[place, rows, :].astype(full)
        grad_input_ref[rows, :] = total.astype(low)

    ends = [turn for place in range(along // 2) for turn in (along - 1 - place, place)]
    out_copy.wait()
    for turn in ends:
        weight_grad(turn)
    small_step()
    give_core()
    small_step()
    give_levels()
    line_steps = sorted(
        ((hop, near) for near in range(along - 1) for hop in range(along - 1 - near)),
        key=lambda step: step[0] + 2 * step[1],
    )
    for step in line_steps[: len(line_steps) // 3]:
        line_step(*step)
        small_step()
    attn_copy.wait()
    for place in range(levels):
        for step in line_steps[len(line_steps) // 3 :][place::levels]:
            line_step(*step)
        rows = block(place, own_len)
        finish_input(place * 2 + core, attn_ref[rows, block(column, width)])
        finish_input(place * 2 + other, attn_in[rows, :])
        small_step()
    share_ref[...] = own_shard(slow)
    while small_turn[0] <= len(partners):
        small_step()
    small_out_ref[...] = small_sums[len(partners)]

    for way in range(2):

        @pl.when((slow > 0) if way == 0 else (slow < along - 1))
        def _():
            line_copy(way, slow).wait_recv()
            share_ref[...] += line_in[way, slow].astype(full)

    layer_keep.wait()
    for copy in layer_copies:
        copy.wait()
    for way in range(2):
        for target in range(along):

            @pl.when((slow < target) if way == 0 else (slow > target))
            def _():
                line_copy(way, target).wait_send()

    @pl.loop(0, along)
    def _(turn):
        for offset in range(1, across):
            across_copy(turn, offset).wait_send()

    @pl.loop(0, cols)
    def _(turn):
        for place in range(levels):
            part_copy(turn, place).wait_send()
        for offset in offsets:
            level_copy(turn, offset).wait_send()


def finish(
    levels, rows, query_key_value, weights, features, attn_full, layer_own, small, up_small, bias, out
):
    low, full = jnp.bfloat16, jnp.float32
    shape = jax.ShapeDtypeStruct
    across = across_of(rows)
    along = rows // across
    seq_len, features_all = features.shape
    width = query_key_value.shape[1] // 3
    own_len = layer_own.shape[0]
    shard = features_all // rows
    others = levels - 1
    cols = 2 * levels
    turns = 1 + (levels - 1).bit_length() + (rows - 1).bit_length()
    small_rows = small.shape[0] + up_small.shape[1] * cols // features_all + 4
    dma = pltpu.SemaphoreType.DMA
    vmem = pltpu.VMEM
    return pl.pallas_call(
        functools.partial(end_kernel, levels, across, along),
        out_shape=(
            shape((seq_len, width), low),
            shape((seq_len, width), low),
            shape((small_rows, features_all), full),
            shape((shard, 4 * width), full),
        ),
        in_specs=[VMEM] * 9,
        out_specs=[VMEM] * 4,
        scratch_shapes=[
            vmem((features_all, width), low),
            vmem((features_all, 4 * width), low),
            vmem((across - 1, along * shard, 4 * width), low),
            vmem((2, along, shard, 4 * width), low),
            vmem((2, along, shard, 4 * width), low),
            vmem((levels, seq_len, width), low),
            vmem((levels, seq_len, width), low),
            vmem((others, seq_len, width), low),
            vmem((others, seq_len, width), low),
            vmem((levels * own_len, width), low),
            vmem((turns + 1, small_rows, features_all), full),
            vmem((turns, small_rows, features_all), full),
            dma((2,)),
            dma((2,)),
            dma((cols, levels)),
            dma((cols, levels)),
            dma((cols, others)),
            dma((cols, others)),
            dma((cols,)),
            dma((cols,)),
            dma((along, across - 1)),
            dma((along, across - 1)),
            dma((2, along)),
            dma((2, along)),
            dma((turns,)),
            dma((turns,)),
            dma,
        ],
        compiler_params=pltpu.CompilerParams(
            collective_id=2, has_side_effects=True, vmem_limit_bytes=56 * 1024 * 1024
        ),
        cost_estimate=pl.CostEstimate(
            flops=4 * seq_len * features_all * 3 * width,
            bytes_accessed=20 * 1024 * 1024,
            transcendentals=0,
        ),
    )(query_key_value, weights, features, attn_full, layer_own, small, up_small, bias, out)


def last_kernel(
    grad_input_ref,
    layer_ref,
    small_ref,
    share_ref,
    down_ref,
    up_own_ref,
    up_first_ref,
    *refs,
):
    more, outs = refs[: len(refs) - 18], refs[len(refs) - 18 :]
    (
        layer_out,
        grad_input,
        grad_query,
        bias_query,
        grad_key,
        grad_value,
        bias_value,
        grad_out,
        bias_out,
        gain1,
        shift1,
        grad_up,
        bias_up,
        grad_down,
        bias_down,
        gain2,
        shift2,
        sems,
    ) = outs
    copies = [
        pltpu.make_async_copy(grad_input_ref, grad_input, sems.at[0]),
        pltpu.make_async_copy(layer_ref, layer_out, sems.at[1]),
    ]
    for copy in copies:
        copy.start()
    width = grad_query.shape[1]
    for place, ref in enumerate((grad_query, grad_key, grad_value)):
        ref[...] = share_ref[:, place * width : (place + 1) * width]
    grad_out[...] = share_ref[:, 3 * width :].T
    grad_down[...] = down_ref[...].T
    total = up_own_ref[...]
    for ref in (up_first_ref, *more):
        total += ref[...].astype(jnp.float32)
    grad_up[...] = total
    features_all = small_ref.shape[1]
    last = small_ref.shape[0] - 4
    for place, ref in (
        (0, gain2),
        (1, shift2),
        (2, bias_down),
        (3, gain1),
        (4, shift1),
        (5, bias_out),
        (last, bias_query),
        (last + 1, bias_value),
    ):
        ref[...] = small_ref[place : place + 1, :]
    for place in range(8, last):
        bias_up[:, (place - 8) * features_all : (place - 7) * features_all] = small_ref[
            place : place + 1, :
        ]
    for copy in copies:
        copy.wait()


def put_out(grad_input, layer_out, small, share, down, up_own, up_others):
    low, full = jnp.bfloat16, jnp.float32
    shape = jax.ShapeDtypeStruct
    hbm = pl.BlockSpec(memory_space=pl.ANY)
    seq_len, width = grad_input.shape
    shard, units = up_own.shape
    features_all = small.shape[1]
    vector = shape((1, features_all), full)
    units_all = (small.shape[0] - 12) * features_all
    grad = shape((shard, width), full)
    return pl.pallas_call(
        last_kernel,
        out_shape=(
            shape((seq_len, width), low),
            shape((seq_len, width), low),
            grad,
            vector,
            grad,
            grad,
            vector,
            shape((width, shard), full),
            vector,
            vector,
            vector,
            shape((shard, units), full),
            shape((1, units_all), full),
            shape((units, shard), full),
            vector,
            vector,
            vector,
        ),
        in_specs=[hbm] * 2 + [VMEM] * (4 + len(up_others)),
        out_specs=[hbm] * 2 + [VMEM] * 15,
        scratch_shapes=[pltpu.SemaphoreType.DMA((2,))],
    )(grad_input, layer_out, small, share, down, up_own, *up_others)


def on_device(
    hidden_in,
    out_grad,
    lengths,
    global_blocks,
    rand_blocks,
    w_query,
    b_query,
    w_key,
    w_value,
    b_value,
    w_out,
    b_out,
    ln1_gain,
    ln1_bias,
    w_up,
    b_up,
    w_down,
    b_down,
    ln2_gain,
    ln2_bias,
):
    cols = lax.axis_size("col")
    rows = lax.axis_size("row")
    tables = (lengths, global_blocks.reshape(-1), rand_blocks.reshape(-1))
    as_row = lambda vector: vector[None, :]
    (
        features,
        own_features,
        upstream,
        queries,
        key_rows,
        value_rows,
        context,
        highest,
        scale,
        full_qkv,
        full_out,
        full_up,
        full_down,
        out_sib,
        up_sib,
        down_sib,
        context_sib,
        normed_full,
        unit1,
        inv1,
    ) = front(
        cols // 2,
        rows,
        tables,
        hidden_in,
        out_grad,
        (as_row(b_query), as_row(b_value)),
        (w_query, w_key, w_value, w_out, w_up, w_down),
        (as_row(b_out), as_row(ln1_gain), as_row(ln1_bias)),
    )
    (
        layer_own,
        context_grad,
        attn_full,
        small,
        up_small,
        down_share,
        up_part,
        up_own,
        grad_out,
    ) = middle(
        cols // 2,
        rows,
        lengths,
        context,
        context_sib,
        upstream,
        (full_out, out_sib, full_up, up_sib, full_down, down_sib),
        normed_full,
        unit1,
        inv1,
        tuple(as_row(each) for each in (ln1_gain, ln1_bias, b_down, ln2_gain, ln2_bias)),
        as_row(b_up),
    )
    across = across_of(rows)
    up_others = [
        lax.ppermute(
            up_part[shift - 1],
            "row",
            [(place, (place + shift * across) % rows) for place in range(rows)],
        )
        for shift in range(1, rows // across)
    ]
    query_key_value, bias_sums = attend_back(
        queries, key_rows, value_rows, tables, (highest, scale), context_grad
    )
    grad_input, layer_out, small, share = finish(
        cols // 2,
        rows,
        query_key_value,
        full_qkv,
        features,
        attn_full,
        layer_own,
        small,
        up_small,
        bias_sums,
        grad_out,
    )
    outs = put_out(grad_input, layer_out, small, share, down_share, up_own, up_others)
    return tuple(each.reshape(-1) if each.shape[0] == 1 else each for each in outs)


def solution(mesh):
    placed = (
        P("row", "col"),
        P("row", "col"),
        P("row"),
        P("row", None),
        P("row", None, "col", None),
        P("row", "col"),
        P(),
        P("row", "col"),
        P("row", "col"),
        P(),
        P("col", "row"),
        P(),
        P(),
        P(),
        P("row", "col"),
        P(),
        P("col", "row"),
        P(),
        P(),
        P(),
    )
    return jax.shard_map(
        on_device,
        mesh=mesh,
        in_specs=placed,
        out_specs=(
            P("row", "col"),
            P("row", "col"),
            P("row", "col"),
            P(),
            P("row", "col"),
            P("row", "col"),
            P(),
            P("col", "row"),
            P(),
            P(),
            P(),
            P("row", "col"),
            P(),
            P("col", "row"),
            P(),
            P(),
            P(),
        ),
        check_vma=False,
    )
```

```python
import functools
import math

import jax
import jax.numpy as jnp
from jax import lax
from jax.experimental import pallas as pl
from jax.experimental.pallas import tpu as pltpu
from jax.sharding import PartitionSpec as P

DH = 64
BLK = 64
MESH = pl.DeviceIdType.MESH


epsilon = 1e-06


def lane_heads(rows, width):
    return lax.broadcasted_iota(jnp.int32, (rows, width), 1) // DH


def by_diagonal(rows, width):
    lane_head = lane_heads(BLK, width)
    zero = jnp.zeros_like(rows)
    return jnp.concatenate(
        [jnp.where(lane_head == head, rows, zero) for head in range(width // DH)], axis=0
    )


def from_diagonal(square, width):
    lane_head = lane_heads(BLK, width)
    result = jnp.zeros((BLK, width), jnp.float32)
    for head in range(width // DH):
        result = jnp.where(lane_head == head, square[head * BLK : (head + 1) * BLK, :], result)
    return result


def slot_starts(step, num_blocks, head_count, globals_ref, random_ref):
    shared = [
        jnp.maximum(step - 1, 0),
        step,
        jnp.minimum(step + 1, num_blocks - 1),
        globals_ref[0],
        globals_ref[1],
    ]
    base = step * (head_count * 3)
    apart = [
        [random_ref[base + head * 3 + slot] for head in range(head_count)] for slot in range(3)
    ]
    return shared, apart


def lane_groups(head_count):
    per_group = min(128 // DH, head_count)
    return [
        (first * DH, per_group * DH, list(range(first, first + per_group)))
        for first in range(0, head_count, per_group)
    ]


def picked_rows(rows_ref, shared, apart, head_count):
    pieces = [rows_ref[block] for block in shared]
    for blocks in apart:
        groups = []
        for lane, width, heads in lane_groups(head_count):
            lane_head = lane_heads(BLK, width)
            piece = rows_ref[blocks[heads[0]], :, lane : lane + width]
            for place, head in enumerate(heads[1:], 1):
                other = rows_ref[blocks[head], :, lane : lane + width]
                piece = jnp.where(lane_head >= place, other, piece)
            groups.append(piece)
        pieces.append(jnp.concatenate(groups, axis=1) if len(groups) > 1 else groups[0])
    return jnp.concatenate(pieces, axis=0)


def put_rows(sums_ref, values_in, shared, apart, head_count):
    for slot, block in enumerate(shared):
        sums_ref[block] += values_in[slot * BLK : (slot + 1) * BLK, :]
    for slot, blocks in enumerate(apart, len(shared)):
        rows = values_in[slot * BLK : (slot + 1) * BLK, :]
        for lane, width, heads in lane_groups(head_count):
            lane_head = lane_heads(BLK, width)
            for place, head in enumerate(heads):
                sums_ref[blocks[head], :, lane : lane + width] += jnp.where(
                    lane_head == place, rows[:, lane : lane + width], 0.0
                )


def masked_scores(picked_keys, grouped, step, num_blocks, length, shared, apart):
    width = grouped.shape[1]
    scores = lax.dot_general(
        picked_keys, grouped, (((1,), (1,)), ((), ())), preferred_element_type=jnp.float32
    )
    listed = [step >= 1, True, step + 1 < num_blocks]
    listed += [(block < step - 1) | (block > step + 1) for block in shared[3:]]
    limits = [
        jnp.where(there, length - block * BLK, 0) for there, block in zip(listed, shared)
    ]
    lane_head = lane_heads(1, width)
    for blocks in apart:
        limit = length - jnp.full((1, width), blocks[0], jnp.int32) * BLK
        for head, block in enumerate(blocks[1:], 1):
            limit = jnp.where(lane_head >= head, length - block * BLK, limit)
        limits.append(limit)
    row = lax.broadcasted_iota(jnp.int32, (BLK, width), 0)
    return [
        jnp.where(row < limit, scores[slot * BLK : (slot + 1) * BLK, :], -1e30)
        for slot, limit in enumerate(limits)
    ]


def attend_blocks(
    first, count, unroll, length_ref, globals_ref, random_ref, refs, context_ref, stat_refs
):
    queries_ref, keys_ref, values_ref = refs
    highest_ref, scale_ref = stat_refs
    seq_len, width = queries_ref.shape
    head_count = width // DH
    num_blocks = seq_len // BLK

    def one_block(step):
        shared, apart = slot_starts(step, num_blocks, head_count, globals_ref, random_ref)
        own = pl.ds(pl.multiple_of(step * BLK, BLK), BLK)
        grouped = by_diagonal(queries_ref[own, :] * jnp.bfloat16(1.0 / math.sqrt(DH)), width)
        scores = masked_scores(
            picked_rows(keys_ref, shared, apart, head_count),
            grouped,
            step,
            num_blocks,
            length_ref[0],
            shared,
            apart,
        )
        highest = jnp.max(functools.reduce(jnp.maximum, scores), axis=0, keepdims=True)
        exponent = [jnp.exp(piece - highest) for piece in scores]
        denominator = jnp.sum(sum(exponent[1:], exponent[0]), axis=0, keepdims=True)
        scale = 1.0 / denominator
        attn_probs = jnp.concatenate(
            [(piece * scale).astype(jnp.bfloat16) for piece in exponent], axis=0
        )
        square = lax.dot_general(
            attn_probs,
            picked_rows(values_ref, shared, apart, head_count),
            (((0,), (0,)), ((), ())),
            preferred_element_type=jnp.float32,
        )
        context_ref[own, :] = from_diagonal(square, width).astype(jnp.bfloat16)
        highest_ref[step] = highest
        scale_ref[step] = scale

    @pl.loop(0, count // unroll)
    def _(turn):
        for place in range(unroll):
            one_block(first + turn * unroll + place)


def attend_back_kernel(
    head_count,
    unroll,
    length_ref,
    globals_ref,
    random_ref,
    queries_ref,
    keys_ref,
    values_ref,
    grads_ref,
    highest_ref,
    scale_ref,
    grads_out_ref,
    bias_ref,
    key_sums,
    value_sums,
    query_total,
):
    width = head_count * DH
    num_blocks = queries_ref.shape[0] // BLK
    factor = 1.0 / math.sqrt(DH)
    key_sums[...] = jnp.zeros_like(key_sums)
    value_sums[...] = jnp.zeros_like(value_sums)
    query_total[...] = jnp.zeros_like(query_total)

    def one_block(step):
        shared, apart = slot_starts(step, num_blocks, head_count, globals_ref, random_ref)
        own = pl.ds(pl.multiple_of(step * BLK, BLK), BLK)
        grouped = by_diagonal(queries_ref[own, :] * jnp.bfloat16(factor), width)
        grouped_grad = by_diagonal(grads_ref[own, :], width)
        picked_keys = picked_rows(keys_ref, shared, apart, head_count)
        picked_values = picked_rows(values_ref, shared, apart, head_count)
        scores = masked_scores(
            picked_keys, grouped, step, num_blocks, length_ref[0], shared, apart
        )
        highest = highest_ref[step]
        scale = scale_ref[step]
        attn_probs = [jnp.exp(piece - highest) * scale for piece in scores]
        prob_grad = lax.dot_general(
            picked_values,
            grouped_grad,
            (((1,), (1,)), ((), ())),
            preferred_element_type=jnp.float32,
        )
        prob_grads = [prob_grad[slot * BLK : (slot + 1) * BLK, :] for slot in range(8)]
        products = [left * right for left, right in zip(attn_probs, prob_grads)]
        total = jnp.sum(sum(products[1:], products[0]), axis=0, keepdims=True)
        score_grad = jnp.concatenate(
            [
                (left * (right - total)).astype(jnp.bfloat16)
                for left, right in zip(attn_probs, prob_grads)
            ],
            axis=0,
        )
        probs_low = jnp.concatenate([piece.astype(jnp.bfloat16) for piece in attn_probs], axis=0)
        square = lax.dot_general(
            score_grad, picked_keys, (((0,), (0,)), ((), ())), preferred_element_type=jnp.float32
        )
        query_grad = (from_diagonal(square, width) * factor).astype(jnp.bfloat16)
        grads_out_ref[own, :width] = query_grad
        query_total[...] += jnp.sum(
            query_grad.astype(jnp.float32).reshape(BLK // 8, 8, width), axis=0
        )
        key_part = jnp.dot(score_grad, grouped, preferred_element_type=jnp.float32)
        value_part = jnp.dot(probs_low, grouped_grad, preferred_element_type=jnp.float32)
        put_rows(key_sums, key_part, shared, apart, head_count)
        put_rows(value_sums, value_part, shared, apart, head_count)

    @pl.loop(0, num_blocks // unroll)
    def _(turn):
        for place in range(unroll):
            one_block(turn * unroll + place)

    value_grad = value_sums[...].reshape(queries_ref.shape).astype(jnp.bfloat16)
    seq_len = queries_ref.shape[0]
    grads_out_ref[:, width : 2 * width] = key_sums[...].reshape(seq_len, width).astype(jnp.bfloat16)
    grads_out_ref[:, 2 * width :] = value_grad
    bias_ref[0:1, :] = jnp.sum(query_total[...], axis=0, keepdims=True)
    bias_ref[1:2, :] = jnp.sum(value_grad.astype(jnp.float32), axis=0, keepdims=True)


VMEM = pl.BlockSpec(memory_space=pltpu.VMEM)
SMEM = pl.BlockSpec(memory_space=pltpu.SMEM)


def attend_back(queries, key_rows, value_rows, tables, stats, context_grad):
    seq_len, width = queries.shape
    head_count = width // DH
    return pl.pallas_call(
        functools.partial(attend_back_kernel, head_count, 8),
        out_shape=(
            jax.ShapeDtypeStruct((seq_len, 3 * width), jnp.bfloat16),
            jax.ShapeDtypeStruct((2, width), jnp.float32),
        ),
        in_specs=[SMEM] * 3 + [VMEM] * 6,
        out_specs=[VMEM] * 2,
        scratch_shapes=[pltpu.VMEM((seq_len // BLK, BLK, width), jnp.float32)] * 2
        + [pltpu.VMEM((8, width), jnp.float32)],
        compiler_params=pltpu.CompilerParams(vmem_limit_bytes=40 * 1024 * 1024),
        cost_estimate=pl.CostEstimate(
            flops=10 * seq_len * 512 * width * head_count,
            bytes_accessed=14 * seq_len * width,
            transcendentals=seq_len * 512 * head_count,
        ),
    )(*tables, queries, key_rows, value_rows, context_grad, *stats)


KINDS = 4
CHUNKS = 4


def front_kernel(
    levels,
    across,
    along,
    length_ref,
    globals_ref,
    random_ref,
    hidden_ref,
    grads_ref,
    b_query_ref,
    b_value_ref,
    w_query_ref,
    w_key_ref,
    w_value_ref,
    w_out_ref,
    w_up_ref,
    w_down_ref,
    b_out,
    gain1,
    shift1,
    features_ref,
    own_ref,
    upstream_ref,
    queries_ref,
    keys_ref,
    values_ref,
    context_ref,
    highest_ref,
    scale_ref,
    full_qkv_ref,
    full_out_ref,
    full_up_ref,
    full_down_ref,
    out_sib,
    up_sib,
    down_sib,
    context_sib,
    normed_full,
    unit1,
    inv1,
    sum_out,
    sum_in,
    level_send,
    level_recv,
    core_send,
    core_recv,
    swap_send,
    swap_recv,
    along_send,
    along_recv,
    across_send,
    across_recv,
    shard_send,
    shard_recv,
    context_send,
    context_recv,
    sum_send,
    sum_recv,
    normed_send,
    normed_recv,
):
    low, full = jnp.bfloat16, jnp.float32
    row, column = lax.axis_index("row"), lax.axis_index("col")
    core, level = lax.rem(column, 2), lax.div(column, 2)
    fast, slow = lax.rem(row, across), lax.div(row, across)
    cols = 2 * levels
    seq_len, width = hidden_ref.shape
    own_len = seq_len // cols
    shard = w_query_ref.shape[0]
    other = 1 - core
    sibling = (row, level * 2 + other)
    offsets = range(1, levels)

    def peer_level(offset):
        return lax.rem(level + offset, levels)

    def fast_peer(offset):
        return slow * across + lax.rem(fast + offset, across)

    def line_peer(shift):
        return ((slow + shift) * across + fast, column)

    barrier = pltpu.get_barrier_semaphore()
    greeted = [sibling]
    for offset in offsets:
        greeted += [(row, peer_level(offset) * 2 + core), (row, peer_level(offset) * 2 + other)]
    greeted += [(fast_peer(offset), column) for offset in range(1, across)]
    greeted += [
        (lax.rem(slow + offset, along) * across + fast, column) for offset in range(1, along)
    ]
    for device in greeted:
        pl.semaphore_signal(barrier, inc=1, device_id=device, device_id_type=MESH)
    pl.semaphore_wait(barrier, len(greeted))

    def remote(source, target, send, recv, device):
        return pltpu.make_async_remote_copy(
            src_ref=source,
            dst_ref=target,
            send_sem=send,
            recv_sem=recv,
            device_id=device,
            device_id_type=MESH,
        )

    def block(start, size):
        return pl.ds(pl.multiple_of(start * size, size), size)

    def level_copy(turn, offset):
        rows = block(turn, own_len)
        return remote(
            hidden_ref.at[rows],
            features_ref.at[rows, block(column, width)],
            level_send.at[turn, offset - 1],
            level_recv.at[turn, levels - offset - 1],
            (row, peer_level(offset) * 2 + core),
        )

    def core_copy(turn, offset):
        view = features_ref.at[block(turn, own_len), block(peer_level(offset) * 2 + core, width)]
        return remote(
            view, view, core_send.at[turn, offset], core_recv.at[turn, offset], sibling
        )

    @pl.loop(0, cols)
    def _(turn):
        for offset in offsets:
            level_copy(turn, offset).start()
        rows = block(turn, own_len)
        features_ref[rows, block(column, width)] = hidden_ref[rows, :]
        core_copy(turn, 0).start()

    fulls = (full_qkv_ref, full_out_ref, full_up_ref, full_down_ref)
    sibs = (None, out_sib, up_sib, down_sib)

    def shard_rows(place):
        return block(place * across + fast, shard)

    def line_copy(kind, way, hop):
        view = fulls[kind].at[shard_rows(slow - (1 - 2 * way) * hop)]
        return remote(
            view,
            view,
            along_send.at[kind, way, hop],
            along_recv.at[kind, way, hop],
            line_peer(1 - 2 * way),
        )

    def line_can_send(way, hop):
        if way == 0:
            return (slow >= hop) & (slow < along - 1)
        return (slow < along - hop) & (slow > 0)

    def line_send(kind, hop):
        for way in range(2):

            @pl.when(line_can_send(way, hop))
            def _():
                line_copy(kind, way, hop).start()

    def line_got(way, hop):
        place = slow - (1 - 2 * way) * (hop + 1)
        return place, ((place >= 0) if way == 0 else (place < along))

    def line_wait(kind, way, hop):
        place, _ = line_got(way, hop)
        view = fulls[kind].at[shard_rows(place)]
        remote(
            view,
            view,
            along_send.at[kind, way, hop],
            along_recv.at[kind, way, hop],
            line_peer(-(1 - 2 * way)),
        ).wait_recv()

    def across_copy(kind, place, offset):
        view = fulls[kind].at[shard_rows(place)]
        return remote(
            view,
            view,
            across_send.at[kind, place, offset - 1],
            across_recv.at[kind, place, across - offset - 1],
            (fast_peer(offset), column),
        )

    def core_shard(kind, place, offset):
        rows = block(place * across + lax.rem(fast + offset, across), shard)
        return remote(
            fulls[kind].at[rows],
            sibs[kind].at[rows],
            shard_send.at[kind - 1, place, offset],
            shard_recv.at[kind - 1, place, offset],
            sibling,
        )

    for place, ref in enumerate((w_query_ref, w_key_ref, w_value_ref)):
        full_qkv_ref[shard_rows(slow), place * width : (place + 1) * width] = ref[...].astype(low)
    line_send(0, 0)
    full_out_ref[shard_rows(slow), :] = w_out_ref[...].T.astype(low)
    full_up_ref[shard_rows(slow), :] = w_up_ref[...].astype(low)
    full_down_ref[shard_rows(slow), :] = w_down_ref[...].T.astype(low)

    def swap_copy(target, place_out, place_in):
        return remote(
            grads_ref.at[block(target, own_len)],
            upstream_ref.at[:, block(column, width)],
            swap_send.at[place_out],
            swap_recv.at[place_in],
            (row, target),
        )

    swaps = [swap_copy(level * 2 + other, 0, 0)]
    for offset in offsets:
        back = levels - offset
        swaps.append(swap_copy(peer_level(offset) * 2 + core, 2 * offset - 1, 2 * back - 1))
        swaps.append(swap_copy(peer_level(offset) * 2 + other, 2 * offset, 2 * back))
    for copy in swaps:
        copy.start()
    upstream_ref[:, block(column, width)] = grads_ref[block(column, own_len), :]

    def pass_shard(kind, place):
        for step in range(1, across):
            across_copy(kind, place, step).start()
        if kind > 0:
            core_shard(kind, place, 0).start()

    hops = range(along - 1)
    waiting = [(1, hop) for hop in hops] + [(3, -1), (2, 0), (3, 0)]
    waiting += [(kind, hop) for hop in hops if hop > 0 for kind in (2, 3)]

    def pass_on(count=1):
        pass_these(waiting[:count])
        del waiting[:count]

    def pass_these(shards):
        for kind, hop in shards:
            if hop < 0:
                pass_shard(kind, slow)
                continue
            for way in range(2):
                place, there = line_got(way, hop)

                @pl.when(there)
                def _():
                    line_wait(kind, way, hop)
                    if hop < along - 2:

                        @pl.when(line_can_send(way, hop + 1))
                        def _():
                            line_copy(kind, way, hop + 1).start()

                    pass_shard(kind, place)
    def await_shards(kind):
        @pl.loop(0, along)
        def _(place):
            for offset in range(1, across):
                across_copy(kind, place, across - offset).wait_recv()
                if kind > 0:
                    core_shard(kind, place, offset).start()

    def await_sibling(kind):
        @pl.loop(0, along)
        def _(place):
            for offset in range(across):
                core_shard(kind, place, offset).wait_recv()

    pass_these([(0, hop) for hop in range(-1, along - 2)])
    for kind in range(1, KINDS):
        line_send(kind, 0)
    pass_these([(0, along - 2), (1, -1), (2, -1)])
    await_shards(0)

    def project(turn):
        rows = block(turn, own_len)
        for offset in offsets:
            level_copy(turn, levels - offset).wait_recv()
            core_copy(turn, offset).start()
        for offset in range(levels):
            core_copy(turn, offset).wait_recv()
        values_in = features_ref[rows, :]
        queries_ref[rows, :] = (
            dot(values_in, full_qkv_ref[:, :width]) + b_query_ref[:, block(column, width)]
        ).astype(low)
        blocks = pl.ds(turn * (own_len // BLK), own_len // BLK)
        by_block = (own_len // BLK, BLK, width)
        keys_ref[blocks] = (
            dot(values_in, full_qkv_ref[:, width : 2 * width]).astype(low).reshape(by_block)
        )
        values_ref[blocks] = (
            (dot(values_in, full_qkv_ref[:, 2 * width :]) + b_value_ref[:, block(column, width)])
            .astype(low)
            .reshape(by_block)
        )

    for turn in range(cols):
        project(turn)
        pass_on(1 if (3, -1) in waiting else 0)
    while (2, 0) in waiting:
        pass_on()
    own_ref[...] = features_ref[block(column, own_len), :]
    step = own_len // CHUNKS
    halves = 2
    count = own_len // BLK // halves

    def attend_half(quarter, half):
        attend_blocks(
            (quarter * halves + half) * count,
            count,
            min(count, 4),
            length_ref,
            globals_ref,
            random_ref,
            (queries_ref, keys_ref, values_ref),
            context_ref,
            (highest_ref, scale_ref),
        )

    def context_copy(place, half):
        rows = own_len // halves
        return remote(
            context_ref.at[block((place * 2 + other) * halves + half, rows)],
            context_sib.at[block(place * halves + half, rows)],
            context_send.at[place, half],
            context_recv.at[place, half],
            sibling,
        )

    def chunk_rows(place, chunk):
        return block(place * CHUNKS + chunk, step)

    def attn_part(place, chunk):
        return dot_nt(
            context_ref[chunk_rows(place * 2 + core, chunk), :], full_out_ref[...]
        ) + dot_nt(context_sib[chunk_rows(place, chunk), :], out_sib[...])

    def sum_copy(chunk, offset):
        rows = block(chunk, step)
        return remote(
            sum_out.at[offset - 1, rows],
            sum_in.at[levels - offset - 1, rows],
            sum_send.at[chunk, offset - 1],
            sum_recv.at[chunk, levels - offset - 1],
            (row, peer_level(offset) * 2 + core),
        )

    def normed_copy(chunk, offset):
        view = normed_full.at[chunk_rows(level, chunk)]
        return remote(
            view,
            view,
            normed_send.at[chunk, offset - 1],
            normed_recv.at[chunk, levels - offset - 1],
            (row, peer_level(offset) * 2 + core),
        )

    for offset in list(offsets) + [0]:
        place = peer_level(offset)
        for half in range(halves):
            attend_half(place * 2 + other, half)
            context_copy(place, half).start()
            pass_on(1 - half if offset else half)
        if offset == 1:
            await_shards(1)
        for half in range(halves):
            attend_half(place * 2 + core, half)
            if offset == 1 and half == 0:
                await_sibling(1)
            context_copy(place, half).wait_recv()
            per_half = CHUNKS // halves
            for chunk in range(half * per_half, (half + 1) * per_half):
                if offset:
                    sum_out[offset - 1, block(chunk, step), :] = attn_part(place, chunk).astype(
                        low
                    )
                    sum_copy(chunk, offset).start()
            pass_on(1 if offset else half)
    pass_on(len(waiting))
    for chunk in range(CHUNKS):
        rows = block(chunk, step)
        summed = own_ref[rows, :].astype(full) + attn_part(level, chunk) + b_out[...]
        for offset in offsets:
            sum_copy(chunk, offset).wait_recv()
        for place in range(levels - 1):
            summed += sum_in[place, rows, :].astype(full)
        normed, inv_std = norm_parts(summed)
        unit1[rows, :] = normed
        inv1[rows, :] = inv_std
        normed_full[chunk_rows(level, chunk), :] = (normed * gain1[...] + shift1[...]).astype(low)
        for offset in offsets:
            normed_copy(chunk, offset).start()
    await_shards(2)
    await_shards(3)
    for chunk in range(CHUNKS):
        for offset in offsets:
            normed_copy(chunk, offset).wait()
            sum_copy(chunk, offset).wait_send()
    for kind in range(2, KINDS):
        await_sibling(kind)
    for place in range(levels):
        for half in range(halves):
            context_copy(place, half).wait_send()
    for copy in swaps:
        copy.wait()
    for kind in range(KINDS):
        for hop in range(along - 1):
            for way in range(2):

                @pl.when(line_can_send(way, hop))
                def _():
                    line_copy(kind, way, hop).wait_send()

        @pl.loop(0, along)
        def _(place):
            for offset in range(1, across):
                across_copy(kind, place, offset).wait_send()
            if kind > 0:
                for offset in range(across):
                    core_shard(kind, place, offset).wait_send()

    @pl.loop(0, cols)
    def _(turn):
        for offset in offsets:
            level_copy(turn, offset).wait_send()
        for offset in range(levels):
            core_copy(turn, offset).wait_send()


def across_of(rows):
    return 2 if rows <= 8 else rows // 4


def front(levels, rows, tables, hidden_in, grads, biases, weights, vectors):
    low, full = jnp.bfloat16, jnp.float32
    shape = jax.ShapeDtypeStruct
    across = across_of(rows)
    along = rows // across
    seq_len, width = hidden_in.shape
    cols = 2 * levels
    own_len = seq_len // cols
    features_all = width * cols
    units = weights[4].shape[1]
    widths = (3 * width, width, units, units)
    others = levels - 1
    stat = shape((seq_len // BLK, 1, width), full)
    dma = pltpu.SemaphoreType.DMA
    return pl.pallas_call(
        functools.partial(front_kernel, levels, across, along),
        out_shape=(
            shape((seq_len, features_all), low),
            shape((own_len, features_all), low),
            shape((own_len, features_all), low),
            shape((seq_len, width), low),
            shape((seq_len // BLK, BLK, width), low),
            shape((seq_len // BLK, BLK, width), low),
            shape((seq_len, width), low),
            stat,
            stat,
            *(shape((features_all, each), low) for each in widths),
            *(shape((features_all, each), low) for each in widths[1:]),
            shape((levels * own_len, width), low),
            shape((levels * own_len, features_all), low),
            shape((own_len, features_all), full),
            shape((own_len, 1), full),
        ),
        in_specs=[SMEM] * 3 + [VMEM] * 13,
        out_specs=[VMEM] * 20,
        scratch_shapes=[
            pltpu.VMEM((others, own_len, features_all), low),
            pltpu.VMEM((others, own_len, features_all), low),
            dma((cols, others)),
            dma((cols, others)),
            dma((cols, levels)),
            dma((cols, levels)),
            dma((cols,)),
            dma((cols,)),
            dma((KINDS, 2, along - 1)),
            dma((KINDS, 2, along - 1)),
            dma((KINDS, along, across - 1)),
            dma((KINDS, along, across - 1)),
            dma((KINDS - 1, along, across)),
            dma((KINDS - 1, along, across)),
            dma((levels, 2)),
            dma((levels, 2)),
            *(dma((CHUNKS, others)) for _ in range(4)),
        ],
        compiler_params=pltpu.CompilerParams(
            collective_id=3, has_side_effects=True, vmem_limit_bytes=56 * 1024 * 1024
        ),
        cost_estimate=pl.CostEstimate(
            flops=2 * seq_len * features_all * 3 * width,
            bytes_accessed=20 * 1024 * 1024,
            transcendentals=seq_len * 512 * (width // DH),
        ),
    )(*tables, hidden_in, grads, *biases, *weights, *vectors)


def dot(left, right):
    return jnp.dot(left, right, preferred_element_type=jnp.float32)


def dot_nt(left, right):
    return lax.dot_general(
        left, right, (((1,), (1,)), ((), ())), preferred_element_type=jnp.float32
    )


def dot_tn(left, right):
    return lax.dot_general(
        left, right, (((0,), (0,)), ((), ())), preferred_element_type=jnp.float32
    )


def gelu_parts(values_in):
    factor = math.sqrt(2.0 / math.pi)
    square = values_in * values_in
    bent = jnp.tanh(factor * (values_in + 0.044715 * (values_in * square)))
    half = 0.5 * (1.0 + bent)
    slope = half + (0.5 * values_in) * (1.0 - bent * bent) * (
        factor + (3.0 * 0.044715 * factor) * square
    )
    return (values_in * half, slope)


def norm_parts(summed):
    average = jnp.mean(summed, axis=1, keepdims=True)
    squares = jnp.mean(summed * summed, axis=1, keepdims=True)
    inv_std = lax.rsqrt(squares - average * average + epsilon)
    return ((summed - average) * inv_std, inv_std)


def norm_back(upstream, normed, inv_std, gain_vec):
    scaled = upstream * gain_vec
    left = jnp.mean(scaled, axis=1, keepdims=True)
    right = jnp.mean(scaled * normed, axis=1, keepdims=True)
    return inv_std * (scaled - left - normed * right)


def middle_kernel(
    levels,
    across,
    along,
    length_ref,
    context_ref,
    context_sib,
    upstream_ref,
    out_ref,
    out_sib,
    up_ref,
    up_sib,
    down_full,
    down_sib,
    normed_full,
    unit1,
    inv1,
    gain1,
    shift1,
    b_down,
    gain2,
    shift2,
    b_up_ref,
    layer_out_ref,
    context_grad_ref,
    attn_full,
    small_ref,
    up_small_ref,
    share_down_ref,
    up_part_ref,
    up_own_ref,
    grad_out_ref,
    ffn_full,
    hidden,
    slope,
    pre_grad,
    ffn_keep,
    part_own,
    send_buf,
    recv_buf,
    context_send,
    stage,
    down_sums,
    up_sums,
    down_got,
    up_got,
    down_pass,
    down_in,
    send_sem,
    recv_sem,
    core_send,
    core_recv,
    along_send,
    along_recv,
    across_send,
    across_recv,
    stage_sem,
):
    low = jnp.bfloat16
    row, column = lax.axis_index("row"), lax.axis_index("col")
    core = lax.rem(column, 2)
    level = lax.div(column, 2)
    sibling = (row, column + 1 - 2 * core)
    fast, slow = lax.rem(row, across), lax.div(row, across)
    shard = share_down_ref.shape[0]
    own_len = upstream_ref.shape[0]
    units = up_ref.shape[1]
    step = own_len // CHUNKS

    def peer_level(offset):
        return lax.rem(level + offset, levels)

    def fast_peer(offset):
        return slow * across + lax.rem(fast + offset, across)

    barrier = pltpu.get_barrier_semaphore()
    greeted = [sibling]
    greeted += [(row, peer_level(offset) * 2 + core) for offset in range(1, levels)]
    greeted += [(fast_peer(offset), column) for offset in range(1, across)]
    greeted += [
        (lax.rem(slow + offset, along) * across + fast, column) for offset in range(1, along)
    ]
    for device in greeted:
        pl.semaphore_signal(barrier, inc=1, device_id=device, device_id_type=MESH)
    pl.semaphore_wait(barrier, len(greeted))

    def remote(source, target, send, recv, device):
        return pltpu.make_async_remote_copy(
            src_ref=source,
            dst_ref=target,
            send_sem=send,
            recv_sem=recv,
            device_id=device,
            device_id_type=MESH,
        )

    def block(start, size):
        return pl.ds(pl.multiple_of(start * size, size), size)

    def to_sibling(source, target, place):
        return remote(source, target, core_send.at[place], core_recv.at[place], sibling)

    def rows_of(place, chunk):
        return pl.ds(pl.multiple_of(place * own_len + chunk * step, step), step)

    def own_rows(chunk):
        return pl.ds(pl.multiple_of(chunk * step, step), step)

    def exchange(kind, chunk, offset, source, target):
        return pltpu.make_async_remote_copy(
            src_ref=source,
            dst_ref=target,
            send_sem=send_sem.at[kind - 2, chunk, offset - 1],
            recv_sem=recv_sem.at[kind - 2, chunk, levels - offset - 1],
            device_id=(row, peer_level(offset) * 2 + core),
            device_id_type=MESH,
        )

    def sum_copy(kind, chunk, offset):
        return exchange(
            kind,
            chunk,
            offset,
            send_buf.at[kind // 2 - 1, offset - 1, own_rows(chunk)],
            recv_buf.at[kind // 2 - 1, levels - offset - 1, own_rows(chunk)],
        )

    def spread_copy(kind, chunk, offset):
        whole = {3: ffn_full, 5: attn_full}[kind]
        rows = rows_of(level, chunk)
        return exchange(kind, chunk, offset, whole.at[rows], whole.at[rows])

    def received(kind, chunk):
        return sum(
            recv_buf[kind // 2 - 1, place, own_rows(chunk), :].astype(jnp.float32)
            for place in range(levels - 1)
        )

    offsets = range(1, levels)
    small_ref[...] = jnp.zeros_like(small_ref)
    up_small_ref[...] = jnp.zeros_like(up_small_ref)
    def context_rows(place, chunk):
        start = (place * 2 + core) * own_len + chunk * step
        return pl.ds(pl.multiple_of(start, step), step)

    sides = ((up_ref, down_full), (up_sib, down_sib))

    def feed_forward(place, chunk):
        rows = rows_of(place, chunk)
        normed = normed_full[rows, :]
        total = None
        for side, (up_side, down_side) in enumerate(sides):
            bias = b_up_ref[:, block(column + side * (1 - 2 * core), units)]
            active, bend = gelu_parts(dot(normed, up_side[...]) + bias)
            active = active.astype(low)
            hidden[side, rows, :] = active
            slope[side, rows, :] = bend.astype(low)
            part = dot_nt(active, down_side[...])
            total = part if total is None else total + part
        return total

    @pl.loop(0, CHUNKS)
    def _(chunk):
        for offset in offsets:
            send_buf[0, offset - 1, own_rows(chunk), :] = feed_forward(
                peer_level(offset), chunk
            ).astype(low)
            sum_copy(2, chunk, offset).start()

    @pl.loop(0, CHUNKS)
    def _(chunk):
        rows = own_rows(chunk)
        part_own[rows, :] = feed_forward(level, chunk)
        normed1 = unit1[rows, :] * gain1[...] + shift1[...]
        summed = normed1 + part_own[rows, :] + b_down[...]
        for offset in offsets:
            sum_copy(2, chunk, offset).wait_recv()
        normed, inv_std = norm_parts(summed + received(2, chunk))
        position = lax.broadcasted_iota(jnp.int32, (step, 1), 0) + (
            column * own_len + chunk * step
        )
        valid = position < length_ref[0]
        layer_out_ref[rows, :] = jnp.where(
            valid, normed * gain2[...] + shift2[...], 0.0
        ).astype(low)
        upstream = jnp.where(valid, upstream_ref[rows, :].astype(jnp.float32), 0.0)
        grad = norm_back(upstream, normed, inv_std, gain2[...])
        ffn_keep[rows, :] = grad
        grad_low = grad.astype(low)
        ffn_full[rows_of(level, chunk), :] = grad_low
        for offset in offsets:
            spread_copy(3, chunk, offset).start()
        small_ref[0:1, :] += jnp.sum(upstream * normed, axis=0, keepdims=True)
        small_ref[1:2, :] += jnp.sum(upstream, axis=0, keepdims=True)
        small_ref[2:3, :] += jnp.sum(grad_low.astype(jnp.float32), axis=0, keepdims=True)

    def feed_back(place, chunk):
        rows = rows_of(place, chunk)
        upstream = ffn_full[rows, :]
        total = None
        for side, (up_side, down_side) in enumerate(sides):
            grad = (
                dot(upstream, down_side[...]) * slope[side, rows, :].astype(jnp.float32)
            ).astype(low)
            pre_grad[side, rows, :] = grad
            up_small_ref[side : side + 1, :] += jnp.sum(
                grad.astype(jnp.float32), axis=0, keepdims=True
            )
            part = dot_nt(grad, up_side[...])
            total = part if total is None else total + part
        return total

    @pl.loop(0, CHUNKS)
    def _(chunk):
        part_own[own_rows(chunk), :] = feed_back(level, chunk)
        for offset in offsets:
            spread_copy(3, chunk, levels - offset).wait_recv()
            send_buf[1, offset - 1, own_rows(chunk), :] = feed_back(
                peer_level(offset), chunk
            ).astype(low)
            sum_copy(4, chunk, offset).start()

    tile = across * shard
    lefts, rights = (ffn_full, normed_full), (hidden, pre_grad)
    sums, got = (down_sums, up_sums), (down_got, up_got)

    def grad_tile(kind, side, turn):
        return dot_tn(lefts[kind][:, block(turn, tile)], rights[kind][side])

    def core_grad(kind):
        return to_sibling(
            slope.at[kind, : sums[kind].shape[0]], sums[kind], levels + kind
        )

    def across_grad(kind, turn, offset):
        return remote(
            sums[kind].at[block(turn * across + lax.rem(fast + offset, across), shard)],
            got[kind].at[across - offset - 1, block(turn, shard)],
            across_send.at[kind, turn, offset - 1],
            across_recv.at[kind, turn, across - offset - 1],
            (fast_peer(offset), column),
        )

    def own_shard(kind, turn):
        for offset in range(1, across):
            across_grad(kind, turn, offset).wait_recv()
        total = sums[kind][block(turn * across + fast, shard), :].astype(jnp.float32)
        for place in range(across - 1):
            total += got[kind][place, block(turn, shard), :].astype(jnp.float32)
        return total

    def line_peer(shift):
        return ((slow + shift) * across + fast, column)

    def line_copy(kind, way, target):
        return remote(
            line_out[kind].at[way, target],
            line_in[kind].at[way, target],
            along_send.at[kind, way, target],
            along_recv.at[kind, way, target],
            line_peer(1 - 2 * way),
        )

    def line_step(kind, hop):
        for way in range(2):
            position = hop if way == 0 else along - 1 - hop
            targets = range(along - 1, hop, -1) if way == 0 else range(0, along - 1 - hop)

            @pl.when(slow == position)
            def _():
                for target in targets:
                    total = own_shard(kind, target)
                    if hop > 0:
                        line_copy(kind, way, target).wait_recv()
                        total += line_in[kind][way, target].astype(jnp.float32)
                    line_out[kind][way, target] = total.astype(jnp.bfloat16)
                    line_copy(kind, way, target).start()

    def line_finish(kind):
        for way in range(2):

            @pl.when((slow > 0) if way == 0 else (slow < along - 1))
            def _():
                line_copy(kind, way, slow).wait_recv()
                shares[kind][...] += line_in[kind][way, slow].astype(jnp.float32)

    def line_sent(kind):
        for way in range(2):
            for target in range(along):

                @pl.when((slow < target) if way == 0 else (slow > target))
                def _():
                    line_copy(kind, way, target).wait_send()

    def sum_grad(kind):
        core_grad(kind).wait_recv()

        @pl.loop(0, along)
        def _(turn):
            rows = block(turn, tile)
            sums[kind][rows, :] = (
                grad_tile(kind, 0, turn) + sums[kind][rows, :].astype(jnp.float32)
            ).astype(low)
            for offset in range(1, across):
                across_grad(kind, turn, offset).start()

    line_out, line_in, shares = (down_pass,), (down_in,), (share_down_ref,)
    for kind in range(2):

        @pl.loop(0, along)
        def _(turn):
            slope[kind, block(turn, tile), :] = grad_tile(kind, 1, turn).astype(low)

        core_grad(kind).start()
        if kind:
            sum_grad(kind - 1)
    sum_grad(1)

    @pl.loop(0, CHUNKS)
    def _(chunk):
        rows = own_rows(chunk)
        upstream = ffn_keep[rows, :] + part_own[rows, :]
        for offset in offsets:
            sum_copy(4, chunk, offset).wait_recv()
        upstream = upstream + received(4, chunk)
        normed = unit1[rows, :]
        grad_low = norm_back(upstream, normed, inv1[rows, :], gain1[...]).astype(low)
        attn_full[rows_of(level, chunk), :] = grad_low
        for offset in offsets:
            spread_copy(5, chunk, offset).start()
        small_ref[3:4, :] += jnp.sum(upstream * normed, axis=0, keepdims=True)
        small_ref[4:5, :] += jnp.sum(upstream, axis=0, keepdims=True)
        small_ref[5:6, :] += jnp.sum(grad_low.astype(jnp.float32), axis=0, keepdims=True)

    share_down_ref[...] = own_shard(0, slow)
    line_step(0, 0)

    def context_back(place, chunk):
        rows = rows_of(place, chunk)
        upstream = attn_full[rows, :]
        context_grad_ref[context_rows(place, chunk), :] = dot(upstream, out_ref[...]).astype(low)
        context_send[rows, :] = dot(upstream, out_sib[...]).astype(low)

    for chunk in range(CHUNKS):
        context_back(level, chunk)
        for offset in offsets:
            spread_copy(5, chunk, levels - offset).wait_recv()
            context_back(peer_level(offset), chunk)
        if 0 < chunk < along - 1:
            line_step(0, chunk)
    for hop in range(CHUNKS, along - 1):
        line_step(0, hop)

    back_copies = [
        to_sibling(
            context_send.at[pl.ds(place * own_len, own_len)],
            context_grad_ref.at[
                pl.ds(pl.multiple_of((place * 2 + core) * own_len, own_len), own_len)
            ],
            place,
        )
        for place in range(levels)
    ]
    for copy in back_copies:
        copy.start()

    own_context = jnp.concatenate(
        [
            context_ref[
                pl.ds(pl.multiple_of((place * 2 + core) * own_len, own_len), own_len), :
            ]
            for place in range(levels)
        ],
        axis=0,
    )

    def out_put(side):
        return pltpu.make_async_copy(stage.at[side], grad_out_ref.at[side], stage_sem.at[side])

    for side, right in enumerate((own_context, context_sib[...])):
        stage[side] = dot_tn(attn_full[...], right).astype(low)
        out_put(side).start()
    for shift in range(1, along):
        up_part_ref[shift - 1] = own_shard(1, lax.rem(slow + shift, along)).astype(low)
    up_own_ref[...] = own_shard(1, slow)
    line_finish(0)
    for side in range(2):
        out_put(side).wait()
    for kind in range(2):
        core_grad(kind).wait_send()
    line_sent(0)

    @pl.loop(0, along)
    def _(place):
        for offset in range(1, across):
            across_grad(0, place, offset).wait_send()
            across_grad(1, place, offset).wait_send()

    for copy in back_copies:
        copy.wait()
    for kind in range(2, 6):

        @pl.loop(0, CHUNKS)
        def _(chunk):
            for offset in offsets:
                if kind % 2:
                    spread_copy(kind, chunk, offset).wait_send()
                else:
                    sum_copy(kind, chunk, offset).wait_send()


def middle(
    levels,
    rows,
    length,
    context,
    context_sib,
    upstream,
    weights,
    normed_full,
    unit1,
    inv1,
    vectors,
    b_up,
):
    low, full = jnp.bfloat16, jnp.float32
    across = across_of(rows)
    along = rows // across
    own_len, features = upstream.shape
    seq_len, width = context.shape
    units = weights[2].shape[1]
    shard = features // rows
    tokens = levels * own_len
    others = levels - 1
    shape = jax.ShapeDtypeStruct
    hbm = pl.BlockSpec(memory_space=pl.ANY)
    dma = pltpu.SemaphoreType.DMA
    vmem = pltpu.VMEM
    return pl.pallas_call(
        functools.partial(middle_kernel, levels, across, along),
        out_shape=(
            shape((own_len, features), low),
            shape((seq_len, width), low),
            shape((tokens, features), low),
            shape((8, features), full),
            shape((2, units), full),
            shape((shard, units), full),
            shape((along - 1, shard, units), low),
            shape((shard, units), full),
            shape((2, features, width), low),
        ),
        in_specs=[SMEM] + [VMEM] * 18,
        out_specs=[VMEM] * 8 + [hbm],
        scratch_shapes=[
            vmem((tokens, features), low),
            vmem((2, tokens, units), low),
            vmem((2, max(tokens, features), units), low),
            vmem((2, tokens, units), low),
            vmem((own_len, features), full),
            vmem((own_len, features), full),
            vmem((2, others, own_len, features), low),
            vmem((2, others, own_len, features), low),
            vmem((tokens, width), low),
            vmem((2, features, width), low),
            vmem((features, units), low),
            vmem((features, units), low),
            vmem((across - 1, along * shard, units), low),
            vmem((across - 1, along * shard, units), low),
            vmem((2, along, shard, units), low),
            vmem((2, along, shard, units), low),
            dma((4, CHUNKS, others)),
            dma((4, CHUNKS, others)),
            dma((levels + 2,)),
            dma((levels + 2,)),
            dma((1, 2, along)),
            dma((1, 2, along)),
            dma((2, along, across - 1)),
            dma((2, along, across - 1)),
            dma((2,)),
        ],
        compiler_params=pltpu.CompilerParams(
            collective_id=1, has_side_effects=True, vmem_limit_bytes=62 * 1024 * 1024
        ),
        cost_estimate=pl.CostEstimate(
            flops=2 * tokens * features * (12 * units + 6 * width),
            bytes_accessed=20 * 1024 * 1024,
            transcendentals=2 * tokens * units,
        ),
    )(
        length,
        context,
        context_sib,
        upstream,
        *weights,
        normed_full,
        unit1,
        inv1,
        *vectors,
        b_up,
    )


def end_kernel(
    levels,
    across,
    along,
    query_key_value_ref,
    weights_ref,
    features_ref,
    attn_ref,
    layer_ref,
    small_ref,
    up_small_ref,
    bias_ref,
    out_ref,
    grad_input_ref,
    layer_out_ref,
    small_out_ref,
    share_ref,
    out_sib,
    sums,
    got,
    line_out,
    line_in,
    core_out,
    core_in,
    level_out,
    level_in,
    attn_in,
    small_sums,
    small_in,
    core_send,
    core_recv,
    part_send,
    part_recv,
    level_send,
    level_recv,
    layer_send,
    layer_recv,
    across_send,
    across_recv,
    along_send,
    along_recv,
    small_send,
    small_recv,
    keep_sem,
):
    low, full = jnp.bfloat16, jnp.float32
    row, column = lax.axis_index("row"), lax.axis_index("col")
    core, level = lax.rem(column, 2), lax.div(column, 2)
    fast, slow = lax.rem(row, across), lax.div(row, across)
    cols = 2 * levels
    seq_len = features_ref.shape[0]
    own_len = seq_len // cols
    width = grad_input_ref.shape[1]
    shard = share_ref.shape[0]
    other = 1 - core
    sibling = (row, level * 2 + other)
    offsets = range(1, levels)

    def peer_level(offset):
        return lax.rem(level + offset, levels)

    def fast_peer(offset):
        return slow * across + lax.rem(fast + offset, across)

    def slow_peer(offset):
        return lax.rem(slow + offset, along) * across + fast

    barrier = pltpu.get_barrier_semaphore()
    greeted = [sibling]
    for offset in offsets:
        greeted += [(row, peer_level(offset) * 2 + core), (row, peer_level(offset) * 2 + other)]
    greeted += [(fast_peer(offset), column) for offset in range(1, across)]
    greeted += [(slow_peer(offset), column) for offset in range(1, along)]
    for device in greeted:
        pl.semaphore_signal(barrier, inc=1, device_id=device, device_id_type=MESH)
    pl.semaphore_wait(barrier, len(greeted))

    def remote(source, target, send, recv, device):
        return pltpu.make_async_remote_copy(
            src_ref=source,
            dst_ref=target,
            send_sem=send,
            recv_sem=recv,
            device_id=device,
            device_id_type=MESH,
        )

    def block(start, size):
        return pl.ds(pl.multiple_of(start * size, size), size)

    out_copy = remote(out_ref.at[1], out_sib, core_send.at[0], core_recv.at[0], sibling)
    attn_copy = remote(
        attn_ref.at[:, block(level * 2 + other, width)],
        attn_in,
        core_send.at[1],
        core_recv.at[1],
        sibling,
    )

    partners = [sibling]
    bit = 1
    while bit < levels:
        partners.append((row, (level + bit - 2 * bit * lax.rem(lax.div(level, bit), 2)) * 2 + core))
        bit *= 2
    bit = 1
    while bit < across * along:
        partners.append((row + bit - 2 * bit * lax.rem(lax.div(row, bit), 2), column))
        bit *= 2

    def small_copy(turn):
        return remote(
            small_sums.at[turn],
            small_in.at[turn],
            small_send.at[turn],
            small_recv.at[turn],
            partners[turn],
        )

    small_turn = [0]

    def small_step():
        turn = small_turn[0]
        if turn > len(partners):
            return
        if turn > 0:
            small_copy(turn - 1).wait()
            small_sums[turn] = small_sums[turn - 1] + small_in[turn - 1]
        if turn < len(partners):
            small_copy(turn).start()
        small_turn[0] += 1

    def layer_copy(target, place_out, place_in):
        return remote(
            layer_ref.at[:, block(target, width)],
            layer_out_ref.at[block(column, own_len)],
            layer_send.at[place_out],
            layer_recv.at[place_in],
            (row, target),
        )

    layer_copies = [layer_copy(level * 2 + other, 0, 0)]
    for offset in offsets:
        back = levels - offset
        layer_copies.append(
            layer_copy(peer_level(offset) * 2 + core, 2 * offset - 1, 2 * back - 1)
        )
        layer_copies.append(layer_copy(peer_level(offset) * 2 + other, 2 * offset, 2 * back))
    layer_keep = pltpu.make_async_copy(
        layer_ref.at[:, block(column, width)], layer_out_ref.at[block(column, own_len)], keep_sem
    )

    features_all = weights_ref.shape[0]
    units = up_small_ref.shape[1]
    first_up = small_ref.shape[0]
    small_sums[0] = jnp.zeros_like(small_in[0])
    small_sums[0, :first_up, :] = small_ref[...]
    for side in range(2):
        start = (column + side * (1 - 2 * core)) * units
        small_sums[
            0,
            pl.ds(first_up + lax.div(start, features_all), 1),
            pl.ds(pl.multiple_of(lax.rem(start, features_all), units), units),
        ] = up_small_ref[side : side + 1, :]
    first_bias = small_in.shape[1] - 4
    small_sums[0, first_bias : first_bias + 2, block(column, width)] = bias_ref[...]
    small_step()
    out_copy.start()
    attn_copy.start()
    layer_keep.start()
    for copy in layer_copies:
        copy.start()

    def input_part(turn, target):
        return dot_nt(
            query_key_value_ref[block(turn, own_len), :], weights_ref[block(target, width), :]
        )

    def part_copy(turn, place):
        rows = block(turn, own_len)
        return remote(
            core_out.at[place, rows],
            core_in.at[place, rows],
            part_send.at[turn, place],
            part_recv.at[turn, place],
            sibling,
        )

    def give_core():
        @pl.loop(0, cols)
        def _(turn):
            for place in range(levels):
                core_out[place, block(turn, own_len), :] = input_part(
                    turn, place * 2 + other
                ).astype(low)
                part_copy(turn, place).start()

    def across_copy(turn, offset):
        return remote(
            sums.at[block(turn * across + lax.rem(fast + offset, across), shard)],
            got.at[across - offset - 1, block(turn, shard)],
            across_send.at[turn, offset - 1],
            across_recv.at[turn, across - offset - 1],
            (fast_peer(offset), column),
        )

    def weight_grad(turn):
        rows = block(turn, across * shard)
        sums[rows, : 3 * width] = dot_tn(features_ref[:, rows], query_key_value_ref[...]).astype(
            low
        )
        sums[rows, 3 * width :] = (
            out_ref[0, rows, :].astype(full) + out_sib[rows, :].astype(full)
        ).astype(low)
        for offset in range(1, across):
            across_copy(turn, offset).start()

    def level_copy(turn, offset):
        rows = block(turn, own_len)
        return remote(
            level_out.at[offset - 1, rows],
            level_in.at[levels - offset - 1, rows],
            level_send.at[turn, offset - 1],
            level_recv.at[turn, levels - offset - 1],
            (row, peer_level(offset) * 2 + core),
        )

    def give_levels():
        @pl.loop(0, cols)
        def _(turn):
            rows = block(turn, own_len)
            for offset in offsets:
                place = peer_level(offset)
                part = input_part(turn, place * 2 + core)
                part_copy(turn, place).wait_recv()
                level_out[offset - 1, rows, :] = (
                    part + core_in[place, rows, :].astype(full)
                ).astype(low)
                level_copy(turn, offset).start()

    def own_shard(turn):
        for offset in range(1, across):
            across_copy(turn, offset).wait_recv()
        total = sums[block(turn * across + fast, shard), :].astype(full)
        for place in range(across - 1):
            total += got[place, block(turn, shard), :].astype(full)
        return total

    def line_copy(way, target):
        return remote(
            line_out.at[way, target],
            line_in.at[way, target],
            along_send.at[way, target],
            along_recv.at[way, target],
            ((slow + 1 - 2 * way) * across + fast, column),
        )

    def line_step(hop, near):
        if hop >= along - 1 - near:
            return
        for way in range(2):
            target = along - 1 - near if way == 0 else near
            position = hop if way == 0 else along - 1 - hop

            @pl.when(slow == position)
            def _():
                total = own_shard(target)
                if hop > 0:
                    line_copy(way, target).wait_recv()
                    total += line_in[way, target].astype(full)
                line_out[way, target] = total.astype(low)
                line_copy(way, target).start()

    def finish_input(turn, attn_part):
        rows = block(turn, own_len)
        total = input_part(turn, column) + attn_part.astype(full)
        part_copy(turn, level).wait_recv()
        total += core_in[level, rows, :].astype(full)
        for offset in offsets:
            level_copy(turn, offset).wait_recv()
        for place in range(levels - 1):
            total += level_in[place, rows, :].astype(full)
        grad_input_ref[rows, :] = total.astype(low)

    ends = [turn for place in range(along // 2) for turn in (along - 1 - place, place)]
    out_copy.wait()
    for turn in ends:
        weight_grad(turn)
    small_step()
    give_core()
    small_step()
    give_levels()
    line_steps = sorted(
        ((hop, near) for near in range(along - 1) for hop in range(along - 1 - near)),
        key=lambda step: step[0] + 2 * step[1],
    )
    for step in line_steps[: len(line_steps) // 3]:
        line_step(*step)
        small_step()
    attn_copy.wait()
    for place in range(levels):
        for step in line_steps[len(line_steps) // 3 :][place::levels]:
            line_step(*step)
        rows = block(place, own_len)
        finish_input(place * 2 + core, attn_ref[rows, block(column, width)])
        finish_input(place * 2 + other, attn_in[rows, :])
        small_step()
    share_ref[...] = own_shard(slow)
    while small_turn[0] <= len(partners):
        small_step()
    small_out_ref[...] = small_sums[len(partners)]

    for way in range(2):

        @pl.when((slow > 0) if way == 0 else (slow < along - 1))
        def _():
            line_copy(way, slow).wait_recv()
            share_ref[...] += line_in[way, slow].astype(full)

    layer_keep.wait()
    for copy in layer_copies:
        copy.wait()
    for way in range(2):
        for target in range(along):

            @pl.when((slow < target) if way == 0 else (slow > target))
            def _():
                line_copy(way, target).wait_send()

    @pl.loop(0, along)
    def _(turn):
        for offset in range(1, across):
            across_copy(turn, offset).wait_send()

    @pl.loop(0, cols)
    def _(turn):
        for place in range(levels):
            part_copy(turn, place).wait_send()
        for offset in offsets:
            level_copy(turn, offset).wait_send()


def finish(
    levels, rows, query_key_value, weights, features, attn_full, layer_own, small, up_small, bias, out
):
    low, full = jnp.bfloat16, jnp.float32
    shape = jax.ShapeDtypeStruct
    across = across_of(rows)
    along = rows // across
    seq_len, features_all = features.shape
    width = query_key_value.shape[1] // 3
    own_len = layer_own.shape[0]
    shard = features_all // rows
    others = levels - 1
    cols = 2 * levels
    turns = 1 + (levels - 1).bit_length() + (rows - 1).bit_length()
    small_rows = small.shape[0] + up_small.shape[1] * cols // features_all + 4
    dma = pltpu.SemaphoreType.DMA
    vmem = pltpu.VMEM
    return pl.pallas_call(
        functools.partial(end_kernel, levels, across, along),
        out_shape=(
            shape((seq_len, width), low),
            shape((seq_len, width), low),
            shape((small_rows, features_all), full),
            shape((shard, 4 * width), full),
        ),
        in_specs=[VMEM] * 9,
        out_specs=[VMEM] * 4,
        scratch_shapes=[
            vmem((features_all, width), low),
            vmem((features_all, 4 * width), low),
            vmem((across - 1, along * shard, 4 * width), low),
            vmem((2, along, shard, 4 * width), low),
            vmem((2, along, shard, 4 * width), low),
            vmem((levels, seq_len, width), low),
            vmem((levels, seq_len, width), low),
            vmem((others, seq_len, width), low),
            vmem((others, seq_len, width), low),
            vmem((levels * own_len, width), low),
            vmem((turns + 1, small_rows, features_all), full),
            vmem((turns, small_rows, features_all), full),
            dma((2,)),
            dma((2,)),
            dma((cols, levels)),
            dma((cols, levels)),
            dma((cols, others)),
            dma((cols, others)),
            dma((cols,)),
            dma((cols,)),
            dma((along, across - 1)),
            dma((along, across - 1)),
            dma((2, along)),
            dma((2, along)),
            dma((turns,)),
            dma((turns,)),
            dma,
        ],
        compiler_params=pltpu.CompilerParams(
            collective_id=2, has_side_effects=True, vmem_limit_bytes=56 * 1024 * 1024
        ),
        cost_estimate=pl.CostEstimate(
            flops=4 * seq_len * features_all * 3 * width,
            bytes_accessed=20 * 1024 * 1024,
            transcendentals=0,
        ),
    )(query_key_value, weights, features, attn_full, layer_own, small, up_small, bias, out)


def last_kernel(
    grad_input_ref,
    layer_ref,
    small_ref,
    share_ref,
    down_ref,
    up_own_ref,
    up_first_ref,
    *refs,
):
    more, outs = refs[: len(refs) - 17], refs[len(refs) - 17 :]
    (
        layer_out,
        grad_input,
        grad_query,
        bias_query,
        grad_key,
        grad_value,
        bias_value,
        grad_out,
        bias_out,
        gain1,
        shift1,
        grad_up,
        bias_up,
        grad_down,
        bias_down,
        gain2,
        shift2,
    ) = outs
    grad_input[...] = grad_input_ref[...]
    layer_out[...] = layer_ref[...]
    width = grad_query.shape[1]
    for place, ref in enumerate((grad_query, grad_key, grad_value)):
        ref[...] = share_ref[:, place * width : (place + 1) * width]
    grad_out[...] = share_ref[:, 3 * width :].T
    grad_down[...] = down_ref[...].T
    total = up_own_ref[...]
    for ref in (up_first_ref, *more):
        total += ref[...].astype(jnp.float32)
    grad_up[...] = total
    features_all = small_ref.shape[1]
    last = small_ref.shape[0] - 4
    for place, ref in (
        (0, gain2),
        (1, shift2),
        (2, bias_down),
        (3, gain1),
        (4, shift1),
        (5, bias_out),
        (last, bias_query),
        (last + 1, bias_value),
    ):
        ref[...] = small_ref[place : place + 1, :]
    for place in range(8, last):
        bias_up[:, (place - 8) * features_all : (place - 7) * features_all] = small_ref[
            place : place + 1, :
        ]


def put_out(grad_input, layer_out, small, share, down, up_own, up_others):
    low, full = jnp.bfloat16, jnp.float32
    shape = jax.ShapeDtypeStruct
    seq_len, width = grad_input.shape
    shard, units = up_own.shape
    features_all = small.shape[1]
    vector = shape((1, features_all), full)
    units_all = (small.shape[0] - 12) * features_all
    grad = shape((shard, width), full)
    return pl.pallas_call(
        last_kernel,
        out_shape=(
            shape((seq_len, width), low),
            shape((seq_len, width), low),
            grad,
            vector,
            grad,
            grad,
            vector,
            shape((width, shard), full),
            vector,
            vector,
            vector,
            shape((shard, units), full),
            shape((1, units_all), full),
            shape((units, shard), full),
            vector,
            vector,
            vector,
        ),
        in_specs=[VMEM] * (6 + len(up_others)),
        out_specs=[VMEM] * 17,
        compiler_params=pltpu.CompilerParams(vmem_limit_bytes=24 * 1024 * 1024),
    )(grad_input, layer_out, small, share, down, up_own, *up_others)


def on_device(
    hidden_in,
    out_grad,
    lengths,
    global_blocks,
    rand_blocks,
    w_query,
    b_query,
    w_key,
    w_value,
    b_value,
    w_out,
    b_out,
    ln1_gain,
    ln1_bias,
    w_up,
    b_up,
    w_down,
    b_down,
    ln2_gain,
    ln2_bias,
):
    cols = lax.axis_size("col")
    rows = lax.axis_size("row")
    tables = (lengths, global_blocks.reshape(-1), rand_blocks.reshape(-1))
    as_row = lambda vector: vector[None, :]
    (
        features,
        own_features,
        upstream,
        queries,
        key_rows,
        value_rows,
        context,
        highest,
        scale,
        full_qkv,
        full_out,
        full_up,
        full_down,
        out_sib,
        up_sib,
        down_sib,
        context_sib,
        normed_full,
        unit1,
        inv1,
    ) = front(
        cols // 2,
        rows,
        tables,
        hidden_in,
        out_grad,
        (as_row(b_query), as_row(b_value)),
        (w_query, w_key, w_value, w_out, w_up, w_down),
        (as_row(b_out), as_row(ln1_gain), as_row(ln1_bias)),
    )
    (
        layer_own,
        context_grad,
        attn_full,
        small,
        up_small,
        down_share,
        up_part,
        up_own,
        grad_out,
    ) = middle(
        cols // 2,
        rows,
        lengths,
        context,
        context_sib,
        upstream,
        (full_out, out_sib, full_up, up_sib, full_down, down_sib),
        normed_full,
        unit1,
        inv1,
        tuple(as_row(each) for each in (ln1_gain, ln1_bias, b_down, ln2_gain, ln2_bias)),
        as_row(b_up),
    )
    across = across_of(rows)
    up_others = [
        lax.ppermute(
            up_part[shift - 1],
            "row",
            [(place, (place + shift * across) % rows) for place in range(rows)],
        )
        for shift in range(1, rows // across)
    ]
    query_key_value, bias_sums = attend_back(
        queries, key_rows, value_rows, tables, (highest, scale), context_grad
    )
    grad_input, layer_out, small, share = finish(
        cols // 2,
        rows,
        query_key_value,
        full_qkv,
        features,
        attn_full,
        layer_own,
        small,
        up_small,
        bias_sums,
        grad_out,
    )
    outs = put_out(grad_input, layer_out, small, share, down_share, up_own, up_others)
    return tuple(each.reshape(-1) if each.shape[0] == 1 else each for each in outs)


def solution(mesh):
    placed = (
        P("row", "col"),
        P("row", "col"),
        P("row"),
        P("row", None),
        P("row", None, "col", None),
        P("row", "col"),
        P(),
        P("row", "col"),
        P("row", "col"),
        P(),
        P("col", "row"),
        P(),
        P(),
        P(),
        P("row", "col"),
        P(),
        P("col", "row"),
        P(),
        P(),
        P(),
    )
    return jax.shard_map(
        on_device,
        mesh=mesh,
        in_specs=placed,
        out_specs=(
            P("row", "col"),
            P("row", "col"),
            P("row", "col"),
            P(),
            P("row", "col"),
            P("row", "col"),
            P(),
            P("col", "row"),
            P(),
            P(),
            P(),
            P("row", "col"),
            P(),
            P("col", "row"),
            P(),
            P(),
            P(),
        ),
        check_vma=False,
    )
```

```python
import functools
import math

import jax
import jax.numpy as jnp
from jax import lax
from jax.experimental import pallas as pl
from jax.experimental.pallas import tpu as pltpu
from jax.sharding import PartitionSpec as P

DH = 64
BLK = 64
MESH = pl.DeviceIdType.MESH


epsilon = 1e-06


def lane_heads(rows, width):
    return lax.broadcasted_iota(jnp.int32, (rows, width), 1) // DH


def by_diagonal(rows, width):
    lane_head = lane_heads(BLK, width)
    zero = jnp.zeros_like(rows)
    return jnp.concatenate(
        [jnp.where(lane_head == head, rows, zero) for head in range(width // DH)], axis=0
    )


def from_diagonal(square, width):
    lane_head = lane_heads(BLK, width)
    result = jnp.zeros((BLK, width), jnp.float32)
    for head in range(width // DH):
        result = jnp.where(lane_head == head, square[head * BLK : (head + 1) * BLK, :], result)
    return result


def slot_starts(step, num_blocks, head_count, globals_ref, random_ref):
    shared = [
        jnp.maximum(step - 1, 0),
        step,
        jnp.minimum(step + 1, num_blocks - 1),
        globals_ref[0],
        globals_ref[1],
    ]
    base = step * (head_count * 3)
    apart = [
        [random_ref[base + head * 3 + slot] for head in range(head_count)] for slot in range(3)
    ]
    return shared, apart


def lane_groups(head_count):
    per_group = min(128 // DH, head_count)
    return [
        (first * DH, per_group * DH, list(range(first, first + per_group)))
        for first in range(0, head_count, per_group)
    ]


def picked_rows(rows_ref, shared, apart, head_count):
    pieces = [rows_ref[block] for block in shared]
    for blocks in apart:
        groups = []
        for lane, width, heads in lane_groups(head_count):
            lane_head = lane_heads(BLK, width)
            piece = rows_ref[blocks[heads[0]], :, lane : lane + width]
            for place, head in enumerate(heads[1:], 1):
                other = rows_ref[blocks[head], :, lane : lane + width]
                piece = jnp.where(lane_head >= place, other, piece)
            groups.append(piece)
        pieces.append(jnp.concatenate(groups, axis=1) if len(groups) > 1 else groups[0])
    return jnp.concatenate(pieces, axis=0)


def put_rows(sums_ref, values_in, shared, apart, head_count):
    for slot, block in enumerate(shared):
        sums_ref[block] += values_in[slot * BLK : (slot + 1) * BLK, :]
    for slot, blocks in enumerate(apart, len(shared)):
        rows = values_in[slot * BLK : (slot + 1) * BLK, :]
        for lane, width, heads in lane_groups(head_count):
            lane_head = lane_heads(BLK, width)
            for place, head in enumerate(heads):
                sums_ref[blocks[head], :, lane : lane + width] += jnp.where(
                    lane_head == place, rows[:, lane : lane + width], 0.0
                )


def masked_scores(picked_keys, grouped, step, num_blocks, length, shared, apart):
    width = grouped.shape[1]
    scores = lax.dot_general(
        picked_keys, grouped, (((1,), (1,)), ((), ())), preferred_element_type=jnp.float32
    )
    listed = [step >= 1, True, step + 1 < num_blocks]
    listed += [(block < step - 1) | (block > step + 1) for block in shared[3:]]
    limits = [
        jnp.where(there, length - block * BLK, 0) for there, block in zip(listed, shared)
    ]
    lane_head = lane_heads(1, width)
    for blocks in apart:
        limit = length - jnp.full((1, width), blocks[0], jnp.int32) * BLK
        for head, block in enumerate(blocks[1:], 1):
            limit = jnp.where(lane_head >= head, length - block * BLK, limit)
        limits.append(limit)
    row = lax.broadcasted_iota(jnp.int32, (BLK, width), 0)
    return [
        jnp.where(row < limit, scores[slot * BLK : (slot + 1) * BLK, :], -1e30)
        for slot, limit in enumerate(limits)
    ]


def attend_blocks(
    first, count, unroll, length_ref, globals_ref, random_ref, refs, context_ref, stat_refs
):
    queries_ref, keys_ref, values_ref = refs
    highest_ref, scale_ref = stat_refs
    seq_len, width = queries_ref.shape
    head_count = width // DH
    num_blocks = seq_len // BLK

    def one_block(step):
        shared, apart = slot_starts(step, num_blocks, head_count, globals_ref, random_ref)
        own = pl.ds(pl.multiple_of(step * BLK, BLK), BLK)
        grouped = by_diagonal(queries_ref[own, :] * jnp.bfloat16(1.0 / math.sqrt(DH)), width)
        scores = masked_scores(
            picked_rows(keys_ref, shared, apart, head_count),
            grouped,
            step,
            num_blocks,
            length_ref[0],
            shared,
            apart,
        )
        highest = jnp.max(functools.reduce(jnp.maximum, scores), axis=0, keepdims=True)
        exponent = [jnp.exp(piece - highest) for piece in scores]
        denominator = jnp.sum(sum(exponent[1:], exponent[0]), axis=0, keepdims=True)
        scale = 1.0 / denominator
        attn_probs = jnp.concatenate(
            [(piece * scale).astype(jnp.bfloat16) for piece in exponent], axis=0
        )
        square = lax.dot_general(
            attn_probs,
            picked_rows(values_ref, shared, apart, head_count),
            (((0,), (0,)), ((), ())),
            preferred_element_type=jnp.float32,
        )
        context_ref[own, :] = from_diagonal(square, width).astype(jnp.bfloat16)
        highest_ref[step] = highest
        scale_ref[step] = scale

    @pl.loop(0, count // unroll)
    def _(turn):
        for place in range(unroll):
            one_block(first + turn * unroll + place)


def attend_back_kernel(
    head_count,
    unroll,
    length_ref,
    globals_ref,
    random_ref,
    queries_ref,
    keys_ref,
    values_ref,
    grads_ref,
    highest_ref,
    scale_ref,
    grads_out_ref,
    bias_ref,
    key_sums,
    value_sums,
    query_total,
):
    width = head_count * DH
    num_blocks = queries_ref.shape[0] // BLK
    factor = 1.0 / math.sqrt(DH)
    key_sums[...] = jnp.zeros_like(key_sums)
    value_sums[...] = jnp.zeros_like(value_sums)
    query_total[...] = jnp.zeros_like(query_total)

    def one_block(step):
        shared, apart = slot_starts(step, num_blocks, head_count, globals_ref, random_ref)
        own = pl.ds(pl.multiple_of(step * BLK, BLK), BLK)
        grouped = by_diagonal(queries_ref[own, :] * jnp.bfloat16(factor), width)
        grouped_grad = by_diagonal(grads_ref[own, :], width)
        picked_keys = picked_rows(keys_ref, shared, apart, head_count)
        picked_values = picked_rows(values_ref, shared, apart, head_count)
        scores = masked_scores(
            picked_keys, grouped, step, num_blocks, length_ref[0], shared, apart
        )
        highest = highest_ref[step]
        scale = scale_ref[step]
        attn_probs = [jnp.exp(piece - highest) * scale for piece in scores]
        prob_grad = lax.dot_general(
            picked_values,
            grouped_grad,
            (((1,), (1,)), ((), ())),
            preferred_element_type=jnp.float32,
        )
        prob_grads = [prob_grad[slot * BLK : (slot + 1) * BLK, :] for slot in range(8)]
        products = [left * right for left, right in zip(attn_probs, prob_grads)]
        total = jnp.sum(sum(products[1:], products[0]), axis=0, keepdims=True)
        score_grad = jnp.concatenate(
            [
                (left * (right - total)).astype(jnp.bfloat16)
                for left, right in zip(attn_probs, prob_grads)
            ],
            axis=0,
        )
        probs_low = jnp.concatenate([piece.astype(jnp.bfloat16) for piece in attn_probs], axis=0)
        square = lax.dot_general(
            score_grad, picked_keys, (((0,), (0,)), ((), ())), preferred_element_type=jnp.float32
        )
        query_grad = (from_diagonal(square, width) * factor).astype(jnp.bfloat16)
        grads_out_ref[own, :width] = query_grad
        query_total[...] += jnp.sum(
            query_grad.astype(jnp.float32).reshape(BLK // 8, 8, width), axis=0
        )
        key_part = jnp.dot(score_grad, grouped, preferred_element_type=jnp.float32)
        value_part = jnp.dot(probs_low, grouped_grad, preferred_element_type=jnp.float32)
        put_rows(key_sums, key_part, shared, apart, head_count)
        put_rows(value_sums, value_part, shared, apart, head_count)

    @pl.loop(0, num_blocks // unroll)
    def _(turn):
        for place in range(unroll):
            one_block(turn * unroll + place)

    value_grad = value_sums[...].reshape(queries_ref.shape).astype(jnp.bfloat16)
    seq_len = queries_ref.shape[0]
    grads_out_ref[:, width : 2 * width] = key_sums[...].reshape(seq_len, width).astype(jnp.bfloat16)
    grads_out_ref[:, 2 * width :] = value_grad
    bias_ref[0:1, :] = jnp.sum(query_total[...], axis=0, keepdims=True)
    bias_ref[1:2, :] = jnp.sum(value_grad.astype(jnp.float32), axis=0, keepdims=True)


VMEM = pl.BlockSpec(memory_space=pltpu.VMEM)
SMEM = pl.BlockSpec(memory_space=pltpu.SMEM)


def attend_back(queries, key_rows, value_rows, tables, stats, context_grad):
    seq_len, width = queries.shape
    head_count = width // DH
    return pl.pallas_call(
        functools.partial(attend_back_kernel, head_count, 8),
        out_shape=(
            jax.ShapeDtypeStruct((seq_len, 3 * width), jnp.bfloat16),
            jax.ShapeDtypeStruct((2, width), jnp.float32),
        ),
        in_specs=[SMEM] * 3 + [VMEM] * 6,
        out_specs=[VMEM] * 2,
        scratch_shapes=[pltpu.VMEM((seq_len // BLK, BLK, width), jnp.float32)] * 2
        + [pltpu.VMEM((8, width), jnp.float32)],
        compiler_params=pltpu.CompilerParams(vmem_limit_bytes=60 * 1024 * 1024),
        cost_estimate=pl.CostEstimate(
            flops=10 * seq_len * 512 * width * head_count,
            bytes_accessed=14 * seq_len * width,
            transcendentals=seq_len * 512 * head_count,
        ),
    )(*tables, queries, key_rows, value_rows, context_grad, *stats)


KINDS = 4
CHUNKS = 4


def front_kernel(
    levels,
    across,
    along,
    length_ref,
    globals_ref,
    random_ref,
    hidden_ref,
    grads_ref,
    b_query_ref,
    b_value_ref,
    w_query_ref,
    w_key_ref,
    w_value_ref,
    w_out_ref,
    w_up_ref,
    w_down_ref,
    b_out,
    gain1,
    shift1,
    features_far,
    own_far,
    upstream_far,
    queries_far,
    keys_far,
    values_far,
    context_far,
    highest_ref,
    scale_ref,
    full_qkv_far,
    full_out_ref,
    full_up_ref,
    full_down_ref,
    out_sib,
    up_sib,
    down_sib,
    context_sib,
    normed_full,
    unit1,
    inv1,
    features_ref,
    own_ref,
    upstream_ref,
    queries_ref,
    keys_ref,
    values_ref,
    context_ref,
    full_qkv_ref,
    far_sem,
    sum_out,
    sum_in,
    level_send,
    level_recv,
    core_send,
    core_recv,
    swap_send,
    swap_recv,
    along_send,
    along_recv,
    across_send,
    across_recv,
    shard_send,
    shard_recv,
    context_send,
    context_recv,
    sum_send,
    sum_recv,
    normed_send,
    normed_recv,
):
    low, full = jnp.bfloat16, jnp.float32
    row, column = lax.axis_index("row"), lax.axis_index("col")
    core, level = lax.rem(column, 2), lax.div(column, 2)
    fast, slow = lax.rem(row, across), lax.div(row, across)
    cols = 2 * levels
    seq_len, width = hidden_ref.shape
    own_len = seq_len // cols
    shard = w_query_ref.shape[0]
    other = 1 - core
    sibling = (row, level * 2 + other)
    offsets = range(1, levels)

    def peer_level(offset):
        return lax.rem(level + offset, levels)

    def fast_peer(offset):
        return slow * across + lax.rem(fast + offset, across)

    def line_peer(shift):
        return ((slow + shift) * across + fast, column)

    barrier = pltpu.get_barrier_semaphore()
    greeted = [sibling]
    for offset in offsets:
        greeted += [(row, peer_level(offset) * 2 + core), (row, peer_level(offset) * 2 + other)]
    greeted += [(fast_peer(offset), column) for offset in range(1, across)]
    greeted += [
        (lax.rem(slow + offset, along) * across + fast, column) for offset in range(1, along)
    ]
    for device in greeted:
        pl.semaphore_signal(barrier, inc=1, device_id=device, device_id_type=MESH)
    pl.semaphore_wait(barrier, len(greeted))

    def remote(source, target, send, recv, device):
        return pltpu.make_async_remote_copy(
            src_ref=source,
            dst_ref=target,
            send_sem=send,
            recv_sem=recv,
            device_id=device,
            device_id_type=MESH,
        )

    def block(start, size):
        return pl.ds(pl.multiple_of(start * size, size), size)

    def level_copy(turn, offset):
        rows = block(turn, own_len)
        return remote(
            hidden_ref.at[rows],
            features_ref.at[rows, block(column, width)],
            level_send.at[turn, offset - 1],
            level_recv.at[turn, levels - offset - 1],
            (row, peer_level(offset) * 2 + core),
        )

    def core_copy(turn, offset):
        view = features_ref.at[block(turn, own_len), block(peer_level(offset) * 2 + core, width)]
        return remote(
            view, view, core_send.at[turn, offset], core_recv.at[turn, offset], sibling
        )

    @pl.loop(0, cols)
    def _(turn):
        for offset in offsets:
            level_copy(turn, offset).start()
        rows = block(turn, own_len)
        features_ref[rows, block(column, width)] = hidden_ref[rows, :]
        core_copy(turn, 0).start()

    fulls = (full_qkv_ref, full_out_ref, full_up_ref, full_down_ref)
    sibs = (None, out_sib, up_sib, down_sib)

    def shard_rows(place):
        return block(place * across + fast, shard)

    def line_copy(kind, way, hop):
        view = fulls[kind].at[shard_rows(slow - (1 - 2 * way) * hop)]
        return remote(
            view,
            view,
            along_send.at[kind, way, hop],
            along_recv.at[kind, way, hop],
            line_peer(1 - 2 * way),
        )

    def line_can_send(way, hop):
        if way == 0:
            return (slow >= hop) & (slow < along - 1)
        return (slow < along - hop) & (slow > 0)

    def line_send(kind, hop):
        for way in range(2):

            @pl.when(line_can_send(way, hop))
            def _():
                line_copy(kind, way, hop).start()

    def line_got(way, hop):
        place = slow - (1 - 2 * way) * (hop + 1)
        return place, ((place >= 0) if way == 0 else (place < along))

    def line_wait(kind, way, hop):
        place, _ = line_got(way, hop)
        view = fulls[kind].at[shard_rows(place)]
        remote(
            view,
            view,
            along_send.at[kind, way, hop],
            along_recv.at[kind, way, hop],
            line_peer(-(1 - 2 * way)),
        ).wait_recv()

    def across_copy(kind, place, offset):
        view = fulls[kind].at[shard_rows(place)]
        return remote(
            view,
            view,
            across_send.at[kind, place, offset - 1],
            across_recv.at[kind, place, across - offset - 1],
            (fast_peer(offset), column),
        )

    def core_shard(kind, place, offset):
        rows = block(place * across + lax.rem(fast + offset, across), shard)
        return remote(
            fulls[kind].at[rows],
            sibs[kind].at[rows],
            shard_send.at[kind - 1, place, offset],
            shard_recv.at[kind - 1, place, offset],
            sibling,
        )

    for place, ref in enumerate((w_query_ref, w_key_ref, w_value_ref)):
        full_qkv_ref[shard_rows(slow), place * width : (place + 1) * width] = ref[...].astype(low)
    line_send(0, 0)
    full_out_ref[shard_rows(slow), :] = w_out_ref[...].T.astype(low)
    full_up_ref[shard_rows(slow), :] = w_up_ref[...].astype(low)
    full_down_ref[shard_rows(slow), :] = w_down_ref[...].T.astype(low)

    def swap_copy(target, place_out, place_in):
        return remote(
            grads_ref.at[block(target, own_len)],
            upstream_ref.at[:, block(column, width)],
            swap_send.at[place_out],
            swap_recv.at[place_in],
            (row, target),
        )

    swaps = [swap_copy(level * 2 + other, 0, 0)]
    for offset in offsets:
        back = levels - offset
        swaps.append(swap_copy(peer_level(offset) * 2 + core, 2 * offset - 1, 2 * back - 1))
        swaps.append(swap_copy(peer_level(offset) * 2 + other, 2 * offset, 2 * back))
    for copy in swaps:
        copy.start()
    upstream_ref[:, block(column, width)] = grads_ref[block(column, own_len), :]

    def pass_shard(kind, place):
        for step in range(1, across):
            across_copy(kind, place, step).start()
        if kind > 0:
            core_shard(kind, place, 0).start()

    hops = range(along - 1)
    waiting = [(1, hop) for hop in hops] + [(3, -1), (2, 0), (3, 0)]
    waiting += [(kind, hop) for hop in hops if hop > 0 for kind in (2, 3)]

    def pass_on(count=1):
        pass_these(waiting[:count])
        del waiting[:count]

    def pass_these(shards):
        for kind, hop in shards:
            if hop < 0:
                pass_shard(kind, slow)
                continue
            for way in range(2):
                place, there = line_got(way, hop)

                @pl.when(there)
                def _():
                    line_wait(kind, way, hop)
                    if hop < along - 2:

                        @pl.when(line_can_send(way, hop + 1))
                        def _():
                            line_copy(kind, way, hop + 1).start()

                    pass_shard(kind, place)
    def await_shards(kind):
        @pl.loop(0, along)
        def _(place):
            for offset in range(1, across):
                across_copy(kind, place, across - offset).wait_recv()
                if kind > 0:
                    core_shard(kind, place, offset).start()

    def await_sibling(kind):
        @pl.loop(0, along)
        def _(place):
            for offset in range(across):
                core_shard(kind, place, offset).wait_recv()

    pass_these([(0, hop) for hop in range(-1, along - 2)])
    for kind in range(1, KINDS):
        line_send(kind, 0)
    pass_these([(0, along - 2), (1, -1), (2, -1)])
    await_shards(0)

    def project(turn):
        rows = block(turn, own_len)
        for offset in offsets:
            level_copy(turn, levels - offset).wait_recv()
            core_copy(turn, offset).start()
        for offset in range(levels):
            core_copy(turn, offset).wait_recv()
        values_in = features_ref[rows, :]
        queries_ref[rows, :] = (
            dot(values_in, full_qkv_ref[:, :width]) + b_query_ref[:, block(column, width)]
        ).astype(low)
        blocks = pl.ds(turn * (own_len // BLK), own_len // BLK)
        by_block = (own_len // BLK, BLK, width)
        keys_ref[blocks] = (
            dot(values_in, full_qkv_ref[:, width : 2 * width]).astype(low).reshape(by_block)
        )
        values_ref[blocks] = (
            (dot(values_in, full_qkv_ref[:, 2 * width :]) + b_value_ref[:, block(column, width)])
            .astype(low)
            .reshape(by_block)
        )

    for turn in range(cols):
        project(turn)
        pass_on(1 if (3, -1) in waiting else 0)
    while (2, 0) in waiting:
        pass_on()
    own_ref[...] = features_ref[block(column, own_len), :]
    far = [
        pltpu.make_async_copy(source, target, far_sem.at[place])
        for place, (source, target) in enumerate(
            [
                (features_ref, features_far),
                (own_ref, own_far),
                (queries_ref, queries_far),
                (keys_ref, keys_far),
                (values_ref, values_far),
                (full_qkv_ref, full_qkv_far),
                (upstream_ref, upstream_far),
                (context_ref, context_far),
            ]
        )
    ]
    @pl.loop(0, cols)
    def _(turn):
        for offset in range(levels):
            core_copy(turn, offset).wait_send()

    for copy in far[:6]:
        copy.start()

    step = own_len // CHUNKS
    halves = 2
    count = own_len // BLK // halves

    def attend_half(quarter, half):
        attend_blocks(
            (quarter * halves + half) * count,
            count,
            min(count, 4),
            length_ref,
            globals_ref,
            random_ref,
            (queries_ref, keys_ref, values_ref),
            context_ref,
            (highest_ref, scale_ref),
        )

    def context_copy(place, half):
        rows = own_len // halves
        return remote(
            context_ref.at[block((place * 2 + other) * halves + half, rows)],
            context_sib.at[block(place * halves + half, rows)],
            context_send.at[place, half],
            context_recv.at[place, half],
            sibling,
        )

    def chunk_rows(place, chunk):
        return block(place * CHUNKS + chunk, step)

    def attn_part(place, chunk):
        return dot_nt(
            context_ref[chunk_rows(place * 2 + core, chunk), :], full_out_ref[...]
        ) + dot_nt(context_sib[chunk_rows(place, chunk), :], out_sib[...])

    def sum_copy(chunk, offset):
        rows = block(chunk, step)
        return remote(
            sum_out.at[offset - 1, rows],
            sum_in.at[levels - offset - 1, rows],
            sum_send.at[chunk, offset - 1],
            sum_recv.at[chunk, levels - offset - 1],
            (row, peer_level(offset) * 2 + core),
        )

    def normed_copy(chunk, offset):
        view = normed_full.at[chunk_rows(level, chunk)]
        return remote(
            view,
            view,
            normed_send.at[chunk, offset - 1],
            normed_recv.at[chunk, levels - offset - 1],
            (row, peer_level(offset) * 2 + core),
        )

    for offset in list(offsets) + [0]:
        place = peer_level(offset)
        for half in range(halves):
            attend_half(place * 2 + other, half)
            context_copy(place, half).start()
            pass_on(1 - half if offset else half)
        if offset == 1:
            await_shards(1)
        for half in range(halves):
            attend_half(place * 2 + core, half)
            if offset == 1 and half == 0:
                await_sibling(1)
            context_copy(place, half).wait_recv()
            per_half = CHUNKS // halves
            for chunk in range(half * per_half, (half + 1) * per_half):
                if offset:
                    sum_out[offset - 1, block(chunk, step), :] = attn_part(place, chunk).astype(
                        low
                    )
                    sum_copy(chunk, offset).start()
            pass_on(1 if offset else half)
    pass_on(len(waiting))
    for copy in swaps:
        copy.wait()
    for copy in far[6:]:
        copy.start()
    for chunk in range(CHUNKS):
        rows = block(chunk, step)
        summed = own_ref[rows, :].astype(full) + attn_part(level, chunk) + b_out[...]
        for offset in offsets:
            sum_copy(chunk, offset).wait_recv()
        for place in range(levels - 1):
            summed += sum_in[place, rows, :].astype(full)
        normed, inv_std = norm_parts(summed)
        unit1[rows, :] = normed
        inv1[rows, :] = inv_std
        normed_full[chunk_rows(level, chunk), :] = (normed * gain1[...] + shift1[...]).astype(low)
        for offset in offsets:
            normed_copy(chunk, offset).start()
    await_shards(2)
    await_shards(3)
    for chunk in range(CHUNKS):
        for offset in offsets:
            normed_copy(chunk, offset).wait()
            sum_copy(chunk, offset).wait_send()
    for kind in range(2, KINDS):
        await_sibling(kind)
    for place in range(levels):
        for half in range(halves):
            context_copy(place, half).wait_send()
    for copy in far:
        copy.wait()
    for kind in range(KINDS):
        for hop in range(along - 1):
            for way in range(2):

                @pl.when(line_can_send(way, hop))
                def _():
                    line_copy(kind, way, hop).wait_send()

        @pl.loop(0, along)
        def _(place):
            for offset in range(1, across):
                across_copy(kind, place, offset).wait_send()
            if kind > 0:
                for offset in range(across):
                    core_shard(kind, place, offset).wait_send()

    @pl.loop(0, cols)
    def _(turn):
        for offset in offsets:
            level_copy(turn, offset).wait_send()


def across_of(rows):
    return 2 if rows <= 8 else rows // 4


def front(levels, rows, tables, hidden_in, grads, biases, weights, vectors):
    low, full = jnp.bfloat16, jnp.float32
    shape = jax.ShapeDtypeStruct
    across = across_of(rows)
    along = rows // across
    seq_len, width = hidden_in.shape
    cols = 2 * levels
    own_len = seq_len // cols
    features_all = width * cols
    units = weights[4].shape[1]
    widths = (3 * width, width, units, units)
    others = levels - 1
    stat = shape((seq_len // BLK, 1, width), full)
    hbm = pl.BlockSpec(memory_space=pl.ANY)
    dma = pltpu.SemaphoreType.DMA
    return pl.pallas_call(
        functools.partial(front_kernel, levels, across, along),
        out_shape=(
            shape((seq_len, features_all), low),
            shape((own_len, features_all), low),
            shape((own_len, features_all), low),
            shape((seq_len, width), low),
            shape((seq_len // BLK, BLK, width), low),
            shape((seq_len // BLK, BLK, width), low),
            shape((seq_len, width), low),
            stat,
            stat,
            *(shape((features_all, each), low) for each in widths),
            *(shape((features_all, each), low) for each in widths[1:]),
            shape((levels * own_len, width), low),
            shape((levels * own_len, features_all), low),
            shape((own_len, features_all), full),
            shape((own_len, 1), full),
        ),
        in_specs=[SMEM] * 3 + [VMEM] * 13,
        out_specs=[hbm] * 7 + [VMEM] * 2 + [hbm] + [VMEM] * 10,
        scratch_shapes=[
            pltpu.VMEM((seq_len, features_all), low),
            pltpu.VMEM((own_len, features_all), low),
            pltpu.VMEM((own_len, features_all), low),
            pltpu.VMEM((seq_len, width), low),
            pltpu.VMEM((seq_len // BLK, BLK, width), low),
            pltpu.VMEM((seq_len // BLK, BLK, width), low),
            pltpu.VMEM((seq_len, width), low),
            pltpu.VMEM((features_all, 3 * width), low),
            dma((8,)),
            pltpu.VMEM((others, own_len, features_all), low),
            pltpu.VMEM((others, own_len, features_all), low),
            dma((cols, others)),
            dma((cols, others)),
            dma((cols, levels)),
            dma((cols, levels)),
            dma((cols,)),
            dma((cols,)),
            dma((KINDS, 2, along - 1)),
            dma((KINDS, 2, along - 1)),
            dma((KINDS, along, across - 1)),
            dma((KINDS, along, across - 1)),
            dma((KINDS - 1, along, across)),
            dma((KINDS - 1, along, across)),
            dma((levels, 2)),
            dma((levels, 2)),
            *(dma((CHUNKS, others)) for _ in range(4)),
        ],
        compiler_params=pltpu.CompilerParams(
            collective_id=3, has_side_effects=True, vmem_limit_bytes=56 * 1024 * 1024
        ),
        cost_estimate=pl.CostEstimate(
            flops=2 * seq_len * features_all * 3 * width,
            bytes_accessed=20 * 1024 * 1024,
            transcendentals=seq_len * 512 * (width // DH),
        ),
    )(*tables, hidden_in, grads, *biases, *weights, *vectors)


def dot(left, right):
    return jnp.dot(left, right, preferred_element_type=jnp.float32)


def dot_nt(left, right):
    return lax.dot_general(
        left, right, (((1,), (1,)), ((), ())), preferred_element_type=jnp.float32
    )


def dot_tn(left, right):
    return lax.dot_general(
        left, right, (((0,), (0,)), ((), ())), preferred_element_type=jnp.float32
    )


def gelu_parts(values_in):
    factor = math.sqrt(2.0 / math.pi)
    square = values_in * values_in
    bent = jnp.tanh(factor * (values_in + 0.044715 * (values_in * square)))
    half = 0.5 * (1.0 + bent)
    slope = half + (0.5 * values_in) * (1.0 - bent * bent) * (
        factor + (3.0 * 0.044715 * factor) * square
    )
    return (values_in * half, slope)


def norm_parts(summed):
    average = jnp.mean(summed, axis=1, keepdims=True)
    squares = jnp.mean(summed * summed, axis=1, keepdims=True)
    inv_std = lax.rsqrt(squares - average * average + epsilon)
    return ((summed - average) * inv_std, inv_std)


def norm_back(upstream, normed, inv_std, gain_vec):
    scaled = upstream * gain_vec
    left = jnp.mean(scaled, axis=1, keepdims=True)
    right = jnp.mean(scaled * normed, axis=1, keepdims=True)
    return inv_std * (scaled - left - normed * right)


def middle_kernel(
    levels,
    across,
    along,
    length_ref,
    context_far,
    context_sib_far,
    upstream_far,
    out_far,
    out_sib_far,
    up_ref,
    up_sib,
    down_full,
    down_sib,
    normed_full,
    unit1_far,
    inv1,
    gain1,
    shift1,
    b_down,
    gain2,
    shift2,
    b_up_ref,
    layer_out_ref,
    context_grad_ref,
    attn_full,
    small_ref,
    up_small_ref,
    share_down_ref,
    up_own_ref,
    grad_out_ref,
    *more,
):
    up_part_refs, refs = more[: along - 1], more[along - 1 :]
    (
        ffn_full,
        hidden,
        slope,
        pre_grad,
        ffn_keep,
        part_own,
        send_buf,
        recv_buf,
        context_send,
        stage,
        down_sums,
        up_sums,
        down_got,
        up_got,
        down_pass,
        down_in,
        send_sem,
        recv_sem,
        core_send,
        core_recv,
        along_send,
        along_recv,
        across_send,
        across_recv,
        stage_sem,
        context_ref,
        context_sib,
        upstream_ref,
        out_ref,
        out_sib,
        unit1,
        late_sem,
    ) = refs
    low = jnp.bfloat16
    row, column = lax.axis_index("row"), lax.axis_index("col")
    core = lax.rem(column, 2)
    level = lax.div(column, 2)
    sibling = (row, column + 1 - 2 * core)
    fast, slow = lax.rem(row, across), lax.div(row, across)
    shard = share_down_ref.shape[0]
    own_len = upstream_ref.shape[0]
    units = up_ref.shape[1]
    step = own_len // CHUNKS

    def peer_level(offset):
        return lax.rem(level + offset, levels)

    def fast_peer(offset):
        return slow * across + lax.rem(fast + offset, across)

    late = [
        pltpu.make_async_copy(source, target, late_sem.at[place])
        for place, (source, target) in enumerate(
            [
                (unit1_far, unit1),
                (upstream_far, upstream_ref),
                (context_far, context_ref),
                (context_sib_far, context_sib),
                (out_far, out_ref),
                (out_sib_far, out_sib),
            ]
        )
    ]
    for copy in late:
        copy.start()

    barrier = pltpu.get_barrier_semaphore()
    greeted = [sibling]
    greeted += [(row, peer_level(offset) * 2 + core) for offset in range(1, levels)]
    greeted += [(fast_peer(offset), column) for offset in range(1, across)]
    greeted += [
        (lax.rem(slow + offset, along) * across + fast, column) for offset in range(1, along)
    ]
    for device in greeted:
        pl.semaphore_signal(barrier, inc=1, device_id=device, device_id_type=MESH)
    pl.semaphore_wait(barrier, len(greeted))

    def remote(source, target, send, recv, device):
        return pltpu.make_async_remote_copy(
            src_ref=source,
            dst_ref=target,
            send_sem=send,
            recv_sem=recv,
            device_id=device,
            device_id_type=MESH,
        )

    def block(start, size):
        return pl.ds(pl.multiple_of(start * size, size), size)

    def to_sibling(source, target, place):
        return remote(source, target, core_send.at[place], core_recv.at[place], sibling)

    def rows_of(place, chunk):
        return pl.ds(pl.multiple_of(place * own_len + chunk * step, step), step)

    def own_rows(chunk):
        return pl.ds(pl.multiple_of(chunk * step, step), step)

    def exchange(kind, chunk, offset, source, target):
        return pltpu.make_async_remote_copy(
            src_ref=source,
            dst_ref=target,
            send_sem=send_sem.at[kind - 2, chunk, offset - 1],
            recv_sem=recv_sem.at[kind - 2, chunk, levels - offset - 1],
            device_id=(row, peer_level(offset) * 2 + core),
            device_id_type=MESH,
        )

    def sum_copy(kind, chunk, offset):
        return exchange(
            kind,
            chunk,
            offset,
            send_buf.at[kind // 2 - 1, offset - 1, own_rows(chunk)],
            recv_buf.at[kind // 2 - 1, levels - offset - 1, own_rows(chunk)],
        )

    def spread_copy(kind, chunk, offset):
        whole = {3: ffn_full, 5: attn_full}[kind]
        rows = rows_of(level, chunk)
        return exchange(kind, chunk, offset, whole.at[rows], whole.at[rows])

    def received(kind, chunk):
        return sum(
            recv_buf[kind // 2 - 1, place, own_rows(chunk), :].astype(jnp.float32)
            for place in range(levels - 1)
        )

    offsets = range(1, levels)
    small_ref[...] = jnp.zeros_like(small_ref)
    up_small_ref[...] = jnp.zeros_like(up_small_ref)
    def context_rows(place, chunk):
        start = (place * 2 + core) * own_len + chunk * step
        return pl.ds(pl.multiple_of(start, step), step)

    sides = ((up_ref, down_full), (up_sib, down_sib))

    def feed_forward(place, chunk):
        rows = rows_of(place, chunk)
        normed = normed_full[rows, :]
        total = None
        for side, (up_side, down_side) in enumerate(sides):
            bias = b_up_ref[:, block(column + side * (1 - 2 * core), units)]
            active, bend = gelu_parts(dot(normed, up_side[...]) + bias)
            active = active.astype(low)
            hidden[side, rows, :] = active
            slope[side, rows, :] = bend.astype(low)
            part = dot_nt(active, down_side[...])
            total = part if total is None else total + part
        return total

    @pl.loop(0, CHUNKS)
    def _(chunk):
        for offset in offsets:
            send_buf[0, offset - 1, own_rows(chunk), :] = feed_forward(
                peer_level(offset), chunk
            ).astype(low)
            sum_copy(2, chunk, offset).start()

    for copy in late:
        copy.wait()

    @pl.loop(0, CHUNKS)
    def _(chunk):
        rows = own_rows(chunk)
        part_own[rows, :] = feed_forward(level, chunk)
        normed1 = unit1[rows, :] * gain1[...] + shift1[...]
        summed = normed1 + part_own[rows, :] + b_down[...]
        for offset in offsets:
            sum_copy(2, chunk, offset).wait_recv()
        normed, inv_std = norm_parts(summed + received(2, chunk))
        position = lax.broadcasted_iota(jnp.int32, (step, 1), 0) + (
            column * own_len + chunk * step
        )
        valid = position < length_ref[0]
        layer_out_ref[rows, :] = jnp.where(
            valid, normed * gain2[...] + shift2[...], 0.0
        ).astype(low)
        upstream = jnp.where(valid, upstream_ref[rows, :].astype(jnp.float32), 0.0)
        grad = norm_back(upstream, normed, inv_std, gain2[...])
        ffn_keep[rows, :] = grad
        grad_low = grad.astype(low)
        ffn_full[rows_of(level, chunk), :] = grad_low
        for offset in offsets:
            spread_copy(3, chunk, offset).start()
        small_ref[0:1, :] += jnp.sum(upstream * normed, axis=0, keepdims=True)
        small_ref[1:2, :] += jnp.sum(upstream, axis=0, keepdims=True)
        small_ref[2:3, :] += jnp.sum(grad_low.astype(jnp.float32), axis=0, keepdims=True)

    def feed_back(place, chunk):
        rows = rows_of(place, chunk)
        upstream = ffn_full[rows, :]
        total = None
        for side, (up_side, down_side) in enumerate(sides):
            grad = (
                dot(upstream, down_side[...]) * slope[side, rows, :].astype(jnp.float32)
            ).astype(low)
            pre_grad[side, rows, :] = grad
            up_small_ref[side : side + 1, :] += jnp.sum(
                grad.astype(jnp.float32), axis=0, keepdims=True
            )
            part = dot_nt(grad, up_side[...])
            total = part if total is None else total + part
        return total

    @pl.loop(0, CHUNKS)
    def _(chunk):
        part_own[own_rows(chunk), :] = feed_back(level, chunk)
        for offset in offsets:
            spread_copy(3, chunk, levels - offset).wait_recv()
            send_buf[1, offset - 1, own_rows(chunk), :] = feed_back(
                peer_level(offset), chunk
            ).astype(low)
            sum_copy(4, chunk, offset).start()

    tile = across * shard
    lefts, rights = (ffn_full, normed_full), (hidden, pre_grad)
    sums, got = (down_sums, up_sums), (down_got, up_got)

    def grad_tile(kind, side, turn):
        return dot_tn(lefts[kind][:, block(turn, tile)], rights[kind][side])

    def core_grad(kind):
        return to_sibling(
            slope.at[kind, : sums[kind].shape[0]], sums[kind], levels + kind
        )

    def across_grad(kind, turn, offset):
        return remote(
            sums[kind].at[block(turn * across + lax.rem(fast + offset, across), shard)],
            got[kind].at[across - offset - 1, block(turn, shard)],
            across_send.at[kind, turn, offset - 1],
            across_recv.at[kind, turn, across - offset - 1],
            (fast_peer(offset), column),
        )

    def own_shard(kind, turn):
        for offset in range(1, across):
            across_grad(kind, turn, offset).wait_recv()
        total = sums[kind][block(turn * across + fast, shard), :].astype(jnp.float32)
        for place in range(across - 1):
            total += got[kind][place, block(turn, shard), :].astype(jnp.float32)
        return total

    def line_peer(shift):
        return ((slow + shift) * across + fast, column)

    def line_copy(kind, way, target):
        return remote(
            line_out[kind].at[way, target],
            line_in[kind].at[way, target],
            along_send.at[kind, way, target],
            along_recv.at[kind, way, target],
            line_peer(1 - 2 * way),
        )

    def line_step(kind, hop):
        for way in range(2):
            position = hop if way == 0 else along - 1 - hop
            targets = range(along - 1, hop, -1) if way == 0 else range(0, along - 1 - hop)

            @pl.when(slow == position)
            def _():
                for target in targets:
                    total = own_shard(kind, target)
                    if hop > 0:
                        line_copy(kind, way, target).wait_recv()
                        total += line_in[kind][way, target].astype(jnp.float32)
                    line_out[kind][way, target] = total.astype(jnp.bfloat16)
                    line_copy(kind, way, target).start()

    def line_finish(kind):
        for way in range(2):

            @pl.when((slow > 0) if way == 0 else (slow < along - 1))
            def _():
                line_copy(kind, way, slow).wait_recv()
                shares[kind][...] += line_in[kind][way, slow].astype(jnp.float32)

    def line_sent(kind):
        for way in range(2):
            for target in range(along):

                @pl.when((slow < target) if way == 0 else (slow > target))
                def _():
                    line_copy(kind, way, target).wait_send()

    def sum_grad(kind):
        core_grad(kind).wait_recv()

        @pl.loop(0, along)
        def _(turn):
            rows = block(turn, tile)
            sums[kind][rows, :] = (
                grad_tile(kind, 0, turn) + sums[kind][rows, :].astype(jnp.float32)
            ).astype(low)
            for offset in range(1, across):
                across_grad(kind, turn, offset).start()

    line_out, line_in, shares = (down_pass,), (down_in,), (share_down_ref,)
    for kind in range(2):

        @pl.loop(0, along)
        def _(turn):
            slope[kind, block(turn, tile), :] = grad_tile(kind, 1, turn).astype(low)

        core_grad(kind).start()
        if kind:
            sum_grad(kind - 1)
    sum_grad(1)

    @pl.loop(0, CHUNKS)
    def _(chunk):
        rows = own_rows(chunk)
        upstream = ffn_keep[rows, :] + part_own[rows, :]
        for offset in offsets:
            sum_copy(4, chunk, offset).wait_recv()
        upstream = upstream + received(4, chunk)
        normed = unit1[rows, :]
        grad_low = norm_back(upstream, normed, inv1[rows, :], gain1[...]).astype(low)
        attn_full[rows_of(level, chunk), :] = grad_low
        for offset in offsets:
            spread_copy(5, chunk, offset).start()
        small_ref[3:4, :] += jnp.sum(upstream * normed, axis=0, keepdims=True)
        small_ref[4:5, :] += jnp.sum(upstream, axis=0, keepdims=True)
        small_ref[5:6, :] += jnp.sum(grad_low.astype(jnp.float32), axis=0, keepdims=True)

    share_down_ref[...] = own_shard(0, slow)
    line_step(0, 0)

    def context_back(place, chunk):
        rows = rows_of(place, chunk)
        upstream = attn_full[rows, :]
        context_grad_ref[context_rows(place, chunk), :] = dot(upstream, out_ref[...]).astype(low)
        context_send[rows, :] = dot(upstream, out_sib[...]).astype(low)

    for chunk in range(CHUNKS):
        context_back(level, chunk)
        for offset in offsets:
            spread_copy(5, chunk, levels - offset).wait_recv()
            context_back(peer_level(offset), chunk)
        if 0 < chunk < along - 1:
            line_step(0, chunk)
    for hop in range(CHUNKS, along - 1):
        line_step(0, hop)

    back_copies = [
        to_sibling(
            context_send.at[pl.ds(place * own_len, own_len)],
            context_grad_ref.at[
                pl.ds(pl.multiple_of((place * 2 + core) * own_len, own_len), own_len)
            ],
            place,
        )
        for place in range(levels)
    ]
    for copy in back_copies:
        copy.start()

    own_context = jnp.concatenate(
        [
            context_ref[
                pl.ds(pl.multiple_of((place * 2 + core) * own_len, own_len), own_len), :
            ]
            for place in range(levels)
        ],
        axis=0,
    )

    def out_put(side):
        return pltpu.make_async_copy(stage.at[side], grad_out_ref.at[side], stage_sem.at[side])

    for side, right in enumerate((own_context, context_sib[...])):
        stage[side] = dot_tn(attn_full[...], right).astype(low)
        out_put(side).start()
    for shift in range(1, along):
        up_part_refs[shift - 1][...] = own_shard(1, lax.rem(slow + shift, along)).astype(low)
    up_own_ref[...] = own_shard(1, slow)
    line_finish(0)
    for side in range(2):
        out_put(side).wait()
    for kind in range(2):
        core_grad(kind).wait_send()
    line_sent(0)

    @pl.loop(0, along)
    def _(place):
        for offset in range(1, across):
            across_grad(0, place, offset).wait_send()
            across_grad(1, place, offset).wait_send()

    for copy in back_copies:
        copy.wait()
    for kind in range(2, 6):

        @pl.loop(0, CHUNKS)
        def _(chunk):
            for offset in offsets:
                if kind % 2:
                    spread_copy(kind, chunk, offset).wait_send()
                else:
                    sum_copy(kind, chunk, offset).wait_send()


def middle(
    levels,
    rows,
    length,
    context,
    context_sib,
    upstream,
    weights,
    normed_full,
    unit1,
    inv1,
    vectors,
    b_up,
):
    low, full = jnp.bfloat16, jnp.float32
    across = across_of(rows)
    along = rows // across
    own_len, features = upstream.shape
    seq_len, width = context.shape
    units = weights[2].shape[1]
    shard = features // rows
    tokens = levels * own_len
    others = levels - 1
    shape = jax.ShapeDtypeStruct
    hbm = pl.BlockSpec(memory_space=pl.ANY)
    dma = pltpu.SemaphoreType.DMA
    vmem = pltpu.VMEM
    return pl.pallas_call(
        functools.partial(middle_kernel, levels, across, along),
        out_shape=(
            shape((own_len, features), low),
            shape((seq_len, width), low),
            shape((tokens, features), low),
            shape((8, features), full),
            shape((2, units), full),
            shape((shard, units), full),
            shape((shard, units), full),
            shape((2, features, width), low),
            *(shape((shard, units), low) for _ in range(along - 1)),
        ),
        in_specs=[SMEM] + [hbm] * 5 + [VMEM] * 5 + [hbm] + [VMEM] * 7,
        out_specs=[VMEM] * 7 + [hbm] + [VMEM] * (along - 1),
        scratch_shapes=[
            vmem((tokens, features), low),
            vmem((2, tokens, units), low),
            vmem((2, max(tokens, features), units), low),
            vmem((2, tokens, units), low),
            vmem((own_len, features), full),
            vmem((own_len, features), full),
            vmem((2, others, own_len, features), low),
            vmem((2, others, own_len, features), low),
            vmem((tokens, width), low),
            vmem((2, features, width), low),
            vmem((features, units), low),
            vmem((features, units), low),
            vmem((across - 1, along * shard, units), low),
            vmem((across - 1, along * shard, units), low),
            vmem((2, along, shard, units), low),
            vmem((2, along, shard, units), low),
            dma((4, CHUNKS, others)),
            dma((4, CHUNKS, others)),
            dma((levels + 2,)),
            dma((levels + 2,)),
            dma((1, 2, along)),
            dma((1, 2, along)),
            dma((2, along, across - 1)),
            dma((2, along, across - 1)),
            dma((2,)),
            vmem((seq_len, width), low),
            vmem((tokens, width), low),
            vmem((own_len, features), low),
            vmem((features, width), low),
            vmem((features, width), low),
            vmem((own_len, features), full),
            dma((6,)),
        ],
        compiler_params=pltpu.CompilerParams(
            collective_id=1, has_side_effects=True, vmem_limit_bytes=62 * 1024 * 1024
        ),
        cost_estimate=pl.CostEstimate(
            flops=2 * tokens * features * (12 * units + 6 * width),
            bytes_accessed=20 * 1024 * 1024,
            transcendentals=2 * tokens * units,
        ),
    )(
        length,
        context,
        context_sib,
        upstream,
        *weights,
        normed_full,
        unit1,
        inv1,
        *vectors,
        b_up,
    )


def end_kernel(
    levels,
    across,
    along,
    query_key_value_ref,
    weights_ref,
    features_ref,
    attn_ref,
    layer_ref,
    small_ref,
    up_small_ref,
    bias_ref,
    out_ref,
    grad_input_ref,
    layer_out_ref,
    small_out_ref,
    share_ref,
    out_sib,
    sums,
    got,
    line_out,
    line_in,
    core_out,
    core_in,
    level_out,
    level_in,
    attn_in,
    attn_own,
    small_sums,
    small_in,
    core_send,
    core_recv,
    part_send,
    part_recv,
    level_send,
    level_recv,
    layer_send,
    layer_recv,
    across_send,
    across_recv,
    along_send,
    along_recv,
    small_send,
    small_recv,
    keep_sem,
):
    low, full = jnp.bfloat16, jnp.float32
    row, column = lax.axis_index("row"), lax.axis_index("col")
    core, level = lax.rem(column, 2), lax.div(column, 2)
    fast, slow = lax.rem(row, across), lax.div(row, across)
    cols = 2 * levels
    seq_len = features_ref.shape[0]
    own_len = seq_len // cols
    width = grad_input_ref.shape[1]
    shard = share_ref.shape[0]
    other = 1 - core
    sibling = (row, level * 2 + other)
    offsets = range(1, levels)

    def peer_level(offset):
        return lax.rem(level + offset, levels)

    def fast_peer(offset):
        return slow * across + lax.rem(fast + offset, across)

    def slow_peer(offset):
        return lax.rem(slow + offset, along) * across + fast

    barrier = pltpu.get_barrier_semaphore()
    greeted = [sibling]
    for offset in offsets:
        greeted += [(row, peer_level(offset) * 2 + core), (row, peer_level(offset) * 2 + other)]
    greeted += [(fast_peer(offset), column) for offset in range(1, across)]
    greeted += [(slow_peer(offset), column) for offset in range(1, along)]
    for device in greeted:
        pl.semaphore_signal(barrier, inc=1, device_id=device, device_id_type=MESH)
    pl.semaphore_wait(barrier, len(greeted))

    def remote(source, target, send, recv, device):
        return pltpu.make_async_remote_copy(
            src_ref=source,
            dst_ref=target,
            send_sem=send,
            recv_sem=recv,
            device_id=device,
            device_id_type=MESH,
        )

    def block(start, size):
        return pl.ds(pl.multiple_of(start * size, size), size)

    out_copy = remote(out_ref.at[1], out_sib, core_send.at[0], core_recv.at[0], sibling)
    attn_copy = remote(
        attn_ref.at[:, block(level * 2 + other, width)],
        attn_in,
        core_send.at[1],
        core_recv.at[1],
        sibling,
    )

    partners = []
    bit = 1
    while bit < levels:
        partners.append((row, (level + bit - 2 * bit * lax.rem(lax.div(level, bit), 2)) * 2 + core))
        bit *= 2
    bit = 1
    while bit < across * along:
        partners.append((row + bit - 2 * bit * lax.rem(lax.div(row, bit), 2), column))
        bit *= 2
    partners.append(sibling)

    def small_copy(turn):
        return remote(
            small_sums.at[turn],
            small_in.at[turn],
            small_send.at[turn],
            small_recv.at[turn],
            partners[turn],
        )

    small_turn = [0]

    def small_step():
        turn = small_turn[0]
        if turn > len(partners):
            return
        if turn > 0:
            small_copy(turn - 1).wait()
            small_sums[turn] = small_sums[turn - 1] + small_in[turn - 1]
        if turn < len(partners):
            small_copy(turn).start()
        small_turn[0] += 1

    def layer_copy(target, place_out, place_in):
        return remote(
            layer_ref.at[:, block(target, width)],
            layer_out_ref.at[block(column, own_len)],
            layer_send.at[place_out],
            layer_recv.at[place_in],
            (row, target),
        )

    layer_copies = [layer_copy(level * 2 + other, 0, 0)]
    for offset in offsets:
        back = levels - offset
        layer_copies.append(
            layer_copy(peer_level(offset) * 2 + core, 2 * offset - 1, 2 * back - 1)
        )
        layer_copies.append(layer_copy(peer_level(offset) * 2 + other, 2 * offset, 2 * back))
    layer_keep = pltpu.make_async_copy(
        layer_ref.at[:, block(column, width)], layer_out_ref.at[block(column, own_len)], keep_sem.at[0]
    )
    attn_keep = pltpu.make_async_copy(
        attn_ref.at[:, block(column, width)], attn_own, keep_sem.at[1]
    )
    attn_keep.start()

    features_all = weights_ref.shape[0]
    units = up_small_ref.shape[1]
    first_up = small_ref.shape[0]
    small_sums[0] = jnp.zeros_like(small_in[0])
    small_sums[0, :first_up, :] = small_ref[...]
    for side in range(2):
        start = (column + side * (1 - 2 * core)) * units
        small_sums[
            0,
            pl.ds(first_up + lax.div(start, features_all), 1),
            pl.ds(pl.multiple_of(lax.rem(start, features_all), units), units),
        ] = up_small_ref[side : side + 1, :]
    first_bias = small_in.shape[1] - 4
    small_sums[0, first_bias : first_bias + 2, block(column, width)] = bias_ref[...]
    small_step()
    out_copy.start()
    attn_copy.start()
    layer_keep.start()
    for copy in layer_copies:
        copy.start()

    def input_part(turn, target):
        return dot_nt(
            query_key_value_ref[block(turn, own_len), :], weights_ref[block(target, width), :]
        )

    def part_copy(turn, place):
        rows = block(turn, own_len)
        return remote(
            core_out.at[place, rows],
            core_in.at[place, rows],
            part_send.at[turn, place],
            part_recv.at[turn, place],
            sibling,
        )

    def give_core():
        @pl.loop(0, cols)
        def _(turn):
            for place in range(levels):
                core_out[place, block(turn, own_len), :] = input_part(
                    turn, place * 2 + other
                ).astype(low)
                part_copy(turn, place).start()

    def across_copy(turn, offset):
        return remote(
            sums.at[block(turn * across + lax.rem(fast + offset, across), shard)],
            got.at[across - offset - 1, block(turn, shard)],
            across_send.at[turn, offset - 1],
            across_recv.at[turn, across - offset - 1],
            (fast_peer(offset), column),
        )

    def weight_grad(turn):
        rows = block(turn, across * shard)
        sums[rows, : 3 * width] = dot_tn(features_ref[:, rows], query_key_value_ref[...]).astype(
            low
        )
        sums[rows, 3 * width :] = (
            out_ref[0, rows, :].astype(full) + out_sib[rows, :].astype(full)
        ).astype(low)
        for offset in range(1, across):
            across_copy(turn, offset).start()

    def level_copy(turn, offset):
        rows = block(turn, own_len)
        return remote(
            level_out.at[offset - 1, rows],
            level_in.at[levels - offset - 1, rows],
            level_send.at[turn, offset - 1],
            level_recv.at[turn, levels - offset - 1],
            (row, peer_level(offset) * 2 + core),
        )

    def give_levels():
        @pl.loop(0, cols)
        def _(turn):
            rows = block(turn, own_len)
            for offset in offsets:
                place = peer_level(offset)
                part = input_part(turn, place * 2 + core)
                part_copy(turn, place).wait_recv()
                level_out[offset - 1, rows, :] = (
                    part + core_in[place, rows, :].astype(full)
                ).astype(low)
                level_copy(turn, offset).start()

    def own_shard(turn):
        for offset in range(1, across):
            across_copy(turn, offset).wait_recv()
        total = sums[block(turn * across + fast, shard), :].astype(full)
        for place in range(across - 1):
            total += got[place, block(turn, shard), :].astype(full)
        return total

    def line_copy(way, target):
        return remote(
            line_out.at[way, target],
            line_in.at[way, target],
            along_send.at[way, target],
            along_recv.at[way, target],
            ((slow + 1 - 2 * way) * across + fast, column),
        )

    def line_step(hop, near):
        if hop >= along - 1 - near:
            return
        for way in range(2):
            target = along - 1 - near if way == 0 else near
            position = hop if way == 0 else along - 1 - hop

            @pl.when(slow == position)
            def _():
                total = own_shard(target)
                if hop > 0:
                    line_copy(way, target).wait_recv()
                    total += line_in[way, target].astype(full)
                line_out[way, target] = total.astype(low)
                line_copy(way, target).start()

    def finish_input(turn, attn_part):
        rows = block(turn, own_len)
        total = input_part(turn, column) + attn_part.astype(full)
        part_copy(turn, level).wait_recv()
        total += core_in[level, rows, :].astype(full)
        for offset in offsets:
            level_copy(turn, offset).wait_recv()
        for place in range(levels - 1):
            total += level_in[place, rows, :].astype(full)
        grad_input_ref[rows, :] = total.astype(low)

    ends = [turn for place in range(along // 2) for turn in (along - 1 - place, place)]
    out_copy.wait()
    small_step()
    for place, turn in enumerate(ends):
        weight_grad(turn)
        if place % 2:
            small_step()
    give_core()
    small_step()
    give_levels()
    small_step()
    line_steps = sorted(
        ((hop, near) for near in range(along - 1) for hop in range(along - 1 - near)),
        key=lambda step: step[0] + 2 * step[1],
    )
    for step in line_steps[: len(line_steps) // 3]:
        line_step(*step)
    attn_keep.wait()
    attn_copy.wait()
    for place in range(levels):
        for step in line_steps[len(line_steps) // 3 :][place::levels]:
            line_step(*step)
        rows = block(place, own_len)
        finish_input(place * 2 + core, attn_own[rows, :])
        finish_input(place * 2 + other, attn_in[rows, :])
    share_ref[...] = own_shard(slow)
    while small_turn[0] <= len(partners):
        small_step()
    small_out_ref[...] = small_sums[len(partners)]

    for way in range(2):

        @pl.when((slow > 0) if way == 0 else (slow < along - 1))
        def _():
            line_copy(way, slow).wait_recv()
            share_ref[...] += line_in[way, slow].astype(full)

    layer_keep.wait()
    for copy in layer_copies:
        copy.wait()
    for way in range(2):
        for target in range(along):

            @pl.when((slow < target) if way == 0 else (slow > target))
            def _():
                line_copy(way, target).wait_send()

    @pl.loop(0, along)
    def _(turn):
        for offset in range(1, across):
            across_copy(turn, offset).wait_send()

    @pl.loop(0, cols)
    def _(turn):
        for place in range(levels):
            part_copy(turn, place).wait_send()
        for offset in offsets:
            level_copy(turn, offset).wait_send()


def finish(
    levels, rows, query_key_value, weights, features, attn_full, layer_own, small, up_small, bias, out
):
    low, full = jnp.bfloat16, jnp.float32
    shape = jax.ShapeDtypeStruct
    across = across_of(rows)
    along = rows // across
    seq_len, features_all = features.shape
    width = query_key_value.shape[1] // 3
    own_len = layer_own.shape[0]
    shard = features_all // rows
    others = levels - 1
    cols = 2 * levels
    turns = 1 + (levels - 1).bit_length() + (rows - 1).bit_length()
    small_rows = small.shape[0] + up_small.shape[1] * cols // features_all + 4
    dma = pltpu.SemaphoreType.DMA
    vmem = pltpu.VMEM
    return pl.pallas_call(
        functools.partial(end_kernel, levels, across, along),
        out_shape=(
            shape((seq_len, width), low),
            shape((seq_len, width), low),
            shape((small_rows, features_all), full),
            shape((shard, 4 * width), full),
        ),
        in_specs=[VMEM] * 3 + [pl.BlockSpec(memory_space=pl.ANY)] * 2 + [VMEM] * 4,
        out_specs=[VMEM] * 4,
        scratch_shapes=[
            vmem((features_all, width), low),
            vmem((features_all, 4 * width), low),
            vmem((across - 1, along * shard, 4 * width), low),
            vmem((2, along, shard, 4 * width), low),
            vmem((2, along, shard, 4 * width), low),
            vmem((levels, seq_len, width), low),
            vmem((levels, seq_len, width), low),
            vmem((others, seq_len, width), low),
            vmem((others, seq_len, width), low),
            vmem((levels * own_len, width), low),
            vmem((levels * own_len, width), low),
            vmem((turns + 1, small_rows, features_all), full),
            vmem((turns, small_rows, features_all), full),
            dma((2,)),
            dma((2,)),
            dma((cols, levels)),
            dma((cols, levels)),
            dma((cols, others)),
            dma((cols, others)),
            dma((cols,)),
            dma((cols,)),
            dma((along, across - 1)),
            dma((along, across - 1)),
            dma((2, along)),
            dma((2, along)),
            dma((turns,)),
            dma((turns,)),
            dma((2,)),
        ],
        compiler_params=pltpu.CompilerParams(
            collective_id=2, has_side_effects=True, vmem_limit_bytes=60 * 1024 * 1024
        ),
        cost_estimate=pl.CostEstimate(
            flops=4 * seq_len * features_all * 3 * width,
            bytes_accessed=20 * 1024 * 1024,
            transcendentals=0,
        ),
    )(query_key_value, weights, features, attn_full, layer_own, small, up_small, bias, out)


def last_kernel(
    grad_input_ref,
    layer_ref,
    small_ref,
    share_ref,
    down_ref,
    up_own_ref,
    up_first_ref,
    *refs,
):
    more, outs = refs[: len(refs) - 17], refs[len(refs) - 17 :]
    (
        layer_out,
        grad_input,
        grad_query,
        bias_query,
        grad_key,
        grad_value,
        bias_value,
        grad_out,
        bias_out,
        gain1,
        shift1,
        grad_up,
        bias_up,
        grad_down,
        bias_down,
        gain2,
        shift2,
    ) = outs
    grad_input[...] = grad_input_ref[...]
    layer_out[...] = layer_ref[...]
    width = grad_query.shape[1]
    for place, ref in enumerate((grad_query, grad_key, grad_value)):
        ref[...] = share_ref[:, place * width : (place + 1) * width]
    grad_out[...] = share_ref[:, 3 * width :].T
    grad_down[...] = down_ref[...].T
    total = up_own_ref[...]
    for ref in (up_first_ref, *more):
        total += ref[...].astype(jnp.float32)
    grad_up[...] = total
    features_all = small_ref.shape[1]
    last = small_ref.shape[0] - 4
    for place, ref in (
        (0, gain2),
        (1, shift2),
        (2, bias_down),
        (3, gain1),
        (4, shift1),
        (5, bias_out),
        (last, bias_query),
        (last + 1, bias_value),
    ):
        ref[...] = small_ref[place : place + 1, :]
    for place in range(8, last):
        bias_up[:, (place - 8) * features_all : (place - 7) * features_all] = small_ref[
            place : place + 1, :
        ]


def put_out(grad_input, layer_out, small, share, down, up_own, up_others):
    low, full = jnp.bfloat16, jnp.float32
    shape = jax.ShapeDtypeStruct
    seq_len, width = grad_input.shape
    shard, units = up_own.shape
    features_all = small.shape[1]
    vector = shape((1, features_all), full)
    units_all = (small.shape[0] - 12) * features_all
    grad = shape((shard, width), full)
    return pl.pallas_call(
        last_kernel,
        out_shape=(
            shape((seq_len, width), low),
            shape((seq_len, width), low),
            grad,
            vector,
            grad,
            grad,
            vector,
            shape((width, shard), full),
            vector,
            vector,
            vector,
            shape((shard, units), full),
            shape((1, units_all), full),
            shape((units, shard), full),
            vector,
            vector,
            vector,
        ),
        in_specs=[VMEM] * (6 + len(up_others)),
        out_specs=[VMEM] * 17,
        compiler_params=pltpu.CompilerParams(vmem_limit_bytes=60 * 1024 * 1024),
    )(grad_input, layer_out, small, share, down, up_own, *up_others)


def on_device(
    hidden_in,
    out_grad,
    lengths,
    global_blocks,
    rand_blocks,
    w_query,
    b_query,
    w_key,
    w_value,
    b_value,
    w_out,
    b_out,
    ln1_gain,
    ln1_bias,
    w_up,
    b_up,
    w_down,
    b_down,
    ln2_gain,
    ln2_bias,
):
    cols = lax.axis_size("col")
    rows = lax.axis_size("row")
    tables = (lengths, global_blocks.reshape(-1), rand_blocks.reshape(-1))
    as_row = lambda vector: vector[None, :]
    (
        features,
        own_features,
        upstream,
        queries,
        key_rows,
        value_rows,
        context,
        highest,
        scale,
        full_qkv,
        full_out,
        full_up,
        full_down,
        out_sib,
        up_sib,
        down_sib,
        context_sib,
        normed_full,
        unit1,
        inv1,
    ) = front(
        cols // 2,
        rows,
        tables,
        hidden_in,
        out_grad,
        (as_row(b_query), as_row(b_value)),
        (w_query, w_key, w_value, w_out, w_up, w_down),
        (as_row(b_out), as_row(ln1_gain), as_row(ln1_bias)),
    )
    (
        layer_own,
        context_grad,
        attn_full,
        small,
        up_small,
        down_share,
        up_own,
        grad_out,
        *up_part,
    ) = middle(
        cols // 2,
        rows,
        lengths,
        context,
        context_sib,
        upstream,
        (full_out, out_sib, full_up, up_sib, full_down, down_sib),
        normed_full,
        unit1,
        inv1,
        tuple(as_row(each) for each in (ln1_gain, ln1_bias, b_down, ln2_gain, ln2_bias)),
        as_row(b_up),
    )
    across = across_of(rows)
    up_others = [
        lax.ppermute(
            up_part[shift - 1],
            "row",
            [(place, (place + shift * across) % rows) for place in range(rows)],
        )
        for shift in range(1, rows // across)
    ]
    query_key_value, bias_sums = attend_back(
        queries, key_rows, value_rows, tables, (highest, scale), context_grad
    )
    grad_input, layer_out, small, share = finish(
        cols // 2,
        rows,
        query_key_value,
        full_qkv,
        features,
        attn_full,
        layer_own,
        small,
        up_small,
        bias_sums,
        grad_out,
    )
    outs = put_out(grad_input, layer_out, small, share, down_share, up_own, up_others)
    return tuple(each.reshape(-1) if each.shape[0] == 1 else each for each in outs)


def solution(mesh):
    placed = (
        P("row", "col"),
        P("row", "col"),
        P("row"),
        P("row", None),
        P("row", None, "col", None),
        P("row", "col"),
        P(),
        P("row", "col"),
        P("row", "col"),
        P(),
        P("col", "row"),
        P(),
        P(),
        P(),
        P("row", "col"),
        P(),
        P("col", "row"),
        P(),
        P(),
        P(),
    )
    return jax.shard_map(
        on_device,
        mesh=mesh,
        in_specs=placed,
        out_specs=(
            P("row", "col"),
            P("row", "col"),
            P("row", "col"),
            P(),
            P("row", "col"),
            P("row", "col"),
            P(),
            P("col", "row"),
            P(),
            P(),
            P(),
            P("row", "col"),
            P(),
            P("col", "row"),
            P(),
            P(),
            P(),
        ),
        check_vma=False,
    )
```

```python
import functools
import math

import jax
import jax.numpy as jnp
from jax import lax
from jax.experimental import pallas as pl
from jax.experimental.pallas import tpu as pltpu
from jax.sharding import PartitionSpec as P

DH = 64
BLK = 64
MESH = pl.DeviceIdType.MESH


epsilon = 1e-06


def lane_heads(rows, width):
    return lax.broadcasted_iota(jnp.int32, (rows, width), 1) // DH


def by_diagonal(rows, width):
    lane_head = lane_heads(BLK, width)
    zero = jnp.zeros_like(rows)
    return jnp.concatenate(
        [jnp.where(lane_head == head, rows, zero) for head in range(width // DH)], axis=0
    )


def from_diagonal(square, width):
    lane_head = lane_heads(BLK, width)
    result = jnp.zeros((BLK, width), jnp.float32)
    for head in range(width // DH):
        result = jnp.where(lane_head == head, square[head * BLK : (head + 1) * BLK, :], result)
    return result


def slot_starts(step, num_blocks, head_count, globals_ref, random_ref):
    shared = [
        jnp.maximum(step - 1, 0),
        step,
        jnp.minimum(step + 1, num_blocks - 1),
        globals_ref[0],
        globals_ref[1],
    ]
    base = step * (head_count * 3)
    apart = [
        [random_ref[base + head * 3 + slot] for head in range(head_count)] for slot in range(3)
    ]
    return shared, apart


def lane_groups(head_count):
    per_group = min(128 // DH, head_count)
    return [
        (first * DH, per_group * DH, list(range(first, first + per_group)))
        for first in range(0, head_count, per_group)
    ]


def picked_rows(rows_ref, shared, apart, head_count):
    pieces = [rows_ref[block] for block in shared]
    for blocks in apart:
        groups = []
        for lane, width, heads in lane_groups(head_count):
            lane_head = lane_heads(BLK, width)
            piece = rows_ref[blocks[heads[0]], :, lane : lane + width]
            for place, head in enumerate(heads[1:], 1):
                other = rows_ref[blocks[head], :, lane : lane + width]
                piece = jnp.where(lane_head >= place, other, piece)
            groups.append(piece)
        pieces.append(jnp.concatenate(groups, axis=1) if len(groups) > 1 else groups[0])
    return jnp.concatenate(pieces, axis=0)


def put_rows(sums_ref, values_in, shared, apart, head_count):
    for slot, block in enumerate(shared):
        sums_ref[block] += values_in[slot * BLK : (slot + 1) * BLK, :]
    for slot, blocks in enumerate(apart, len(shared)):
        rows = values_in[slot * BLK : (slot + 1) * BLK, :]
        for lane, width, heads in lane_groups(head_count):
            lane_head = lane_heads(BLK, width)
            for place, head in enumerate(heads):
                sums_ref[blocks[head], :, lane : lane + width] += jnp.where(
                    lane_head == place, rows[:, lane : lane + width], 0.0
                )


def masked_scores(picked_keys, grouped, step, num_blocks, length, shared, apart):
    width = grouped.shape[1]
    scores = lax.dot_general(
        picked_keys, grouped, (((1,), (1,)), ((), ())), preferred_element_type=jnp.float32
    )
    listed = [step >= 1, True, step + 1 < num_blocks]
    listed += [(block < step - 1) | (block > step + 1) for block in shared[3:]]
    limits = [
        jnp.where(there, length - block * BLK, 0) for there, block in zip(listed, shared)
    ]
    lane_head = lane_heads(1, width)
    for blocks in apart:
        limit = length - jnp.full((1, width), blocks[0], jnp.int32) * BLK
        for head, block in enumerate(blocks[1:], 1):
            limit = jnp.where(lane_head >= head, length - block * BLK, limit)
        limits.append(limit)
    row = lax.broadcasted_iota(jnp.int32, (BLK, width), 0)
    return [
        jnp.where(row < limit, scores[slot * BLK : (slot + 1) * BLK, :], -1e30)
        for slot, limit in enumerate(limits)
    ]


def attend_blocks(
    first, count, unroll, length_ref, globals_ref, random_ref, refs, context_ref, stat_refs
):
    queries_ref, keys_ref, values_ref = refs
    highest_ref, scale_ref = stat_refs
    seq_len, width = queries_ref.shape
    head_count = width // DH
    num_blocks = seq_len // BLK

    def one_block(step):
        shared, apart = slot_starts(step, num_blocks, head_count, globals_ref, random_ref)
        own = pl.ds(pl.multiple_of(step * BLK, BLK), BLK)
        grouped = by_diagonal(queries_ref[own, :] * jnp.bfloat16(1.0 / math.sqrt(DH)), width)
        scores = masked_scores(
            picked_rows(keys_ref, shared, apart, head_count),
            grouped,
            step,
            num_blocks,
            length_ref[0],
            shared,
            apart,
        )
        highest = jnp.max(functools.reduce(jnp.maximum, scores), axis=0, keepdims=True)
        exponent = [jnp.exp(piece - highest) for piece in scores]
        denominator = jnp.sum(sum(exponent[1:], exponent[0]), axis=0, keepdims=True)
        scale = 1.0 / denominator
        attn_probs = jnp.concatenate(
            [(piece * scale).astype(jnp.bfloat16) for piece in exponent], axis=0
        )
        square = lax.dot_general(
            attn_probs,
            picked_rows(values_ref, shared, apart, head_count),
            (((0,), (0,)), ((), ())),
            preferred_element_type=jnp.float32,
        )
        context_ref[own, :] = from_diagonal(square, width).astype(jnp.bfloat16)
        highest_ref[step] = highest
        scale_ref[step] = scale

    @pl.loop(0, count // unroll)
    def _(turn):
        for place in range(unroll):
            one_block(first + turn * unroll + place)


def attend_back_kernel(
    head_count,
    unroll,
    length_ref,
    globals_ref,
    random_ref,
    queries_ref,
    keys_ref,
    values_ref,
    grads_ref,
    highest_ref,
    scale_ref,
    grads_out_ref,
    bias_ref,
    key_sums,
    value_sums,
    query_total,
):
    width = head_count * DH
    num_blocks = queries_ref.shape[0] // BLK
    factor = 1.0 / math.sqrt(DH)
    key_sums[...] = jnp.zeros_like(key_sums)
    value_sums[...] = jnp.zeros_like(value_sums)
    query_total[...] = jnp.zeros_like(query_total)

    def one_block(step):
        shared, apart = slot_starts(step, num_blocks, head_count, globals_ref, random_ref)
        own = pl.ds(pl.multiple_of(step * BLK, BLK), BLK)
        grouped = by_diagonal(queries_ref[own, :] * jnp.bfloat16(factor), width)
        grouped_grad = by_diagonal(grads_ref[own, :], width)
        picked_keys = picked_rows(keys_ref, shared, apart, head_count)
        picked_values = picked_rows(values_ref, shared, apart, head_count)
        scores = masked_scores(
            picked_keys, grouped, step, num_blocks, length_ref[0], shared, apart
        )
        highest = highest_ref[step]
        scale = scale_ref[step]
        attn_probs = [jnp.exp(piece - highest) * scale for piece in scores]
        prob_grad = lax.dot_general(
            picked_values,
            grouped_grad,
            (((1,), (1,)), ((), ())),
            preferred_element_type=jnp.float32,
        )
        prob_grads = [prob_grad[slot * BLK : (slot + 1) * BLK, :] for slot in range(8)]
        products = [left * right for left, right in zip(attn_probs, prob_grads)]
        total = jnp.sum(sum(products[1:], products[0]), axis=0, keepdims=True)
        score_grad = jnp.concatenate(
            [
                (left * (right - total)).astype(jnp.bfloat16)
                for left, right in zip(attn_probs, prob_grads)
            ],
            axis=0,
        )
        probs_low = jnp.concatenate([piece.astype(jnp.bfloat16) for piece in attn_probs], axis=0)
        square = lax.dot_general(
            score_grad, picked_keys, (((0,), (0,)), ((), ())), preferred_element_type=jnp.float32
        )
        query_grad = (from_diagonal(square, width) * factor).astype(jnp.bfloat16)
        grads_out_ref[own, :width] = query_grad
        query_total[...] += jnp.sum(
            query_grad.astype(jnp.float32).reshape(BLK // 8, 8, width), axis=0
        )
        key_part = jnp.dot(score_grad, grouped, preferred_element_type=jnp.float32)
        value_part = jnp.dot(probs_low, grouped_grad, preferred_element_type=jnp.float32)
        put_rows(key_sums, key_part, shared, apart, head_count)
        put_rows(value_sums, value_part, shared, apart, head_count)

    @pl.loop(0, num_blocks // unroll)
    def _(turn):
        for place in range(unroll):
            one_block(turn * unroll + place)

    value_grad = value_sums[...].reshape(queries_ref.shape).astype(jnp.bfloat16)
    seq_len = queries_ref.shape[0]
    grads_out_ref[:, width : 2 * width] = key_sums[...].reshape(seq_len, width).astype(jnp.bfloat16)
    grads_out_ref[:, 2 * width :] = value_grad
    bias_ref[0:1, :] = jnp.sum(query_total[...], axis=0, keepdims=True)
    bias_ref[1:2, :] = jnp.sum(value_grad.astype(jnp.float32), axis=0, keepdims=True)


VMEM = pl.BlockSpec(memory_space=pltpu.VMEM)
SMEM = pl.BlockSpec(memory_space=pltpu.SMEM)


def attend_back(queries, key_rows, value_rows, tables, stats, context_grad):
    seq_len, width = queries.shape
    head_count = width // DH
    return pl.pallas_call(
        functools.partial(attend_back_kernel, head_count, 8),
        out_shape=(
            jax.ShapeDtypeStruct((seq_len, 3 * width), jnp.bfloat16),
            jax.ShapeDtypeStruct((2, width), jnp.float32),
        ),
        in_specs=[SMEM] * 3 + [VMEM] * 6,
        out_specs=[VMEM] * 2,
        scratch_shapes=[pltpu.VMEM((seq_len // BLK, BLK, width), jnp.float32)] * 2
        + [pltpu.VMEM((8, width), jnp.float32)],
        compiler_params=pltpu.CompilerParams(vmem_limit_bytes=60 * 1024 * 1024),
        cost_estimate=pl.CostEstimate(
            flops=10 * seq_len * 512 * width * head_count,
            bytes_accessed=14 * seq_len * width,
            transcendentals=seq_len * 512 * head_count,
        ),
    )(*tables, queries, key_rows, value_rows, context_grad, *stats)


KINDS = 4
CHUNKS = 4


def front_kernel(
    levels,
    across,
    along,
    length_ref,
    globals_ref,
    random_ref,
    hidden_ref,
    grads_ref,
    b_query_ref,
    b_value_ref,
    w_query_ref,
    w_key_ref,
    w_value_ref,
    w_out_ref,
    w_up_ref,
    w_down_ref,
    b_out,
    gain1,
    shift1,
    features_far,
    own_far,
    upstream_far,
    queries_far,
    keys_far,
    values_far,
    context_far,
    highest_ref,
    scale_ref,
    full_qkv_far,
    full_out_ref,
    full_up_far,
    full_down_far,
    out_sib,
    up_sib_far,
    down_sib_far,
    context_sib,
    normed_full,
    unit1,
    inv1,
    features_ref,
    own_ref,
    upstream_ref,
    queries_ref,
    keys_ref,
    values_ref,
    context_ref,
    full_qkv_ref,
    full_up_ref,
    full_down_ref,
    up_sib,
    down_sib,
    far_sem,
    sum_out,
    sum_in,
    level_send,
    level_recv,
    core_send,
    core_recv,
    swap_send,
    swap_recv,
    along_send,
    along_recv,
    across_send,
    across_recv,
    shard_send,
    shard_recv,
    context_send,
    context_recv,
    sum_send,
    sum_recv,
    normed_send,
    normed_recv,
):
    low, full = jnp.bfloat16, jnp.float32
    row, column = lax.axis_index("row"), lax.axis_index("col")
    core, level = lax.rem(column, 2), lax.div(column, 2)
    fast, slow = lax.rem(row, across), lax.div(row, across)
    cols = 2 * levels
    seq_len, width = hidden_ref.shape
    own_len = seq_len // cols
    shard = w_query_ref.shape[0]
    other = 1 - core
    sibling = (row, level * 2 + other)
    offsets = range(1, levels)

    def peer_level(offset):
        return lax.rem(level + offset, levels)

    def fast_peer(offset):
        return slow * across + lax.rem(fast + offset, across)

    def line_peer(shift):
        return ((slow + shift) * across + fast, column)

    barrier = pltpu.get_barrier_semaphore()
    greeted = [sibling]
    for offset in offsets:
        greeted += [(row, peer_level(offset) * 2 + core), (row, peer_level(offset) * 2 + other)]
    greeted += [(fast_peer(offset), column) for offset in range(1, across)]
    greeted += [
        (lax.rem(slow + offset, along) * across + fast, column) for offset in range(1, along)
    ]
    for device in greeted:
        pl.semaphore_signal(barrier, inc=1, device_id=device, device_id_type=MESH)
    pl.semaphore_wait(barrier, len(greeted))

    def remote(source, target, send, recv, device):
        return pltpu.make_async_remote_copy(
            src_ref=source,
            dst_ref=target,
            send_sem=send,
            recv_sem=recv,
            device_id=device,
            device_id_type=MESH,
        )

    def block(start, size):
        return pl.ds(pl.multiple_of(start * size, size), size)

    def level_copy(turn, offset):
        rows = block(turn, own_len)
        return remote(
            hidden_ref.at[rows],
            features_ref.at[rows, block(column, width)],
            level_send.at[turn, offset - 1],
            level_recv.at[turn, levels - offset - 1],
            (row, peer_level(offset) * 2 + core),
        )

    def core_copy(turn, offset):
        view = features_ref.at[block(turn, own_len), block(peer_level(offset) * 2 + core, width)]
        return remote(
            view, view, core_send.at[turn, offset], core_recv.at[turn, offset], sibling
        )

    @pl.loop(0, cols)
    def _(turn):
        for offset in offsets:
            level_copy(turn, offset).start()
        rows = block(turn, own_len)
        features_ref[rows, block(column, width)] = hidden_ref[rows, :]
        core_copy(turn, 0).start()

    fulls = (full_qkv_ref, full_out_ref, full_up_ref, full_down_ref)
    sibs = (None, out_sib, up_sib, down_sib)

    def shard_rows(place):
        return block(place * across + fast, shard)

    def line_copy(kind, way, hop):
        view = fulls[kind].at[shard_rows(slow - (1 - 2 * way) * hop)]
        return remote(
            view,
            view,
            along_send.at[kind, way, hop],
            along_recv.at[kind, way, hop],
            line_peer(1 - 2 * way),
        )

    def line_can_send(way, hop):
        if way == 0:
            return (slow >= hop) & (slow < along - 1)
        return (slow < along - hop) & (slow > 0)

    def line_send(kind, hop):
        for way in range(2):

            @pl.when(line_can_send(way, hop))
            def _():
                line_copy(kind, way, hop).start()

    def line_got(way, hop):
        place = slow - (1 - 2 * way) * (hop + 1)
        return place, ((place >= 0) if way == 0 else (place < along))

    def line_wait(kind, way, hop):
        place, _ = line_got(way, hop)
        view = fulls[kind].at[shard_rows(place)]
        remote(
            view,
            view,
            along_send.at[kind, way, hop],
            along_recv.at[kind, way, hop],
            line_peer(-(1 - 2 * way)),
        ).wait_recv()

    def across_copy(kind, place, offset):
        view = fulls[kind].at[shard_rows(place)]
        return remote(
            view,
            view,
            across_send.at[kind, place, offset - 1],
            across_recv.at[kind, place, across - offset - 1],
            (fast_peer(offset), column),
        )

    def core_shard(kind, place, offset):
        rows = block(place * across + lax.rem(fast + offset, across), shard)
        return remote(
            fulls[kind].at[rows],
            sibs[kind].at[rows],
            shard_send.at[kind - 1, place, offset],
            shard_recv.at[kind - 1, place, offset],
            sibling,
        )

    for place, ref in enumerate((w_query_ref, w_key_ref, w_value_ref)):
        full_qkv_ref[shard_rows(slow), place * width : (place + 1) * width] = ref[...].astype(low)
    line_send(0, 0)
    full_out_ref[shard_rows(slow), :] = w_out_ref[...].T.astype(low)
    full_up_ref[shard_rows(slow), :] = w_up_ref[...].astype(low)
    full_down_ref[shard_rows(slow), :] = w_down_ref[...].T.astype(low)

    def swap_copy(target, place_out, place_in):
        return remote(
            grads_ref.at[block(target, own_len)],
            upstream_ref.at[:, block(column, width)],
            swap_send.at[place_out],
            swap_recv.at[place_in],
            (row, target),
        )

    swaps = [swap_copy(level * 2 + other, 0, 0)]
    for offset in offsets:
        back = levels - offset
        swaps.append(swap_copy(peer_level(offset) * 2 + core, 2 * offset - 1, 2 * back - 1))
        swaps.append(swap_copy(peer_level(offset) * 2 + other, 2 * offset, 2 * back))
    for copy in swaps:
        copy.start()
    upstream_ref[:, block(column, width)] = grads_ref[block(column, own_len), :]

    def pass_shard(kind, place):
        for step in range(1, across):
            across_copy(kind, place, step).start()
        if kind > 0:
            core_shard(kind, place, 0).start()

    hops = range(along - 1)
    waiting = [(1, hop) for hop in hops] + [(3, -1), (2, 0), (3, 0)]
    waiting += [(kind, hop) for hop in hops if hop > 0 for kind in (2, 3)]

    def pass_on(count=1):
        pass_these(waiting[:count])
        del waiting[:count]

    def pass_these(shards):
        for kind, hop in shards:
            if hop < 0:
                pass_shard(kind, slow)
                continue
            for way in range(2):
                place, there = line_got(way, hop)

                @pl.when(there)
                def _():
                    line_wait(kind, way, hop)
                    if hop < along - 2:

                        @pl.when(line_can_send(way, hop + 1))
                        def _():
                            line_copy(kind, way, hop + 1).start()

                    pass_shard(kind, place)
    def await_shards(kind):
        @pl.loop(0, along)
        def _(place):
            for offset in range(1, across):
                across_copy(kind, place, across - offset).wait_recv()
                if kind > 0:
                    core_shard(kind, place, offset).start()

    def await_sibling(kind):
        @pl.loop(0, along)
        def _(place):
            for offset in range(across):
                core_shard(kind, place, offset).wait_recv()

    pass_these([(0, hop) for hop in range(-1, along - 2)])
    for kind in range(1, KINDS):
        line_send(kind, 0)
    pass_these([(0, along - 2), (1, -1), (2, -1)])
    await_shards(0)

    def project(turn):
        rows = block(turn, own_len)
        for offset in offsets:
            level_copy(turn, levels - offset).wait_recv()
            core_copy(turn, offset).start()
        for offset in range(levels):
            core_copy(turn, offset).wait_recv()
        values_in = features_ref[rows, :]
        queries_ref[rows, :] = (
            dot(values_in, full_qkv_ref[:, :width]) + b_query_ref[:, block(column, width)]
        ).astype(low)
        blocks = pl.ds(turn * (own_len // BLK), own_len // BLK)
        by_block = (own_len // BLK, BLK, width)
        keys_ref[blocks] = (
            dot(values_in, full_qkv_ref[:, width : 2 * width]).astype(low).reshape(by_block)
        )
        values_ref[blocks] = (
            (dot(values_in, full_qkv_ref[:, 2 * width :]) + b_value_ref[:, block(column, width)])
            .astype(low)
            .reshape(by_block)
        )

    for turn in range(cols):
        project(turn)
        pass_on(1 if (3, -1) in waiting else 0)
    while (2, 0) in waiting:
        pass_on()
    own_ref[...] = features_ref[block(column, own_len), :]
    far = [
        pltpu.make_async_copy(source, target, far_sem.at[place])
        for place, (source, target) in enumerate(
            [
                (features_ref, features_far),
                (own_ref, own_far),
                (queries_ref, queries_far),
                (keys_ref, keys_far),
                (values_ref, values_far),
                (full_qkv_ref, full_qkv_far),
                (upstream_ref, upstream_far),
                (context_ref, context_far),
                (full_up_ref, full_up_far),
                (up_sib, up_sib_far),
                (full_down_ref, full_down_far),
                (down_sib, down_sib_far),
            ]
        )
    ]
    @pl.loop(0, cols)
    def _(turn):
        for offset in range(levels):
            core_copy(turn, offset).wait_send()

    for copy in far[:6]:
        copy.start()

    step = own_len // CHUNKS
    halves = 2
    count = own_len // BLK // halves

    def attend_half(quarter, half):
        attend_blocks(
            (quarter * halves + half) * count,
            count,
            min(count, 4),
            length_ref,
            globals_ref,
            random_ref,
            (queries_ref, keys_ref, values_ref),
            context_ref,
            (highest_ref, scale_ref),
        )

    def context_copy(place, half):
        rows = own_len // halves
        return remote(
            context_ref.at[block((place * 2 + other) * halves + half, rows)],
            context_sib.at[block(place * halves + half, rows)],
            context_send.at[place, half],
            context_recv.at[place, half],
            sibling,
        )

    def chunk_rows(place, chunk):
        return block(place * CHUNKS + chunk, step)

    def attn_part(place, chunk):
        return dot_nt(
            context_ref[chunk_rows(place * 2 + core, chunk), :], full_out_ref[...]
        ) + dot_nt(context_sib[chunk_rows(place, chunk), :], out_sib[...])

    def sum_copy(chunk, offset):
        rows = block(chunk, step)
        return remote(
            sum_out.at[offset - 1, rows],
            sum_in.at[levels - offset - 1, rows],
            sum_send.at[chunk, offset - 1],
            sum_recv.at[chunk, levels - offset - 1],
            (row, peer_level(offset) * 2 + core),
        )

    def normed_copy(chunk, offset):
        view = normed_full.at[chunk_rows(level, chunk)]
        return remote(
            view,
            view,
            normed_send.at[chunk, offset - 1],
            normed_recv.at[chunk, levels - offset - 1],
            (row, peer_level(offset) * 2 + core),
        )

    for offset in list(offsets) + [0]:
        place = peer_level(offset)
        for half in range(halves):
            attend_half(place * 2 + other, half)
            context_copy(place, half).start()
            pass_on(1 - half if offset else half)
        if offset == 1:
            await_shards(1)
        for half in range(halves):
            attend_half(place * 2 + core, half)
            if offset == 1 and half == 0:
                await_sibling(1)
            context_copy(place, half).wait_recv()
            per_half = CHUNKS // halves
            for chunk in range(half * per_half, (half + 1) * per_half):
                if offset:
                    sum_out[offset - 1, block(chunk, step), :] = attn_part(place, chunk).astype(
                        low
                    )
                    sum_copy(chunk, offset).start()
            pass_on(1 if offset else half)
    pass_on(len(waiting))
    for copy in swaps:
        copy.wait()
    for copy in far[6:8]:
        copy.start()
    for chunk in range(CHUNKS):
        rows = block(chunk, step)
        summed = own_ref[rows, :].astype(full) + attn_part(level, chunk) + b_out[...]
        for offset in offsets:
            sum_copy(chunk, offset).wait_recv()
        for place in range(levels - 1):
            summed += sum_in[place, rows, :].astype(full)
        normed, inv_std = norm_parts(summed)
        unit1[rows, :] = normed
        inv1[rows, :] = inv_std
        normed_full[chunk_rows(level, chunk), :] = (normed * gain1[...] + shift1[...]).astype(low)
        for offset in offsets:
            normed_copy(chunk, offset).start()
    await_shards(2)
    await_shards(3)
    for kind in range(2, KINDS):
        await_sibling(kind)
        for copy in far[4 + 2 * kind : 6 + 2 * kind]:
            copy.start()
    for chunk in range(CHUNKS):
        for offset in offsets:
            normed_copy(chunk, offset).wait()
            sum_copy(chunk, offset).wait_send()
    for place in range(levels):
        for half in range(halves):
            context_copy(place, half).wait_send()
    for copy in far:
        copy.wait()
    for kind in range(KINDS):
        for hop in range(along - 1):
            for way in range(2):

                @pl.when(line_can_send(way, hop))
                def _():
                    line_copy(kind, way, hop).wait_send()

        @pl.loop(0, along)
        def _(place):
            for offset in range(1, across):
                across_copy(kind, place, offset).wait_send()
            if kind > 0:
                for offset in range(across):
                    core_shard(kind, place, offset).wait_send()

    @pl.loop(0, cols)
    def _(turn):
        for offset in offsets:
            level_copy(turn, offset).wait_send()


def across_of(rows):
    return 2 if rows <= 8 else rows // 4


def front(levels, rows, tables, hidden_in, grads, biases, weights, vectors):
    low, full = jnp.bfloat16, jnp.float32
    shape = jax.ShapeDtypeStruct
    across = across_of(rows)
    along = rows // across
    seq_len, width = hidden_in.shape
    cols = 2 * levels
    own_len = seq_len // cols
    features_all = width * cols
    units = weights[4].shape[1]
    widths = (3 * width, width, units, units)
    others = levels - 1
    stat = shape((seq_len // BLK, 1, width), full)
    hbm = pl.BlockSpec(memory_space=pl.ANY)
    dma = pltpu.SemaphoreType.DMA
    return pl.pallas_call(
        functools.partial(front_kernel, levels, across, along),
        out_shape=(
            shape((seq_len, features_all), low),
            shape((own_len, features_all), low),
            shape((own_len, features_all), low),
            shape((seq_len, width), low),
            shape((seq_len // BLK, BLK, width), low),
            shape((seq_len // BLK, BLK, width), low),
            shape((seq_len, width), low),
            stat,
            stat,
            *(shape((features_all, each), low) for each in widths),
            *(shape((features_all, each), low) for each in widths[1:]),
            shape((levels * own_len, width), low),
            shape((levels * own_len, features_all), low),
            shape((own_len, features_all), full),
            shape((own_len, 1), full),
        ),
        in_specs=[SMEM] * 3 + [VMEM] * 13,
        out_specs=[hbm] * 7 + [VMEM] * 2 + [hbm] + [VMEM, hbm, hbm] * 2 + [VMEM] * 4,
        scratch_shapes=[
            pltpu.VMEM((seq_len, features_all), low),
            pltpu.VMEM((own_len, features_all), low),
            pltpu.VMEM((own_len, features_all), low),
            pltpu.VMEM((seq_len, width), low),
            pltpu.VMEM((seq_len // BLK, BLK, width), low),
            pltpu.VMEM((seq_len // BLK, BLK, width), low),
            pltpu.VMEM((seq_len, width), low),
            pltpu.VMEM((features_all, 3 * width), low),
            *(pltpu.VMEM((features_all, units), low) for _ in range(4)),
            dma((12,)),
            pltpu.VMEM((others, own_len, features_all), low),
            pltpu.VMEM((others, own_len, features_all), low),
            dma((cols, others)),
            dma((cols, others)),
            dma((cols, levels)),
            dma((cols, levels)),
            dma((cols,)),
            dma((cols,)),
            dma((KINDS, 2, along - 1)),
            dma((KINDS, 2, along - 1)),
            dma((KINDS, along, across - 1)),
            dma((KINDS, along, across - 1)),
            dma((KINDS - 1, along, across)),
            dma((KINDS - 1, along, across)),
            dma((levels, 2)),
            dma((levels, 2)),
            *(dma((CHUNKS, others)) for _ in range(4)),
        ],
        compiler_params=pltpu.CompilerParams(
            collective_id=3, has_side_effects=True, vmem_limit_bytes=56 * 1024 * 1024
        ),
        cost_estimate=pl.CostEstimate(
            flops=2 * seq_len * features_all * 3 * width,
            bytes_accessed=20 * 1024 * 1024,
            transcendentals=seq_len * 512 * (width // DH),
        ),
    )(*tables, hidden_in, grads, *biases, *weights, *vectors)


def dot(left, right):
    return jnp.dot(left, right, preferred_element_type=jnp.float32)


def dot_nt(left, right):
    return lax.dot_general(
        left, right, (((1,), (1,)), ((), ())), preferred_element_type=jnp.float32
    )


def dot_tn(left, right):
    return lax.dot_general(
        left, right, (((0,), (0,)), ((), ())), preferred_element_type=jnp.float32
    )


def gelu_parts(values_in):
    factor = math.sqrt(2.0 / math.pi)
    square = values_in * values_in
    bent = jnp.tanh(factor * (values_in + 0.044715 * (values_in * square)))
    half = 0.5 * (1.0 + bent)
    slope = half + (0.5 * values_in) * (1.0 - bent * bent) * (
        factor + (3.0 * 0.044715 * factor) * square
    )
    return (values_in * half, slope)


def norm_parts(summed):
    average = jnp.mean(summed, axis=1, keepdims=True)
    squares = jnp.mean(summed * summed, axis=1, keepdims=True)
    inv_std = lax.rsqrt(squares - average * average + epsilon)
    return ((summed - average) * inv_std, inv_std)


def norm_back(upstream, normed, inv_std, gain_vec):
    scaled = upstream * gain_vec
    left = jnp.mean(scaled, axis=1, keepdims=True)
    right = jnp.mean(scaled * normed, axis=1, keepdims=True)
    return inv_std * (scaled - left - normed * right)


def middle_kernel(
    levels,
    across,
    along,
    length_ref,
    context_far,
    context_sib_far,
    upstream_far,
    out_far,
    out_sib_far,
    up_ref,
    up_sib,
    down_full,
    down_sib,
    normed_full,
    unit1_far,
    inv1,
    gain1,
    shift1,
    b_down,
    gain2,
    shift2,
    b_up_ref,
    layer_out_ref,
    context_grad_ref,
    attn_full,
    small_ref,
    up_small_ref,
    share_down_ref,
    up_own_ref,
    grad_out_ref,
    *more,
):
    up_part_refs, refs = more[: along - 1], more[along - 1 :]
    (
        ffn_full,
        hidden,
        slope,
        pre_grad,
        ffn_keep,
        part_own,
        send_buf,
        recv_buf,
        context_send,
        stage,
        down_sums,
        up_sums,
        down_got,
        up_got,
        down_pass,
        down_in,
        send_sem,
        recv_sem,
        core_send,
        core_recv,
        along_send,
        along_recv,
        across_send,
        across_recv,
        stage_sem,
        context_ref,
        context_sib,
        upstream_ref,
        out_ref,
        out_sib,
        unit1,
        late_sem,
        free_sem,
    ) = refs
    low = jnp.bfloat16
    row, column = lax.axis_index("row"), lax.axis_index("col")
    core = lax.rem(column, 2)
    level = lax.div(column, 2)
    sibling = (row, column + 1 - 2 * core)
    fast, slow = lax.rem(row, across), lax.div(row, across)
    shard = share_down_ref.shape[0]
    own_len = upstream_ref.shape[0]
    units = up_ref.shape[1]
    step = own_len // CHUNKS

    def peer_level(offset):
        return lax.rem(level + offset, levels)

    def fast_peer(offset):
        return slow * across + lax.rem(fast + offset, across)

    late = [
        pltpu.make_async_copy(source, target, late_sem.at[place])
        for place, (source, target) in enumerate(
            [
                (unit1_far, unit1),
                (upstream_far, upstream_ref),
                (context_far, context_ref),
                (context_sib_far, context_sib),
                (out_far, out_ref),
                (out_sib_far, out_sib),
            ]
        )
    ]
    for copy in late:
        copy.start()

    barrier = pltpu.get_barrier_semaphore()
    greeted = [sibling]
    greeted += [(row, peer_level(offset) * 2 + core) for offset in range(1, levels)]
    greeted += [(fast_peer(offset), column) for offset in range(1, across)]
    greeted += [
        (lax.rem(slow + offset, along) * across + fast, column) for offset in range(1, along)
    ]
    for device in greeted:
        pl.semaphore_signal(barrier, inc=1, device_id=device, device_id_type=MESH)
    pl.semaphore_wait(barrier, len(greeted))

    def remote(source, target, send, recv, device):
        return pltpu.make_async_remote_copy(
            src_ref=source,
            dst_ref=target,
            send_sem=send,
            recv_sem=recv,
            device_id=device,
            device_id_type=MESH,
        )

    def block(start, size):
        return pl.ds(pl.multiple_of(start * size, size), size)

    def to_sibling(source, target, place):
        return remote(source, target, core_send.at[place], core_recv.at[place], sibling)

    def rows_of(place, chunk):
        return pl.ds(pl.multiple_of(place * own_len + chunk * step, step), step)

    def own_rows(chunk):
        return pl.ds(pl.multiple_of(chunk * step, step), step)

    def exchange(kind, chunk, offset, source, target):
        return pltpu.make_async_remote_copy(
            src_ref=source,
            dst_ref=target,
            send_sem=send_sem.at[kind - 2, chunk, offset - 1],
            recv_sem=recv_sem.at[kind - 2, chunk, levels - offset - 1],
            device_id=(row, peer_level(offset) * 2 + core),
            device_id_type=MESH,
        )

    def sum_copy(kind, chunk, offset):
        return exchange(
            kind,
            chunk,
            offset,
            send_buf.at[kind // 2 - 1, offset - 1, own_rows(chunk)],
            recv_buf.at[kind // 2 - 1, levels - offset - 1, own_rows(chunk)],
        )

    def spread_copy(kind, chunk, offset):
        whole = {3: ffn_full, 5: attn_full}[kind]
        rows = rows_of(level, chunk)
        return exchange(kind, chunk, offset, whole.at[rows], whole.at[rows])

    def received(kind, chunk):
        return sum(
            recv_buf[kind // 2 - 1, place, own_rows(chunk), :].astype(jnp.float32)
            for place in range(levels - 1)
        )

    offsets = range(1, levels)
    small_ref[...] = jnp.zeros_like(small_ref)
    up_small_ref[...] = jnp.zeros_like(up_small_ref)
    def context_rows(place, chunk):
        start = (place * 2 + core) * own_len + chunk * step
        return pl.ds(pl.multiple_of(start, step), step)

    sides = ((up_ref, down_full), (up_sib, down_sib))

    def feed_forward(place, chunk):
        rows = rows_of(place, chunk)
        normed = normed_full[rows, :]
        total = None
        for side, (up_side, down_side) in enumerate(sides):
            bias = b_up_ref[:, block(column + side * (1 - 2 * core), units)]
            active, bend = gelu_parts(dot(normed, up_side[...]) + bias)
            active = active.astype(low)
            hidden[side, rows, :] = active
            slope[side, rows, :] = bend.astype(low)
            part = dot_nt(active, down_side[...])
            total = part if total is None else total + part
        return total

    @pl.loop(0, CHUNKS)
    def _(chunk):
        for offset in offsets:
            send_buf[0, offset - 1, own_rows(chunk), :] = feed_forward(
                peer_level(offset), chunk
            ).astype(low)
            sum_copy(2, chunk, offset).start()

    for copy in late:
        copy.wait()

    @pl.loop(0, CHUNKS)
    def _(chunk):
        rows = own_rows(chunk)
        part_own[rows, :] = feed_forward(level, chunk)
        normed1 = unit1[rows, :] * gain1[...] + shift1[...]
        summed = normed1 + part_own[rows, :] + b_down[...]
        for offset in offsets:
            sum_copy(2, chunk, offset).wait_recv()
        normed, inv_std = norm_parts(summed + received(2, chunk))
        position = lax.broadcasted_iota(jnp.int32, (step, 1), 0) + (
            column * own_len + chunk * step
        )
        valid = position < length_ref[0]
        layer_out_ref[rows, :] = jnp.where(
            valid, normed * gain2[...] + shift2[...], 0.0
        ).astype(low)
        upstream = jnp.where(valid, upstream_ref[rows, :].astype(jnp.float32), 0.0)
        grad = norm_back(upstream, normed, inv_std, gain2[...])
        ffn_keep[rows, :] = grad
        grad_low = grad.astype(low)
        ffn_full[rows_of(level, chunk), :] = grad_low
        for offset in offsets:
            spread_copy(3, chunk, offset).start()
        small_ref[0:1, :] += jnp.sum(upstream * normed, axis=0, keepdims=True)
        small_ref[1:2, :] += jnp.sum(upstream, axis=0, keepdims=True)
        small_ref[2:3, :] += jnp.sum(grad_low.astype(jnp.float32), axis=0, keepdims=True)

    def feed_back(place, chunk):
        rows = rows_of(place, chunk)
        upstream = ffn_full[rows, :]
        total = None
        for side, (up_side, down_side) in enumerate(sides):
            grad = (
                dot(upstream, down_side[...]) * slope[side, rows, :].astype(jnp.float32)
            ).astype(low)
            pre_grad[side, rows, :] = grad
            up_small_ref[side : side + 1, :] += jnp.sum(
                grad.astype(jnp.float32), axis=0, keepdims=True
            )
            part = dot_nt(grad, up_side[...])
            total = part if total is None else total + part
        return total

    def back_own(chunk):
        part_own[own_rows(chunk), :] = feed_back(level, chunk)
        for offset in offsets:
            spread_copy(3, chunk, levels - offset).wait_recv()

    def back_peers(chunk):
        for offset in offsets:
            send_buf[1, offset - 1, own_rows(chunk), :] = feed_back(
                peer_level(offset), chunk
            ).astype(low)
            sum_copy(4, chunk, offset).start()

    @pl.loop(0, CHUNKS - 1)
    def _(chunk):
        back_own(chunk)
        back_peers(chunk)

    back_own(CHUNKS - 1)

    tile = across * shard
    lefts, rights = (ffn_full, normed_full), (hidden, pre_grad)
    sums, got = (down_sums, up_sums), (down_got, up_got)
    spare = (up_sums, slope.at[0])

    def grad_tile(kind, side, turn):
        return dot_tn(lefts[kind][:, block(turn, tile)], rights[kind][side])

    def core_grad(kind):
        return to_sibling(
            spare[kind].at[: sums[kind].shape[0]], sums[kind], levels + kind
        )

    def across_grad(kind, turn, offset):
        return remote(
            sums[kind].at[block(turn * across + lax.rem(fast + offset, across), shard)],
            got[kind].at[across - offset - 1, block(turn, shard)],
            across_send.at[kind, turn, offset - 1],
            across_recv.at[kind, turn, across - offset - 1],
            (fast_peer(offset), column),
        )

    def own_shard(kind, turn):
        for offset in range(1, across):
            across_grad(kind, turn, offset).wait_recv()
        total = sums[kind][block(turn * across + fast, shard), :].astype(jnp.float32)
        for place in range(across - 1):
            total += got[kind][place, block(turn, shard), :].astype(jnp.float32)
        return total

    def line_peer(shift):
        return ((slow + shift) * across + fast, column)

    def line_copy(kind, way, target):
        return remote(
            line_out[kind].at[way, target],
            line_in[kind].at[way, target],
            along_send.at[kind, way, target],
            along_recv.at[kind, way, target],
            line_peer(1 - 2 * way),
        )

    def line_step(kind, hop):
        for way in range(2):
            position = hop if way == 0 else along - 1 - hop
            targets = range(along - 1, hop, -1) if way == 0 else range(0, along - 1 - hop)

            @pl.when(slow == position)
            def _():
                for target in targets:
                    total = own_shard(kind, target)
                    if hop > 0:
                        line_copy(kind, way, target).wait_recv()
                        total += line_in[kind][way, target].astype(jnp.float32)
                    line_out[kind][way, target] = total.astype(jnp.bfloat16)
                    line_copy(kind, way, target).start()

    def line_finish(kind):
        for way in range(2):

            @pl.when((slow > 0) if way == 0 else (slow < along - 1))
            def _():
                line_copy(kind, way, slow).wait_recv()
                shares[kind][...] += line_in[kind][way, slow].astype(jnp.float32)

    def line_sent(kind):
        for way in range(2):
            for target in range(along):

                @pl.when((slow < target) if way == 0 else (slow > target))
                def _():
                    line_copy(kind, way, target).wait_send()

    def sum_grad(kind):
        core_grad(kind).wait_recv()

        @pl.loop(0, along)
        def _(turn):
            rows = block(turn, tile)
            sums[kind][rows, :] = (
                grad_tile(kind, 0, turn) + sums[kind][rows, :].astype(jnp.float32)
            ).astype(low)
            for offset in range(1, across):
                across_grad(kind, turn, offset).start()

    line_out, line_in, shares = (down_pass,), (down_in,), (share_down_ref,)
    def give_grad(kind):
        @pl.loop(0, along)
        def _(turn):
            spare[kind][block(turn, tile), :] = grad_tile(kind, 1, turn).astype(low)

    give_grad(0)
    core_grad(0).start()
    back_peers(CHUNKS - 1)
    core_grad(0).wait_send()
    pl.semaphore_signal(free_sem, inc=1, device_id=sibling, device_id_type=MESH)
    sum_grad(0)
    give_grad(1)
    pl.semaphore_wait(free_sem, 1)
    core_grad(1).start()
    sum_grad(1)

    @pl.loop(0, CHUNKS)
    def _(chunk):
        rows = own_rows(chunk)
        upstream = ffn_keep[rows, :] + part_own[rows, :]
        for offset in offsets:
            sum_copy(4, chunk, offset).wait_recv()
        upstream = upstream + received(4, chunk)
        normed = unit1[rows, :]
        grad_low = norm_back(upstream, normed, inv1[rows, :], gain1[...]).astype(low)
        attn_full[rows_of(level, chunk), :] = grad_low
        for offset in offsets:
            spread_copy(5, chunk, offset).start()
        small_ref[3:4, :] += jnp.sum(upstream * normed, axis=0, keepdims=True)
        small_ref[4:5, :] += jnp.sum(upstream, axis=0, keepdims=True)
        small_ref[5:6, :] += jnp.sum(grad_low.astype(jnp.float32), axis=0, keepdims=True)

    share_down_ref[...] = own_shard(0, slow)
    line_step(0, 0)

    def context_back(place, chunk):
        rows = rows_of(place, chunk)
        upstream = attn_full[rows, :]
        context_grad_ref[context_rows(place, chunk), :] = dot(upstream, out_ref[...]).astype(low)
        context_send[rows, :] = dot(upstream, out_sib[...]).astype(low)

    for chunk in range(CHUNKS):
        context_back(level, chunk)
        for offset in offsets:
            spread_copy(5, chunk, levels - offset).wait_recv()
            context_back(peer_level(offset), chunk)
        if 0 < chunk < along - 1:
            line_step(0, chunk)
    for hop in range(CHUNKS, along - 1):
        line_step(0, hop)

    back_copies = [
        to_sibling(
            context_send.at[pl.ds(place * own_len, own_len)],
            context_grad_ref.at[
                pl.ds(pl.multiple_of((place * 2 + core) * own_len, own_len), own_len)
            ],
            place,
        )
        for place in range(levels)
    ]
    for copy in back_copies:
        copy.start()

    own_context = jnp.concatenate(
        [
            context_ref[
                pl.ds(pl.multiple_of((place * 2 + core) * own_len, own_len), own_len), :
            ]
            for place in range(levels)
        ],
        axis=0,
    )

    def out_put(side):
        return pltpu.make_async_copy(stage.at[side], grad_out_ref.at[side], stage_sem.at[side])

    for side, right in enumerate((own_context, context_sib[...])):
        stage[side] = dot_tn(attn_full[...], right).astype(low)
        out_put(side).start()
    for shift in range(1, along):
        up_part_refs[shift - 1][...] = own_shard(1, lax.rem(slow + shift, along)).astype(low)
    up_own_ref[...] = own_shard(1, slow)
    line_finish(0)
    for side in range(2):
        out_put(side).wait()
    core_grad(1).wait_send()
    line_sent(0)

    @pl.loop(0, along)
    def _(place):
        for offset in range(1, across):
            across_grad(0, place, offset).wait_send()
            across_grad(1, place, offset).wait_send()

    for copy in back_copies:
        copy.wait()
    for kind in range(2, 6):

        @pl.loop(0, CHUNKS)
        def _(chunk):
            for offset in offsets:
                if kind % 2:
                    spread_copy(kind, chunk, offset).wait_send()
                else:
                    sum_copy(kind, chunk, offset).wait_send()


def middle(
    levels,
    rows,
    length,
    context,
    context_sib,
    upstream,
    weights,
    normed_full,
    unit1,
    inv1,
    vectors,
    b_up,
):
    low, full = jnp.bfloat16, jnp.float32
    across = across_of(rows)
    along = rows // across
    own_len, features = upstream.shape
    seq_len, width = context.shape
    units = weights[2].shape[1]
    shard = features // rows
    tokens = levels * own_len
    others = levels - 1
    shape = jax.ShapeDtypeStruct
    hbm = pl.BlockSpec(memory_space=pl.ANY)
    dma = pltpu.SemaphoreType.DMA
    vmem = pltpu.VMEM
    return pl.pallas_call(
        functools.partial(middle_kernel, levels, across, along),
        out_shape=(
            shape((own_len, features), low),
            shape((seq_len, width), low),
            shape((tokens, features), low),
            shape((8, features), full),
            shape((2, units), full),
            shape((shard, units), full),
            shape((shard, units), full),
            shape((2, features, width), low),
            *(shape((shard, units), low) for _ in range(along - 1)),
        ),
        in_specs=[SMEM] + [hbm] * 5 + [VMEM] * 5 + [hbm] + [VMEM] * 7,
        out_specs=[VMEM] * 7 + [hbm] + [VMEM] * (along - 1),
        scratch_shapes=[
            vmem((tokens, features), low),
            vmem((2, tokens, units), low),
            vmem((2, max(tokens, features), units), low),
            vmem((2, tokens, units), low),
            vmem((own_len, features), full),
            vmem((own_len, features), full),
            vmem((2, others, own_len, features), low),
            vmem((2, others, own_len, features), low),
            vmem((tokens, width), low),
            vmem((2, features, width), low),
            vmem((features, units), low),
            vmem((features, units), low),
            vmem((across - 1, along * shard, units), low),
            vmem((across - 1, along * shard, units), low),
            vmem((2, along, shard, units), low),
            vmem((2, along, shard, units), low),
            dma((4, CHUNKS, others)),
            dma((4, CHUNKS, others)),
            dma((levels + 2,)),
            dma((levels + 2,)),
            dma((1, 2, along)),
            dma((1, 2, along)),
            dma((2, along, across - 1)),
            dma((2, along, across - 1)),
            dma((2,)),
            vmem((seq_len, width), low),
            vmem((tokens, width), low),
            vmem((own_len, features), low),
            vmem((features, width), low),
            vmem((features, width), low),
            vmem((own_len, features), full),
            dma((6,)),
            pltpu.SemaphoreType.REGULAR,
        ],
        compiler_params=pltpu.CompilerParams(
            collective_id=1, has_side_effects=True, vmem_limit_bytes=62 * 1024 * 1024
        ),
        cost_estimate=pl.CostEstimate(
            flops=2 * tokens * features * (12 * units + 6 * width),
            bytes_accessed=20 * 1024 * 1024,
            transcendentals=2 * tokens * units,
        ),
    )(
        length,
        context,
        context_sib,
        upstream,
        *weights,
        normed_full,
        unit1,
        inv1,
        *vectors,
        b_up,
    )


def end_kernel(
    levels,
    across,
    along,
    query_key_value_ref,
    weights_ref,
    features_ref,
    attn_ref,
    layer_ref,
    small_ref,
    up_small_ref,
    bias_ref,
    out_ref,
    grad_input_ref,
    layer_out_ref,
    small_out_ref,
    share_ref,
    out_sib,
    sums,
    got,
    line_out,
    line_in,
    core_out,
    core_in,
    level_out,
    level_in,
    attn_in,
    attn_own,
    small_sums,
    small_in,
    core_send,
    core_recv,
    part_send,
    part_recv,
    level_send,
    level_recv,
    layer_send,
    layer_recv,
    across_send,
    across_recv,
    along_send,
    along_recv,
    small_send,
    small_recv,
    keep_sem,
):
    low, full = jnp.bfloat16, jnp.float32
    row, column = lax.axis_index("row"), lax.axis_index("col")
    core, level = lax.rem(column, 2), lax.div(column, 2)
    fast, slow = lax.rem(row, across), lax.div(row, across)
    cols = 2 * levels
    seq_len = features_ref.shape[0]
    own_len = seq_len // cols
    width = grad_input_ref.shape[1]
    shard = share_ref.shape[0]
    other = 1 - core
    sibling = (row, level * 2 + other)
    offsets = range(1, levels)

    def peer_level(offset):
        return lax.rem(level + offset, levels)

    def fast_peer(offset):
        return slow * across + lax.rem(fast + offset, across)

    def slow_peer(offset):
        return lax.rem(slow + offset, along) * across + fast

    barrier = pltpu.get_barrier_semaphore()
    greeted = [sibling]
    for offset in offsets:
        greeted += [(row, peer_level(offset) * 2 + core), (row, peer_level(offset) * 2 + other)]
    greeted += [(fast_peer(offset), column) for offset in range(1, across)]
    greeted += [(slow_peer(offset), column) for offset in range(1, along)]
    for device in greeted:
        pl.semaphore_signal(barrier, inc=1, device_id=device, device_id_type=MESH)
    pl.semaphore_wait(barrier, len(greeted))

    def remote(source, target, send, recv, device):
        return pltpu.make_async_remote_copy(
            src_ref=source,
            dst_ref=target,
            send_sem=send,
            recv_sem=recv,
            device_id=device,
            device_id_type=MESH,
        )

    def block(start, size):
        return pl.ds(pl.multiple_of(start * size, size), size)

    out_copy = remote(out_ref.at[1], out_sib, core_send.at[0], core_recv.at[0], sibling)
    attn_copy = remote(
        attn_ref.at[:, block(level * 2 + other, width)],
        attn_in,
        core_send.at[1],
        core_recv.at[1],
        sibling,
    )

    partners = []
    bit = 1
    while bit < levels:
        partners.append((row, (level + bit - 2 * bit * lax.rem(lax.div(level, bit), 2)) * 2 + core))
        bit *= 2
    bit = 1
    while bit < across * along:
        partners.append((row + bit - 2 * bit * lax.rem(lax.div(row, bit), 2), column))
        bit *= 2
    partners.append(sibling)

    def small_copy(turn):
        return remote(
            small_sums.at[turn],
            small_in.at[turn],
            small_send.at[turn],
            small_recv.at[turn],
            partners[turn],
        )

    small_turn = [0]

    def small_step():
        turn = small_turn[0]
        if turn > len(partners):
            return
        if turn > 0:
            small_copy(turn - 1).wait()
            small_sums[turn] = small_sums[turn - 1] + small_in[turn - 1]
        if turn < len(partners):
            small_copy(turn).start()
        small_turn[0] += 1

    def layer_copy(target, place_out, place_in):
        return remote(
            layer_ref.at[:, block(target, width)],
            layer_out_ref.at[block(column, own_len)],
            layer_send.at[place_out],
            layer_recv.at[place_in],
            (row, target),
        )

    layer_copies = [layer_copy(level * 2 + other, 0, 0)]
    for offset in offsets:
        back = levels - offset
        layer_copies.append(
            layer_copy(peer_level(offset) * 2 + core, 2 * offset - 1, 2 * back - 1)
        )
        layer_copies.append(layer_copy(peer_level(offset) * 2 + other, 2 * offset, 2 * back))
    layer_keep = pltpu.make_async_copy(
        layer_ref.at[:, block(column, width)], layer_out_ref.at[block(column, own_len)], keep_sem.at[0]
    )
    attn_keep = pltpu.make_async_copy(
        attn_ref.at[:, block(column, width)], attn_own, keep_sem.at[1]
    )
    attn_keep.start()

    features_all = weights_ref.shape[0]
    units = up_small_ref.shape[1]
    first_up = small_ref.shape[0]
    small_sums[0] = jnp.zeros_like(small_in[0])
    small_sums[0, :first_up, :] = small_ref[...]
    for side in range(2):
        start = (column + side * (1 - 2 * core)) * units
        small_sums[
            0,
            pl.ds(first_up + lax.div(start, features_all), 1),
            pl.ds(pl.multiple_of(lax.rem(start, features_all), units), units),
        ] = up_small_ref[side : side + 1, :]
    first_bias = small_in.shape[1] - 4
    small_sums[0, first_bias : first_bias + 2, block(column, width)] = bias_ref[...]
    small_step()
    out_copy.start()
    attn_copy.start()
    layer_keep.start()
    for copy in layer_copies:
        copy.start()

    def input_part(turn, target):
        return dot_nt(
            query_key_value_ref[block(turn, own_len), :], weights_ref[block(target, width), :]
        )

    def part_copy(turn, place):
        rows = block(turn, own_len)
        return remote(
            core_out.at[place, rows],
            core_in.at[place, rows],
            part_send.at[turn, place],
            part_recv.at[turn, place],
            sibling,
        )

    def give_core():
        @pl.loop(0, cols)
        def _(turn):
            for place in range(levels):
                core_out[place, block(turn, own_len), :] = input_part(
                    turn, place * 2 + other
                ).astype(low)
                part_copy(turn, place).start()

    def across_copy(turn, offset):
        return remote(
            sums.at[block(turn * across + lax.rem(fast + offset, across), shard)],
            got.at[across - offset - 1, block(turn, shard)],
            across_send.at[turn, offset - 1],
            across_recv.at[turn, across - offset - 1],
            (fast_peer(offset), column),
        )

    def weight_grad(turn):
        rows = block(turn, across * shard)
        sums[rows, : 3 * width] = dot_tn(features_ref[:, rows], query_key_value_ref[...]).astype(
            low
        )
        sums[rows, 3 * width :] = (
            out_ref[0, rows, :].astype(full) + out_sib[rows, :].astype(full)
        ).astype(low)
        for offset in range(1, across):
            across_copy(turn, offset).start()

    def level_copy(turn, offset):
        rows = block(turn, own_len)
        return remote(
            level_out.at[offset - 1, rows],
            level_in.at[levels - offset - 1, rows],
            level_send.at[turn, offset - 1],
            level_recv.at[turn, levels - offset - 1],
            (row, peer_level(offset) * 2 + core),
        )

    def give_levels():
        @pl.loop(0, cols)
        def _(turn):
            rows = block(turn, own_len)
            for offset in offsets:
                place = peer_level(offset)
                part = input_part(turn, place * 2 + core)
                part_copy(turn, place).wait_recv()
                level_out[offset - 1, rows, :] = (
                    part + core_in[place, rows, :].astype(full)
                ).astype(low)
                level_copy(turn, offset).start()

    def own_shard(turn):
        for offset in range(1, across):
            across_copy(turn, offset).wait_recv()
        total = sums[block(turn * across + fast, shard), :].astype(full)
        for place in range(across - 1):
            total += got[place, block(turn, shard), :].astype(full)
        return total

    def line_copy(way, target):
        return remote(
            line_out.at[way, target],
            line_in.at[way, target],
            along_send.at[way, target],
            along_recv.at[way, target],
            ((slow + 1 - 2 * way) * across + fast, column),
        )

    def line_step(hop, near):
        if hop >= along - 1 - near:
            return
        for way in range(2):
            target = along - 1 - near if way == 0 else near
            position = hop if way == 0 else along - 1 - hop

            @pl.when(slow == position)
            def _():
                total = own_shard(target)
                if hop > 0:
                    line_copy(way, target).wait_recv()
                    total += line_in[way, target].astype(full)
                line_out[way, target] = total.astype(low)
                line_copy(way, target).start()

    def finish_input(turn, attn_part):
        rows = block(turn, own_len)
        total = input_part(turn, column) + attn_part.astype(full)
        part_copy(turn, level).wait_recv()
        total += core_in[level, rows, :].astype(full)
        for offset in offsets:
            level_copy(turn, offset).wait_recv()
        for place in range(levels - 1):
            total += level_in[place, rows, :].astype(full)
        grad_input_ref[rows, :] = total.astype(low)

    ends = [turn for place in range(along // 2) for turn in (along - 1 - place, place)]
    out_copy.wait()
    small_step()
    for place, turn in enumerate(ends):
        weight_grad(turn)
        if place % 2:
            small_step()
    give_core()
    small_step()
    give_levels()
    small_step()
    line_steps = sorted(
        ((hop, near) for near in range(along - 1) for hop in range(along - 1 - near)),
        key=lambda step: step[0] + 2 * step[1],
    )
    for step in line_steps[: len(line_steps) // 3]:
        line_step(*step)
    attn_keep.wait()
    attn_copy.wait()
    for place in range(levels):
        for step in line_steps[len(line_steps) // 3 :][place::levels]:
            line_step(*step)
        rows = block(place, own_len)
        finish_input(place * 2 + core, attn_own[rows, :])
        finish_input(place * 2 + other, attn_in[rows, :])
    share_ref[...] = own_shard(slow)
    while small_turn[0] <= len(partners):
        small_step()
    small_out_ref[...] = small_sums[len(partners)]

    for way in range(2):

        @pl.when((slow > 0) if way == 0 else (slow < along - 1))
        def _():
            line_copy(way, slow).wait_recv()
            share_ref[...] += line_in[way, slow].astype(full)

    layer_keep.wait()
    for copy in layer_copies:
        copy.wait()
    for way in range(2):
        for target in range(along):

            @pl.when((slow < target) if way == 0 else (slow > target))
            def _():
                line_copy(way, target).wait_send()

    @pl.loop(0, along)
    def _(turn):
        for offset in range(1, across):
            across_copy(turn, offset).wait_send()

    @pl.loop(0, cols)
    def _(turn):
        for place in range(levels):
            part_copy(turn, place).wait_send()
        for offset in offsets:
            level_copy(turn, offset).wait_send()


def finish(
    levels, rows, query_key_value, weights, features, attn_full, layer_own, small, up_small, bias, out
):
    low, full = jnp.bfloat16, jnp.float32
    shape = jax.ShapeDtypeStruct
    across = across_of(rows)
    along = rows // across
    seq_len, features_all = features.shape
    width = query_key_value.shape[1] // 3
    own_len = layer_own.shape[0]
    shard = features_all // rows
    others = levels - 1
    cols = 2 * levels
    turns = 1 + (levels - 1).bit_length() + (rows - 1).bit_length()
    small_rows = small.shape[0] + up_small.shape[1] * cols // features_all + 4
    dma = pltpu.SemaphoreType.DMA
    vmem = pltpu.VMEM
    return pl.pallas_call(
        functools.partial(end_kernel, levels, across, along),
        out_shape=(
            shape((seq_len, width), low),
            shape((seq_len, width), low),
            shape((small_rows, features_all), full),
            shape((shard, 4 * width), full),
        ),
        in_specs=[VMEM] * 3 + [pl.BlockSpec(memory_space=pl.ANY)] * 2 + [VMEM] * 4,
        out_specs=[VMEM] * 4,
        scratch_shapes=[
            vmem((features_all, width), low),
            vmem((features_all, 4 * width), low),
            vmem((across - 1, along * shard, 4 * width), low),
            vmem((2, along, shard, 4 * width), low),
            vmem((2, along, shard, 4 * width), low),
            vmem((levels, seq_len, width), low),
            vmem((levels, seq_len, width), low),
            vmem((others, seq_len, width), low),
            vmem((others, seq_len, width), low),
            vmem((levels * own_len, width), low),
            vmem((levels * own_len, width), low),
            vmem((turns + 1, small_rows, features_all), full),
            vmem((turns, small_rows, features_all), full),
            dma((2,)),
            dma((2,)),
            dma((cols, levels)),
            dma((cols, levels)),
            dma((cols, others)),
            dma((cols, others)),
            dma((cols,)),
            dma((cols,)),
            dma((along, across - 1)),
            dma((along, across - 1)),
            dma((2, along)),
            dma((2, along)),
            dma((turns,)),
            dma((turns,)),
            dma((2,)),
        ],
        compiler_params=pltpu.CompilerParams(
            collective_id=2, has_side_effects=True, vmem_limit_bytes=60 * 1024 * 1024
        ),
        cost_estimate=pl.CostEstimate(
            flops=4 * seq_len * features_all * 3 * width,
            bytes_accessed=20 * 1024 * 1024,
            transcendentals=0,
        ),
    )(query_key_value, weights, features, attn_full, layer_own, small, up_small, bias, out)


def last_kernel(
    grad_input_ref,
    layer_ref,
    small_ref,
    share_ref,
    down_ref,
    up_own_ref,
    up_first_ref,
    *refs,
):
    more, outs = refs[: len(refs) - 17], refs[len(refs) - 17 :]
    (
        layer_out,
        grad_input,
        grad_query,
        bias_query,
        grad_key,
        grad_value,
        bias_value,
        grad_out,
        bias_out,
        gain1,
        shift1,
        grad_up,
        bias_up,
        grad_down,
        bias_down,
        gain2,
        shift2,
    ) = outs
    grad_input[...] = grad_input_ref[...]
    layer_out[...] = layer_ref[...]
    width = grad_query.shape[1]
    for place, ref in enumerate((grad_query, grad_key, grad_value)):
        ref[...] = share_ref[:, place * width : (place + 1) * width]
    grad_out[...] = share_ref[:, 3 * width :].T
    grad_down[...] = down_ref[...].T
    total = up_own_ref[...]
    for ref in (up_first_ref, *more):
        total += ref[...].astype(jnp.float32)
    grad_up[...] = total
    features_all = small_ref.shape[1]
    last = small_ref.shape[0] - 4
    for place, ref in (
        (0, gain2),
        (1, shift2),
        (2, bias_down),
        (3, gain1),
        (4, shift1),
        (5, bias_out),
        (last, bias_query),
        (last + 1, bias_value),
    ):
        ref[...] = small_ref[place : place + 1, :]
    for place in range(8, last):
        bias_up[:, (place - 8) * features_all : (place - 7) * features_all] = small_ref[
            place : place + 1, :
        ]


def put_out(grad_input, layer_out, small, share, down, up_own, up_others):
    low, full = jnp.bfloat16, jnp.float32
    shape = jax.ShapeDtypeStruct
    seq_len, width = grad_input.shape
    shard, units = up_own.shape
    features_all = small.shape[1]
    vector = shape((1, features_all), full)
    units_all = (small.shape[0] - 12) * features_all
    grad = shape((shard, width), full)
    return pl.pallas_call(
        last_kernel,
        out_shape=(
            shape((seq_len, width), low),
            shape((seq_len, width), low),
            grad,
            vector,
            grad,
            grad,
            vector,
            shape((width, shard), full),
            vector,
            vector,
            vector,
            shape((shard, units), full),
            shape((1, units_all), full),
            shape((units, shard), full),
            vector,
            vector,
            vector,
        ),
        in_specs=[VMEM] * (6 + len(up_others)),
        out_specs=[VMEM] * 17,
        compiler_params=pltpu.CompilerParams(vmem_limit_bytes=60 * 1024 * 1024),
    )(grad_input, layer_out, small, share, down, up_own, *up_others)


def on_device(
    hidden_in,
    out_grad,
    lengths,
    global_blocks,
    rand_blocks,
    w_query,
    b_query,
    w_key,
    w_value,
    b_value,
    w_out,
    b_out,
    ln1_gain,
    ln1_bias,
    w_up,
    b_up,
    w_down,
    b_down,
    ln2_gain,
    ln2_bias,
):
    cols = lax.axis_size("col")
    rows = lax.axis_size("row")
    tables = (lengths, global_blocks.reshape(-1), rand_blocks.reshape(-1))
    as_row = lambda vector: vector[None, :]
    (
        features,
        own_features,
        upstream,
        queries,
        key_rows,
        value_rows,
        context,
        highest,
        scale,
        full_qkv,
        full_out,
        full_up,
        full_down,
        out_sib,
        up_sib,
        down_sib,
        context_sib,
        normed_full,
        unit1,
        inv1,
    ) = front(
        cols // 2,
        rows,
        tables,
        hidden_in,
        out_grad,
        (as_row(b_query), as_row(b_value)),
        (w_query, w_key, w_value, w_out, w_up, w_down),
        (as_row(b_out), as_row(ln1_gain), as_row(ln1_bias)),
    )
    (
        layer_own,
        context_grad,
        attn_full,
        small,
        up_small,
        down_share,
        up_own,
        grad_out,
        *up_part,
    ) = middle(
        cols // 2,
        rows,
        lengths,
        context,
        context_sib,
        upstream,
        (full_out, out_sib, full_up, up_sib, full_down, down_sib),
        normed_full,
        unit1,
        inv1,
        tuple(as_row(each) for each in (ln1_gain, ln1_bias, b_down, ln2_gain, ln2_bias)),
        as_row(b_up),
    )
    across = across_of(rows)
    up_others = [
        lax.ppermute(
            up_part[shift - 1],
            "row",
            [(place, (place + shift * across) % rows) for place in range(rows)],
        )
        for shift in range(1, rows // across)
    ]
    query_key_value, bias_sums = attend_back(
        queries, key_rows, value_rows, tables, (highest, scale), context_grad
    )
    grad_input, layer_out, small, share = finish(
        cols // 2,
        rows,
        query_key_value,
        full_qkv,
        features,
        attn_full,
        layer_own,
        small,
        up_small,
        bias_sums,
        grad_out,
    )
    outs = put_out(grad_input, layer_out, small, share, down_share, up_own, up_others)
    return tuple(each.reshape(-1) if each.shape[0] == 1 else each for each in outs)


def solution(mesh):
    placed = (
        P("row", "col"),
        P("row", "col"),
        P("row"),
        P("row", None),
        P("row", None, "col", None),
        P("row", "col"),
        P(),
        P("row", "col"),
        P("row", "col"),
        P(),
        P("col", "row"),
        P(),
        P(),
        P(),
        P("row", "col"),
        P(),
        P("col", "row"),
        P(),
        P(),
        P(),
    )
    return jax.shard_map(
        on_device,
        mesh=mesh,
        in_specs=placed,
        out_specs=(
            P("row", "col"),
            P("row", "col"),
            P("row", "col"),
            P(),
            P("row", "col"),
            P("row", "col"),
            P(),
            P("col", "row"),
            P(),
            P(),
            P(),
            P("row", "col"),
            P(),
            P("col", "row"),
            P(),
            P(),
            P(),
        ),
        check_vma=False,
    )
```

```python
import functools
import math

import jax
import jax.numpy as jnp
from jax import lax
from jax.experimental import pallas as pl
from jax.experimental.pallas import tpu as pltpu
from jax.sharding import PartitionSpec as P

DH = 64
BLK = 64
MESH = pl.DeviceIdType.MESH


epsilon = 1e-06


def lane_heads(rows, width):
    return lax.broadcasted_iota(jnp.int32, (rows, width), 1) // DH


def by_diagonal(rows, width):
    lane_head = lane_heads(BLK, width)
    zero = jnp.zeros_like(rows)
    return jnp.concatenate(
        [jnp.where(lane_head == head, rows, zero) for head in range(width // DH)], axis=0
    )


def from_diagonal(square, width):
    lane_head = lane_heads(BLK, width)
    result = jnp.zeros((BLK, width), jnp.float32)
    for head in range(width // DH):
        result = jnp.where(lane_head == head, square[head * BLK : (head + 1) * BLK, :], result)
    return result


def slot_starts(step, num_blocks, head_count, globals_ref, random_ref):
    shared = [
        jnp.maximum(step - 1, 0),
        step,
        jnp.minimum(step + 1, num_blocks - 1),
        globals_ref[0],
        globals_ref[1],
    ]
    base = step * (head_count * 3)
    apart = [
        [random_ref[base + head * 3 + slot] for head in range(head_count)] for slot in range(3)
    ]
    return shared, apart


def lane_groups(head_count):
    per_group = min(128 // DH, head_count)
    return [
        (first * DH, per_group * DH, list(range(first, first + per_group)))
        for first in range(0, head_count, per_group)
    ]


def picked_rows(rows_ref, shared, apart, head_count):
    pieces = [rows_ref[block] for block in shared]
    for blocks in apart:
        groups = []
        for lane, width, heads in lane_groups(head_count):
            lane_head = lane_heads(BLK, width)
            piece = rows_ref[blocks[heads[0]], :, lane : lane + width]
            for place, head in enumerate(heads[1:], 1):
                other = rows_ref[blocks[head], :, lane : lane + width]
                piece = jnp.where(lane_head >= place, other, piece)
            groups.append(piece)
        pieces.append(jnp.concatenate(groups, axis=1) if len(groups) > 1 else groups[0])
    return jnp.concatenate(pieces, axis=0)


def put_rows(sums_ref, values_in, shared, apart, head_count):
    for slot, block in enumerate(shared):
        sums_ref[block] += values_in[slot * BLK : (slot + 1) * BLK, :]
    for slot, blocks in enumerate(apart, len(shared)):
        rows = values_in[slot * BLK : (slot + 1) * BLK, :]
        for lane, width, heads in lane_groups(head_count):
            lane_head = lane_heads(BLK, width)
            for place, head in enumerate(heads):
                sums_ref[blocks[head], :, lane : lane + width] += jnp.where(
                    lane_head == place, rows[:, lane : lane + width], 0.0
                )


def masked_scores(picked_keys, grouped, step, num_blocks, length, shared, apart):
    width = grouped.shape[1]
    scores = lax.dot_general(
        picked_keys, grouped, (((1,), (1,)), ((), ())), preferred_element_type=jnp.float32
    )
    listed = [step >= 1, True, step + 1 < num_blocks]
    listed += [(block < step - 1) | (block > step + 1) for block in shared[3:]]
    limits = [
        jnp.where(there, length - block * BLK, 0) for there, block in zip(listed, shared)
    ]
    lane_head = lane_heads(1, width)
    for blocks in apart:
        limit = length - jnp.full((1, width), blocks[0], jnp.int32) * BLK
        for head, block in enumerate(blocks[1:], 1):
            limit = jnp.where(lane_head >= head, length - block * BLK, limit)
        limits.append(limit)
    row = lax.broadcasted_iota(jnp.int32, (BLK, width), 0)
    return [
        jnp.where(row < limit, scores[slot * BLK : (slot + 1) * BLK, :], -1e30)
        for slot, limit in enumerate(limits)
    ]


def attend_blocks(
    first, count, unroll, length_ref, globals_ref, random_ref, refs, context_ref, stat_refs
):
    queries_ref, keys_ref, values_ref = refs
    highest_ref, scale_ref = stat_refs
    seq_len, width = queries_ref.shape
    head_count = width // DH
    num_blocks = seq_len // BLK

    def one_block(step):
        shared, apart = slot_starts(step, num_blocks, head_count, globals_ref, random_ref)
        own = pl.ds(pl.multiple_of(step * BLK, BLK), BLK)
        grouped = by_diagonal(queries_ref[own, :] * jnp.bfloat16(1.0 / math.sqrt(DH)), width)
        scores = masked_scores(
            picked_rows(keys_ref, shared, apart, head_count),
            grouped,
            step,
            num_blocks,
            length_ref[0],
            shared,
            apart,
        )
        highest = jnp.max(functools.reduce(jnp.maximum, scores), axis=0, keepdims=True)
        exponent = [jnp.exp(piece - highest) for piece in scores]
        denominator = jnp.sum(sum(exponent[1:], exponent[0]), axis=0, keepdims=True)
        scale = 1.0 / denominator
        attn_probs = jnp.concatenate(
            [(piece * scale).astype(jnp.bfloat16) for piece in exponent], axis=0
        )
        square = lax.dot_general(
            attn_probs,
            picked_rows(values_ref, shared, apart, head_count),
            (((0,), (0,)), ((), ())),
            preferred_element_type=jnp.float32,
        )
        context_ref[own, :] = from_diagonal(square, width).astype(jnp.bfloat16)
        highest_ref[step] = highest
        scale_ref[step] = scale

    @pl.loop(0, count // unroll)
    def _(turn):
        for place in range(unroll):
            one_block(first + turn * unroll + place)


def attend_back_kernel(
    head_count,
    unroll,
    length_ref,
    globals_ref,
    random_ref,
    queries_ref,
    keys_ref,
    values_ref,
    grads_ref,
    highest_ref,
    scale_ref,
    grads_out_ref,
    bias_ref,
    key_sums,
    value_sums,
    query_total,
):
    width = head_count * DH
    num_blocks = queries_ref.shape[0] // BLK
    factor = 1.0 / math.sqrt(DH)
    key_sums[...] = jnp.zeros_like(key_sums)
    value_sums[...] = jnp.zeros_like(value_sums)
    query_total[...] = jnp.zeros_like(query_total)

    def one_block(step):
        shared, apart = slot_starts(step, num_blocks, head_count, globals_ref, random_ref)
        own = pl.ds(pl.multiple_of(step * BLK, BLK), BLK)
        grouped = by_diagonal(queries_ref[own, :] * jnp.bfloat16(factor), width)
        grouped_grad = by_diagonal(grads_ref[own, :], width)
        picked_keys = picked_rows(keys_ref, shared, apart, head_count)
        picked_values = picked_rows(values_ref, shared, apart, head_count)
        scores = masked_scores(
            picked_keys, grouped, step, num_blocks, length_ref[0], shared, apart
        )
        highest = highest_ref[step]
        scale = scale_ref[step]
        attn_probs = [jnp.exp(piece - highest) * scale for piece in scores]
        prob_grad = lax.dot_general(
            picked_values,
            grouped_grad,
            (((1,), (1,)), ((), ())),
            preferred_element_type=jnp.float32,
        )
        prob_grads = [prob_grad[slot * BLK : (slot + 1) * BLK, :] for slot in range(8)]
        products = [left * right for left, right in zip(attn_probs, prob_grads)]
        total = jnp.sum(sum(products[1:], products[0]), axis=0, keepdims=True)
        score_grad = jnp.concatenate(
            [
                (left * (right - total)).astype(jnp.bfloat16)
                for left, right in zip(attn_probs, prob_grads)
            ],
            axis=0,
        )
        probs_low = jnp.concatenate([piece.astype(jnp.bfloat16) for piece in attn_probs], axis=0)
        square = lax.dot_general(
            score_grad, picked_keys, (((0,), (0,)), ((), ())), preferred_element_type=jnp.float32
        )
        query_grad = (from_diagonal(square, width) * factor).astype(jnp.bfloat16)
        grads_out_ref[own, :width] = query_grad
        query_total[...] += jnp.sum(
            query_grad.astype(jnp.float32).reshape(BLK // 8, 8, width), axis=0
        )
        key_part = jnp.dot(score_grad, grouped, preferred_element_type=jnp.float32)
        value_part = jnp.dot(probs_low, grouped_grad, preferred_element_type=jnp.float32)
        put_rows(key_sums, key_part, shared, apart, head_count)
        put_rows(value_sums, value_part, shared, apart, head_count)

    @pl.loop(0, num_blocks // unroll)
    def _(turn):
        for place in range(unroll):
            one_block(turn * unroll + place)

    value_grad = value_sums[...].reshape(queries_ref.shape).astype(jnp.bfloat16)
    seq_len = queries_ref.shape[0]
    grads_out_ref[:, width : 2 * width] = key_sums[...].reshape(seq_len, width).astype(jnp.bfloat16)
    grads_out_ref[:, 2 * width :] = value_grad
    bias_ref[0:1, :] = jnp.sum(query_total[...], axis=0, keepdims=True)
    bias_ref[1:2, :] = jnp.sum(value_grad.astype(jnp.float32), axis=0, keepdims=True)


VMEM = pl.BlockSpec(memory_space=pltpu.VMEM)
SMEM = pl.BlockSpec(memory_space=pltpu.SMEM)


def attend_back(queries, key_rows, value_rows, tables, stats, context_grad):
    seq_len, width = queries.shape
    head_count = width // DH
    return pl.pallas_call(
        functools.partial(attend_back_kernel, head_count, 8),
        out_shape=(
            jax.ShapeDtypeStruct((seq_len, 3 * width), jnp.bfloat16),
            jax.ShapeDtypeStruct((2, width), jnp.float32),
        ),
        in_specs=[SMEM] * 3 + [VMEM] * 6,
        out_specs=[VMEM] * 2,
        scratch_shapes=[pltpu.VMEM((seq_len // BLK, BLK, width), jnp.float32)] * 2
        + [pltpu.VMEM((8, width), jnp.float32)],
        compiler_params=pltpu.CompilerParams(vmem_limit_bytes=60 * 1024 * 1024),
        cost_estimate=pl.CostEstimate(
            flops=10 * seq_len * 512 * width * head_count,
            bytes_accessed=14 * seq_len * width,
            transcendentals=seq_len * 512 * head_count,
        ),
    )(*tables, queries, key_rows, value_rows, context_grad, *stats)


KINDS = 4
CHUNKS = 4


def front_kernel(
    levels,
    across,
    along,
    length_ref,
    globals_ref,
    random_ref,
    hidden_ref,
    grads_ref,
    b_query_ref,
    b_value_ref,
    w_query_ref,
    w_key_ref,
    w_value_ref,
    w_out_ref,
    w_up_ref,
    w_down_ref,
    b_out,
    gain1,
    shift1,
    features_far,
    own_far,
    upstream_far,
    queries_far,
    keys_far,
    values_far,
    context_far,
    highest_ref,
    scale_ref,
    full_qkv_far,
    full_out_ref,
    full_up_far,
    full_down_far,
    out_sib,
    up_sib_far,
    down_sib_far,
    context_sib,
    normed_full,
    unit1,
    inv1,
    features_ref,
    own_ref,
    upstream_ref,
    queries_ref,
    keys_ref,
    values_ref,
    context_ref,
    full_qkv_ref,
    full_up_ref,
    full_down_ref,
    up_sib,
    down_sib,
    far_sem,
    sum_out,
    sum_in,
    level_send,
    level_recv,
    core_send,
    core_recv,
    swap_send,
    swap_recv,
    along_send,
    along_recv,
    across_send,
    across_recv,
    shard_send,
    shard_recv,
    context_send,
    context_recv,
    sum_send,
    sum_recv,
    normed_send,
    normed_recv,
):
    low, full = jnp.bfloat16, jnp.float32
    row, column = lax.axis_index("row"), lax.axis_index("col")
    core, level = lax.rem(column, 2), lax.div(column, 2)
    fast, slow = lax.rem(row, across), lax.div(row, across)
    cols = 2 * levels
    seq_len, width = hidden_ref.shape
    own_len = seq_len // cols
    shard = w_query_ref.shape[0]
    other = 1 - core
    sibling = (row, level * 2 + other)
    offsets = range(1, levels)

    def peer_level(offset):
        return lax.rem(level + offset, levels)

    def fast_peer(offset):
        return slow * across + lax.rem(fast + offset, across)

    def line_peer(shift):
        return ((slow + shift) * across + fast, column)

    barrier = pltpu.get_barrier_semaphore()
    greeted = [sibling]
    for offset in offsets:
        greeted += [(row, peer_level(offset) * 2 + core), (row, peer_level(offset) * 2 + other)]
    greeted += [(fast_peer(offset), column) for offset in range(1, across)]
    greeted += [
        (lax.rem(slow + offset, along) * across + fast, column) for offset in range(1, along)
    ]
    for device in greeted:
        pl.semaphore_signal(barrier, inc=1, device_id=device, device_id_type=MESH)
    pl.semaphore_wait(barrier, len(greeted))

    def remote(source, target, send, recv, device):
        return pltpu.make_async_remote_copy(
            src_ref=source,
            dst_ref=target,
            send_sem=send,
            recv_sem=recv,
            device_id=device,
            device_id_type=MESH,
        )

    def block(start, size):
        return pl.ds(pl.multiple_of(start * size, size), size)

    def level_copy(turn, offset):
        rows = block(turn, own_len)
        return remote(
            hidden_ref.at[rows],
            features_ref.at[rows, block(column, width)],
            level_send.at[turn, offset - 1],
            level_recv.at[turn, levels - offset - 1],
            (row, peer_level(offset) * 2 + core),
        )

    def core_copy(turn, offset):
        view = features_ref.at[block(turn, own_len), block(peer_level(offset) * 2 + core, width)]
        return remote(
            view, view, core_send.at[turn, offset], core_recv.at[turn, offset], sibling
        )

    @pl.loop(0, cols)
    def _(turn):
        for offset in offsets:
            level_copy(turn, offset).start()
        rows = block(turn, own_len)
        features_ref[rows, block(column, width)] = hidden_ref[rows, :]
        core_copy(turn, 0).start()

    fulls = (full_qkv_ref, full_out_ref, full_up_ref, full_down_ref)
    sibs = (None, out_sib, up_sib, down_sib)

    def shard_rows(place):
        return block(place * across + fast, shard)

    def line_copy(kind, way, hop):
        view = fulls[kind].at[shard_rows(slow - (1 - 2 * way) * hop)]
        return remote(
            view,
            view,
            along_send.at[kind, way, hop],
            along_recv.at[kind, way, hop],
            line_peer(1 - 2 * way),
        )

    def line_can_send(way, hop):
        if way == 0:
            return (slow >= hop) & (slow < along - 1)
        return (slow < along - hop) & (slow > 0)

    def line_send(kind, hop):
        for way in range(2):

            @pl.when(line_can_send(way, hop))
            def _():
                line_copy(kind, way, hop).start()

    def line_got(way, hop):
        place = slow - (1 - 2 * way) * (hop + 1)
        return place, ((place >= 0) if way == 0 else (place < along))

    def line_wait(kind, way, hop):
        place, _ = line_got(way, hop)
        view = fulls[kind].at[shard_rows(place)]
        remote(
            view,
            view,
            along_send.at[kind, way, hop],
            along_recv.at[kind, way, hop],
            line_peer(-(1 - 2 * way)),
        ).wait_recv()

    def across_copy(kind, place, offset):
        view = fulls[kind].at[shard_rows(place)]
        return remote(
            view,
            view,
            across_send.at[kind, place, offset - 1],
            across_recv.at[kind, place, across - offset - 1],
            (fast_peer(offset), column),
        )

    def core_shard(kind, place, offset):
        rows = block(place * across + lax.rem(fast + offset, across), shard)
        return remote(
            fulls[kind].at[rows],
            sibs[kind].at[rows],
            shard_send.at[kind - 1, place, offset],
            shard_recv.at[kind - 1, place, offset],
            sibling,
        )

    for place, ref in enumerate((w_query_ref, w_key_ref, w_value_ref)):
        full_qkv_ref[shard_rows(slow), place * width : (place + 1) * width] = ref[...].astype(low)
    line_send(0, 0)
    full_out_ref[shard_rows(slow), :] = w_out_ref[...].T.astype(low)
    full_up_ref[shard_rows(slow), :] = w_up_ref[...].astype(low)
    full_down_ref[shard_rows(slow), :] = w_down_ref[...].T.astype(low)

    def swap_copy(target, place_out, place_in):
        return remote(
            grads_ref.at[block(target, own_len)],
            upstream_ref.at[:, block(column, width)],
            swap_send.at[place_out],
            swap_recv.at[place_in],
            (row, target),
        )

    swaps = [swap_copy(level * 2 + other, 0, 0)]
    for offset in offsets:
        back = levels - offset
        swaps.append(swap_copy(peer_level(offset) * 2 + core, 2 * offset - 1, 2 * back - 1))
        swaps.append(swap_copy(peer_level(offset) * 2 + other, 2 * offset, 2 * back))
    for copy in swaps:
        copy.start()
    upstream_ref[:, block(column, width)] = grads_ref[block(column, own_len), :]

    def pass_shard(kind, place):
        for step in range(1, across):
            across_copy(kind, place, step).start()
        if kind > 0:
            core_shard(kind, place, 0).start()

    hops = range(along - 1)
    waiting = [(1, hop) for hop in hops] + [(3, -1), (2, 0), (3, 0)]
    waiting += [(kind, hop) for hop in hops if hop > 0 for kind in (2, 3)]

    def pass_on(count=1):
        pass_these(waiting[:count])
        del waiting[:count]

    def pass_these(shards):
        for kind, hop in shards:
            if hop < 0:
                pass_shard(kind, slow)
                continue
            for way in range(2):
                place, there = line_got(way, hop)

                @pl.when(there)
                def _():
                    line_wait(kind, way, hop)
                    if hop < along - 2:

                        @pl.when(line_can_send(way, hop + 1))
                        def _():
                            line_copy(kind, way, hop + 1).start()

                    pass_shard(kind, place)
    def await_shards(kind):
        @pl.loop(0, along)
        def _(place):
            for offset in range(1, across):
                across_copy(kind, place, across - offset).wait_recv()
                if kind > 0:
                    core_shard(kind, place, offset).start()

    def await_sibling(kind):
        @pl.loop(0, along)
        def _(place):
            for offset in range(across):
                core_shard(kind, place, offset).wait_recv()

    pass_these([(0, hop) for hop in range(-1, along - 2)])
    for kind in range(1, KINDS):
        line_send(kind, 0)
    pass_these([(0, along - 2), (1, -1), (2, -1)])
    await_shards(0)

    def project(turn):
        rows = block(turn, own_len)
        for offset in offsets:
            level_copy(turn, levels - offset).wait_recv()
            core_copy(turn, offset).start()
        for offset in range(levels):
            core_copy(turn, offset).wait_recv()
        values_in = features_ref[rows, :]
        queries_ref[rows, :] = (
            dot(values_in, full_qkv_ref[:, :width]) + b_query_ref[:, block(column, width)]
        ).astype(low)
        blocks = pl.ds(turn * (own_len // BLK), own_len // BLK)
        by_block = (own_len // BLK, BLK, width)
        keys_ref[blocks] = (
            dot(values_in, full_qkv_ref[:, width : 2 * width]).astype(low).reshape(by_block)
        )
        values_ref[blocks] = (
            (dot(values_in, full_qkv_ref[:, 2 * width :]) + b_value_ref[:, block(column, width)])
            .astype(low)
            .reshape(by_block)
        )

    for turn in range(cols):
        project(turn)
        pass_on(1 if (3, -1) in waiting else 0)
    while (2, 0) in waiting:
        pass_on()
    own_ref[...] = features_ref[block(column, own_len), :]
    far = [
        pltpu.make_async_copy(source, target, far_sem.at[place])
        for place, (source, target) in enumerate(
            [
                (features_ref, features_far),
                (own_ref, own_far),
                (queries_ref, queries_far),
                (keys_ref, keys_far),
                (values_ref, values_far),
                (full_qkv_ref, full_qkv_far),
                (upstream_ref, upstream_far),
                (context_ref, context_far),
                (full_up_ref, full_up_far),
                (up_sib, up_sib_far),
                (full_down_ref, full_down_far),
                (down_sib, down_sib_far),
            ]
        )
    ]
    @pl.loop(0, cols)
    def _(turn):
        for offset in range(levels):
            core_copy(turn, offset).wait_send()

    for copy in far[:6]:
        copy.start()

    step = own_len // CHUNKS
    halves = 2
    count = own_len // BLK // halves

    def attend_half(quarter, half):
        attend_blocks(
            (quarter * halves + half) * count,
            count,
            min(count, 4),
            length_ref,
            globals_ref,
            random_ref,
            (queries_ref, keys_ref, values_ref),
            context_ref,
            (highest_ref, scale_ref),
        )

    def context_copy(place, half):
        rows = own_len // halves
        return remote(
            context_ref.at[block((place * 2 + other) * halves + half, rows)],
            context_sib.at[block(place * halves + half, rows)],
            context_send.at[place, half],
            context_recv.at[place, half],
            sibling,
        )

    def chunk_rows(place, chunk):
        return block(place * CHUNKS + chunk, step)

    def attn_part(place, chunk):
        return dot_nt(
            context_ref[chunk_rows(place * 2 + core, chunk), :], full_out_ref[...]
        ) + dot_nt(context_sib[chunk_rows(place, chunk), :], out_sib[...])

    def sum_copy(chunk, offset):
        rows = block(chunk, step)
        return remote(
            sum_out.at[offset - 1, rows],
            sum_in.at[levels - offset - 1, rows],
            sum_send.at[chunk, offset - 1],
            sum_recv.at[chunk, levels - offset - 1],
            (row, peer_level(offset) * 2 + core),
        )

    def normed_copy(chunk, offset):
        view = normed_full.at[chunk_rows(level, chunk)]
        return remote(
            view,
            view,
            normed_send.at[chunk, offset - 1],
            normed_recv.at[chunk, levels - offset - 1],
            (row, peer_level(offset) * 2 + core),
        )

    for offset in list(offsets) + [0]:
        place = peer_level(offset)
        for half in range(halves):
            attend_half(place * 2 + other, half)
            context_copy(place, half).start()
            pass_on(1 - half if offset else half)
        if offset == 1:
            await_shards(1)
        for half in range(halves):
            attend_half(place * 2 + core, half)
            if offset == 1 and half == 0:
                await_sibling(1)
            context_copy(place, half).wait_recv()
            per_half = CHUNKS // halves
            for chunk in range(half * per_half, (half + 1) * per_half):
                if offset:
                    sum_out[offset - 1, block(chunk, step), :] = attn_part(place, chunk).astype(
                        low
                    )
                    sum_copy(chunk, offset).start()
            pass_on(1 if offset else half)
    pass_on(len(waiting))
    for copy in swaps:
        copy.wait()
    for copy in far[6:8]:
        copy.start()
    for chunk in range(CHUNKS):
        rows = block(chunk, step)
        summed = own_ref[rows, :].astype(full) + attn_part(level, chunk) + b_out[...]
        for offset in offsets:
            sum_copy(chunk, offset).wait_recv()
        for place in range(levels - 1):
            summed += sum_in[place, rows, :].astype(full)
        normed, inv_std = norm_parts(summed)
        unit1[rows, :] = normed
        inv1[rows, :] = inv_std
        normed_full[chunk_rows(level, chunk), :] = (normed * gain1[...] + shift1[...]).astype(low)
        for offset in offsets:
            normed_copy(chunk, offset).start()
    await_shards(2)
    await_shards(3)
    for kind in range(2, KINDS):
        await_sibling(kind)
        for copy in far[4 + 2 * kind : 6 + 2 * kind]:
            copy.start()
    for chunk in range(CHUNKS):
        for offset in offsets:
            normed_copy(chunk, offset).wait()
            sum_copy(chunk, offset).wait_send()
    for place in range(levels):
        for half in range(halves):
            context_copy(place, half).wait_send()
    for copy in far:
        copy.wait()
    for kind in range(KINDS):
        for hop in range(along - 1):
            for way in range(2):

                @pl.when(line_can_send(way, hop))
                def _():
                    line_copy(kind, way, hop).wait_send()

        @pl.loop(0, along)
        def _(place):
            for offset in range(1, across):
                across_copy(kind, place, offset).wait_send()
            if kind > 0:
                for offset in range(across):
                    core_shard(kind, place, offset).wait_send()

    @pl.loop(0, cols)
    def _(turn):
        for offset in offsets:
            level_copy(turn, offset).wait_send()


def across_of(rows):
    return 2 if rows <= 8 else rows // 4


def front(levels, rows, tables, hidden_in, grads, biases, weights, vectors):
    low, full = jnp.bfloat16, jnp.float32
    shape = jax.ShapeDtypeStruct
    across = across_of(rows)
    along = rows // across
    seq_len, width = hidden_in.shape
    cols = 2 * levels
    own_len = seq_len // cols
    features_all = width * cols
    units = weights[4].shape[1]
    widths = (3 * width, width, units, units)
    others = levels - 1
    stat = shape((seq_len // BLK, 1, width), full)
    hbm = pl.BlockSpec(memory_space=pl.ANY)
    dma = pltpu.SemaphoreType.DMA
    return pl.pallas_call(
        functools.partial(front_kernel, levels, across, along),
        out_shape=(
            shape((seq_len, features_all), low),
            shape((own_len, features_all), low),
            shape((own_len, features_all), low),
            shape((seq_len, width), low),
            shape((seq_len // BLK, BLK, width), low),
            shape((seq_len // BLK, BLK, width), low),
            shape((seq_len, width), low),
            stat,
            stat,
            *(shape((features_all, each), low) for each in widths),
            *(shape((features_all, each), low) for each in widths[1:]),
            shape((levels * own_len, width), low),
            shape((levels * own_len, features_all), low),
            shape((own_len, features_all), full),
            shape((own_len, 1), full),
        ),
        in_specs=[SMEM] * 3 + [VMEM] * 13,
        out_specs=[hbm] * 7 + [VMEM] * 2 + [hbm] + [VMEM, hbm, hbm] * 2 + [VMEM] * 4,
        scratch_shapes=[
            pltpu.VMEM((seq_len, features_all), low),
            pltpu.VMEM((own_len, features_all), low),
            pltpu.VMEM((own_len, features_all), low),
            pltpu.VMEM((seq_len, width), low),
            pltpu.VMEM((seq_len // BLK, BLK, width), low),
            pltpu.VMEM((seq_len // BLK, BLK, width), low),
            pltpu.VMEM((seq_len, width), low),
            pltpu.VMEM((features_all, 3 * width), low),
            *(pltpu.VMEM((features_all, units), low) for _ in range(4)),
            dma((12,)),
            pltpu.VMEM((others, own_len, features_all), low),
            pltpu.VMEM((others, own_len, features_all), low),
            dma((cols, others)),
            dma((cols, others)),
            dma((cols, levels)),
            dma((cols, levels)),
            dma((cols,)),
            dma((cols,)),
            dma((KINDS, 2, along - 1)),
            dma((KINDS, 2, along - 1)),
            dma((KINDS, along, across - 1)),
            dma((KINDS, along, across - 1)),
            dma((KINDS - 1, along, across)),
            dma((KINDS - 1, along, across)),
            dma((levels, 2)),
            dma((levels, 2)),
            *(dma((CHUNKS, others)) for _ in range(4)),
        ],
        compiler_params=pltpu.CompilerParams(
            collective_id=3, has_side_effects=True, vmem_limit_bytes=56 * 1024 * 1024
        ),
        cost_estimate=pl.CostEstimate(
            flops=2 * seq_len * features_all * 3 * width,
            bytes_accessed=20 * 1024 * 1024,
            transcendentals=seq_len * 512 * (width // DH),
        ),
    )(*tables, hidden_in, grads, *biases, *weights, *vectors)


def dot(left, right):
    return jnp.dot(left, right, preferred_element_type=jnp.float32)


def dot_nt(left, right):
    return lax.dot_general(
        left, right, (((1,), (1,)), ((), ())), preferred_element_type=jnp.float32
    )


def dot_tn(left, right):
    return lax.dot_general(
        left, right, (((0,), (0,)), ((), ())), preferred_element_type=jnp.float32
    )


def gelu_parts(values_in):
    factor = math.sqrt(2.0 / math.pi)
    square = values_in * values_in
    bent = jnp.tanh(factor * (values_in + 0.044715 * (values_in * square)))
    half = 0.5 * (1.0 + bent)
    slope = half + (0.5 * values_in) * (1.0 - bent * bent) * (
        factor + (3.0 * 0.044715 * factor) * square
    )
    return (values_in * half, slope)


def norm_parts(summed):
    average = jnp.mean(summed, axis=1, keepdims=True)
    squares = jnp.mean(summed * summed, axis=1, keepdims=True)
    inv_std = lax.rsqrt(squares - average * average + epsilon)
    return ((summed - average) * inv_std, inv_std)


def norm_back(upstream, normed, inv_std, gain_vec):
    scaled = upstream * gain_vec
    left = jnp.mean(scaled, axis=1, keepdims=True)
    right = jnp.mean(scaled * normed, axis=1, keepdims=True)
    return inv_std * (scaled - left - normed * right)


def middle_kernel(
    levels,
    across,
    along,
    length_ref,
    context_far,
    context_sib_far,
    upstream_far,
    out_far,
    out_sib_far,
    up_ref,
    up_sib,
    down_full,
    down_sib,
    normed_full,
    unit1_far,
    inv1,
    gain1,
    shift1,
    b_down,
    gain2,
    shift2,
    b_up_ref,
    layer_out_ref,
    context_grad_ref,
    attn_full,
    small_ref,
    up_small_ref,
    share_down_ref,
    up_part_ref,
    grad_out_ref,
    *refs,
):
    (
        ffn_full,
        hidden,
        slope,
        pre_grad,
        ffn_keep,
        part_own,
        send_buf,
        recv_buf,
        context_send,
        stage,
        down_sums,
        up_sums,
        down_got,
        up_got,
        down_pass,
        down_in,
        send_sem,
        recv_sem,
        core_send,
        core_recv,
        along_send,
        along_recv,
        across_send,
        across_recv,
        stage_sem,
        context_ref,
        context_sib,
        upstream_ref,
        out_ref,
        out_sib,
        unit1,
        late_sem,
        free_sem,
    ) = refs
    low = jnp.bfloat16
    row, column = lax.axis_index("row"), lax.axis_index("col")
    core = lax.rem(column, 2)
    level = lax.div(column, 2)
    sibling = (row, column + 1 - 2 * core)
    fast, slow = lax.rem(row, across), lax.div(row, across)
    shard = share_down_ref.shape[0]
    own_len = upstream_ref.shape[0]
    units = up_ref.shape[1]
    step = own_len // CHUNKS

    def peer_level(offset):
        return lax.rem(level + offset, levels)

    def fast_peer(offset):
        return slow * across + lax.rem(fast + offset, across)

    late = [
        pltpu.make_async_copy(source, target, late_sem.at[place])
        for place, (source, target) in enumerate(
            [
                (unit1_far, unit1),
                (upstream_far, upstream_ref),
                (context_far, context_ref),
                (context_sib_far, context_sib),
                (out_far, out_ref),
                (out_sib_far, out_sib),
            ]
        )
    ]
    for copy in late:
        copy.start()

    barrier = pltpu.get_barrier_semaphore()
    greeted = [sibling]
    greeted += [(row, peer_level(offset) * 2 + core) for offset in range(1, levels)]
    greeted += [(fast_peer(offset), column) for offset in range(1, across)]
    greeted += [
        (lax.rem(slow + offset, along) * across + fast, column) for offset in range(1, along)
    ]
    for device in greeted:
        pl.semaphore_signal(barrier, inc=1, device_id=device, device_id_type=MESH)
    pl.semaphore_wait(barrier, len(greeted))

    def remote(source, target, send, recv, device):
        return pltpu.make_async_remote_copy(
            src_ref=source,
            dst_ref=target,
            send_sem=send,
            recv_sem=recv,
            device_id=device,
            device_id_type=MESH,
        )

    def block(start, size):
        return pl.ds(pl.multiple_of(start * size, size), size)

    def to_sibling(source, target, place):
        return remote(source, target, core_send.at[place], core_recv.at[place], sibling)

    def rows_of(place, chunk):
        return pl.ds(pl.multiple_of(place * own_len + chunk * step, step), step)

    def own_rows(chunk):
        return pl.ds(pl.multiple_of(chunk * step, step), step)

    def exchange(kind, chunk, offset, source, target):
        return pltpu.make_async_remote_copy(
            src_ref=source,
            dst_ref=target,
            send_sem=send_sem.at[kind - 2, chunk, offset - 1],
            recv_sem=recv_sem.at[kind - 2, chunk, levels - offset - 1],
            device_id=(row, peer_level(offset) * 2 + core),
            device_id_type=MESH,
        )

    def sum_copy(kind, chunk, offset):
        return exchange(
            kind,
            chunk,
            offset,
            send_buf.at[kind // 2 - 1, offset - 1, own_rows(chunk)],
            recv_buf.at[kind // 2 - 1, levels - offset - 1, own_rows(chunk)],
        )

    def spread_copy(kind, chunk, offset):
        whole = {3: ffn_full, 5: attn_full}[kind]
        rows = rows_of(level, chunk)
        return exchange(kind, chunk, offset, whole.at[rows], whole.at[rows])

    def received(kind, chunk):
        return sum(
            recv_buf[kind // 2 - 1, place, own_rows(chunk), :].astype(jnp.float32)
            for place in range(levels - 1)
        )

    offsets = range(1, levels)
    small_ref[...] = jnp.zeros_like(small_ref)
    up_small_ref[...] = jnp.zeros_like(up_small_ref)
    def context_rows(place, chunk):
        start = (place * 2 + core) * own_len + chunk * step
        return pl.ds(pl.multiple_of(start, step), step)

    sides = ((up_ref, down_full), (up_sib, down_sib))

    def feed_forward(place, chunk):
        rows = rows_of(place, chunk)
        normed = normed_full[rows, :]
        total = None
        for side, (up_side, down_side) in enumerate(sides):
            bias = b_up_ref[:, block(column + side * (1 - 2 * core), units)]
            active, bend = gelu_parts(dot(normed, up_side[...]) + bias)
            active = active.astype(low)
            hidden[side, rows, :] = active
            slope[side, rows, :] = bend.astype(low)
            part = dot_nt(active, down_side[...])
            total = part if total is None else total + part
        return total

    @pl.loop(0, CHUNKS)
    def _(chunk):
        for offset in offsets:
            send_buf[0, offset - 1, own_rows(chunk), :] = feed_forward(
                peer_level(offset), chunk
            ).astype(low)
            sum_copy(2, chunk, offset).start()

    for copy in late:
        copy.wait()

    @pl.loop(0, CHUNKS)
    def _(chunk):
        rows = own_rows(chunk)
        part_own[rows, :] = feed_forward(level, chunk)
        normed1 = unit1[rows, :] * gain1[...] + shift1[...]
        summed = normed1 + part_own[rows, :] + b_down[...]
        for offset in offsets:
            sum_copy(2, chunk, offset).wait_recv()
        normed, inv_std = norm_parts(summed + received(2, chunk))
        position = lax.broadcasted_iota(jnp.int32, (step, 1), 0) + (
            column * own_len + chunk * step
        )
        valid = position < length_ref[0]
        layer_out_ref[rows, :] = jnp.where(
            valid, normed * gain2[...] + shift2[...], 0.0
        ).astype(low)
        upstream = jnp.where(valid, upstream_ref[rows, :].astype(jnp.float32), 0.0)
        grad = norm_back(upstream, normed, inv_std, gain2[...])
        ffn_keep[rows, :] = grad
        grad_low = grad.astype(low)
        ffn_full[rows_of(level, chunk), :] = grad_low
        for offset in offsets:
            spread_copy(3, chunk, offset).start()
        small_ref[0:1, :] += jnp.sum(upstream * normed, axis=0, keepdims=True)
        small_ref[1:2, :] += jnp.sum(upstream, axis=0, keepdims=True)
        small_ref[2:3, :] += jnp.sum(grad_low.astype(jnp.float32), axis=0, keepdims=True)

    def feed_back(place, chunk):
        rows = rows_of(place, chunk)
        upstream = ffn_full[rows, :]
        total = None
        for side, (up_side, down_side) in enumerate(sides):
            grad = (
                dot(upstream, down_side[...]) * slope[side, rows, :].astype(jnp.float32)
            ).astype(low)
            pre_grad[side, rows, :] = grad
            up_small_ref[side : side + 1, :] += jnp.sum(
                grad.astype(jnp.float32), axis=0, keepdims=True
            )
            part = dot_nt(grad, up_side[...])
            total = part if total is None else total + part
        return total

    def back_own(chunk):
        part_own[own_rows(chunk), :] = feed_back(level, chunk)
        for offset in offsets:
            spread_copy(3, chunk, levels - offset).wait_recv()

    def back_peers(chunk):
        for offset in offsets:
            send_buf[1, offset - 1, own_rows(chunk), :] = feed_back(
                peer_level(offset), chunk
            ).astype(low)
            sum_copy(4, chunk, offset).start()

    @pl.loop(0, CHUNKS - 1)
    def _(chunk):
        back_own(chunk)
        back_peers(chunk)

    back_own(CHUNKS - 1)

    tile = across * shard
    lefts, rights = (ffn_full, normed_full), (hidden, pre_grad)
    sums, got = (down_sums, up_sums), (down_got, up_got)
    spare = (up_sums, slope.at[0])

    def grad_tile(kind, side, turn):
        return dot_tn(lefts[kind][:, block(turn, tile)], rights[kind][side])

    def core_grad(kind):
        return to_sibling(
            spare[kind].at[: sums[kind].shape[0]], sums[kind], levels + kind
        )

    def across_grad(kind, turn, offset):
        return remote(
            sums[kind].at[block(turn * across + lax.rem(fast + offset, across), shard)],
            got[kind].at[across - offset - 1, block(turn, shard)],
            across_send.at[kind, turn, offset - 1],
            across_recv.at[kind, turn, across - offset - 1],
            (fast_peer(offset), column),
        )

    def own_shard(kind, turn):
        for offset in range(1, across):
            across_grad(kind, turn, offset).wait_recv()
        total = sums[kind][block(turn * across + fast, shard), :].astype(jnp.float32)
        for place in range(across - 1):
            total += got[kind][place, block(turn, shard), :].astype(jnp.float32)
        return total

    def line_peer(shift):
        return ((slow + shift) * across + fast, column)

    def line_copy(kind, way, target):
        return remote(
            line_out[kind].at[way, target],
            line_in[kind].at[way, target],
            along_send.at[kind, way, target],
            along_recv.at[kind, way, target],
            line_peer(1 - 2 * way),
        )

    def line_step(kind, hop):
        for way in range(2):
            position = hop if way == 0 else along - 1 - hop
            targets = range(along - 1, hop, -1) if way == 0 else range(0, along - 1 - hop)

            @pl.when(slow == position)
            def _():
                for target in targets:
                    total = own_shard(kind, target)
                    if hop > 0:
                        line_copy(kind, way, target).wait_recv()
                        total += line_in[kind][way, target].astype(jnp.float32)
                    line_out[kind][way, target] = total.astype(jnp.bfloat16)
                    line_copy(kind, way, target).start()

    def line_finish(kind):
        for way in range(2):

            @pl.when((slow > 0) if way == 0 else (slow < along - 1))
            def _():
                line_copy(kind, way, slow).wait_recv()
                shares[kind][...] += line_in[kind][way, slow].astype(jnp.float32)

    def line_sent(kind):
        for way in range(2):
            for target in range(along):

                @pl.when((slow < target) if way == 0 else (slow > target))
                def _():
                    line_copy(kind, way, target).wait_send()

    def sum_grad(kind):
        core_grad(kind).wait_recv()

        @pl.loop(0, along)
        def _(turn):
            rows = block(turn, tile)
            sums[kind][rows, :] = (
                grad_tile(kind, 0, turn) + sums[kind][rows, :].astype(jnp.float32)
            ).astype(low)
            for offset in range(1, across):
                across_grad(kind, turn, offset).start()

    line_out, line_in, shares = (down_pass,), (down_in,), (share_down_ref,)
    def give_grad(kind):
        @pl.loop(0, along)
        def _(turn):
            spare[kind][block(turn, tile), :] = grad_tile(kind, 1, turn).astype(low)

    give_grad(0)
    core_grad(0).start()
    back_peers(CHUNKS - 1)
    core_grad(0).wait_send()
    pl.semaphore_signal(free_sem, inc=1, device_id=sibling, device_id_type=MESH)
    sum_grad(0)
    give_grad(1)
    pl.semaphore_wait(free_sem, 1)
    core_grad(1).start()
    sum_grad(1)

    @pl.loop(0, CHUNKS)
    def _(chunk):
        rows = own_rows(chunk)
        upstream = ffn_keep[rows, :] + part_own[rows, :]
        for offset in offsets:
            sum_copy(4, chunk, offset).wait_recv()
        upstream = upstream + received(4, chunk)
        normed = unit1[rows, :]
        grad_low = norm_back(upstream, normed, inv1[rows, :], gain1[...]).astype(low)
        attn_full[rows_of(level, chunk), :] = grad_low
        for offset in offsets:
            spread_copy(5, chunk, offset).start()
        small_ref[3:4, :] += jnp.sum(upstream * normed, axis=0, keepdims=True)
        small_ref[4:5, :] += jnp.sum(upstream, axis=0, keepdims=True)
        small_ref[5:6, :] += jnp.sum(grad_low.astype(jnp.float32), axis=0, keepdims=True)

    share_down_ref[...] = own_shard(0, slow)
    line_step(0, 0)

    def context_back(place, chunk):
        rows = rows_of(place, chunk)
        upstream = attn_full[rows, :]
        context_grad_ref[context_rows(place, chunk), :] = dot(upstream, out_ref[...]).astype(low)
        context_send[rows, :] = dot(upstream, out_sib[...]).astype(low)

    for chunk in range(CHUNKS):
        context_back(level, chunk)
        for offset in offsets:
            spread_copy(5, chunk, levels - offset).wait_recv()
            context_back(peer_level(offset), chunk)
        if 0 < chunk < along - 1:
            line_step(0, chunk)
    for hop in range(CHUNKS, along - 1):
        line_step(0, hop)

    back_copies = [
        to_sibling(
            context_send.at[pl.ds(place * own_len, own_len)],
            context_grad_ref.at[
                pl.ds(pl.multiple_of((place * 2 + core) * own_len, own_len), own_len)
            ],
            place,
        )
        for place in range(levels)
    ]
    for copy in back_copies:
        copy.start()

    own_context = jnp.concatenate(
        [
            context_ref[
                pl.ds(pl.multiple_of((place * 2 + core) * own_len, own_len), own_len), :
            ]
            for place in range(levels)
        ],
        axis=0,
    )

    def out_put(side):
        return pltpu.make_async_copy(stage.at[side], grad_out_ref.at[side], stage_sem.at[side])

    for side, right in enumerate((own_context, context_sib[...])):
        stage[side] = dot_tn(attn_full[...], right).astype(low)
        out_put(side).start()
    for turn in range(along):
        up_part_ref[block(turn, shard), :] = own_shard(1, turn).astype(low)
    line_finish(0)
    for side in range(2):
        out_put(side).wait()
    core_grad(1).wait_send()
    line_sent(0)

    @pl.loop(0, along)
    def _(place):
        for offset in range(1, across):
            across_grad(0, place, offset).wait_send()
            across_grad(1, place, offset).wait_send()

    for copy in back_copies:
        copy.wait()
    for kind in range(2, 6):

        @pl.loop(0, CHUNKS)
        def _(chunk):
            for offset in offsets:
                if kind % 2:
                    spread_copy(kind, chunk, offset).wait_send()
                else:
                    sum_copy(kind, chunk, offset).wait_send()


def middle(
    levels,
    rows,
    length,
    context,
    context_sib,
    upstream,
    weights,
    normed_full,
    unit1,
    inv1,
    vectors,
    b_up,
):
    low, full = jnp.bfloat16, jnp.float32
    across = across_of(rows)
    along = rows // across
    own_len, features = upstream.shape
    seq_len, width = context.shape
    units = weights[2].shape[1]
    shard = features // rows
    tokens = levels * own_len
    others = levels - 1
    shape = jax.ShapeDtypeStruct
    hbm = pl.BlockSpec(memory_space=pl.ANY)
    dma = pltpu.SemaphoreType.DMA
    vmem = pltpu.VMEM
    return pl.pallas_call(
        functools.partial(middle_kernel, levels, across, along),
        out_shape=(
            shape((own_len, features), low),
            shape((seq_len, width), low),
            shape((tokens, features), low),
            shape((8, features), full),
            shape((2, units), full),
            shape((shard, units), full),
            shape((along * shard, units), low),
            shape((2, features, width), low),
        ),
        in_specs=[SMEM] + [hbm] * 5 + [VMEM] * 5 + [hbm] + [VMEM] * 7,
        out_specs=[VMEM] * 7 + [hbm],
        scratch_shapes=[
            vmem((tokens, features), low),
            vmem((2, tokens, units), low),
            vmem((2, max(tokens, features), units), low),
            vmem((2, tokens, units), low),
            vmem((own_len, features), full),
            vmem((own_len, features), full),
            vmem((2, others, own_len, features), low),
            vmem((2, others, own_len, features), low),
            vmem((tokens, width), low),
            vmem((2, features, width), low),
            vmem((features, units), low),
            vmem((features, units), low),
            vmem((across - 1, along * shard, units), low),
            vmem((across - 1, along * shard, units), low),
            vmem((2, along, shard, units), low),
            vmem((2, along, shard, units), low),
            dma((4, CHUNKS, others)),
            dma((4, CHUNKS, others)),
            dma((levels + 2,)),
            dma((levels + 2,)),
            dma((1, 2, along)),
            dma((1, 2, along)),
            dma((2, along, across - 1)),
            dma((2, along, across - 1)),
            dma((2,)),
            vmem((seq_len, width), low),
            vmem((tokens, width), low),
            vmem((own_len, features), low),
            vmem((features, width), low),
            vmem((features, width), low),
            vmem((own_len, features), full),
            dma((6,)),
            pltpu.SemaphoreType.REGULAR,
        ],
        compiler_params=pltpu.CompilerParams(
            collective_id=1, has_side_effects=True, vmem_limit_bytes=62 * 1024 * 1024
        ),
        cost_estimate=pl.CostEstimate(
            flops=2 * tokens * features * (12 * units + 6 * width),
            bytes_accessed=20 * 1024 * 1024,
            transcendentals=2 * tokens * units,
        ),
    )(
        length,
        context,
        context_sib,
        upstream,
        *weights,
        normed_full,
        unit1,
        inv1,
        *vectors,
        b_up,
    )


def end_kernel(
    levels,
    across,
    along,
    query_key_value_ref,
    weights_ref,
    features_ref,
    attn_ref,
    layer_ref,
    small_ref,
    up_small_ref,
    bias_ref,
    out_ref,
    grad_input_ref,
    layer_out_ref,
    small_out_ref,
    share_ref,
    out_sib,
    sums,
    got,
    line_out,
    line_in,
    core_out,
    core_in,
    level_out,
    level_in,
    attn_in,
    attn_own,
    small_sums,
    small_in,
    core_send,
    core_recv,
    part_send,
    part_recv,
    level_send,
    level_recv,
    layer_send,
    layer_recv,
    across_send,
    across_recv,
    along_send,
    along_recv,
    small_send,
    small_recv,
    keep_sem,
):
    low, full = jnp.bfloat16, jnp.float32
    row, column = lax.axis_index("row"), lax.axis_index("col")
    core, level = lax.rem(column, 2), lax.div(column, 2)
    fast, slow = lax.rem(row, across), lax.div(row, across)
    cols = 2 * levels
    seq_len = features_ref.shape[0]
    own_len = seq_len // cols
    width = grad_input_ref.shape[1]
    shard = share_ref.shape[0]
    other = 1 - core
    sibling = (row, level * 2 + other)
    offsets = range(1, levels)

    def peer_level(offset):
        return lax.rem(level + offset, levels)

    def fast_peer(offset):
        return slow * across + lax.rem(fast + offset, across)

    def slow_peer(offset):
        return lax.rem(slow + offset, along) * across + fast

    barrier = pltpu.get_barrier_semaphore()
    greeted = [sibling]
    for offset in offsets:
        greeted += [(row, peer_level(offset) * 2 + core), (row, peer_level(offset) * 2 + other)]
    greeted += [(fast_peer(offset), column) for offset in range(1, across)]
    greeted += [(slow_peer(offset), column) for offset in range(1, along)]
    for device in greeted:
        pl.semaphore_signal(barrier, inc=1, device_id=device, device_id_type=MESH)
    pl.semaphore_wait(barrier, len(greeted))

    def remote(source, target, send, recv, device):
        return pltpu.make_async_remote_copy(
            src_ref=source,
            dst_ref=target,
            send_sem=send,
            recv_sem=recv,
            device_id=device,
            device_id_type=MESH,
        )

    def block(start, size):
        return pl.ds(pl.multiple_of(start * size, size), size)

    out_copy = remote(out_ref.at[1], out_sib, core_send.at[0], core_recv.at[0], sibling)
    attn_copy = remote(
        attn_ref.at[:, block(level * 2 + other, width)],
        attn_in,
        core_send.at[1],
        core_recv.at[1],
        sibling,
    )

    partners = []
    bit = 1
    while bit < levels:
        partners.append((row, (level + bit - 2 * bit * lax.rem(lax.div(level, bit), 2)) * 2 + core))
        bit *= 2
    bit = 1
    while bit < across * along:
        partners.append((row + bit - 2 * bit * lax.rem(lax.div(row, bit), 2), column))
        bit *= 2
    partners.append(sibling)

    def small_copy(turn):
        return remote(
            small_sums.at[turn],
            small_in.at[turn],
            small_send.at[turn],
            small_recv.at[turn],
            partners[turn],
        )

    small_turn = [0]

    def small_step():
        turn = small_turn[0]
        if turn > len(partners):
            return
        if turn > 0:
            small_copy(turn - 1).wait()
            small_sums[turn] = small_sums[turn - 1] + small_in[turn - 1]
        if turn < len(partners):
            small_copy(turn).start()
        small_turn[0] += 1

    def layer_copy(target, place_out, place_in):
        return remote(
            layer_ref.at[:, block(target, width)],
            layer_out_ref.at[block(column, own_len)],
            layer_send.at[place_out],
            layer_recv.at[place_in],
            (row, target),
        )

    layer_copies = [layer_copy(level * 2 + other, 0, 0)]
    for offset in offsets:
        back = levels - offset
        layer_copies.append(
            layer_copy(peer_level(offset) * 2 + core, 2 * offset - 1, 2 * back - 1)
        )
        layer_copies.append(layer_copy(peer_level(offset) * 2 + other, 2 * offset, 2 * back))
    layer_keep = pltpu.make_async_copy(
        layer_ref.at[:, block(column, width)], layer_out_ref.at[block(column, own_len)], keep_sem.at[0]
    )
    attn_keep = pltpu.make_async_copy(
        attn_ref.at[:, block(column, width)], attn_own, keep_sem.at[1]
    )
    attn_keep.start()

    features_all = weights_ref.shape[0]
    units = up_small_ref.shape[1]
    first_up = small_ref.shape[0]
    small_sums[0] = jnp.zeros_like(small_in[0])
    small_sums[0, :first_up, :] = small_ref[...]
    for side in range(2):
        start = (column + side * (1 - 2 * core)) * units
        small_sums[
            0,
            pl.ds(first_up + lax.div(start, features_all), 1),
            pl.ds(pl.multiple_of(lax.rem(start, features_all), units), units),
        ] = up_small_ref[side : side + 1, :]
    first_bias = small_in.shape[1] - 4
    small_sums[0, first_bias : first_bias + 2, block(column, width)] = bias_ref[...]
    small_step()
    out_copy.start()
    attn_copy.start()
    layer_keep.start()
    for copy in layer_copies:
        copy.start()

    def input_part(turn, target):
        return dot_nt(
            query_key_value_ref[block(turn, own_len), :], weights_ref[block(target, width), :]
        )

    def part_copy(turn, place):
        rows = block(turn, own_len)
        return remote(
            core_out.at[place, rows],
            core_in.at[place, rows],
            part_send.at[turn, place],
            part_recv.at[turn, place],
            sibling,
        )

    def give_core():
        @pl.loop(0, cols)
        def _(turn):
            for place in range(levels):
                core_out[place, block(turn, own_len), :] = input_part(
                    turn, place * 2 + other
                ).astype(low)
                part_copy(turn, place).start()

    def across_copy(turn, offset):
        return remote(
            sums.at[block(turn * across + lax.rem(fast + offset, across), shard)],
            got.at[across - offset - 1, block(turn, shard)],
            across_send.at[turn, offset - 1],
            across_recv.at[turn, across - offset - 1],
            (fast_peer(offset), column),
        )

    def weight_grad(turn):
        rows = block(turn, across * shard)
        sums[rows, : 3 * width] = dot_tn(features_ref[:, rows], query_key_value_ref[...]).astype(
            low
        )
        sums[rows, 3 * width :] = (
            out_ref[0, rows, :].astype(full) + out_sib[rows, :].astype(full)
        ).astype(low)
        for offset in range(1, across):
            across_copy(turn, offset).start()

    def level_copy(turn, offset):
        rows = block(turn, own_len)
        return remote(
            level_out.at[offset - 1, rows],
            level_in.at[levels - offset - 1, rows],
            level_send.at[turn, offset - 1],
            level_recv.at[turn, levels - offset - 1],
            (row, peer_level(offset) * 2 + core),
        )

    def give_levels():
        @pl.loop(0, cols)
        def _(turn):
            rows = block(turn, own_len)
            for offset in offsets:
                place = peer_level(offset)
                part = input_part(turn, place * 2 + core)
                part_copy(turn, place).wait_recv()
                level_out[offset - 1, rows, :] = (
                    part + core_in[place, rows, :].astype(full)
                ).astype(low)
                level_copy(turn, offset).start()

    def own_shard(turn):
        for offset in range(1, across):
            across_copy(turn, offset).wait_recv()
        total = sums[block(turn * across + fast, shard), :].astype(full)
        for place in range(across - 1):
            total += got[place, block(turn, shard), :].astype(full)
        return total

    def line_copy(way, target):
        return remote(
            line_out.at[way, target],
            line_in.at[way, target],
            along_send.at[way, target],
            along_recv.at[way, target],
            ((slow + 1 - 2 * way) * across + fast, column),
        )

    def line_step(hop, near):
        if hop >= along - 1 - near:
            return
        for way in range(2):
            target = along - 1 - near if way == 0 else near
            position = hop if way == 0 else along - 1 - hop

            @pl.when(slow == position)
            def _():
                total = own_shard(target)
                if hop > 0:
                    line_copy(way, target).wait_recv()
                    total += line_in[way, target].astype(full)
                line_out[way, target] = total.astype(low)
                line_copy(way, target).start()

    def finish_input(turn, attn_part):
        rows = block(turn, own_len)
        total = input_part(turn, column) + attn_part.astype(full)
        part_copy(turn, level).wait_recv()
        total += core_in[level, rows, :].astype(full)
        for offset in offsets:
            level_copy(turn, offset).wait_recv()
        for place in range(levels - 1):
            total += level_in[place, rows, :].astype(full)
        grad_input_ref[rows, :] = total.astype(low)

    ends = [turn for place in range(along // 2) for turn in (along - 1 - place, place)]
    out_copy.wait()
    small_step()
    for place, turn in enumerate(ends):
        weight_grad(turn)
        if place % 2:
            small_step()
    give_core()
    small_step()
    give_levels()
    small_step()
    line_steps = sorted(
        ((hop, near) for near in range(along - 1) for hop in range(along - 1 - near)),
        key=lambda step: step[0] + 2 * step[1],
    )
    for step in line_steps[: len(line_steps) // 3]:
        line_step(*step)
    attn_keep.wait()
    attn_copy.wait()
    for place in range(levels):
        for step in line_steps[len(line_steps) // 3 :][place::levels]:
            line_step(*step)
        rows = block(place, own_len)
        finish_input(place * 2 + core, attn_own[rows, :])
        finish_input(place * 2 + other, attn_in[rows, :])
    share_ref[...] = own_shard(slow)
    while small_turn[0] <= len(partners):
        small_step()
    small_out_ref[...] = small_sums[len(partners)]

    for way in range(2):

        @pl.when((slow > 0) if way == 0 else (slow < along - 1))
        def _():
            line_copy(way, slow).wait_recv()
            share_ref[...] += line_in[way, slow].astype(full)

    layer_keep.wait()
    for copy in layer_copies:
        copy.wait()
    for way in range(2):
        for target in range(along):

            @pl.when((slow < target) if way == 0 else (slow > target))
            def _():
                line_copy(way, target).wait_send()

    @pl.loop(0, along)
    def _(turn):
        for offset in range(1, across):
            across_copy(turn, offset).wait_send()

    @pl.loop(0, cols)
    def _(turn):
        for place in range(levels):
            part_copy(turn, place).wait_send()
        for offset in offsets:
            level_copy(turn, offset).wait_send()


def finish(
    levels, rows, query_key_value, weights, features, attn_full, layer_own, small, up_small, bias, out
):
    low, full = jnp.bfloat16, jnp.float32
    shape = jax.ShapeDtypeStruct
    across = across_of(rows)
    along = rows // across
    seq_len, features_all = features.shape
    width = query_key_value.shape[1] // 3
    own_len = layer_own.shape[0]
    shard = features_all // rows
    others = levels - 1
    cols = 2 * levels
    turns = 1 + (levels - 1).bit_length() + (rows - 1).bit_length()
    small_rows = small.shape[0] + up_small.shape[1] * cols // features_all + 4
    dma = pltpu.SemaphoreType.DMA
    vmem = pltpu.VMEM
    return pl.pallas_call(
        functools.partial(end_kernel, levels, across, along),
        out_shape=(
            shape((seq_len, width), low),
            shape((seq_len, width), low),
            shape((small_rows, features_all), full),
            shape((shard, 4 * width), full),
        ),
        in_specs=[VMEM] * 3 + [pl.BlockSpec(memory_space=pl.ANY)] * 2 + [VMEM] * 4,
        out_specs=[VMEM] * 4,
        scratch_shapes=[
            vmem((features_all, width), low),
            vmem((features_all, 4 * width), low),
            vmem((across - 1, along * shard, 4 * width), low),
            vmem((2, along, shard, 4 * width), low),
            vmem((2, along, shard, 4 * width), low),
            vmem((levels, seq_len, width), low),
            vmem((levels, seq_len, width), low),
            vmem((others, seq_len, width), low),
            vmem((others, seq_len, width), low),
            vmem((levels * own_len, width), low),
            vmem((levels * own_len, width), low),
            vmem((turns + 1, small_rows, features_all), full),
            vmem((turns, small_rows, features_all), full),
            dma((2,)),
            dma((2,)),
            dma((cols, levels)),
            dma((cols, levels)),
            dma((cols, others)),
            dma((cols, others)),
            dma((cols,)),
            dma((cols,)),
            dma((along, across - 1)),
            dma((along, across - 1)),
            dma((2, along)),
            dma((2, along)),
            dma((turns,)),
            dma((turns,)),
            dma((2,)),
        ],
        compiler_params=pltpu.CompilerParams(
            collective_id=2, has_side_effects=True, vmem_limit_bytes=60 * 1024 * 1024
        ),
        cost_estimate=pl.CostEstimate(
            flops=4 * seq_len * features_all * 3 * width,
            bytes_accessed=20 * 1024 * 1024,
            transcendentals=0,
        ),
    )(query_key_value, weights, features, attn_full, layer_own, small, up_small, bias, out)


def last_kernel(
    grad_input_ref,
    layer_ref,
    small_ref,
    share_ref,
    down_ref,
    up_ref,
    *outs,
):
    (
        layer_out,
        grad_input,
        grad_query,
        bias_query,
        grad_key,
        grad_value,
        bias_value,
        grad_out,
        bias_out,
        gain1,
        shift1,
        grad_up,
        bias_up,
        grad_down,
        bias_down,
        gain2,
        shift2,
    ) = outs
    grad_input[...] = grad_input_ref[...]
    layer_out[...] = layer_ref[...]
    width = grad_query.shape[1]
    for place, ref in enumerate((grad_query, grad_key, grad_value)):
        ref[...] = share_ref[:, place * width : (place + 1) * width]
    grad_out[...] = share_ref[:, 3 * width :].T
    grad_down[...] = down_ref[...].T
    grad_up[...] = up_ref[...].astype(jnp.float32)
    features_all = small_ref.shape[1]
    last = small_ref.shape[0] - 4
    for place, ref in (
        (0, gain2),
        (1, shift2),
        (2, bias_down),
        (3, gain1),
        (4, shift1),
        (5, bias_out),
        (last, bias_query),
        (last + 1, bias_value),
    ):
        ref[...] = small_ref[place : place + 1, :]
    for place in range(8, last):
        bias_up[:, (place - 8) * features_all : (place - 7) * features_all] = small_ref[
            place : place + 1, :
        ]


def put_out(grad_input, layer_out, small, share, down, up):
    low, full = jnp.bfloat16, jnp.float32
    shape = jax.ShapeDtypeStruct
    seq_len, width = grad_input.shape
    shard, units = up.shape
    features_all = small.shape[1]
    vector = shape((1, features_all), full)
    units_all = (small.shape[0] - 12) * features_all
    grad = shape((shard, width), full)
    return pl.pallas_call(
        last_kernel,
        out_shape=(
            shape((seq_len, width), low),
            shape((seq_len, width), low),
            grad,
            vector,
            grad,
            grad,
            vector,
            shape((width, shard), full),
            vector,
            vector,
            vector,
            shape((shard, units), full),
            shape((1, units_all), full),
            shape((units, shard), full),
            vector,
            vector,
            vector,
        ),
        in_specs=[VMEM] * 6,
        out_specs=[VMEM] * 17,
        compiler_params=pltpu.CompilerParams(vmem_limit_bytes=60 * 1024 * 1024),
    )(grad_input, layer_out, small, share, down, up)


def on_device(
    hidden_in,
    out_grad,
    lengths,
    global_blocks,
    rand_blocks,
    w_query,
    b_query,
    w_key,
    w_value,
    b_value,
    w_out,
    b_out,
    ln1_gain,
    ln1_bias,
    w_up,
    b_up,
    w_down,
    b_down,
    ln2_gain,
    ln2_bias,
):
    cols = lax.axis_size("col")
    rows = lax.axis_size("row")
    tables = (lengths, global_blocks.reshape(-1), rand_blocks.reshape(-1))
    as_row = lambda vector: vector[None, :]
    (
        features,
        own_features,
        upstream,
        queries,
        key_rows,
        value_rows,
        context,
        highest,
        scale,
        full_qkv,
        full_out,
        full_up,
        full_down,
        out_sib,
        up_sib,
        down_sib,
        context_sib,
        normed_full,
        unit1,
        inv1,
    ) = front(
        cols // 2,
        rows,
        tables,
        hidden_in,
        out_grad,
        (as_row(b_query), as_row(b_value)),
        (w_query, w_key, w_value, w_out, w_up, w_down),
        (as_row(b_out), as_row(ln1_gain), as_row(ln1_bias)),
    )
    (
        layer_own,
        context_grad,
        attn_full,
        small,
        up_small,
        down_share,
        up_part,
        grad_out,
    ) = middle(
        cols // 2,
        rows,
        lengths,
        context,
        context_sib,
        upstream,
        (full_out, out_sib, full_up, up_sib, full_down, down_sib),
        normed_full,
        unit1,
        inv1,
        tuple(as_row(each) for each in (ln1_gain, ln1_bias, b_down, ln2_gain, ln2_bias)),
        as_row(b_up),
    )
    across = across_of(rows)
    up_share = lax.psum_scatter(
        up_part,
        "row",
        scatter_dimension=0,
        axis_index_groups=[list(range(place, rows, across)) for place in range(across)],
        tiled=True,
    )
    query_key_value, bias_sums = attend_back(
        queries, key_rows, value_rows, tables, (highest, scale), context_grad
    )
    grad_input, layer_out, small, share = finish(
        cols // 2,
        rows,
        query_key_value,
        full_qkv,
        features,
        attn_full,
        layer_own,
        small,
        up_small,
        bias_sums,
        grad_out,
    )
    outs = put_out(grad_input, layer_out, small, share, down_share, up_share)
    return tuple(each.reshape(-1) if each.shape[0] == 1 else each for each in outs)


def solution(mesh):
    placed = (
        P("row", "col"),
        P("row", "col"),
        P("row"),
        P("row", None),
        P("row", None, "col", None),
        P("row", "col"),
        P(),
        P("row", "col"),
        P("row", "col"),
        P(),
        P("col", "row"),
        P(),
        P(),
        P(),
        P("row", "col"),
        P(),
        P("col", "row"),
        P(),
        P(),
        P(),
    )
    return jax.shard_map(
        on_device,
        mesh=mesh,
        in_specs=placed,
        out_specs=(
            P("row", "col"),
            P("row", "col"),
            P("row", "col"),
            P(),
            P("row", "col"),
            P("row", "col"),
            P(),
            P("col", "row"),
            P(),
            P(),
            P(),
            P("row", "col"),
            P(),
            P("col", "row"),
            P(),
            P(),
            P(),
        ),
        check_vma=False,
    )
```

```python
import functools
import math

import jax
import jax.numpy as jnp
from jax import lax
from jax.experimental import pallas as pl
from jax.experimental.pallas import tpu as pltpu
from jax.sharding import PartitionSpec as P

DH = 64
BLK = 64
MESH = pl.DeviceIdType.MESH


epsilon = 1e-06


def lane_heads(rows, width):
    return lax.broadcasted_iota(jnp.int32, (rows, width), 1) // DH


def by_diagonal(rows, width):
    lane_head = lane_heads(BLK, width)
    zero = jnp.zeros_like(rows)
    return jnp.concatenate(
        [jnp.where(lane_head == head, rows, zero) for head in range(width // DH)], axis=0
    )


def from_diagonal(square, width):
    lane_head = lane_heads(BLK, width)
    result = jnp.zeros((BLK, width), jnp.float32)
    for head in range(width // DH):
        result = jnp.where(lane_head == head, square[head * BLK : (head + 1) * BLK, :], result)
    return result


def slot_starts(step, num_blocks, head_count, globals_ref, random_ref):
    shared = [
        jnp.maximum(step - 1, 0),
        step,
        jnp.minimum(step + 1, num_blocks - 1),
        globals_ref[0],
        globals_ref[1],
    ]
    base = step * (head_count * 3)
    apart = [
        [random_ref[base + head * 3 + slot] for head in range(head_count)] for slot in range(3)
    ]
    return shared, apart


def lane_groups(head_count):
    per_group = min(128 // DH, head_count)
    return [
        (first * DH, per_group * DH, list(range(first, first + per_group)))
        for first in range(0, head_count, per_group)
    ]


def picked_rows(rows_ref, shared, apart, head_count):
    pieces = [rows_ref[block] for block in shared]
    for blocks in apart:
        groups = []
        for lane, width, heads in lane_groups(head_count):
            lane_head = lane_heads(BLK, width)
            piece = rows_ref[blocks[heads[0]], :, lane : lane + width]
            for place, head in enumerate(heads[1:], 1):
                other = rows_ref[blocks[head], :, lane : lane + width]
                piece = jnp.where(lane_head >= place, other, piece)
            groups.append(piece)
        pieces.append(jnp.concatenate(groups, axis=1) if len(groups) > 1 else groups[0])
    return jnp.concatenate(pieces, axis=0)


def put_rows(sums_ref, values_in, shared, apart, head_count):
    for slot, block in enumerate(shared):
        sums_ref[block] += values_in[slot * BLK : (slot + 1) * BLK, :]
    for slot, blocks in enumerate(apart, len(shared)):
        rows = values_in[slot * BLK : (slot + 1) * BLK, :]
        for lane, width, heads in lane_groups(head_count):
            lane_head = lane_heads(BLK, width)
            for place, head in enumerate(heads):
                sums_ref[blocks[head], :, lane : lane + width] += jnp.where(
                    lane_head == place, rows[:, lane : lane + width], 0.0
                )


def masked_scores(picked_keys, grouped, step, num_blocks, length, shared, apart):
    width = grouped.shape[1]
    scores = lax.dot_general(
        picked_keys, grouped, (((1,), (1,)), ((), ())), preferred_element_type=jnp.float32
    )
    listed = [step >= 1, True, step + 1 < num_blocks]
    listed += [(block < step - 1) | (block > step + 1) for block in shared[3:]]
    limits = [
        jnp.where(there, length - block * BLK, 0) for there, block in zip(listed, shared)
    ]
    lane_head = lane_heads(1, width)
    for blocks in apart:
        limit = length - jnp.full((1, width), blocks[0], jnp.int32) * BLK
        for head, block in enumerate(blocks[1:], 1):
            limit = jnp.where(lane_head >= head, length - block * BLK, limit)
        limits.append(limit)
    row = lax.broadcasted_iota(jnp.int32, (BLK, width), 0)
    return [
        jnp.where(row < limit, scores[slot * BLK : (slot + 1) * BLK, :], -1e30)
        for slot, limit in enumerate(limits)
    ]


def attend_blocks(
    first, count, unroll, length_ref, globals_ref, random_ref, refs, context_ref, stat_refs
):
    queries_ref, keys_ref, values_ref = refs
    highest_ref, scale_ref = stat_refs
    seq_len, width = queries_ref.shape
    head_count = width // DH
    num_blocks = seq_len // BLK

    def one_block(step):
        shared, apart = slot_starts(step, num_blocks, head_count, globals_ref, random_ref)
        own = pl.ds(pl.multiple_of(step * BLK, BLK), BLK)
        grouped = by_diagonal(queries_ref[own, :] * jnp.bfloat16(1.0 / math.sqrt(DH)), width)
        scores = masked_scores(
            picked_rows(keys_ref, shared, apart, head_count),
            grouped,
            step,
            num_blocks,
            length_ref[0],
            shared,
            apart,
        )
        highest = jnp.max(functools.reduce(jnp.maximum, scores), axis=0, keepdims=True)
        exponent = [jnp.exp(piece - highest) for piece in scores]
        denominator = jnp.sum(sum(exponent[1:], exponent[0]), axis=0, keepdims=True)
        scale = 1.0 / denominator
        attn_probs = jnp.concatenate(
            [(piece * scale).astype(jnp.bfloat16) for piece in exponent], axis=0
        )
        square = lax.dot_general(
            attn_probs,
            picked_rows(values_ref, shared, apart, head_count),
            (((0,), (0,)), ((), ())),
            preferred_element_type=jnp.float32,
        )
        context_ref[own, :] = from_diagonal(square, width).astype(jnp.bfloat16)
        highest_ref[step] = highest
        scale_ref[step] = scale

    @pl.loop(0, count // unroll)
    def _(turn):
        for place in range(unroll):
            one_block(first + turn * unroll + place)


def attend_back_kernel(
    head_count,
    unroll,
    length_ref,
    globals_ref,
    random_ref,
    queries_ref,
    keys_ref,
    values_ref,
    grads_ref,
    highest_ref,
    scale_ref,
    grads_out_ref,
    bias_ref,
    key_sums,
    value_sums,
    query_total,
):
    width = head_count * DH
    num_blocks = queries_ref.shape[0] // BLK
    factor = 1.0 / math.sqrt(DH)
    key_sums[...] = jnp.zeros_like(key_sums)
    value_sums[...] = jnp.zeros_like(value_sums)
    query_total[...] = jnp.zeros_like(query_total)

    def one_block(step):
        shared, apart = slot_starts(step, num_blocks, head_count, globals_ref, random_ref)
        own = pl.ds(pl.multiple_of(step * BLK, BLK), BLK)
        grouped = by_diagonal(queries_ref[own, :] * jnp.bfloat16(factor), width)
        grouped_grad = by_diagonal(grads_ref[own, :], width)
        picked_keys = picked_rows(keys_ref, shared, apart, head_count)
        picked_values = picked_rows(values_ref, shared, apart, head_count)
        scores = masked_scores(
            picked_keys, grouped, step, num_blocks, length_ref[0], shared, apart
        )
        highest = highest_ref[step]
        scale = scale_ref[step]
        attn_probs = [jnp.exp(piece - highest) * scale for piece in scores]
        prob_grad = lax.dot_general(
            picked_values,
            grouped_grad,
            (((1,), (1,)), ((), ())),
            preferred_element_type=jnp.float32,
        )
        prob_grads = [prob_grad[slot * BLK : (slot + 1) * BLK, :] for slot in range(8)]
        products = [left * right for left, right in zip(attn_probs, prob_grads)]
        total = jnp.sum(sum(products[1:], products[0]), axis=0, keepdims=True)
        score_grad = jnp.concatenate(
            [
                (left * (right - total)).astype(jnp.bfloat16)
                for left, right in zip(attn_probs, prob_grads)
            ],
            axis=0,
        )
        probs_low = jnp.concatenate([piece.astype(jnp.bfloat16) for piece in attn_probs], axis=0)
        square = lax.dot_general(
            score_grad, picked_keys, (((0,), (0,)), ((), ())), preferred_element_type=jnp.float32
        )
        query_grad = (from_diagonal(square, width) * factor).astype(jnp.bfloat16)
        grads_out_ref[own, :width] = query_grad
        query_total[...] += jnp.sum(
            query_grad.astype(jnp.float32).reshape(BLK // 8, 8, width), axis=0
        )
        key_part = jnp.dot(score_grad, grouped, preferred_element_type=jnp.float32)
        value_part = jnp.dot(probs_low, grouped_grad, preferred_element_type=jnp.float32)
        put_rows(key_sums, key_part, shared, apart, head_count)
        put_rows(value_sums, value_part, shared, apart, head_count)

    @pl.loop(0, num_blocks // unroll)
    def _(turn):
        for place in range(unroll):
            one_block(turn * unroll + place)

    value_grad = value_sums[...].reshape(queries_ref.shape).astype(jnp.bfloat16)
    seq_len = queries_ref.shape[0]
    grads_out_ref[:, width : 2 * width] = key_sums[...].reshape(seq_len, width).astype(jnp.bfloat16)
    grads_out_ref[:, 2 * width :] = value_grad
    bias_ref[0:1, :] = jnp.sum(query_total[...], axis=0, keepdims=True)
    bias_ref[1:2, :] = jnp.sum(value_grad.astype(jnp.float32), axis=0, keepdims=True)


VMEM = pl.BlockSpec(memory_space=pltpu.VMEM)
SMEM = pl.BlockSpec(memory_space=pltpu.SMEM)


def attend_back(queries, key_rows, value_rows, tables, stats, context_grad):
    seq_len, width = queries.shape
    head_count = width // DH
    return pl.pallas_call(
        functools.partial(attend_back_kernel, head_count, 16),
        out_shape=(
            jax.ShapeDtypeStruct((seq_len, 3 * width), jnp.bfloat16),
            jax.ShapeDtypeStruct((2, width), jnp.float32),
        ),
        in_specs=[SMEM] * 3 + [VMEM] * 6,
        out_specs=[VMEM] * 2,
        scratch_shapes=[pltpu.VMEM((seq_len // BLK, BLK, width), jnp.float32)] * 2
        + [pltpu.VMEM((8, width), jnp.float32)],
        compiler_params=pltpu.CompilerParams(vmem_limit_bytes=60 * 1024 * 1024),
        cost_estimate=pl.CostEstimate(
            flops=10 * seq_len * 512 * width * head_count,
            bytes_accessed=14 * seq_len * width,
            transcendentals=seq_len * 512 * head_count,
        ),
    )(*tables, queries, key_rows, value_rows, context_grad, *stats)


KINDS = 4
CHUNKS = 4


def front_kernel(
    levels,
    across,
    along,
    length_ref,
    globals_ref,
    random_ref,
    hidden_ref,
    grads_ref,
    b_query_ref,
    b_value_ref,
    w_query_ref,
    w_key_ref,
    w_value_ref,
    w_out_ref,
    w_up_ref,
    w_down_ref,
    b_out,
    gain1,
    shift1,
    features_far,
    own_far,
    upstream_far,
    queries_far,
    keys_far,
    values_far,
    context_far,
    highest_ref,
    scale_ref,
    full_qkv_far,
    full_out_ref,
    full_up_far,
    full_down_far,
    out_sib,
    up_sib_far,
    down_sib_far,
    context_sib,
    normed_full,
    unit1,
    inv1,
    features_ref,
    own_ref,
    upstream_ref,
    queries_ref,
    keys_ref,
    values_ref,
    context_ref,
    full_qkv_ref,
    full_up_ref,
    full_down_ref,
    up_sib,
    down_sib,
    far_sem,
    sum_out,
    sum_in,
    level_send,
    level_recv,
    core_send,
    core_recv,
    swap_send,
    swap_recv,
    along_send,
    along_recv,
    across_send,
    across_recv,
    shard_send,
    shard_recv,
    context_send,
    context_recv,
    sum_send,
    sum_recv,
    normed_send,
    normed_recv,
):
    low, full = jnp.bfloat16, jnp.float32
    row, column = lax.axis_index("row"), lax.axis_index("col")
    core, level = lax.rem(column, 2), lax.div(column, 2)
    fast, slow = lax.rem(row, across), lax.div(row, across)
    cols = 2 * levels
    seq_len, width = hidden_ref.shape
    own_len = seq_len // cols
    shard = w_query_ref.shape[0]
    other = 1 - core
    sibling = (row, level * 2 + other)
    offsets = range(1, levels)

    def peer_level(offset):
        return lax.rem(level + offset, levels)

    def fast_peer(offset):
        return slow * across + lax.rem(fast + offset, across)

    def line_peer(shift):
        return ((slow + shift) * across + fast, column)

    barrier = pltpu.get_barrier_semaphore()
    greeted = [sibling]
    for offset in offsets:
        greeted += [(row, peer_level(offset) * 2 + core), (row, peer_level(offset) * 2 + other)]
    greeted += [(fast_peer(offset), column) for offset in range(1, across)]
    greeted += [
        (lax.rem(slow + offset, along) * across + fast, column) for offset in range(1, along)
    ]
    for device in greeted:
        pl.semaphore_signal(barrier, inc=1, device_id=device, device_id_type=MESH)
    pl.semaphore_wait(barrier, len(greeted))

    def remote(source, target, send, recv, device):
        return pltpu.make_async_remote_copy(
            src_ref=source,
            dst_ref=target,
            send_sem=send,
            recv_sem=recv,
            device_id=device,
            device_id_type=MESH,
        )

    def block(start, size):
        return pl.ds(pl.multiple_of(start * size, size), size)

    def level_copy(turn, offset):
        rows = block(turn, own_len)
        return remote(
            hidden_ref.at[rows],
            features_ref.at[rows, block(column, width)],
            level_send.at[turn, offset - 1],
            level_recv.at[turn, levels - offset - 1],
            (row, peer_level(offset) * 2 + core),
        )

    def core_copy(turn, offset):
        view = features_ref.at[block(turn, own_len), block(peer_level(offset) * 2 + core, width)]
        return remote(
            view, view, core_send.at[turn, offset], core_recv.at[turn, offset], sibling
        )

    @pl.loop(0, cols)
    def _(turn):
        for offset in offsets:
            level_copy(turn, offset).start()
        rows = block(turn, own_len)
        features_ref[rows, block(column, width)] = hidden_ref[rows, :]
        core_copy(turn, 0).start()

    fulls = (full_qkv_ref, full_out_ref, full_up_ref, full_down_ref)
    sibs = (None, out_sib, up_sib, down_sib)

    def shard_rows(place):
        return block(place * across + fast, shard)

    def line_copy(kind, way, hop):
        view = fulls[kind].at[shard_rows(slow - (1 - 2 * way) * hop)]
        return remote(
            view,
            view,
            along_send.at[kind, way, hop],
            along_recv.at[kind, way, hop],
            line_peer(1 - 2 * way),
        )

    def line_can_send(way, hop):
        if way == 0:
            return (slow >= hop) & (slow < along - 1)
        return (slow < along - hop) & (slow > 0)

    def line_send(kind, hop):
        for way in range(2):

            @pl.when(line_can_send(way, hop))
            def _():
                line_copy(kind, way, hop).start()

    def line_got(way, hop):
        place = slow - (1 - 2 * way) * (hop + 1)
        return place, ((place >= 0) if way == 0 else (place < along))

    def line_wait(kind, way, hop):
        place, _ = line_got(way, hop)
        view = fulls[kind].at[shard_rows(place)]
        remote(
            view,
            view,
            along_send.at[kind, way, hop],
            along_recv.at[kind, way, hop],
            line_peer(-(1 - 2 * way)),
        ).wait_recv()

    def across_copy(kind, place, offset):
        view = fulls[kind].at[shard_rows(place)]
        return remote(
            view,
            view,
            across_send.at[kind, place, offset - 1],
            across_recv.at[kind, place, across - offset - 1],
            (fast_peer(offset), column),
        )

    def core_shard(kind, place, offset):
        rows = block(place * across + lax.rem(fast + offset, across), shard)
        return remote(
            fulls[kind].at[rows],
            sibs[kind].at[rows],
            shard_send.at[kind - 1, place, offset],
            shard_recv.at[kind - 1, place, offset],
            sibling,
        )

    for place, ref in enumerate((w_query_ref, w_key_ref, w_value_ref)):
        full_qkv_ref[shard_rows(slow), place * width : (place + 1) * width] = ref[...].astype(low)
    line_send(0, 0)
    full_out_ref[shard_rows(slow), :] = w_out_ref[...].T.astype(low)
    full_up_ref[shard_rows(slow), :] = w_up_ref[...].astype(low)
    full_down_ref[shard_rows(slow), :] = w_down_ref[...].T.astype(low)

    def swap_copy(target, place_out, place_in):
        return remote(
            grads_ref.at[block(target, own_len)],
            upstream_ref.at[:, block(column, width)],
            swap_send.at[place_out],
            swap_recv.at[place_in],
            (row, target),
        )

    swaps = [swap_copy(level * 2 + other, 0, 0)]
    for offset in offsets:
        back = levels - offset
        swaps.append(swap_copy(peer_level(offset) * 2 + core, 2 * offset - 1, 2 * back - 1))
        swaps.append(swap_copy(peer_level(offset) * 2 + other, 2 * offset, 2 * back))
    for copy in swaps:
        copy.start()
    upstream_ref[:, block(column, width)] = grads_ref[block(column, own_len), :]

    def pass_shard(kind, place):
        for step in range(1, across):
            across_copy(kind, place, step).start()
        if kind > 0:
            core_shard(kind, place, 0).start()

    hops = range(along - 1)
    waiting = [(1, hop) for hop in hops] + [(3, -1), (2, 0), (3, 0)]
    waiting += [(kind, hop) for hop in hops if hop > 0 for kind in (2, 3)]

    def pass_on(count=1):
        pass_these(waiting[:count])
        del waiting[:count]

    def pass_these(shards):
        for kind, hop in shards:
            if hop < 0:
                pass_shard(kind, slow)
                continue
            for way in range(2):
                place, there = line_got(way, hop)

                @pl.when(there)
                def _():
                    line_wait(kind, way, hop)
                    if hop < along - 2:

                        @pl.when(line_can_send(way, hop + 1))
                        def _():
                            line_copy(kind, way, hop + 1).start()

                    pass_shard(kind, place)
    def await_shards(kind):
        @pl.loop(0, along)
        def _(place):
            for offset in range(1, across):
                across_copy(kind, place, across - offset).wait_recv()
                if kind > 0:
                    core_shard(kind, place, offset).start()

    def await_sibling(kind):
        @pl.loop(0, along)
        def _(place):
            for offset in range(across):
                core_shard(kind, place, offset).wait_recv()

    pass_these([(0, hop) for hop in range(-1, along - 2)])
    for kind in range(1, KINDS):
        line_send(kind, 0)
    pass_these([(0, along - 2), (1, -1), (2, -1)])
    await_shards(0)

    def project(turn):
        rows = block(turn, own_len)
        for offset in offsets:
            level_copy(turn, levels - offset).wait_recv()
            core_copy(turn, offset).start()
        for offset in range(levels):
            core_copy(turn, offset).wait_recv()
        values_in = features_ref[rows, :]
        queries_ref[rows, :] = (
            dot(values_in, full_qkv_ref[:, :width]) + b_query_ref[:, block(column, width)]
        ).astype(low)
        blocks = pl.ds(turn * (own_len // BLK), own_len // BLK)
        by_block = (own_len // BLK, BLK, width)
        keys_ref[blocks] = (
            dot(values_in, full_qkv_ref[:, width : 2 * width]).astype(low).reshape(by_block)
        )
        values_ref[blocks] = (
            (dot(values_in, full_qkv_ref[:, 2 * width :]) + b_value_ref[:, block(column, width)])
            .astype(low)
            .reshape(by_block)
        )

    for turn in range(cols):
        project(turn)
        pass_on(1 if (3, -1) in waiting else 0)
    while (2, 0) in waiting:
        pass_on()
    own_ref[...] = features_ref[block(column, own_len), :]
    far = [
        pltpu.make_async_copy(source, target, far_sem.at[place])
        for place, (source, target) in enumerate(
            [
                (features_ref, features_far),
                (own_ref, own_far),
                (queries_ref, queries_far),
                (keys_ref, keys_far),
                (values_ref, values_far),
                (full_qkv_ref, full_qkv_far),
                (upstream_ref, upstream_far),
                (context_ref, context_far),
                (full_up_ref, full_up_far),
                (up_sib, up_sib_far),
                (full_down_ref, full_down_far),
                (down_sib, down_sib_far),
            ]
        )
    ]
    @pl.loop(0, cols)
    def _(turn):
        for offset in range(levels):
            core_copy(turn, offset).wait_send()

    for copy in far[:6]:
        copy.start()

    step = own_len // CHUNKS
    halves = 2
    count = own_len // BLK // halves

    def attend_half(quarter, half):
        attend_blocks(
            (quarter * halves + half) * count,
            count,
            min(count, 4),
            length_ref,
            globals_ref,
            random_ref,
            (queries_ref, keys_ref, values_ref),
            context_ref,
            (highest_ref, scale_ref),
        )

    def context_copy(place, half):
        rows = own_len // halves
        return remote(
            context_ref.at[block((place * 2 + other) * halves + half, rows)],
            context_sib.at[block(place * halves + half, rows)],
            context_send.at[place, half],
            context_recv.at[place, half],
            sibling,
        )

    def chunk_rows(place, chunk):
        return block(place * CHUNKS + chunk, step)

    def attn_part(place, chunk):
        return dot_nt(
            context_ref[chunk_rows(place * 2 + core, chunk), :], full_out_ref[...]
        ) + dot_nt(context_sib[chunk_rows(place, chunk), :], out_sib[...])

    def sum_copy(chunk, offset):
        rows = block(chunk, step)
        return remote(
            sum_out.at[offset - 1, rows],
            sum_in.at[levels - offset - 1, rows],
            sum_send.at[chunk, offset - 1],
            sum_recv.at[chunk, levels - offset - 1],
            (row, peer_level(offset) * 2 + core),
        )

    def normed_copy(chunk, offset):
        view = normed_full.at[chunk_rows(level, chunk)]
        return remote(
            view,
            view,
            normed_send.at[chunk, offset - 1],
            normed_recv.at[chunk, levels - offset - 1],
            (row, peer_level(offset) * 2 + core),
        )

    for offset in list(offsets) + [0]:
        place = peer_level(offset)
        for half in range(halves):
            attend_half(place * 2 + other, half)
            context_copy(place, half).start()
            pass_on(1 - half if offset else half)
        if offset == 1:
            await_shards(1)
        for half in range(halves):
            attend_half(place * 2 + core, half)
            if offset == 1 and half == 0:
                await_sibling(1)
            context_copy(place, half).wait_recv()
            per_half = CHUNKS // halves
            for chunk in range(half * per_half, (half + 1) * per_half):
                if offset:
                    sum_out[offset - 1, block(chunk, step), :] = attn_part(place, chunk).astype(
                        low
                    )
                    sum_copy(chunk, offset).start()
            pass_on(1 if offset else half)
    pass_on(len(waiting))
    for copy in swaps:
        copy.wait()
    for copy in far[6:8]:
        copy.start()
    for chunk in range(CHUNKS):
        rows = block(chunk, step)
        summed = own_ref[rows, :].astype(full) + attn_part(level, chunk) + b_out[...]
        for offset in offsets:
            sum_copy(chunk, offset).wait_recv()
        for place in range(levels - 1):
            summed += sum_in[place, rows, :].astype(full)
        normed, inv_std = norm_parts(summed)
        unit1[rows, :] = normed
        inv1[rows, :] = inv_std
        normed_full[chunk_rows(level, chunk), :] = (normed * gain1[...] + shift1[...]).astype(low)
        for offset in offsets:
            normed_copy(chunk, offset).start()
    await_shards(2)
    await_shards(3)
    for kind in range(2, KINDS):
        await_sibling(kind)
        for copy in far[4 + 2 * kind : 6 + 2 * kind]:
            copy.start()
    for chunk in range(CHUNKS):
        for offset in offsets:
            normed_copy(chunk, offset).wait()
            sum_copy(chunk, offset).wait_send()
    for place in range(levels):
        for half in range(halves):
            context_copy(place, half).wait_send()
    for copy in far:
        copy.wait()
    for kind in range(KINDS):
        for hop in range(along - 1):
            for way in range(2):

                @pl.when(line_can_send(way, hop))
                def _():
                    line_copy(kind, way, hop).wait_send()

        @pl.loop(0, along)
        def _(place):
            for offset in range(1, across):
                across_copy(kind, place, offset).wait_send()
            if kind > 0:
                for offset in range(across):
                    core_shard(kind, place, offset).wait_send()

    @pl.loop(0, cols)
    def _(turn):
        for offset in offsets:
            level_copy(turn, offset).wait_send()


def across_of(rows):
    return 2 if rows <= 8 else rows // 4


def front(levels, rows, tables, hidden_in, grads, biases, weights, vectors):
    low, full = jnp.bfloat16, jnp.float32
    shape = jax.ShapeDtypeStruct
    across = across_of(rows)
    along = rows // across
    seq_len, width = hidden_in.shape
    cols = 2 * levels
    own_len = seq_len // cols
    features_all = width * cols
    units = weights[4].shape[1]
    widths = (3 * width, width, units, units)
    others = levels - 1
    stat = shape((seq_len // BLK, 1, width), full)
    hbm = pl.BlockSpec(memory_space=pl.ANY)
    dma = pltpu.SemaphoreType.DMA
    return pl.pallas_call(
        functools.partial(front_kernel, levels, across, along),
        out_shape=(
            shape((seq_len, features_all), low),
            shape((own_len, features_all), low),
            shape((own_len, features_all), low),
            shape((seq_len, width), low),
            shape((seq_len // BLK, BLK, width), low),
            shape((seq_len // BLK, BLK, width), low),
            shape((seq_len, width), low),
            stat,
            stat,
            *(shape((features_all, each), low) for each in widths),
            *(shape((features_all, each), low) for each in widths[1:]),
            shape((levels * own_len, width), low),
            shape((levels * own_len, features_all), low),
            shape((own_len, features_all), full),
            shape((own_len, 1), full),
        ),
        in_specs=[SMEM] * 3 + [VMEM] * 13,
        out_specs=[hbm] * 7 + [VMEM] * 2 + [hbm] + [VMEM, hbm, hbm] * 2 + [VMEM] * 4,
        scratch_shapes=[
            pltpu.VMEM((seq_len, features_all), low),
            pltpu.VMEM((own_len, features_all), low),
            pltpu.VMEM((own_len, features_all), low),
            pltpu.VMEM((seq_len, width), low),
            pltpu.VMEM((seq_len // BLK, BLK, width), low),
            pltpu.VMEM((seq_len // BLK, BLK, width), low),
            pltpu.VMEM((seq_len, width), low),
            pltpu.VMEM((features_all, 3 * width), low),
            *(pltpu.VMEM((features_all, units), low) for _ in range(4)),
            dma((12,)),
            pltpu.VMEM((others, own_len, features_all), low),
            pltpu.VMEM((others, own_len, features_all), low),
            dma((cols, others)),
            dma((cols, others)),
            dma((cols, levels)),
            dma((cols, levels)),
            dma((cols,)),
            dma((cols,)),
            dma((KINDS, 2, along - 1)),
            dma((KINDS, 2, along - 1)),
            dma((KINDS, along, across - 1)),
            dma((KINDS, along, across - 1)),
            dma((KINDS - 1, along, across)),
            dma((KINDS - 1, along, across)),
            dma((levels, 2)),
            dma((levels, 2)),
            *(dma((CHUNKS, others)) for _ in range(4)),
        ],
        compiler_params=pltpu.CompilerParams(
            collective_id=3, has_side_effects=True, vmem_limit_bytes=56 * 1024 * 1024
        ),
        cost_estimate=pl.CostEstimate(
            flops=2 * seq_len * features_all * 3 * width,
            bytes_accessed=20 * 1024 * 1024,
            transcendentals=seq_len * 512 * (width // DH),
        ),
    )(*tables, hidden_in, grads, *biases, *weights, *vectors)


def dot(left, right):
    return jnp.dot(left, right, preferred_element_type=jnp.float32)


def dot_nt(left, right):
    return lax.dot_general(
        left, right, (((1,), (1,)), ((), ())), preferred_element_type=jnp.float32
    )


def dot_tn(left, right):
    return lax.dot_general(
        left, right, (((0,), (0,)), ((), ())), preferred_element_type=jnp.float32
    )


def gelu_parts(values_in):
    factor = math.sqrt(2.0 / math.pi)
    square = values_in * values_in
    bent = jnp.tanh(factor * (values_in + 0.044715 * (values_in * square)))
    half = 0.5 * (1.0 + bent)
    slope = half + (0.5 * values_in) * (1.0 - bent * bent) * (
        factor + (3.0 * 0.044715 * factor) * square
    )
    return (values_in * half, slope)


def norm_parts(summed):
    average = jnp.mean(summed, axis=1, keepdims=True)
    squares = jnp.mean(summed * summed, axis=1, keepdims=True)
    inv_std = lax.rsqrt(squares - average * average + epsilon)
    return ((summed - average) * inv_std, inv_std)


def norm_back(upstream, normed, inv_std, gain_vec):
    scaled = upstream * gain_vec
    left = jnp.mean(scaled, axis=1, keepdims=True)
    right = jnp.mean(scaled * normed, axis=1, keepdims=True)
    return inv_std * (scaled - left - normed * right)


def middle_kernel(
    levels,
    across,
    along,
    length_ref,
    context_far,
    context_sib_far,
    upstream_far,
    out_far,
    out_sib_far,
    up_ref,
    up_sib,
    down_full,
    down_sib,
    normed_full,
    unit1_far,
    inv1,
    gain1,
    shift1,
    b_down,
    gain2,
    shift2,
    b_up_ref,
    layer_out_ref,
    context_grad_ref,
    attn_full,
    small_ref,
    up_small_ref,
    share_down_ref,
    up_own_ref,
    grad_out_ref,
    *more,
):
    up_part_refs, refs = more[: along - 1], more[along - 1 :]
    (
        ffn_full,
        hidden,
        slope,
        pre_grad,
        ffn_keep,
        part_own,
        send_buf,
        recv_buf,
        context_send,
        stage,
        down_sums,
        up_sums,
        down_got,
        up_got,
        down_pass,
        down_in,
        send_sem,
        recv_sem,
        core_send,
        core_recv,
        along_send,
        along_recv,
        across_send,
        across_recv,
        stage_sem,
        context_ref,
        context_sib,
        upstream_ref,
        out_ref,
        out_sib,
        unit1,
        late_sem,
        free_sem,
    ) = refs
    low = jnp.bfloat16
    row, column = lax.axis_index("row"), lax.axis_index("col")
    core = lax.rem(column, 2)
    level = lax.div(column, 2)
    sibling = (row, column + 1 - 2 * core)
    fast, slow = lax.rem(row, across), lax.div(row, across)
    shard = share_down_ref.shape[0]
    own_len = upstream_ref.shape[0]
    units = up_ref.shape[1]
    step = own_len // CHUNKS

    def peer_level(offset):
        return lax.rem(level + offset, levels)

    def fast_peer(offset):
        return slow * across + lax.rem(fast + offset, across)

    late = [
        pltpu.make_async_copy(source, target, late_sem.at[place])
        for place, (source, target) in enumerate(
            [
                (unit1_far, unit1),
                (upstream_far, upstream_ref),
                (context_far, context_ref),
                (context_sib_far, context_sib),
                (out_far, out_ref),
                (out_sib_far, out_sib),
            ]
        )
    ]
    for copy in late:
        copy.start()

    barrier = pltpu.get_barrier_semaphore()
    greeted = [sibling]
    greeted += [(row, peer_level(offset) * 2 + core) for offset in range(1, levels)]
    greeted += [(fast_peer(offset), column) for offset in range(1, across)]
    greeted += [
        (lax.rem(slow + offset, along) * across + fast, column) for offset in range(1, along)
    ]
    for device in greeted:
        pl.semaphore_signal(barrier, inc=1, device_id=device, device_id_type=MESH)
    pl.semaphore_wait(barrier, len(greeted))

    def remote(source, target, send, recv, device):
        return pltpu.make_async_remote_copy(
            src_ref=source,
            dst_ref=target,
            send_sem=send,
            recv_sem=recv,
            device_id=device,
            device_id_type=MESH,
        )

    def block(start, size):
        return pl.ds(pl.multiple_of(start * size, size), size)

    def to_sibling(source, target, place):
        return remote(source, target, core_send.at[place], core_recv.at[place], sibling)

    def rows_of(place, chunk):
        return pl.ds(pl.multiple_of(place * own_len + chunk * step, step), step)

    def own_rows(chunk):
        return pl.ds(pl.multiple_of(chunk * step, step), step)

    def exchange(kind, chunk, offset, source, target):
        return pltpu.make_async_remote_copy(
            src_ref=source,
            dst_ref=target,
            send_sem=send_sem.at[kind - 2, chunk, offset - 1],
            recv_sem=recv_sem.at[kind - 2, chunk, levels - offset - 1],
            device_id=(row, peer_level(offset) * 2 + core),
            device_id_type=MESH,
        )

    def sum_copy(kind, chunk, offset):
        return exchange(
            kind,
            chunk,
            offset,
            send_buf.at[kind // 2 - 1, offset - 1, own_rows(chunk)],
            recv_buf.at[kind // 2 - 1, levels - offset - 1, own_rows(chunk)],
        )

    def spread_copy(kind, chunk, offset):
        whole = {3: ffn_full, 5: attn_full}[kind]
        rows = rows_of(level, chunk)
        return exchange(kind, chunk, offset, whole.at[rows], whole.at[rows])

    def received(kind, chunk):
        return sum(
            recv_buf[kind // 2 - 1, place, own_rows(chunk), :].astype(jnp.float32)
            for place in range(levels - 1)
        )

    offsets = range(1, levels)
    small_ref[...] = jnp.zeros_like(small_ref)
    up_small_ref[...] = jnp.zeros_like(up_small_ref)
    def context_rows(place, chunk):
        start = (place * 2 + core) * own_len + chunk * step
        return pl.ds(pl.multiple_of(start, step), step)

    sides = ((up_ref, down_full), (up_sib, down_sib))

    def feed_forward(place, chunk):
        rows = rows_of(place, chunk)
        normed = normed_full[rows, :]
        total = None
        for side, (up_side, down_side) in enumerate(sides):
            bias = b_up_ref[:, block(column + side * (1 - 2 * core), units)]
            active, bend = gelu_parts(dot(normed, up_side[...]) + bias)
            active = active.astype(low)
            hidden[side, rows, :] = active
            slope[side, rows, :] = bend.astype(low)
            part = dot_nt(active, down_side[...])
            total = part if total is None else total + part
        return total

    @pl.loop(0, CHUNKS)
    def _(chunk):
        for offset in offsets:
            send_buf[0, offset - 1, own_rows(chunk), :] = feed_forward(
                peer_level(offset), chunk
            ).astype(low)
            sum_copy(2, chunk, offset).start()

    for copy in late:
        copy.wait()

    @pl.loop(0, CHUNKS)
    def _(chunk):
        rows = own_rows(chunk)
        part_own[rows, :] = feed_forward(level, chunk)
        normed1 = unit1[rows, :] * gain1[...] + shift1[...]
        summed = normed1 + part_own[rows, :] + b_down[...]
        for offset in offsets:
            sum_copy(2, chunk, offset).wait_recv()
        normed, inv_std = norm_parts(summed + received(2, chunk))
        position = lax.broadcasted_iota(jnp.int32, (step, 1), 0) + (
            column * own_len + chunk * step
        )
        valid = position < length_ref[0]
        layer_out_ref[rows, :] = jnp.where(
            valid, normed * gain2[...] + shift2[...], 0.0
        ).astype(low)
        upstream = jnp.where(valid, upstream_ref[rows, :].astype(jnp.float32), 0.0)
        grad = norm_back(upstream, normed, inv_std, gain2[...])
        ffn_keep[rows, :] = grad
        grad_low = grad.astype(low)
        ffn_full[rows_of(level, chunk), :] = grad_low
        for offset in offsets:
            spread_copy(3, chunk, offset).start()
        small_ref[0:1, :] += jnp.sum(upstream * normed, axis=0, keepdims=True)
        small_ref[1:2, :] += jnp.sum(upstream, axis=0, keepdims=True)
        small_ref[2:3, :] += jnp.sum(grad_low.astype(jnp.float32), axis=0, keepdims=True)

    def feed_back(place, chunk):
        rows = rows_of(place, chunk)
        upstream = ffn_full[rows, :]
        total = None
        for side, (up_side, down_side) in enumerate(sides):
            grad = (
                dot(upstream, down_side[...]) * slope[side, rows, :].astype(jnp.float32)
            ).astype(low)
            pre_grad[side, rows, :] = grad
            up_small_ref[side : side + 1, :] += jnp.sum(
                grad.astype(jnp.float32), axis=0, keepdims=True
            )
            part = dot_nt(grad, up_side[...])
            total = part if total is None else total + part
        return total

    def back_own(chunk):
        part_own[own_rows(chunk), :] = feed_back(level, chunk)
        for offset in offsets:
            spread_copy(3, chunk, levels - offset).wait_recv()

    def back_peers(chunk):
        for offset in offsets:
            send_buf[1, offset - 1, own_rows(chunk), :] = feed_back(
                peer_level(offset), chunk
            ).astype(low)
            sum_copy(4, chunk, offset).start()

    @pl.loop(0, CHUNKS - 1)
    def _(chunk):
        back_own(chunk)
        back_peers(chunk)

    back_own(CHUNKS - 1)

    tile = across * shard
    lefts, rights = (ffn_full, normed_full), (hidden, pre_grad)
    sums, got = (down_sums, up_sums), (down_got, up_got)
    spare = (up_sums, slope.at[0])

    def grad_tile(kind, side, turn):
        return dot_tn(lefts[kind][:, block(turn, tile)], rights[kind][side])

    def core_grad(kind):
        return to_sibling(
            spare[kind].at[: sums[kind].shape[0]], sums[kind], levels + kind
        )

    def across_grad(kind, turn, offset):
        return remote(
            sums[kind].at[block(turn * across + lax.rem(fast + offset, across), shard)],
            got[kind].at[across - offset - 1, block(turn, shard)],
            across_send.at[kind, turn, offset - 1],
            across_recv.at[kind, turn, across - offset - 1],
            (fast_peer(offset), column),
        )

    def own_shard(kind, turn):
        for offset in range(1, across):
            across_grad(kind, turn, offset).wait_recv()
        total = sums[kind][block(turn * across + fast, shard), :].astype(jnp.float32)
        for place in range(across - 1):
            total += got[kind][place, block(turn, shard), :].astype(jnp.float32)
        return total

    def line_peer(shift):
        return ((slow + shift) * across + fast, column)

    def line_copy(kind, way, target):
        return remote(
            line_out[kind].at[way, target],
            line_in[kind].at[way, target],
            along_send.at[kind, way, target],
            along_recv.at[kind, way, target],
            line_peer(1 - 2 * way),
        )

    def line_step(kind, hop):
        for way in range(2):
            position = hop if way == 0 else along - 1 - hop
            targets = range(along - 1, hop, -1) if way == 0 else range(0, along - 1 - hop)

            @pl.when(slow == position)
            def _():
                for target in targets:
                    total = own_shard(kind, target)
                    if hop > 0:
                        line_copy(kind, way, target).wait_recv()
                        total += line_in[kind][way, target].astype(jnp.float32)
                    line_out[kind][way, target] = total.astype(jnp.bfloat16)
                    line_copy(kind, way, target).start()

    def line_finish(kind):
        for way in range(2):

            @pl.when((slow > 0) if way == 0 else (slow < along - 1))
            def _():
                line_copy(kind, way, slow).wait_recv()
                shares[kind][...] += line_in[kind][way, slow].astype(jnp.float32)

    def line_sent(kind):
        for way in range(2):
            for target in range(along):

                @pl.when((slow < target) if way == 0 else (slow > target))
                def _():
                    line_copy(kind, way, target).wait_send()

    def sum_grad(kind):
        core_grad(kind).wait_recv()

        @pl.loop(0, along)
        def _(turn):
            rows = block(turn, tile)
            sums[kind][rows, :] = (
                grad_tile(kind, 0, turn) + sums[kind][rows, :].astype(jnp.float32)
            ).astype(low)
            for offset in range(1, across):
                across_grad(kind, turn, offset).start()

    line_out, line_in, shares = (down_pass,), (down_in,), (share_down_ref,)
    def give_grad(kind):
        @pl.loop(0, along)
        def _(turn):
            spare[kind][block(turn, tile), :] = grad_tile(kind, 1, turn).astype(low)

    give_grad(0)
    core_grad(0).start()
    back_peers(CHUNKS - 1)
    core_grad(0).wait_send()
    pl.semaphore_signal(free_sem, inc=1, device_id=sibling, device_id_type=MESH)
    sum_grad(0)
    give_grad(1)
    pl.semaphore_wait(free_sem, 1)
    core_grad(1).start()
    sum_grad(1)

    @pl.loop(0, CHUNKS)
    def _(chunk):
        rows = own_rows(chunk)
        upstream = ffn_keep[rows, :] + part_own[rows, :]
        for offset in offsets:
            sum_copy(4, chunk, offset).wait_recv()
        upstream = upstream + received(4, chunk)
        normed = unit1[rows, :]
        grad_low = norm_back(upstream, normed, inv1[rows, :], gain1[...]).astype(low)
        attn_full[rows_of(level, chunk), :] = grad_low
        for offset in offsets:
            spread_copy(5, chunk, offset).start()
        small_ref[3:4, :] += jnp.sum(upstream * normed, axis=0, keepdims=True)
        small_ref[4:5, :] += jnp.sum(upstream, axis=0, keepdims=True)
        small_ref[5:6, :] += jnp.sum(grad_low.astype(jnp.float32), axis=0, keepdims=True)

    share_down_ref[...] = own_shard(0, slow)
    line_step(0, 0)

    def context_back(place, chunk):
        rows = rows_of(place, chunk)
        upstream = attn_full[rows, :]
        context_grad_ref[context_rows(place, chunk), :] = dot(upstream, out_ref[...]).astype(low)
        context_send[rows, :] = dot(upstream, out_sib[...]).astype(low)

    for chunk in range(CHUNKS):
        context_back(level, chunk)
        for offset in offsets:
            spread_copy(5, chunk, levels - offset).wait_recv()
            context_back(peer_level(offset), chunk)
        if 0 < chunk < along - 1:
            line_step(0, chunk)
    for hop in range(CHUNKS, along - 1):
        line_step(0, hop)

    back_copies = [
        to_sibling(
            context_send.at[pl.ds(place * own_len, own_len)],
            context_grad_ref.at[
                pl.ds(pl.multiple_of((place * 2 + core) * own_len, own_len), own_len)
            ],
            place,
        )
        for place in range(levels)
    ]
    for copy in back_copies:
        copy.start()

    own_context = jnp.concatenate(
        [
            context_ref[
                pl.ds(pl.multiple_of((place * 2 + core) * own_len, own_len), own_len), :
            ]
            for place in range(levels)
        ],
        axis=0,
    )

    def out_put(side):
        return pltpu.make_async_copy(stage.at[side], grad_out_ref.at[side], stage_sem.at[side])

    for side, right in enumerate((own_context, context_sib[...])):
        stage[side] = dot_tn(attn_full[...], right).astype(low)
        out_put(side).start()
    for shift in range(1, along):
        up_part_refs[shift - 1][...] = own_shard(1, lax.rem(slow + shift, along)).astype(low)
    up_own_ref[...] = own_shard(1, slow)
    line_finish(0)
    for side in range(2):
        out_put(side).wait()
    core_grad(1).wait_send()
    line_sent(0)

    @pl.loop(0, along)
    def _(place):
        for offset in range(1, across):
            across_grad(0, place, offset).wait_send()
            across_grad(1, place, offset).wait_send()

    for copy in back_copies:
        copy.wait()
    for kind in range(2, 6):

        @pl.loop(0, CHUNKS)
        def _(chunk):
            for offset in offsets:
                if kind % 2:
                    spread_copy(kind, chunk, offset).wait_send()
                else:
                    sum_copy(kind, chunk, offset).wait_send()


def middle(
    levels,
    rows,
    length,
    context,
    context_sib,
    upstream,
    weights,
    normed_full,
    unit1,
    inv1,
    vectors,
    b_up,
):
    low, full = jnp.bfloat16, jnp.float32
    across = across_of(rows)
    along = rows // across
    own_len, features = upstream.shape
    seq_len, width = context.shape
    units = weights[2].shape[1]
    shard = features // rows
    tokens = levels * own_len
    others = levels - 1
    shape = jax.ShapeDtypeStruct
    hbm = pl.BlockSpec(memory_space=pl.ANY)
    dma = pltpu.SemaphoreType.DMA
    vmem = pltpu.VMEM
    return pl.pallas_call(
        functools.partial(middle_kernel, levels, across, along),
        out_shape=(
            shape((own_len, features), low),
            shape((seq_len, width), low),
            shape((tokens, features), low),
            shape((8, features), full),
            shape((2, units), full),
            shape((shard, units), full),
            shape((shard, units), full),
            shape((2, features, width), low),
            *(shape((shard, units), low) for _ in range(along - 1)),
        ),
        in_specs=[SMEM] + [hbm] * 5 + [VMEM] * 5 + [hbm] + [VMEM] * 7,
        out_specs=[VMEM] * 7 + [hbm] + [VMEM] * (along - 1),
        scratch_shapes=[
            vmem((tokens, features), low),
            vmem((2, tokens, units), low),
            vmem((2, max(tokens, features), units), low),
            vmem((2, tokens, units), low),
            vmem((own_len, features), full),
            vmem((own_len, features), full),
            vmem((2, others, own_len, features), low),
            vmem((2, others, own_len, features), low),
            vmem((tokens, width), low),
            vmem((2, features, width), low),
            vmem((features, units), low),
            vmem((features, units), low),
            vmem((across - 1, along * shard, units), low),
            vmem((across - 1, along * shard, units), low),
            vmem((2, along, shard, units), low),
            vmem((2, along, shard, units), low),
            dma((4, CHUNKS, others)),
            dma((4, CHUNKS, others)),
            dma((levels + 2,)),
            dma((levels + 2,)),
            dma((1, 2, along)),
            dma((1, 2, along)),
            dma((2, along, across - 1)),
            dma((2, along, across - 1)),
            dma((2,)),
            vmem((seq_len, width), low),
            vmem((tokens, width), low),
            vmem((own_len, features), low),
            vmem((features, width), low),
            vmem((features, width), low),
            vmem((own_len, features), full),
            dma((6,)),
            pltpu.SemaphoreType.REGULAR,
        ],
        compiler_params=pltpu.CompilerParams(
            collective_id=1, has_side_effects=True, vmem_limit_bytes=62 * 1024 * 1024
        ),
        cost_estimate=pl.CostEstimate(
            flops=2 * tokens * features * (12 * units + 6 * width),
            bytes_accessed=20 * 1024 * 1024,
            transcendentals=2 * tokens * units,
        ),
    )(
        length,
        context,
        context_sib,
        upstream,
        *weights,
        normed_full,
        unit1,
        inv1,
        *vectors,
        b_up,
    )


def end_kernel(
    levels,
    across,
    along,
    query_key_value_ref,
    weights_ref,
    features_ref,
    attn_ref,
    layer_ref,
    small_ref,
    up_small_ref,
    bias_ref,
    out_ref,
    grad_input_ref,
    layer_out_ref,
    small_out_ref,
    share_ref,
    out_sib,
    sums,
    got,
    line_out,
    line_in,
    core_out,
    core_in,
    level_out,
    level_in,
    attn_in,
    attn_own,
    small_sums,
    small_in,
    core_send,
    core_recv,
    part_send,
    part_recv,
    level_send,
    level_recv,
    layer_send,
    layer_recv,
    across_send,
    across_recv,
    along_send,
    along_recv,
    small_send,
    small_recv,
    keep_sem,
):
    low, full = jnp.bfloat16, jnp.float32
    row, column = lax.axis_index("row"), lax.axis_index("col")
    core, level = lax.rem(column, 2), lax.div(column, 2)
    fast, slow = lax.rem(row, across), lax.div(row, across)
    cols = 2 * levels
    seq_len = features_ref.shape[0]
    own_len = seq_len // cols
    width = grad_input_ref.shape[1]
    shard = share_ref.shape[0]
    other = 1 - core
    sibling = (row, level * 2 + other)
    offsets = range(1, levels)

    def peer_level(offset):
        return lax.rem(level + offset, levels)

    def fast_peer(offset):
        return slow * across + lax.rem(fast + offset, across)

    def slow_peer(offset):
        return lax.rem(slow + offset, along) * across + fast

    barrier = pltpu.get_barrier_semaphore()
    greeted = [sibling]
    for offset in offsets:
        greeted += [(row, peer_level(offset) * 2 + core), (row, peer_level(offset) * 2 + other)]
    greeted += [(fast_peer(offset), column) for offset in range(1, across)]
    greeted += [(slow_peer(offset), column) for offset in range(1, along)]
    for device in greeted:
        pl.semaphore_signal(barrier, inc=1, device_id=device, device_id_type=MESH)
    pl.semaphore_wait(barrier, len(greeted))

    def remote(source, target, send, recv, device):
        return pltpu.make_async_remote_copy(
            src_ref=source,
            dst_ref=target,
            send_sem=send,
            recv_sem=recv,
            device_id=device,
            device_id_type=MESH,
        )

    def block(start, size):
        return pl.ds(pl.multiple_of(start * size, size), size)

    out_copy = remote(out_ref.at[1], out_sib, core_send.at[0], core_recv.at[0], sibling)
    attn_copy = remote(
        attn_ref.at[:, block(level * 2 + other, width)],
        attn_in,
        core_send.at[1],
        core_recv.at[1],
        sibling,
    )

    partners = []
    bit = 1
    while bit < levels:
        partners.append((row, (level + bit - 2 * bit * lax.rem(lax.div(level, bit), 2)) * 2 + core))
        bit *= 2
    bit = 1
    while bit < across * along:
        partners.append((row + bit - 2 * bit * lax.rem(lax.div(row, bit), 2), column))
        bit *= 2
    partners.append(sibling)

    def small_copy(turn):
        return remote(
            small_sums.at[turn],
            small_in.at[turn],
            small_send.at[turn],
            small_recv.at[turn],
            partners[turn],
        )

    small_turn = [0]

    def small_step():
        turn = small_turn[0]
        if turn > len(partners):
            return
        if turn > 0:
            small_copy(turn - 1).wait()
            small_sums[turn] = small_sums[turn - 1] + small_in[turn - 1]
        if turn < len(partners):
            small_copy(turn).start()
        small_turn[0] += 1

    def layer_copy(target, place_out, place_in):
        return remote(
            layer_ref.at[:, block(target, width)],
            layer_out_ref.at[block(column, own_len)],
            layer_send.at[place_out],
            layer_recv.at[place_in],
            (row, target),
        )

    layer_copies = [layer_copy(level * 2 + other, 0, 0)]
    for offset in offsets:
        back = levels - offset
        layer_copies.append(
            layer_copy(peer_level(offset) * 2 + core, 2 * offset - 1, 2 * back - 1)
        )
        layer_copies.append(layer_copy(peer_level(offset) * 2 + other, 2 * offset, 2 * back))
    layer_keep = pltpu.make_async_copy(
        layer_ref.at[:, block(column, width)], layer_out_ref.at[block(column, own_len)], keep_sem.at[0]
    )
    attn_keep = pltpu.make_async_copy(
        attn_ref.at[:, block(column, width)], attn_own, keep_sem.at[1]
    )
    attn_keep.start()

    features_all = weights_ref.shape[0]
    units = up_small_ref.shape[1]
    first_up = small_ref.shape[0]
    small_sums[0] = jnp.zeros_like(small_in[0])
    small_sums[0, :first_up, :] = small_ref[...]
    for side in range(2):
        start = (column + side * (1 - 2 * core)) * units
        small_sums[
            0,
            pl.ds(first_up + lax.div(start, features_all), 1),
            pl.ds(pl.multiple_of(lax.rem(start, features_all), units), units),
        ] = up_small_ref[side : side + 1, :]
    first_bias = small_in.shape[1] - 4
    small_sums[0, first_bias : first_bias + 2, block(column, width)] = bias_ref[...]
    small_step()
    out_copy.start()
    attn_copy.start()
    layer_keep.start()
    for copy in layer_copies:
        copy.start()

    def input_part(turn, target):
        return dot_nt(
            query_key_value_ref[block(turn, own_len), :], weights_ref[block(target, width), :]
        )

    def part_copy(turn, place):
        rows = block(turn, own_len)
        return remote(
            core_out.at[place, rows],
            core_in.at[place, rows],
            part_send.at[turn, place],
            part_recv.at[turn, place],
            sibling,
        )

    def give_core():
        @pl.loop(0, cols)
        def _(turn):
            for place in range(levels):
                core_out[place, block(turn, own_len), :] = input_part(
                    turn, place * 2 + other
                ).astype(low)
                part_copy(turn, place).start()

    def across_copy(turn, offset):
        return remote(
            sums.at[block(turn * across + lax.rem(fast + offset, across), shard)],
            got.at[across - offset - 1, block(turn, shard)],
            across_send.at[turn, offset - 1],
            across_recv.at[turn, across - offset - 1],
            (fast_peer(offset), column),
        )

    def weight_grad(turn):
        rows = block(turn, across * shard)
        sums[rows, : 3 * width] = dot_tn(features_ref[:, rows], query_key_value_ref[...]).astype(
            low
        )
        sums[rows, 3 * width :] = (
            out_ref[0, rows, :].astype(full) + out_sib[rows, :].astype(full)
        ).astype(low)
        for offset in range(1, across):
            across_copy(turn, offset).start()

    def level_copy(turn, offset):
        rows = block(turn, own_len)
        return remote(
            level_out.at[offset - 1, rows],
            level_in.at[levels - offset - 1, rows],
            level_send.at[turn, offset - 1],
            level_recv.at[turn, levels - offset - 1],
            (row, peer_level(offset) * 2 + core),
        )

    def give_levels():
        @pl.loop(0, cols)
        def _(turn):
            rows = block(turn, own_len)
            for offset in offsets:
                place = peer_level(offset)
                part = input_part(turn, place * 2 + core)
                part_copy(turn, place).wait_recv()
                level_out[offset - 1, rows, :] = (
                    part + core_in[place, rows, :].astype(full)
                ).astype(low)
                level_copy(turn, offset).start()

    def own_shard(turn):
        for offset in range(1, across):
            across_copy(turn, offset).wait_recv()
        total = sums[block(turn * across + fast, shard), :].astype(full)
        for place in range(across - 1):
            total += got[place, block(turn, shard), :].astype(full)
        return total

    def line_copy(way, target):
        return remote(
            line_out.at[way, target],
            line_in.at[way, target],
            along_send.at[way, target],
            along_recv.at[way, target],
            ((slow + 1 - 2 * way) * across + fast, column),
        )

    def line_step(hop, near):
        if hop >= along - 1 - near:
            return
        for way in range(2):
            target = along - 1 - near if way == 0 else near
            position = hop if way == 0 else along - 1 - hop

            @pl.when(slow == position)
            def _():
                total = own_shard(target)
                if hop > 0:
                    line_copy(way, target).wait_recv()
                    total += line_in[way, target].astype(full)
                line_out[way, target] = total.astype(low)
                line_copy(way, target).start()

    def finish_input(turn, attn_part):
        rows = block(turn, own_len)
        total = input_part(turn, column) + attn_part.astype(full)
        part_copy(turn, level).wait_recv()
        total += core_in[level, rows, :].astype(full)
        for offset in offsets:
            level_copy(turn, offset).wait_recv()
        for place in range(levels - 1):
            total += level_in[place, rows, :].astype(full)
        grad_input_ref[rows, :] = total.astype(low)

    ends = [turn for place in range(along // 2) for turn in (along - 1 - place, place)]
    out_copy.wait()
    small_step()
    for place, turn in enumerate(ends):
        weight_grad(turn)
        if place % 2:
            small_step()
    give_core()
    small_step()
    give_levels()
    small_step()
    line_steps = sorted(
        ((hop, near) for near in range(along - 1) for hop in range(along - 1 - near)),
        key=lambda step: step[0] + 2 * step[1],
    )
    for step in line_steps[: len(line_steps) // 3]:
        line_step(*step)
    attn_keep.wait()
    attn_copy.wait()
    for place in range(levels):
        for step in line_steps[len(line_steps) // 3 :][place::levels]:
            line_step(*step)
        rows = block(place, own_len)
        finish_input(place * 2 + core, attn_own[rows, :])
        finish_input(place * 2 + other, attn_in[rows, :])
    share_ref[...] = own_shard(slow)
    while small_turn[0] <= len(partners):
        small_step()
    small_out_ref[...] = small_sums[len(partners)]

    for way in range(2):

        @pl.when((slow > 0) if way == 0 else (slow < along - 1))
        def _():
            line_copy(way, slow).wait_recv()
            share_ref[...] += line_in[way, slow].astype(full)

    layer_keep.wait()
    for copy in layer_copies:
        copy.wait()
    for way in range(2):
        for target in range(along):

            @pl.when((slow < target) if way == 0 else (slow > target))
            def _():
                line_copy(way, target).wait_send()

    @pl.loop(0, along)
    def _(turn):
        for offset in range(1, across):
            across_copy(turn, offset).wait_send()

    @pl.loop(0, cols)
    def _(turn):
        for place in range(levels):
            part_copy(turn, place).wait_send()
        for offset in offsets:
            level_copy(turn, offset).wait_send()


def finish(
    levels, rows, query_key_value, weights, features, attn_full, layer_own, small, up_small, bias, out
):
    low, full = jnp.bfloat16, jnp.float32
    shape = jax.ShapeDtypeStruct
    across = across_of(rows)
    along = rows // across
    seq_len, features_all = features.shape
    width = query_key_value.shape[1] // 3
    own_len = layer_own.shape[0]
    shard = features_all // rows
    others = levels - 1
    cols = 2 * levels
    turns = 1 + (levels - 1).bit_length() + (rows - 1).bit_length()
    small_rows = small.shape[0] + up_small.shape[1] * cols // features_all + 4
    dma = pltpu.SemaphoreType.DMA
    vmem = pltpu.VMEM
    return pl.pallas_call(
        functools.partial(end_kernel, levels, across, along),
        out_shape=(
            shape((seq_len, width), low),
            shape((seq_len, width), low),
            shape((small_rows, features_all), full),
            shape((shard, 4 * width), full),
        ),
        in_specs=[VMEM] * 3 + [pl.BlockSpec(memory_space=pl.ANY)] * 2 + [VMEM] * 4,
        out_specs=[VMEM] * 4,
        scratch_shapes=[
            vmem((features_all, width), low),
            vmem((features_all, 4 * width), low),
            vmem((across - 1, along * shard, 4 * width), low),
            vmem((2, along, shard, 4 * width), low),
            vmem((2, along, shard, 4 * width), low),
            vmem((levels, seq_len, width), low),
            vmem((levels, seq_len, width), low),
            vmem((others, seq_len, width), low),
            vmem((others, seq_len, width), low),
            vmem((levels * own_len, width), low),
            vmem((levels * own_len, width), low),
            vmem((turns + 1, small_rows, features_all), full),
            vmem((turns, small_rows, features_all), full),
            dma((2,)),
            dma((2,)),
            dma((cols, levels)),
            dma((cols, levels)),
            dma((cols, others)),
            dma((cols, others)),
            dma((cols,)),
            dma((cols,)),
            dma((along, across - 1)),
            dma((along, across - 1)),
            dma((2, along)),
            dma((2, along)),
            dma((turns,)),
            dma((turns,)),
            dma((2,)),
        ],
        compiler_params=pltpu.CompilerParams(
            collective_id=2, has_side_effects=True, vmem_limit_bytes=60 * 1024 * 1024
        ),
        cost_estimate=pl.CostEstimate(
            flops=4 * seq_len * features_all * 3 * width,
            bytes_accessed=20 * 1024 * 1024,
            transcendentals=0,
        ),
    )(query_key_value, weights, features, attn_full, layer_own, small, up_small, bias, out)


def last_kernel(
    grad_input_ref,
    layer_ref,
    small_ref,
    share_ref,
    down_ref,
    up_own_ref,
    up_first_ref,
    *refs,
):
    more, outs = refs[: len(refs) - 17], refs[len(refs) - 17 :]
    (
        layer_out,
        grad_input,
        grad_query,
        bias_query,
        grad_key,
        grad_value,
        bias_value,
        grad_out,
        bias_out,
        gain1,
        shift1,
        grad_up,
        bias_up,
        grad_down,
        bias_down,
        gain2,
        shift2,
    ) = outs
    grad_input[...] = grad_input_ref[...]
    layer_out[...] = layer_ref[...]
    width = grad_query.shape[1]
    for place, ref in enumerate((grad_query, grad_key, grad_value)):
        ref[...] = share_ref[:, place * width : (place + 1) * width]
    grad_out[...] = share_ref[:, 3 * width :].T
    grad_down[...] = down_ref[...].T
    total = up_own_ref[...]
    for ref in (up_first_ref, *more):
        total += ref[...].astype(jnp.float32)
    grad_up[...] = total
    features_all = small_ref.shape[1]
    last = small_ref.shape[0] - 4
    for place, ref in (
        (0, gain2),
        (1, shift2),
        (2, bias_down),
        (3, gain1),
        (4, shift1),
        (5, bias_out),
        (last, bias_query),
        (last + 1, bias_value),
    ):
        ref[...] = small_ref[place : place + 1, :]
    for place in range(8, last):
        bias_up[:, (place - 8) * features_all : (place - 7) * features_all] = small_ref[
            place : place + 1, :
        ]


def put_out(grad_input, layer_out, small, share, down, up_own, up_others):
    low, full = jnp.bfloat16, jnp.float32
    shape = jax.ShapeDtypeStruct
    seq_len, width = grad_input.shape
    shard, units = up_own.shape
    features_all = small.shape[1]
    vector = shape((1, features_all), full)
    units_all = (small.shape[0] - 12) * features_all
    grad = shape((shard, width), full)
    return pl.pallas_call(
        last_kernel,
        out_shape=(
            shape((seq_len, width), low),
            shape((seq_len, width), low),
            grad,
            vector,
            grad,
            grad,
            vector,
            shape((width, shard), full),
            vector,
            vector,
            vector,
            shape((shard, units), full),
            shape((1, units_all), full),
            shape((units, shard), full),
            vector,
            vector,
            vector,
        ),
        in_specs=[VMEM] * (6 + len(up_others)),
        out_specs=[VMEM] * 17,
        compiler_params=pltpu.CompilerParams(vmem_limit_bytes=60 * 1024 * 1024),
    )(grad_input, layer_out, small, share, down, up_own, *up_others)


def on_device(
    hidden_in,
    out_grad,
    lengths,
    global_blocks,
    rand_blocks,
    w_query,
    b_query,
    w_key,
    w_value,
    b_value,
    w_out,
    b_out,
    ln1_gain,
    ln1_bias,
    w_up,
    b_up,
    w_down,
    b_down,
    ln2_gain,
    ln2_bias,
):
    cols = lax.axis_size("col")
    rows = lax.axis_size("row")
    tables = (lengths, global_blocks.reshape(-1), rand_blocks.reshape(-1))
    as_row = lambda vector: vector[None, :]
    (
        features,
        own_features,
        upstream,
        queries,
        key_rows,
        value_rows,
        context,
        highest,
        scale,
        full_qkv,
        full_out,
        full_up,
        full_down,
        out_sib,
        up_sib,
        down_sib,
        context_sib,
        normed_full,
        unit1,
        inv1,
    ) = front(
        cols // 2,
        rows,
        tables,
        hidden_in,
        out_grad,
        (as_row(b_query), as_row(b_value)),
        (w_query, w_key, w_value, w_out, w_up, w_down),
        (as_row(b_out), as_row(ln1_gain), as_row(ln1_bias)),
    )
    (
        layer_own,
        context_grad,
        attn_full,
        small,
        up_small,
        down_share,
        up_own,
        grad_out,
        *up_part,
    ) = middle(
        cols // 2,
        rows,
        lengths,
        context,
        context_sib,
        upstream,
        (full_out, out_sib, full_up, up_sib, full_down, down_sib),
        normed_full,
        unit1,
        inv1,
        tuple(as_row(each) for each in (ln1_gain, ln1_bias, b_down, ln2_gain, ln2_bias)),
        as_row(b_up),
    )
    across = across_of(rows)
    up_others = [
        lax.ppermute(
            up_part[shift - 1],
            "row",
            [(place, (place + shift * across) % rows) for place in range(rows)],
        )
        for shift in range(1, rows // across)
    ]
    query_key_value, bias_sums = attend_back(
        queries, key_rows, value_rows, tables, (highest, scale), context_grad
    )
    grad_input, layer_out, small, share = finish(
        cols // 2,
        rows,
        query_key_value,
        full_qkv,
        features,
        attn_full,
        layer_own,
        small,
        up_small,
        bias_sums,
        grad_out,
    )
    outs = put_out(grad_input, layer_out, small, share, down_share, up_own, up_others)
    return tuple(each.reshape(-1) if each.shape[0] == 1 else each for each in outs)


def solution(mesh):
    placed = (
        P("row", "col"),
        P("row", "col"),
        P("row"),
        P("row", None),
        P("row", None, "col", None),
        P("row", "col"),
        P(),
        P("row", "col"),
        P("row", "col"),
        P(),
        P("col", "row"),
        P(),
        P(),
        P(),
        P("row", "col"),
        P(),
        P("col", "row"),
        P(),
        P(),
        P(),
    )
    return jax.shard_map(
        on_device,
        mesh=mesh,
        in_specs=placed,
        out_specs=(
            P("row", "col"),
            P("row", "col"),
            P("row", "col"),
            P(),
            P("row", "col"),
            P("row", "col"),
            P(),
            P("col", "row"),
            P(),
            P(),
            P(),
            P("row", "col"),
            P(),
            P("col", "row"),
            P(),
            P(),
            P(),
        ),
        check_vma=False,
    )
```
